32 devices in a mesh: grp: 4 (over z), gx: 2 (over y), gy: 4 (over x, core).
Axes of the slice: x: 2, y: 2, z: 4, core: 2. Of those that a mesh axis runs over, the one named last changes fastest.
Arguments:
- populations: float32 [27, 8, 32, 512], P(None, 'gx', 'gy', 'grp'), may hold values from 0 to 1, as said below
- thermal: float32 [7, 8, 32, 512], P(None, ('gx', 'grp'), 'gy'), may hold values from 0 to 1, as said below
- velocity_prev: float32 [3, 8, 32, 512], P(None, 'gx', 'gy', 'grp'), may hold values from -0.3 to 0.3
- solid: int32 [8, 32, 512], P('gx', 'gy', 'grp'), may hold values 0 or 1
- phase_ids: int32 [8, 32, 512], P(('gx', 'grp'), 'gy'), may hold values from 0 to 3
- conductivity: float32 [4], replicated, may hold values from 0.02 to 0.3
- rates: float32 [27], replicated, may hold values from 0.7 to 1.7
Outputs:
- populations_out: float32 [27, 8, 32, 512], P(None, 'gx', 'gy', 'grp')
- thermal_out: float32 [7, 8, 32, 512], P(None, ('gx', 'grp'), 'gy')
The draws below stay inside these ranges and needn't reach their ends.
Inputs may be any that keep to these rules, and one draw needn't show every extreme that they name: `populations`: positive. `thermal`: positive.
All inputs are finite; a program needn't handle non-finite values. No bound on the sum of `solid` on one device may be relied on, other than what follows from the above.
Results may differ from the reference program's by a relative error of at most 0.0001.
Values sent between devices are 32-bit elements; how exact they have to be, the bound alone decides.
No kernel may reach another device: no remote copies, remote signals or barrier semaphores. Data moves between devices by JAX's collectives and lax.ppermute only.
A program may use at most 64 MiB of HBM per device.

```python
import math
import jax
import jax.numpy as jnp
import numpy as np
from jax import lax

STEPS = 4
WINDOWS = 2
PHASES = 4
NX = 8
NY = 32
NZ = 512


OFFSET_TABLE = [(number // 9 - 1, number // 3 % 3 - 1, number % 3 - 1) for number in range(27)]


LATTICE_WEIGHTS = np.array([np.prod([2.0 / 3.0 if component == 0 else 1.0 / 6.0 for component in triple]) for triple in OFFSET_TABLE])


HEAT_WEIGHTS = np.array([0.25] + [0.125] * 6)


def draw_populations(key, part):
    weights = jnp.asarray(LATTICE_WEIGHTS, jnp.float32)
    noise = jax.random.normal(jax.random.fold_in(key, 12), (27, NX, NY, NZ), jnp.float32)
    factor = jnp.exp(0.25 * jnp.clip(noise, -3.0, 3.0))
    return weights[:, None, None, None] * factor


def draw_thermal(key, part):
    weights = jnp.asarray(HEAT_WEIGHTS, jnp.float32)
    level = jax.random.uniform(jax.random.fold_in(key, 23), (NX, NY, NZ), jnp.float32, 0.5, 1.5)
    noise = jax.random.normal(jax.random.fold_in(key, 24), (7, NX, NY, NZ), jnp.float32)
    factor = jnp.exp(0.2 * jnp.clip(noise, -3.0, 3.0))
    return weights[:, None, None, None] * level[None] * factor


def touch_ends(values, key, least, top_value):
    longest = values.shape.index(max(values.shape))
    spots = []
    for shift in (0, 1):
        where = [jax.random.randint(jax.random.fold_in(key, axis), (), 0, length) for axis, length in enumerate(values.shape)]
        where[longest] = (where[longest] + shift) % values.shape[longest]
        spots.append(tuple(where))
    return values.at[spots[0]].set(least).at[spots[1]].set(top_value)


def block_levels(own_key, extent, split, least, high):
    def one(dim, shards_of):
        steps = jax.random.uniform(jax.random.fold_in(jax.random.fold_in(own_key, 6), dim), (shards_of,), jnp.float32, least / len(split), high / len(split))
        return jnp.repeat(jnp.exp(steps), extent[dim] // shards_of).reshape((-1,) + (1,) * (len(extent) - dim - 1))

    factor_of = one(*split[0])
    for cut in split[1:]:
        factor_of = factor_of * one(*cut)
    return factor_of


def bell_draw(own_key, shape, deviation, bound, split=(), held_as=jnp.bfloat16):
    values = jax.random.normal(own_key, shape, jnp.float32) * deviation
    if len(split) > 0:
        values = block_levels(own_key, shape, split, -0.22, 0.18) * values
    return jnp.clip(values, min=-bound, max=bound).astype(held_as)


def setup_inputs(seed: int = 0) -> dict:
    splits = jax.random.split(jax.random.key(seed), 8)
    populations = draw_populations(jax.random.fold_in(splits[7], 71), 0)
    thermal = draw_thermal(jax.random.fold_in(splits[7], 71), 0)
    velocity_prev = bell_draw(splits[2], (3, NX, NY, NZ), 0.1, 0.3, ((1, 2), (2, 4), (3, 4)), jnp.float32)
    solid = touch_ends((jax.random.randint(splits[3], (NX, NY, NZ), 0, 4) < 1).astype(jnp.int32), jax.random.fold_in(splits[3], 1), 0, 1)
    phase_ids = touch_ends(jax.random.randint(splits[4], (NX, NY, NZ), 0, PHASES), jax.random.fold_in(splits[4], 1), 0, PHASES - 1).astype(jnp.int32)
    conductivity = jnp.clip(jnp.exp(jax.random.uniform(splits[5], (PHASES,), jnp.float32, math.log(0.02), math.log(0.3))), 0.02, 0.3)
    rates = jnp.clip(jax.random.uniform(splits[6], (27,), jnp.float32, 0.7, 1.7), 0.7, 1.7)
    return dict(populations=populations, thermal=thermal, velocity_prev=velocity_prev, solid=solid, phase_ids=phase_ids, conductivity=conductivity, rates=rates)


HIGHEST = lax.Precision.HIGHEST
BUOYANCY = 0.03
REFERENCE_HEAT = 1.0
OFFSET_TABLE = [(number // 9 - 1, (number // 3) % 3 - 1, number % 3 - 1) for number in range(27)]
LATTICE_WEIGHTS = np.array([np.prod([2.0 / 3.0 if component == 0 else 1.0 / 6.0 for component in triple]) for triple in OFFSET_TABLE])
VANDERMONDE = np.array([[1.0, 1.0, 1.0], [-1.0, 0.0, 1.0], [1.0, 0.0, 1.0]])
VANDER_INVERSE = np.array([[0.0, -0.5, 0.5], [1.0, 0.0, -1.0], [0.0, 0.5, 0.5]])
MOMENT_MATRIX = np.kron(np.kron(VANDERMONDE, VANDERMONDE), VANDERMONDE)
MOMENT_INVERSE = np.kron(np.kron(VANDER_INVERSE, VANDER_INVERSE), VANDER_INVERSE)
RELAXED = np.array([0.0 if number in (0, 1, 3, 9) else 1.0 for number in range(27)])
SUMMING = np.concatenate([np.ones((1, 27)), 1.0 * np.array(OFFSET_TABLE).T], axis=0)
HEAT_WEIGHTS = np.array([0.25] + [0.125] * 6)
HEAT_TABLE = [(0, 0, 0), (1, 0, 0), (-1, 0, 0), (0, 1, 0), (0, -1, 0), (0, 0, 1), (0, 0, -1)]


def flow_state(flat, heat_flat):
    sums = jnp.dot(jnp.asarray(SUMMING, jnp.float32), flat, precision=HIGHEST)
    density = sums[0]
    force = BUOYANCY * (heat_flat - REFERENCE_HEAT)
    speed = jnp.stack([sums[1], sums[2], sums[3] + 0.5 * force]) / density
    return density, force, speed


def collide(popul, heat, rates):
    flat = popul.reshape(27, -1)
    density, force, speed = flow_state(flat, heat.reshape(-1))
    along = jnp.dot(jnp.asarray(SUMMING[1:].T, jnp.float32), speed, precision=HIGHEST)
    square = jnp.sum(speed * speed, axis=0)
    balance = density * jnp.asarray(LATTICE_WEIGHTS, jnp.float32)[:, None] * (1.0 + 3.0 * along + 4.5 * along * along - 1.5 * square)
    scaled = jnp.asarray(MOMENT_INVERSE, jnp.float32) * (rates * jnp.asarray(RELAXED, jnp.float32))[None, :]
    relax = jnp.dot(scaled, jnp.asarray(MOMENT_MATRIX, jnp.float32), precision=HIGHEST)
    post = flat - jnp.dot(relax, flat - balance, precision=HIGHEST) + jnp.asarray(MOMENT_INVERSE[:, 1], jnp.float32)[:, None] * force[None, :]
    return post.reshape(popul.shape)


def flow_speed(popul, heat, solid):
    density, force, speed = flow_state(popul.reshape(27, -1), heat.reshape(-1))
    return jnp.where(solid[None] == 0, speed.reshape((3,) + solid.shape), 0.0)


def heat_collide(heat_pops, speed, relax_time):
    total = jnp.sum(heat_pops, axis=0)
    still = jnp.zeros_like(speed[0])
    along = jnp.stack([still, speed[0], -speed[0], speed[1], -speed[1], speed[2], -speed[2]])
    balance = jnp.asarray(HEAT_WEIGHTS, jnp.float32)[:, None, None, None] * total[None] * (1.0 + 4.0 * along)
    return heat_pops - (heat_pops - balance) / relax_time[None]


def relaxation(phase_ids, conductivity):
    levels = jnp.arange(conductivity.shape[0], dtype=jnp.int32)
    chosen = jnp.sum(jnp.where(phase_ids[None] == levels[:, None, None, None], conductivity[:, None, None, None], 0.0), axis=0)
    return 0.5 + 4.0 * chosen


def stream_flow(post, popul, solid):
    fluid_cells = solid == 0
    layers = []
    for number in range(27):
        offset_triple = OFFSET_TABLE[number]
        arrived = jnp.roll(post[number], offset_triple, axis=(0, 1, 2))
        blocked = jnp.roll(solid, offset_triple, axis=(0, 1, 2)) != 0
        layers.append(jnp.where(fluid_cells, jnp.where(blocked, post[26 - number], arrived), popul[number]))
    return jnp.stack(layers)


def stream_heat(post):
    return jnp.stack([jnp.roll(post[number], HEAT_TABLE[number], axis=(0, 1, 2)) for number in range(7)])


def reference(populations, thermal, velocity_prev, solid, phase_ids, conductivity, rates):
    relax_time = relaxation(phase_ids, conductivity)
    speed = velocity_prev
    popul = populations
    heat_pops = thermal
    for window_number in range(WINDOWS):
        heat = jnp.sum(heat_pops, axis=0)
        for step_number in range(STEPS):
            popul = stream_flow(collide(popul, heat, rates), popul, solid)
        for step_number in range(STEPS):
            heat_pops = stream_heat(heat_collide(heat_pops, speed, relax_time))
        if window_number + 1 < WINDOWS:
            speed = flow_speed(popul, heat, solid)
    return popul, heat_pops
```

```python
import jax
import jax.numpy as jnp
import numpy as np
from jax import lax
from jax.experimental import pallas as pl
from jax.experimental.pallas import tpu as pltpu
from jax.sharding import PartitionSpec as P

STEPS = 4
WINDOWS = 2


HIGHEST = lax.Precision.HIGHEST
BUOYANCY = 0.03
REFERENCE_HEAT = 1.0
OFFSET_TABLE = [(number // 9 - 1, number // 3 % 3 - 1, number % 3 - 1) for number in range(27)]
LATTICE_WEIGHTS = np.array(
    [
        np.prod([2.0 / 3.0 if component == 0 else 1.0 / 6.0 for component in triple])
        for triple in OFFSET_TABLE
    ]
)
VANDERMONDE = np.array([[1.0, 1.0, 1.0], [-1.0, 0.0, 1.0], [1.0, 0.0, 1.0]])
VANDER_INVERSE = np.array([[0.0, -0.5, 0.5], [1.0, 0.0, -1.0], [0.0, 0.5, 0.5]])
MOMENT_MATRIX = np.kron(np.kron(VANDERMONDE, VANDERMONDE), VANDERMONDE)
MOMENT_INVERSE = np.kron(np.kron(VANDER_INVERSE, VANDER_INVERSE), VANDER_INVERSE)
RELAXED = np.array([0.0 if number in (0, 1, 3, 9) else 1.0 for number in range(27)])
SUMMING = np.concatenate([np.ones((1, 27)), 1.0 * np.array(OFFSET_TABLE).T], axis=0)
HEAT_WEIGHTS = np.array([0.25] + [0.125] * 6)


def from_behind(value, axis, steps):
    count = lax.axis_size(axis)
    pairs = [(source, (source + steps) % count) for source in range(count)]
    return lax.ppermute(value, axis, pairs)


def extended(cells, sides, width):
    for axis, dim in sides:
        count = lax.axis_size(axis)
        head = lax.slice_in_dim(cells, 0, width, axis=dim)
        tail = lax.slice_in_dim(cells, cells.shape[dim] - width, cells.shape[dim], axis=dim)
        cells = jnp.concatenate(
            [
                lax.ppermute(tail, axis, [(i, (i + 1) % count) for i in range(count)]),
                cells,
                lax.ppermute(head, axis, [((i + 1) % count, i) for i in range(count)]),
            ],
            axis=dim,
        )
    return cells


def flow_state(flat, heat_flat):
    sums = jnp.dot(jnp.asarray(SUMMING, jnp.float32), flat, precision=HIGHEST)
    density = sums[0]
    force = BUOYANCY * (heat_flat - REFERENCE_HEAT)
    speed = jnp.stack([sums[1], sums[2], sums[3] + 0.5 * force]) / density
    return (density, force, speed)


def collide(popul, heat, rates):
    flat = popul.reshape(27, -1)
    density, force, speed = flow_state(flat, heat.reshape(-1))
    along = jnp.dot(jnp.asarray(SUMMING[1:].T, jnp.float32), speed, precision=HIGHEST)
    square = jnp.sum(speed * speed, axis=0)
    balance = (
        density
        * jnp.asarray(LATTICE_WEIGHTS, jnp.float32)[:, None]
        * (1.0 + 3.0 * along + 4.5 * along * along - 1.5 * square)
    )
    scaled = (
        jnp.asarray(MOMENT_INVERSE, jnp.float32)
        * (rates * jnp.asarray(RELAXED, jnp.float32))[None, :]
    )
    relax = jnp.dot(scaled, jnp.asarray(MOMENT_MATRIX, jnp.float32), precision=HIGHEST)
    post = (
        flat
        - jnp.dot(relax, flat - balance, precision=HIGHEST)
        + jnp.asarray(MOMENT_INVERSE[:, 1], jnp.float32)[:, None] * force[None, :]
    )
    return post.reshape(popul.shape)


def flow_speed(popul, heat, solid):
    density, force, speed = flow_state(popul.reshape(27, -1), heat.reshape(-1))
    return jnp.where(solid[None] == 0, speed.reshape((3,) + solid.shape), 0.0)


def heat_collide(heat_pops, speed, relax_time):
    total = jnp.sum(heat_pops, axis=0)
    still = jnp.zeros_like(speed[0])
    along = jnp.stack([still, speed[0], -speed[0], speed[1], -speed[1], speed[2], -speed[2]])
    balance = (
        jnp.asarray(HEAT_WEIGHTS, jnp.float32)[:, None, None, None]
        * total[None]
        * (1.0 + 4.0 * along)
    )
    return heat_pops - (heat_pops - balance) / relax_time[None]


def relaxation(phase_ids, conductivity):
    levels = jnp.arange(conductivity.shape[0], dtype=jnp.int32)
    chosen = jnp.sum(
        jnp.where(
            phase_ids[None] == levels[:, None, None, None], conductivity[:, None, None, None], 0.0
        ),
        axis=0,
    )
    return 0.5 + 4.0 * chosen


def inner_window(padded, triple, sizes):
    return padded[
        1 - triple[0] : 1 - triple[0] + sizes[0],
        1 - triple[1] : 1 - triple[1] + sizes[1],
        1 - triple[2] : 1 - triple[2] + sizes[2],
    ]


def advance(grid, axis_number, send_up, send_down):
    space = 3 + axis_number
    length = grid.shape[space]
    rising = lax.index_in_dim(grid, 2, axis_number, keepdims=True)
    resting = lax.index_in_dim(grid, 1, axis_number, keepdims=True)
    falling = lax.index_in_dim(grid, 0, axis_number, keepdims=True)
    from_below = send_up(lax.slice_in_dim(rising, length - 1, length, axis=space))
    from_above = send_down(lax.slice_in_dim(falling, 0, 1, axis=space))
    rising = jnp.concatenate(
        [from_below, lax.slice_in_dim(rising, 0, length - 1, axis=space)], axis=space
    )
    falling = jnp.concatenate(
        [lax.slice_in_dim(falling, 1, length, axis=space), from_above], axis=space
    )
    return jnp.concatenate([falling, resting, rising], axis=axis_number)


def flow_arrivals(post):
    sizes = post.shape[1:]
    grid = post.reshape((3, 3, 3) + sizes)
    grid = advance(
        grid,
        0,
        lambda plane: from_behind(plane, "gx", 1),
        lambda plane: from_behind(plane, "gx", -1),
    )
    grid = advance(
        grid,
        1,
        lambda plane: from_behind(plane, "gy", 1),
        lambda plane: from_behind(plane, "gy", -1),
    )
    grid = advance(
        grid,
        2,
        lambda plane: from_behind(plane, "grp", 1),
        lambda plane: from_behind(plane, "grp", -1),
    )
    return grid.reshape(post.shape)


def stream_heat(post, grp_index, last_grp):
    length = post.shape[1]
    size_y = post.shape[2]
    eastward = post[1]
    westward = post[2]
    lower_first = from_behind(eastward, "grp", 1)
    lower_second = from_behind(lower_first, "gx", 1)
    entering = jnp.where(grp_index == 0, lower_second, lower_first)
    eastward = jnp.concatenate([entering, eastward[: length - 1]], axis=0)
    upper_first = from_behind(westward, "grp", -1)
    upper_second = from_behind(upper_first, "gx", -1)
    entering = jnp.where(grp_index == last_grp, upper_second, upper_first)
    westward = jnp.concatenate([westward[1:], entering], axis=0)
    sides = extended(post[3:5], (("gy", 2),), 1)
    northward = sides[0, :, 0:size_y]
    southward = sides[1, :, 2 : size_y + 2]
    upward = jnp.roll(post[5], 1, axis=2)
    downward = jnp.roll(post[6], -1, axis=2)
    return jnp.stack([post[0], eastward, westward, northward, southward, upward, downward])


def on_device(populations, thermal, velocity_prev, solid, phase_ids, conductivity, rates):
    padded_solid = extended(solid, (("grp", 2), ("gx", 0), ("gy", 1)), 1)
    sizes = solid.shape
    blocked = jnp.stack(
        [inner_window(padded_solid, OFFSET_TABLE[number], sizes) != 0 for number in range(27)]
    )
    fluid_cells = (solid == 0)[None]
    grp_index = lax.axis_index("grp")
    last_grp = lax.axis_size("grp") - 1
    relax_time = relaxation(phase_ids, conductivity)
    speed_brick = velocity_prev
    popul = populations
    heat_pops = thermal
    for window_number in range(WINDOWS):
        heat_brick = lax.all_to_all(
            jnp.sum(heat_pops, axis=0), "grp", split_axis=2, concat_axis=0, tiled=True
        )
        speed_column = lax.all_to_all(speed_brick, "grp", split_axis=1, concat_axis=3, tiled=True)
        for step_number in range(STEPS):
            post = collide(popul, heat_brick, rates)
            arrived = flow_arrivals(post)
            popul = jnp.where(fluid_cells, jnp.where(blocked, post[::-1], arrived), popul)
        for step_number in range(STEPS):
            heat_pops = stream_heat(
                heat_collide(heat_pops, speed_column, relax_time), grp_index, last_grp
            )
        if window_number + 1 < WINDOWS:
            speed_brick = flow_speed(popul, heat_brick, solid)
    return (popul, heat_pops)


SUBLANES = 8
LANES = 128
F32 = jnp.float32


class Slab:
    def __init__(self, mesh_shape, flow_block, heat_block):
        self.grp, self.gx, self.gy = (mesh_shape[name] for name in ("grp", "gx", "gy"))
        self.block_x, self.block_y, self.block_z = flow_block
        self.sub = self.gx * self.gy
        self.size_x = self.block_x * self.gx
        self.planes = self.block_z // self.sub
        self.deep = LANES // (self.size_x * self.gy) if self.size_x * self.gy <= LANES else 0
        self.fits = (
            self.block_y == SUBLANES
            and self.block_z == LANES
            and self.block_z % self.sub == 0
            and self.deep >= STEPS
            and self.deep * self.size_x * self.gy == LANES
            and self.planes == self.deep * self.gy
            and 2 * self.block_x == self.sub
            and self.size_x == self.sub
            and self.gx == 2
            and self.block_x == self.grp
            and heat_block == (1, SUBLANES, self.grp * LANES)
            and self.sub & (self.sub - 1) == 0
            and self.gy & (self.gy - 1) == 0
        )
        if self.fits:
            self.tiles = self.planes // self.deep
            self.padded = self.tiles + 2


def lane_index():
    return lax.broadcasted_iota(jnp.int32, (SUBLANES, LANES), 1)


def row_index():
    return lax.broadcasted_iota(jnp.int32, (SUBLANES, LANES), 0)


def lane_roll(value, amount):
    amount = amount % LANES
    return value if amount == 0 else pltpu.roll(value, amount, 1)


def swap_groups(values, group):
    count = len(values)
    lane = lane_index()
    values = list(values)
    bit = 1
    while bit < count:
        low = (lane // (group * bit)) % 2 == 0
        for first in range(count):
            if first & bit == 0:
                a, b = values[first], values[first | bit]
                values[first] = jnp.where(low, a, lane_roll(b, group * bit))
                values[first | bit] = jnp.where(low, lane_roll(a, -group * bit), b)
        bit *= 2
    return values


def pack_in(slab, popul_ref, speed_ref, solid_ref, heat_ref, phase_ref, levels_ref, flow_out, heat_out):
    zero = jnp.zeros((SUBLANES, LANES), F32)

    def field(number, x):
        if number < 27:
            return popul_ref[number, x]
        if number < 30:
            return speed_ref[number - 27, x]
        if number == 30:
            return solid_ref[x].astype(F32)
        return zero

    for pair in range(16):
        sources = [field(2 * pair + h, x) for h in range(2) for x in range(slab.block_x)]
        for target, value in enumerate(swap_groups(sources, slab.planes)):
            flow_out[target, pair] = value
    for part in range(slab.grp):
        span = pl.ds(part * LANES, LANES)
        phase = phase_ref[0, :, span]
        chosen = zero
        for level in range(levels_ref.shape[0]):
            chosen = jnp.where(phase == level, levels_ref[level], chosen)
        sources = [heat_ref[k, 0, :, span] for k in range(7)] + [1.0 / (0.5 + 4.0 * chosen)]
        for target, value in enumerate(swap_groups(sources, slab.planes)):
            heat_out[part * slab.sub + target] = value


HEAT_AT, RATE_AT, SPEED_AT, SOLID_AT, ROWS = 27, 34, 35, 38, 39
MOVING = 34


def row_of_flow(number):
    if number < 27:
        return number
    return SPEED_AT + number - 27 if number < 31 else None


def unpack_in(slab, flow_ref, heat_ref, state_out, low_out, high_out):
    half = slab.block_x * slab.planes
    first_half = lane_index() < half

    def put(row, by_gy):
        for tile, value in enumerate(swap_groups(by_gy, slab.deep)):
            state_out[row, tile] = value
            if tile == 0:
                low_out[row] = value
            if tile == slab.tiles - 1:
                high_out[row] = value

    for pair in range(16):
        firsts, seconds = [], []
        for y in range(slab.gy):
            a, b = flow_ref[y, pair], flow_ref[slab.gy + y, pair]
            firsts.append(jnp.where(first_half, a, lane_roll(b, half)))
            seconds.append(jnp.where(first_half, lane_roll(a, half), b))
        put(row_of_flow(2 * pair), firsts)
        if row_of_flow(2 * pair + 1) is not None:
            put(row_of_flow(2 * pair + 1), seconds)
    columns = []
    for y in range(slab.gy):
        sources = [
            heat_ref[(part * slab.gx + x) * slab.gy + y]
            for x in range(slab.gx)
            for part in range(slab.grp)
        ]
        columns.append(swap_groups(sources, slab.planes))
    for k in range(8):
        put(HEAT_AT + k, [columns[y][k] for y in range(slab.gy)])


def pack_out(slab, take, flow_out, heat_out):
    half = slab.block_x * slab.planes
    first_half = lane_index() < half
    zero = jnp.zeros((SUBLANES, LANES), F32)

    def by_gy(row):
        return swap_groups([take(row, tile) for tile in range(slab.tiles)], slab.deep)

    for pair in range(14):
        firsts = by_gy(2 * pair)
        seconds = by_gy(2 * pair + 1) if 2 * pair + 1 < 27 else [zero] * slab.gy
        for y in range(slab.gy):
            a, b = firsts[y], seconds[y]
            flow_out[y, pair] = jnp.where(first_half, a, lane_roll(b, half))
            flow_out[slab.gy + y, pair] = jnp.where(first_half, lane_roll(a, half), b)
    fields = [by_gy(HEAT_AT + k) for k in range(7)]
    for y in range(slab.gy):
        sources = [fields[k][y] for k in range(7)] + [zero]
        for number, value in enumerate(swap_groups(sources, slab.planes)):
            x, part = number // slab.grp, number % slab.grp
            heat_out[(part * slab.gx + x) * slab.gy + y] = value


def unpack_out(slab, flow_ref, heat_ref, popul_out, thermal_out):
    for pair in range(14):
        sources = [flow_ref[source, pair] for source in range(slab.sub)]
        for number, value in enumerate(swap_groups(sources, slab.planes)):
            field, x = 2 * pair + number // slab.block_x, number % slab.block_x
            if field < 27:
                popul_out[field, x] = value
    for part in range(slab.grp):
        sources = [heat_ref[part * slab.sub + source] for source in range(slab.sub)]
        for k, value in enumerate(swap_groups(sources, slab.planes)[:7]):
            thermal_out[k, 0, :, pl.ds(part * LANES, LANES)] = value


def forward3(values):
    for stride in (9, 3, 1):
        out = [None] * 27
        for n in range(27):
            if n // stride % 3 == 0:
                a, b, c = values[n], values[n + stride], values[n + 2 * stride]
                both = a + c
                out[n], out[n + stride], out[n + 2 * stride] = both + b, c - a, both
        values = out
    return values


def backward3(values):
    for stride in (9, 3, 1):
        out = [None] * 27
        for n in range(27):
            if n // stride % 3 == 0:
                a, b, c = values[n], values[n + stride], values[n + 2 * stride]
                even, odd = 0.5 * c, 0.5 * b
                out[n], out[n + stride], out[n + 2 * stride] = even - odd, a - c, even + odd
        values = out
    return values


def collide_tile(values, force, rate):
    moments = forward3(values)
    density = moments[0]
    jx, jy, jz = moments[9], moments[3], moments[1] + 0.5 * force
    inverse = 1.0 / density
    flux = (jx, jy, jz)
    u = tuple(j * inverse for j in flux)
    third = 1.0 / 3.0
    base = {0: density}
    for k in (1, 2, 3):
        base[k] = density * third**k
    squares = [flux[d] * u[d] for d in range(3)]
    square_at = {}
    scaled = {}

    def scale(key, value, count):
        if count == 0:
            return value
        if (key, count) not in scaled:
            scaled[key, count] = value * third**count
        return scaled[key, count]

    cross = {(0, 1): jx * u[1], (0, 2): jx * u[2], (1, 2): jy * u[2]}
    out = [None] * 27
    for n in range(27):
        powers = (n // 9, n // 3 % 3, n % 3)
        if n in (0, 3, 9):
            out[n] = moments[n]
            continue
        if n == 1:
            out[n] = moments[n] + force
            continue
        odd = tuple(d for d in range(3) if powers[d] == 1)
        even = tuple(d for d in range(3) if powers[d] == 2)
        count = len(even)
        if len(odd) == 3:
            out[n] = moments[n] - rate(n) * moments[n]
            continue
        if len(odd) == 0:
            if even not in square_at:
                total = squares[even[0]]
                for d in even[1:]:
                    total = total + squares[d]
                square_at[even] = base[count] + (total * (3.0 * third**count) if count > 1 else total)
            level = square_at[even]
        elif len(odd) == 1:
            level = scale(odd, flux[odd[0]], count)
        else:
            level = scale(odd, cross[odd], count)
        out[n] = moments[n] - rate(n) * (moments[n] - level)
    return backward3(out)


def shifters(slab):
    lane, row = lane_index(), row_index()
    per_x = slab.gy * slab.deep
    in_z = lane % slab.deep
    in_y = (lane // slab.deep) % slab.gy
    z_edge = {1: in_z == 0, -1: in_z == slab.deep - 1}
    y_edge = {1: in_y == 0, -1: in_y == slab.gy - 1}
    row_edge = {1: row == 0, -1: row == SUBLANES - 1}

    def along_x(value, step):
        return lane_roll(value, step * per_x)

    def along_y(value, step):
        turned = pltpu.roll(value, step % SUBLANES, 0)
        near = lane_roll(turned, step * slab.deep)
        far = lane_roll(turned, step * (slab.deep - per_x))
        return jnp.where(row_edge[step], jnp.where(y_edge[step], far, near), turned)

    def along_z(value, beside, step):
        return jnp.where(z_edge[step], lane_roll(beside, step * (1 - slab.deep)), lane_roll(value, step))

    return along_x, along_y, along_z


HEAT_OFFSETS = [(0, 0, 0), (1, 0, 0), (-1, 0, 0), (0, 1, 0), (0, -1, 0), (0, 0, 1), (0, 0, -1)]


def run_steps(slab, rates_ref, state, post, force_ref, rate_ref, speed_ref, solid_ref):
    last = slab.padded - 1

    def collide_one(tile, _):
        values = [state[n, tile] for n in range(27)]
        solid = solid_ref[tile] != 0.0
        moved = collide_tile(values, force_ref[tile], lambda n: rates_ref[n])
        for n in range(27):
            post[n, tile] = jnp.where(solid, jnp.nan, moved[n])
        heat = [state[HEAT_AT + k, tile] for k in range(7)]
        total = heat[0]
        for k in range(1, 7):
            total = total + heat[k]
        omega = rate_ref[tile]
        side = 0.125 * total
        for k in range(7):
            if k == 0:
                level = 0.25 * total
            else:
                drift = (0.5 * total) * speed_ref[(k - 1) // 2, tile]
                level = side + drift if k % 2 == 1 else side - drift
            post[HEAT_AT + k, tile] = heat[k] - (heat[k] - level) * omega
        return 0

    def stream_one(tile, _):
        along_x, along_y, along_z = shifters(slab)
        before = jnp.where(tile == 0, last, tile - 1)
        after = jnp.where(tile == last, 0, tile + 1)
        solid = solid_ref[tile] != 0.0

        def arrive(row, offset):
            value = post[row, tile]
            if offset[2] != 0:
                value = along_z(value, post[row, before if offset[2] == 1 else after], offset[2])
            if offset[1] != 0:
                value = along_y(value, offset[1])
            if offset[0] != 0:
                value = along_x(value, offset[0])
            return value

        for n in range(27):
            value = arrive(n, OFFSET_TABLE[n])
            value = jnp.where(value != value, post[26 - n, tile], value)
            state[n, tile] = jnp.where(solid, state[n, tile], value)
        for k in range(7):
            state[HEAT_AT + k, tile] = arrive(HEAT_AT + k, HEAT_OFFSETS[k])
        return 0

    def step(number, _):
        lax.fori_loop(0, slab.padded, collide_one, 0)
        lax.fori_loop(0, slab.padded, stream_one, 0)
        return 0

    lax.fori_loop(0, STEPS, step, 0)


def heat_force(state, tile):
    total = state[HEAT_AT, tile]
    for k in range(1, 7):
        total = total + state[HEAT_AT + k, tile]
    return BUOYANCY * (total - REFERENCE_HEAT)


def first_window(slab, rates_ref, own_ref, low_ref, high_ref, own_out, low_out, high_out, keep_out, state, post, speed):
    def gather(row, tile):
        if tile == 0:
            return low_ref[row]
        if tile == slab.padded - 1:
            return high_ref[row]
        return own_ref[row, tile - 1]

    for tile in range(slab.padded):
        for row in range(MOVING):
            state[row, tile] = gather(row, tile)
        for d in range(3):
            speed[d, tile] = gather(SPEED_AT + d, tile)
        keep_out[0, tile] = gather(RATE_AT, tile)
        keep_out[1, tile] = gather(SOLID_AT, tile)
        keep_out[2, tile] = heat_force(state, tile)
    run_steps(slab, rates_ref, state, post, keep_out.at[2], keep_out.at[0], speed, keep_out.at[1])
    for row in range(MOVING):
        for tile in range(slab.tiles):
            own_out[row, tile] = state[row, tile + 1]
        low_out[row] = state[row, 1]
        high_out[row] = state[row, slab.tiles]


def next_state(slab, own_ref, low_ref, high_ref, keep_ref, state, speed, force):
    for tile in range(slab.padded):
        for row in range(MOVING):
            if tile == 0:
                state[row, tile] = low_ref[row]
            elif tile == slab.padded - 1:
                state[row, tile] = high_ref[row]
            else:
                state[row, tile] = own_ref[row, tile - 1]
        values = [state[n, tile] for n in range(27)]
        total = values[0]
        for n in range(1, 27):
            total = total + values[n]
        sums = []
        for d in range(3):
            plus, minus = None, None
            for n in range(27):
                part = OFFSET_TABLE[n][d]
                if part == 1:
                    plus = values[n] if plus is None else plus + values[n]
                if part == -1:
                    minus = values[n] if minus is None else minus + values[n]
            sums.append(plus - minus)
        sums[2] = sums[2] + 0.5 * keep_ref[2, tile]
        solid = keep_ref[1, tile] != 0.0
        for d in range(3):
            speed[d, tile] = jnp.where(solid, 0.0, sums[d] / total)
        force[tile] = heat_force(state, tile)


def last_window(slab, rates_ref, own_ref, low_ref, high_ref, keep_ref, flow_out, heat_out, state, post, speed, force):
    next_state(slab, own_ref, low_ref, high_ref, keep_ref, state, speed, force)
    run_steps(slab, rates_ref, state, post, force, keep_ref.at[0], speed, keep_ref.at[1])
    pack_out(slab, lambda row, tile: state[row, tile + 1], flow_out, heat_out)


def middle_window(slab, rates_ref, own_ref, low_ref, high_ref, keep_ref, own_out, low_out, high_out, keep_out, state, post, speed):
    for k in range(2):
        for tile in range(slab.padded):
            keep_out[k, tile] = keep_ref[k, tile]
    next_state(slab, own_ref, low_ref, high_ref, keep_ref, state, speed, keep_out.at[2])
    run_steps(slab, rates_ref, state, post, keep_out.at[2], keep_out.at[0], speed, keep_out.at[1])
    for row in range(MOVING):
        for tile in range(slab.tiles):
            own_out[row, tile] = state[row, tile + 1]
        low_out[row] = state[row, 1]
        high_out[row] = state[row, slab.tiles]


def local_call(body, slab, scalars, arrays, outs, scratch=()):
    def kernel(*refs):
        body(slab, *refs)

    return pl.pallas_call(
        kernel,
        out_shape=[jax.ShapeDtypeStruct(shape, F32) for shape in outs],
        in_specs=[pl.BlockSpec(memory_space=pltpu.SMEM)] * len(scalars)
        + [pl.BlockSpec(memory_space=pltpu.VMEM)] * len(arrays),
        out_specs=[pl.BlockSpec(memory_space=pltpu.VMEM)] * len(outs),
        scratch_shapes=[pltpu.VMEM(shape, F32) for shape in scratch],
        compiler_params=pltpu.CompilerParams(vmem_limit_bytes=24 * 1024 * 1024),
    )(*scalars, *arrays)


RING = ("grp", "gx", "gy")


def exchange(low, high, count):
    from_below = lax.ppermute(high, RING, [(i, (i + 1) % count) for i in range(count)])
    from_above = lax.ppermute(low, RING, [((i + 1) % count, i) for i in range(count)])
    return from_below, from_above


def on_slabs(slab, populations, thermal, velocity_prev, solid, phase_ids, conductivity, rates):
    tile = (SUBLANES, LANES)
    count = slab.grp * slab.sub

    def pack_body(slab, levels_ref, popul_ref, speed_ref, solid_ref, heat_ref, phase_ref, flow_out, heat_out):
        pack_in(slab, popul_ref, speed_ref, solid_ref, heat_ref, phase_ref, levels_ref, flow_out, heat_out)

    flow, heat = local_call(
        pack_body,
        slab,
        [conductivity],
        [populations, velocity_prev, solid, thermal, phase_ids],
        [(slab.sub, 16) + tile, (count,) + tile],
    )
    heat = lax.all_to_all(heat, RING, split_axis=0, concat_axis=0, tiled=True)
    flow = lax.all_to_all(flow, ("gx", "gy"), split_axis=0, concat_axis=0, tiled=True)
    own, low, high = local_call(
        unpack_in,
        slab,
        [],
        [flow, heat],
        [(ROWS, slab.tiles) + tile, (ROWS,) + tile, (ROWS,) + tile],
    )
    window_outs = [
        (MOVING, slab.tiles) + tile,
        (MOVING,) + tile,
        (MOVING,) + tile,
        (3, slab.padded) + tile,
    ]
    lattice = (MOVING, slab.padded) + tile
    below, above = exchange(low, high, count)
    own, low, high, keep = local_call(
        first_window,
        slab,
        [rates],
        [own, below, above],
        window_outs,
        [lattice, lattice, (3, slab.padded) + tile],
    )
    for number in range(1, WINDOWS):
        below, above = exchange(low, high, count)
        if number + 1 < WINDOWS:
            own, low, high, keep = local_call(
                middle_window,
                slab,
                [rates],
                [own, below, above, keep],
                window_outs,
                [lattice, lattice, (3, slab.padded) + tile],
            )
        else:
            flow, heat = local_call(
                last_window,
                slab,
                [rates],
                [own, below, above, keep],
                [(slab.sub, 14) + tile, (count,) + tile],
                [lattice, lattice, (3, slab.padded) + tile, (slab.padded,) + tile],
            )
    flow = lax.all_to_all(flow, ("gx", "gy"), split_axis=0, concat_axis=0, tiled=True)
    heat = lax.all_to_all(heat, RING, split_axis=0, concat_axis=0, tiled=True)
    return tuple(
        local_call(unpack_out, slab, [], [flow, heat], [populations.shape, thermal.shape])
    )


def solution(mesh):
    in_specs = (
        P(None, "gx", "gy", "grp"),
        P(None, ("gx", "grp"), "gy", None),
        P(None, "gx", "gy", "grp"),
        P("gx", "gy", "grp"),
        P(("gx", "grp"), "gy", None),
        P(),
        P(),
    )
    out_specs = (P(None, "gx", "gy", "grp"), P(None, ("gx", "grp"), "gy", None))

    def per_device(populations, thermal, *others):
        slab = Slab(mesh.shape, populations.shape[1:], thermal.shape[1:])
        plan = (lambda *arrays: on_slabs(slab, *arrays)) if slab.fits and WINDOWS > 1 else on_device
        return plan(populations, thermal, *others)

    return jax.shard_map(
        per_device, mesh=mesh, in_specs=in_specs, out_specs=out_specs, check_vma=False
    )
```

```python
import jax
import jax.numpy as jnp
import numpy as np
from jax import lax
from jax.experimental import pallas as pl
from jax.experimental.pallas import tpu as pltpu
from jax.sharding import PartitionSpec as P

STEPS = 4
WINDOWS = 2


HIGHEST = lax.Precision.HIGHEST
BUOYANCY = 0.03
REFERENCE_HEAT = 1.0
OFFSET_TABLE = [(number // 9 - 1, number // 3 % 3 - 1, number % 3 - 1) for number in range(27)]
LATTICE_WEIGHTS = np.array(
    [
        np.prod([2.0 / 3.0 if component == 0 else 1.0 / 6.0 for component in triple])
        for triple in OFFSET_TABLE
    ]
)
VANDERMONDE = np.array([[1.0, 1.0, 1.0], [-1.0, 0.0, 1.0], [1.0, 0.0, 1.0]])
VANDER_INVERSE = np.array([[0.0, -0.5, 0.5], [1.0, 0.0, -1.0], [0.0, 0.5, 0.5]])
MOMENT_MATRIX = np.kron(np.kron(VANDERMONDE, VANDERMONDE), VANDERMONDE)
MOMENT_INVERSE = np.kron(np.kron(VANDER_INVERSE, VANDER_INVERSE), VANDER_INVERSE)
RELAXED = np.array([0.0 if number in (0, 1, 3, 9) else 1.0 for number in range(27)])
SUMMING = np.concatenate([np.ones((1, 27)), 1.0 * np.array(OFFSET_TABLE).T], axis=0)
HEAT_WEIGHTS = np.array([0.25] + [0.125] * 6)


def from_behind(value, axis, steps):
    count = lax.axis_size(axis)
    pairs = [(source, (source + steps) % count) for source in range(count)]
    return lax.ppermute(value, axis, pairs)


def extended(cells, sides, width):
    for axis, dim in sides:
        count = lax.axis_size(axis)
        head = lax.slice_in_dim(cells, 0, width, axis=dim)
        tail = lax.slice_in_dim(cells, cells.shape[dim] - width, cells.shape[dim], axis=dim)
        cells = jnp.concatenate(
            [
                lax.ppermute(tail, axis, [(i, (i + 1) % count) for i in range(count)]),
                cells,
                lax.ppermute(head, axis, [((i + 1) % count, i) for i in range(count)]),
            ],
            axis=dim,
        )
    return cells


def flow_state(flat, heat_flat):
    sums = jnp.dot(jnp.asarray(SUMMING, jnp.float32), flat, precision=HIGHEST)
    density = sums[0]
    force = BUOYANCY * (heat_flat - REFERENCE_HEAT)
    speed = jnp.stack([sums[1], sums[2], sums[3] + 0.5 * force]) / density
    return (density, force, speed)


def collide(popul, heat, rates):
    flat = popul.reshape(27, -1)
    density, force, speed = flow_state(flat, heat.reshape(-1))
    along = jnp.dot(jnp.asarray(SUMMING[1:].T, jnp.float32), speed, precision=HIGHEST)
    square = jnp.sum(speed * speed, axis=0)
    balance = (
        density
        * jnp.asarray(LATTICE_WEIGHTS, jnp.float32)[:, None]
        * (1.0 + 3.0 * along + 4.5 * along * along - 1.5 * square)
    )
    scaled = (
        jnp.asarray(MOMENT_INVERSE, jnp.float32)
        * (rates * jnp.asarray(RELAXED, jnp.float32))[None, :]
    )
    relax = jnp.dot(scaled, jnp.asarray(MOMENT_MATRIX, jnp.float32), precision=HIGHEST)
    post = (
        flat
        - jnp.dot(relax, flat - balance, precision=HIGHEST)
        + jnp.asarray(MOMENT_INVERSE[:, 1], jnp.float32)[:, None] * force[None, :]
    )
    return post.reshape(popul.shape)


def flow_speed(popul, heat, solid):
    density, force, speed = flow_state(popul.reshape(27, -1), heat.reshape(-1))
    return jnp.where(solid[None] == 0, speed.reshape((3,) + solid.shape), 0.0)


def heat_collide(heat_pops, speed, relax_time):
    total = jnp.sum(heat_pops, axis=0)
    still = jnp.zeros_like(speed[0])
    along = jnp.stack([still, speed[0], -speed[0], speed[1], -speed[1], speed[2], -speed[2]])
    balance = (
        jnp.asarray(HEAT_WEIGHTS, jnp.float32)[:, None, None, None]
        * total[None]
        * (1.0 + 4.0 * along)
    )
    return heat_pops - (heat_pops - balance) / relax_time[None]


def relaxation(phase_ids, conductivity):
    levels = jnp.arange(conductivity.shape[0], dtype=jnp.int32)
    chosen = jnp.sum(
        jnp.where(
            phase_ids[None] == levels[:, None, None, None], conductivity[:, None, None, None], 0.0
        ),
        axis=0,
    )
    return 0.5 + 4.0 * chosen


def inner_window(padded, triple, sizes):
    return padded[
        1 - triple[0] : 1 - triple[0] + sizes[0],
        1 - triple[1] : 1 - triple[1] + sizes[1],
        1 - triple[2] : 1 - triple[2] + sizes[2],
    ]


def advance(grid, axis_number, send_up, send_down):
    space = 3 + axis_number
    length = grid.shape[space]
    rising = lax.index_in_dim(grid, 2, axis_number, keepdims=True)
    resting = lax.index_in_dim(grid, 1, axis_number, keepdims=True)
    falling = lax.index_in_dim(grid, 0, axis_number, keepdims=True)
    from_below = send_up(lax.slice_in_dim(rising, length - 1, length, axis=space))
    from_above = send_down(lax.slice_in_dim(falling, 0, 1, axis=space))
    rising = jnp.concatenate(
        [from_below, lax.slice_in_dim(rising, 0, length - 1, axis=space)], axis=space
    )
    falling = jnp.concatenate(
        [lax.slice_in_dim(falling, 1, length, axis=space), from_above], axis=space
    )
    return jnp.concatenate([falling, resting, rising], axis=axis_number)


def flow_arrivals(post):
    sizes = post.shape[1:]
    grid = post.reshape((3, 3, 3) + sizes)
    grid = advance(
        grid,
        0,
        lambda plane: from_behind(plane, "gx", 1),
        lambda plane: from_behind(plane, "gx", -1),
    )
    grid = advance(
        grid,
        1,
        lambda plane: from_behind(plane, "gy", 1),
        lambda plane: from_behind(plane, "gy", -1),
    )
    grid = advance(
        grid,
        2,
        lambda plane: from_behind(plane, "grp", 1),
        lambda plane: from_behind(plane, "grp", -1),
    )
    return grid.reshape(post.shape)


def stream_heat(post, grp_index, last_grp):
    length = post.shape[1]
    size_y = post.shape[2]
    eastward = post[1]
    westward = post[2]
    lower_first = from_behind(eastward, "grp", 1)
    lower_second = from_behind(lower_first, "gx", 1)
    entering = jnp.where(grp_index == 0, lower_second, lower_first)
    eastward = jnp.concatenate([entering, eastward[: length - 1]], axis=0)
    upper_first = from_behind(westward, "grp", -1)
    upper_second = from_behind(upper_first, "gx", -1)
    entering = jnp.where(grp_index == last_grp, upper_second, upper_first)
    westward = jnp.concatenate([westward[1:], entering], axis=0)
    sides = extended(post[3:5], (("gy", 2),), 1)
    northward = sides[0, :, 0:size_y]
    southward = sides[1, :, 2 : size_y + 2]
    upward = jnp.roll(post[5], 1, axis=2)
    downward = jnp.roll(post[6], -1, axis=2)
    return jnp.stack([post[0], eastward, westward, northward, southward, upward, downward])


def on_device(populations, thermal, velocity_prev, solid, phase_ids, conductivity, rates):
    padded_solid = extended(solid, (("grp", 2), ("gx", 0), ("gy", 1)), 1)
    sizes = solid.shape
    blocked = jnp.stack(
        [inner_window(padded_solid, OFFSET_TABLE[number], sizes) != 0 for number in range(27)]
    )
    fluid_cells = (solid == 0)[None]
    grp_index = lax.axis_index("grp")
    last_grp = lax.axis_size("grp") - 1
    relax_time = relaxation(phase_ids, conductivity)
    speed_brick = velocity_prev
    popul = populations
    heat_pops = thermal
    for window_number in range(WINDOWS):
        heat_brick = lax.all_to_all(
            jnp.sum(heat_pops, axis=0), "grp", split_axis=2, concat_axis=0, tiled=True
        )
        speed_column = lax.all_to_all(speed_brick, "grp", split_axis=1, concat_axis=3, tiled=True)
        for step_number in range(STEPS):
            post = collide(popul, heat_brick, rates)
            arrived = flow_arrivals(post)
            popul = jnp.where(fluid_cells, jnp.where(blocked, post[::-1], arrived), popul)
        for step_number in range(STEPS):
            heat_pops = stream_heat(
                heat_collide(heat_pops, speed_column, relax_time), grp_index, last_grp
            )
        if window_number + 1 < WINDOWS:
            speed_brick = flow_speed(popul, heat_brick, solid)
    return (popul, heat_pops)


SUBLANES = 8
LANES = 128
F32 = jnp.float32


class Slab:
    def __init__(self, mesh_shape, flow_block, heat_block):
        self.grp, self.gx, self.gy = (mesh_shape[name] for name in ("grp", "gx", "gy"))
        self.block_x, self.block_y, self.block_z = flow_block
        self.sub = self.gx * self.gy
        self.size_x = self.block_x * self.gx
        self.planes = self.block_z // self.sub
        self.deep = LANES // (self.size_x * self.gy) if self.size_x * self.gy <= LANES else 0
        self.fits = (
            self.block_y == SUBLANES
            and self.block_z == LANES
            and self.block_z % self.sub == 0
            and self.deep >= STEPS
            and self.deep * self.size_x * self.gy == LANES
            and self.planes == self.deep * self.gy
            and 2 * self.block_x == self.sub
            and self.size_x == self.sub
            and self.gx == 2
            and self.block_x == self.grp
            and heat_block == (1, SUBLANES, self.grp * LANES)
            and self.sub & (self.sub - 1) == 0
            and self.gy & (self.gy - 1) == 0
            and self.grp & (self.grp - 1) == 0
        )
        if self.fits:
            self.tiles = self.planes // self.deep
            self.padded = self.tiles + 2
            self.snake = [
                x * self.gy + (y if x % 2 == 0 else self.gy - 1 - y)
                for x in range(self.gx)
                for y in range(self.gy)
            ]
            self.ring = [
                part * self.sub + self.snake[place if part % 2 == 0 else self.sub - 1 - place]
                for part in range(self.grp)
                for place in range(self.sub)
            ]

    def holder(self, place, part):
        return jnp.where(part % 2 == 0, self.snake[place], self.snake[self.sub - 1 - place])


def lane_index():
    return lax.broadcasted_iota(jnp.int32, (SUBLANES, LANES), 1)


def row_index():
    return lax.broadcasted_iota(jnp.int32, (SUBLANES, LANES), 0)


def lane_roll(value, amount):
    amount = amount % LANES
    return value if amount == 0 else pltpu.roll(value, amount, 1)


def swap_groups(values, group):
    count = len(values)
    lane = lane_index()
    values = list(values)
    bit = 1
    while bit < count:
        low = (lane // (group * bit)) % 2 == 0
        for first in range(count):
            if first & bit == 0:
                a, b = values[first], values[first | bit]
                values[first] = jnp.where(low, a, lane_roll(b, group * bit))
                values[first | bit] = jnp.where(low, lane_roll(a, -group * bit), b)
        bit *= 2
    return values


SENT_SPEED, SENT_SOLID, SENT_HEAT, SENT_RATE, SENT = 27, 30, 31, 38, 40
HEAT_AT, RATE_AT, SPEED_AT, SOLID_AT, ROWS = 27, 34, 35, 38, 39
MOVING = 34


def row_of(number):
    if number < SENT_SPEED:
        return number
    if number < SENT_SOLID:
        return SPEED_AT + number - SENT_SPEED
    if number == SENT_SOLID:
        return SOLID_AT
    return HEAT_AT + number - SENT_HEAT if number <= SENT_RATE else None


def offer_heat(slab, levels_hbm, heat_hbm, phase_hbm, *refs):
    outs, (levels_ref, heat_ref, phase_ref, sems) = refs[: slab.grp], refs[slab.grp :]
    copies = [
        pltpu.make_async_copy(heat_hbm, heat_ref, sems.at[0]),
        pltpu.make_async_copy(phase_hbm, phase_ref, sems.at[1]),
        pltpu.make_async_copy(levels_hbm, levels_ref, sems.at[2]),
    ]
    for copy in copies:
        copy.start()
    for copy in copies:
        copy.wait()
    mine = lax.axis_index("grp")
    for step in range(slab.grp):
        part = jnp.bitwise_xor(mine, step)
        span = pl.ds(pl.multiple_of(part * LANES, LANES), LANES)
        phase = phase_ref[0, :, span]
        chosen = jnp.zeros((SUBLANES, LANES), F32)
        for level in range(levels_ref.shape[0]):
            chosen = jnp.where(phase == level, levels_ref[level], chosen)
        for k in range(7):
            outs[step][k] = heat_ref[k, 0, :, span]
        outs[step][7] = 1.0 / (0.5 + 4.0 * chosen)


def pack_flow(
    slab, popul_hbm, speed_hbm, solid_hbm, sent, flags, popul_ref, speed_ref, solid_ref, sems
):
    half = 14
    copies = [
        pltpu.make_async_copy(popul_hbm.at[pl.ds(0, half)], popul_ref.at[pl.ds(0, half)], sems.at[0]),
        pltpu.make_async_copy(
            popul_hbm.at[pl.ds(half, 27 - half)], popul_ref.at[pl.ds(half, 27 - half)], sems.at[1]
        ),
        pltpu.make_async_copy(speed_hbm, speed_ref, sems.at[2]),
        pltpu.make_async_copy(solid_hbm, solid_ref, sems.at[3]),
    ]
    for copy in copies:
        copy.start()
    mine = lax.axis_index("grp")
    holders = [slab.holder(place, mine) for place in range(slab.sub)]

    def field(number, x):
        if number < SENT_SPEED:
            return popul_ref[number, x]
        return speed_ref[number - SENT_SPEED, x]

    copies[0].wait()
    for pair in range(SENT_SOLID // 2):
        if 2 * pair == half:
            copies[1].wait()
        if pair == SENT_SPEED // 2:
            copies[2].wait()
            copies[3].wait()
        sources = [field(2 * pair + h, x) for h in range(2) for x in range(slab.block_x)]
        for place, value in enumerate(swap_groups(sources, slab.planes)):
            sent[holders[place], pair] = value
    for x in range(slab.block_x):
        flags[x] = solid_ref[x].astype(F32)


def pack_heat(slab, sent_in, flags, *refs):
    parts, (sent, held, packed, sem) = refs[: slab.grp], refs[slab.grp :]
    mine = lax.axis_index("grp")
    holders = [slab.holder(place, mine) for place in range(slab.sub)]
    for step in range(slab.grp):
        held[jnp.bitwise_xor(mine, step)] = parts[step][...]
    zero = jnp.zeros((SUBLANES, LANES), F32)
    first = SENT_SOLID // 2

    def field(number, x):
        if number == SENT_SOLID:
            return flags[x]
        return held[x, number - SENT_HEAT] if number <= SENT_RATE else zero

    for pair in range(first, SENT // 2):
        sources = [field(2 * pair + h, x) for h in range(2) for x in range(slab.block_x)]
        for place, value in enumerate(swap_groups(sources, slab.planes)):
            packed[holders[place], pair - first] = value
    copy = pltpu.make_async_copy(packed, sent.at[:, pl.ds(first, SENT // 2 - first)], sem)
    copy.start()
    copy.wait()


def unpack_in(slab, came, state_out, low_out, high_out):
    half = slab.block_x * slab.planes
    first_half = lane_index() < half

    def put(row, by_gy):
        for tile, value in enumerate(swap_groups(by_gy, slab.deep)):
            state_out[row, tile] = value
            if tile == 0:
                low_out[row] = value
            if tile == slab.tiles - 1:
                high_out[row] = value

    for pair in range(SENT // 2):
        firsts, seconds = [], []
        for y in range(slab.gy):
            a, b = came[y, pair], came[slab.gy + y, pair]
            firsts.append(jnp.where(first_half, a, lane_roll(b, half)))
            seconds.append(jnp.where(first_half, lane_roll(a, half), b))
        put(row_of(2 * pair), firsts)
        if row_of(2 * pair + 1) is not None:
            put(row_of(2 * pair + 1), seconds)


def pack_out(slab, take, sent):
    half = slab.block_x * slab.planes
    first_half = lane_index() < half

    def by_gy(row):
        return swap_groups([take(row, tile) for tile in range(slab.tiles)], slab.deep)

    for pair in range(MOVING // 2):
        firsts, seconds = by_gy(2 * pair), by_gy(2 * pair + 1)
        for y in range(slab.gy):
            a, b = firsts[y], seconds[y]
            sent[y, pair] = jnp.where(first_half, a, lane_roll(b, half))
            sent[slab.gy + y, pair] = jnp.where(first_half, lane_roll(a, half), b)


def unpack_pair(slab, came, pair):
    mine = lax.axis_index("grp")
    sources = [came[slab.holder(place, mine), pair] for place in range(slab.sub)]
    for number, value in enumerate(swap_groups(sources, slab.planes)):
        yield 2 * pair + number // slab.block_x, number % slab.block_x, value


def return_heat(slab, came, *refs):
    outs, held = refs[: slab.grp], refs[slab.grp]
    for pair in range(HEAT_AT // 2, MOVING // 2):
        for row, x, value in unpack_pair(slab, came, pair):
            if row >= HEAT_AT:
                held[x, row - HEAT_AT] = value
    mine = lax.axis_index("grp")
    for step in range(slab.grp):
        outs[step][...] = held[jnp.bitwise_xor(mine, step)]


def unpack_flow(slab, came, popul_out):
    for pair in range((HEAT_AT + 1) // 2):
        for row, x, value in unpack_pair(slab, came, pair):
            if row < HEAT_AT:
                popul_out[row, x] = value


def join_heat(slab, *refs):
    parts, thermal_out = refs[: slab.grp], refs[slab.grp]
    mine = lax.axis_index("grp")
    for step in range(slab.grp):
        part = jnp.bitwise_xor(mine, step)
        span = pl.ds(pl.multiple_of(part * LANES, LANES), LANES)
        for k in range(7):
            thermal_out[k, 0, :, span] = parts[step][k]


def forward3(values):
    for stride in (9, 3, 1):
        out = [None] * 27
        for n in range(27):
            if n // stride % 3 == 0:
                a, b, c = values[n], values[n + stride], values[n + 2 * stride]
                both = a + c
                out[n], out[n + stride], out[n + 2 * stride] = both + b, c - a, both
        values = out
    return values


def backward3(values):
    for stride in (9, 3, 1):
        out = [None] * 27
        for n in range(27):
            if n // stride % 3 == 0:
                a, b, c = values[n], values[n + stride], values[n + 2 * stride]
                even, odd = 0.5 * c, 0.5 * b
                out[n], out[n + stride], out[n + 2 * stride] = even - odd, a - c, even + odd
        values = out
    return values


def collide_tile(values, force, rate):
    moments = forward3(values)
    density = moments[0]
    jx, jy, jz = moments[9], moments[3], moments[1] + 0.5 * force
    inverse = 1.0 / density
    flux = (jx, jy, jz)
    u = tuple(j * inverse for j in flux)
    third = 1.0 / 3.0
    base = {0: density}
    for k in (1, 2, 3):
        base[k] = density * third**k
    squares = [flux[d] * u[d] for d in range(3)]
    square_at = {}
    scaled = {}

    def scale(key, value, count):
        if count == 0:
            return value
        if (key, count) not in scaled:
            scaled[key, count] = value * third**count
        return scaled[key, count]

    cross = {(0, 1): jx * u[1], (0, 2): jx * u[2], (1, 2): jy * u[2]}
    out = [None] * 27
    for n in range(27):
        powers = (n // 9, n // 3 % 3, n % 3)
        if n in (0, 3, 9):
            out[n] = moments[n]
            continue
        if n == 1:
            out[n] = moments[n] + force
            continue
        odd = tuple(d for d in range(3) if powers[d] == 1)
        even = tuple(d for d in range(3) if powers[d] == 2)
        count = len(even)
        if len(odd) == 3:
            out[n] = moments[n] - rate(n) * moments[n]
            continue
        if len(odd) == 0:
            if even not in square_at:
                total = squares[even[0]]
                for d in even[1:]:
                    total = total + squares[d]
                square_at[even] = base[count] + (total * (3.0 * third**count) if count > 1 else total)
            level = square_at[even]
        elif len(odd) == 1:
            level = scale(odd, flux[odd[0]], count)
        else:
            level = scale(odd, cross[odd], count)
        out[n] = moments[n] - rate(n) * (moments[n] - level)
    return backward3(out)


def shifters(slab):
    lane, row = lane_index(), row_index()
    per_x = slab.gy * slab.deep
    in_z = lane % slab.deep
    in_y = (lane // slab.deep) % slab.gy
    z_edge = {1: in_z == 0, -1: in_z == slab.deep - 1}
    y_edge = {1: in_y == 0, -1: in_y == slab.gy - 1}
    row_edge = {1: row == 0, -1: row == SUBLANES - 1}

    def along_x(value, step):
        return lane_roll(value, step * per_x)

    def along_y(value, step):
        turned = pltpu.roll(value, step % SUBLANES, 0)
        near = lane_roll(turned, step * slab.deep)
        far = lane_roll(turned, step * (slab.deep - per_x))
        return jnp.where(row_edge[step], jnp.where(y_edge[step], far, near), turned)

    def along_z(value, beside, step):
        return jnp.where(z_edge[step], lane_roll(beside, step * (1 - slab.deep)), lane_roll(value, step))

    return along_x, along_y, along_z


HEAT_OFFSETS = [(0, 0, 0), (1, 0, 0), (-1, 0, 0), (0, 1, 0), (0, -1, 0), (0, 0, 1), (0, 0, -1)]


def run_steps(slab, rates_ref, state, post, force_ref, rate_ref, speed_ref, solid_ref):
    last = slab.padded - 1

    def collide_one(tile, _):
        values = [state[n, tile] for n in range(27)]
        solid = solid_ref[tile] != 0.0
        moved = collide_tile(values, force_ref[tile], lambda n: rates_ref[n])
        for n in range(27):
            post[n, tile] = jnp.where(solid, jnp.nan, moved[n])
        heat = [state[HEAT_AT + k, tile] for k in range(7)]
        total = heat[0]
        for k in range(1, 7):
            total = total + heat[k]
        omega = rate_ref[tile]
        side = 0.125 * total
        for k in range(7):
            if k == 0:
                level = 0.25 * total
            else:
                drift = (0.5 * total) * speed_ref[(k - 1) // 2, tile]
                level = side + drift if k % 2 == 1 else side - drift
            post[HEAT_AT + k, tile] = heat[k] - (heat[k] - level) * omega
        return 0

    def stream_one(tile, _):
        along_x, along_y, along_z = shifters(slab)
        before = jnp.where(tile == 0, last, tile - 1)
        after = jnp.where(tile == last, 0, tile + 1)
        solid = solid_ref[tile] != 0.0

        def arrive(row, offset):
            value = post[row, tile]
            if offset[2] != 0:
                value = along_z(value, post[row, before if offset[2] == 1 else after], offset[2])
            if offset[1] != 0:
                value = along_y(value, offset[1])
            if offset[0] != 0:
                value = along_x(value, offset[0])
            return value

        for n in range(27):
            value = arrive(n, OFFSET_TABLE[n])
            value = jnp.where(value != value, post[26 - n, tile], value)
            state[n, tile] = jnp.where(solid, state[n, tile], value)
        for k in range(7):
            state[HEAT_AT + k, tile] = arrive(HEAT_AT + k, HEAT_OFFSETS[k])
        return 0

    def step(number, _):
        lax.fori_loop(0, slab.padded, collide_one, 0)
        lax.fori_loop(0, slab.padded, stream_one, 0)
        return 0

    lax.fori_loop(0, STEPS, step, 0)


def heat_force(state, tile):
    total = state[HEAT_AT, tile]
    for k in range(1, 7):
        total = total + state[HEAT_AT + k, tile]
    return BUOYANCY * (total - REFERENCE_HEAT)


def fetch(source, target, sem):
    copy = pltpu.make_async_copy(source, target, sem)
    copy.start()
    copy.wait()


def first_window(slab, rates_hbm, own_ref, low_ref, high_ref, *refs):
    own_out, low_out, high_out, keep_out, rates_ref, sem, state, post, speed = refs
    fetch(rates_hbm, rates_ref, sem)

    def gather(row, tile):
        if tile == 0:
            return low_ref[row]
        if tile == slab.padded - 1:
            return high_ref[row]
        return own_ref[row, tile - 1]

    for tile in range(slab.padded):
        for row in range(MOVING):
            state[row, tile] = gather(row, tile)
        for d in range(3):
            speed[d, tile] = gather(SPEED_AT + d, tile)
        keep_out[0, tile] = gather(RATE_AT, tile)
        keep_out[1, tile] = gather(SOLID_AT, tile)
        keep_out[2, tile] = heat_force(state, tile)
    run_steps(slab, rates_ref, state, post, keep_out.at[2], keep_out.at[0], speed, keep_out.at[1])
    for row in range(MOVING):
        for tile in range(slab.tiles):
            own_out[row, tile] = state[row, tile + 1]
        low_out[row] = state[row, 1]
        high_out[row] = state[row, slab.tiles]


def next_state(slab, own_ref, low_ref, high_ref, keep_ref, state, speed, force):
    for tile in range(slab.padded):
        for row in range(MOVING):
            if tile == 0:
                state[row, tile] = low_ref[row]
            elif tile == slab.padded - 1:
                state[row, tile] = high_ref[row]
            else:
                state[row, tile] = own_ref[row, tile - 1]
        values = [state[n, tile] for n in range(27)]
        total = values[0]
        for n in range(1, 27):
            total = total + values[n]
        sums = []
        for d in range(3):
            plus, minus = None, None
            for n in range(27):
                part = OFFSET_TABLE[n][d]
                if part == 1:
                    plus = values[n] if plus is None else plus + values[n]
                if part == -1:
                    minus = values[n] if minus is None else minus + values[n]
            sums.append(plus - minus)
        sums[2] = sums[2] + 0.5 * keep_ref[2, tile]
        solid = keep_ref[1, tile] != 0.0
        for d in range(3):
            speed[d, tile] = jnp.where(solid, 0.0, sums[d] / total)
        force[tile] = heat_force(state, tile)


def last_window(slab, rates_hbm, own_ref, low_ref, high_ref, keep_ref, *refs):
    sent, rates_ref, sem, state, post, speed, force = refs
    fetch(rates_hbm, rates_ref, sem)
    next_state(slab, own_ref, low_ref, high_ref, keep_ref, state, speed, force)
    run_steps(slab, rates_ref, state, post, force, keep_ref.at[0], speed, keep_ref.at[1])
    pack_out(slab, lambda row, tile: state[row, tile + 1], sent)


def local_call(body, slab, arrays, outs, scratch=(), in_hbm=0, carried=False):
    def kernel(*refs):
        body(slab, *refs)

    return pl.pallas_call(
        kernel,
        out_shape=[jax.ShapeDtypeStruct(shape, F32) for shape in outs],
        in_specs=[
            pl.BlockSpec(
                memory_space=pltpu.HBM if i < in_hbm else pl.ANY if carried and i == 0 else pltpu.VMEM
            )
            for i in range(len(arrays))
        ],
        out_specs=[pl.BlockSpec(memory_space=pl.ANY if carried else pltpu.VMEM)] * len(outs),
        input_output_aliases={0: 0} if carried else {},
        scratch_shapes=[pltpu.VMEM(s, F32) if isinstance(s, tuple) else s for s in scratch],
        compiler_params=pltpu.CompilerParams(vmem_limit_bytes=24 * 1024 * 1024),
    )(*(pltpu.with_memory_space_constraint(a, pltpu.HBM) if i < in_hbm else a for i, a in enumerate(arrays)))


RING = ("grp", "gx", "gy")


def exchange(slab, low, high):
    ring = slab.ring
    upward = [(ring[i - 1], ring[i]) for i in range(len(ring))]
    from_below = lax.ppermute(high, RING, upward)
    from_above = lax.ppermute(low, RING, [(b, a) for a, b in upward])
    return from_below, from_above


def across_planes(slab, parts):
    return [parts[0]] + [
        lax.ppermute(parts[step], "grp", [(i, i ^ step) for i in range(slab.grp)])
        for step in range(1, slab.grp)
    ]


def on_slabs(slab, populations, thermal, velocity_prev, solid, phase_ids, conductivity, rates):
    tile = (SUBLANES, LANES)

    def vmem_like(array):
        return pltpu.VMEM(array.shape, array.dtype)

    parts = local_call(
        offer_heat,
        slab,
        [conductivity, thermal, phase_ids],
        [(8,) + tile] * slab.grp,
        [
            pltpu.SMEM(conductivity.shape, F32),
            vmem_like(thermal),
            vmem_like(phase_ids),
            pltpu.SemaphoreType.DMA((3,)),
        ],
        in_hbm=3,
    )
    parts = across_planes(slab, parts)
    sent_shape = (slab.sub, SENT // 2) + tile
    sent, flags = local_call(
        pack_flow,
        slab,
        [populations, velocity_prev, solid],
        [sent_shape, solid.shape],
        [
            vmem_like(populations),
            vmem_like(velocity_prev),
            vmem_like(solid),
            pltpu.SemaphoreType.DMA((4,)),
        ],
        in_hbm=3,
    )
    (sent,) = local_call(
        pack_heat,
        slab,
        [sent, flags] + parts,
        [sent_shape],
        [
            (slab.grp, 8) + tile,
            (slab.sub, (SENT - SENT_SOLID) // 2) + tile,
            pltpu.SemaphoreType.DMA,
        ],
        carried=True,
    )
    came = lax.all_to_all(sent, ("gx", "gy"), split_axis=0, concat_axis=0, tiled=True)
    own, low, high = local_call(
        unpack_in,
        slab,
        [came],
        [(ROWS, slab.tiles) + tile, (ROWS,) + tile, (ROWS,) + tile],
    )
    window_outs = [
        (MOVING, slab.tiles) + tile,
        (MOVING,) + tile,
        (MOVING,) + tile,
        (3, slab.padded) + tile,
    ]
    window_scratch = [
        pltpu.SMEM(rates.shape, F32),
        pltpu.SemaphoreType.DMA,
        (MOVING, slab.padded) + tile,
        (MOVING, slab.padded) + tile,
        (3, slab.padded) + tile,
    ]
    below, above = exchange(slab, low, high)
    own, low, high, keep = local_call(
        first_window, slab, [rates, own, below, above], window_outs, window_scratch, in_hbm=1
    )
    below, above = exchange(slab, low, high)
    (sent,) = local_call(
        last_window,
        slab,
        [rates, own, below, above, keep],
        [(slab.sub, MOVING // 2) + tile],
        window_scratch + [(slab.padded,) + tile],
        in_hbm=1,
    )
    came = lax.all_to_all(sent, ("gx", "gy"), split_axis=0, concat_axis=0, tiled=True)
    parts = local_call(
        return_heat, slab, [came], [(7,) + tile] * slab.grp, [(slab.grp, 7) + tile]
    )
    parts = across_planes(slab, parts)
    (populations_out,) = local_call(unpack_flow, slab, [came], [populations.shape])
    (thermal_out,) = local_call(join_heat, slab, parts, [thermal.shape])
    return populations_out, thermal_out


def solution(mesh):
    in_specs = (
        P(None, "gx", "gy", "grp"),
        P(None, ("gx", "grp"), "gy", None),
        P(None, "gx", "gy", "grp"),
        P("gx", "gy", "grp"),
        P(("gx", "grp"), "gy", None),
        P(),
        P(),
    )
    out_specs = (P(None, "gx", "gy", "grp"), P(None, ("gx", "grp"), "gy", None))

    def per_device(populations, thermal, *others):
        slab = Slab(mesh.shape, populations.shape[1:], thermal.shape[1:])
        plan = (lambda *arrays: on_slabs(slab, *arrays)) if slab.fits and WINDOWS == 2 else on_device
        return plan(populations, thermal, *others)

    return jax.shard_map(
        per_device, mesh=mesh, in_specs=in_specs, out_specs=out_specs, check_vma=False
    )
```

```python
import jax
import jax.numpy as jnp
import numpy as np
from jax import lax
from jax.experimental import pallas as pl
from jax.experimental.pallas import tpu as pltpu
from jax.sharding import PartitionSpec as P

STEPS = 4
WINDOWS = 2


HIGHEST = lax.Precision.HIGHEST
BUOYANCY = 0.03
REFERENCE_HEAT = 1.0
OFFSET_TABLE = [(number // 9 - 1, number // 3 % 3 - 1, number % 3 - 1) for number in range(27)]
LATTICE_WEIGHTS = np.array(
    [
        np.prod([2.0 / 3.0 if component == 0 else 1.0 / 6.0 for component in triple])
        for triple in OFFSET_TABLE
    ]
)
VANDERMONDE = np.array([[1.0, 1.0, 1.0], [-1.0, 0.0, 1.0], [1.0, 0.0, 1.0]])
VANDER_INVERSE = np.array([[0.0, -0.5, 0.5], [1.0, 0.0, -1.0], [0.0, 0.5, 0.5]])
MOMENT_MATRIX = np.kron(np.kron(VANDERMONDE, VANDERMONDE), VANDERMONDE)
MOMENT_INVERSE = np.kron(np.kron(VANDER_INVERSE, VANDER_INVERSE), VANDER_INVERSE)
RELAXED = np.array([0.0 if number in (0, 1, 3, 9) else 1.0 for number in range(27)])
SUMMING = np.concatenate([np.ones((1, 27)), 1.0 * np.array(OFFSET_TABLE).T], axis=0)
HEAT_WEIGHTS = np.array([0.25] + [0.125] * 6)


def from_behind(value, axis, steps):
    count = lax.axis_size(axis)
    pairs = [(source, (source + steps) % count) for source in range(count)]
    return lax.ppermute(value, axis, pairs)


def extended(cells, sides, width):
    for axis, dim in sides:
        count = lax.axis_size(axis)
        head = lax.slice_in_dim(cells, 0, width, axis=dim)
        tail = lax.slice_in_dim(cells, cells.shape[dim] - width, cells.shape[dim], axis=dim)
        cells = jnp.concatenate(
            [
                lax.ppermute(tail, axis, [(i, (i + 1) % count) for i in range(count)]),
                cells,
                lax.ppermute(head, axis, [((i + 1) % count, i) for i in range(count)]),
            ],
            axis=dim,
        )
    return cells


def flow_state(flat, heat_flat):
    sums = jnp.dot(jnp.asarray(SUMMING, jnp.float32), flat, precision=HIGHEST)
    density = sums[0]
    force = BUOYANCY * (heat_flat - REFERENCE_HEAT)
    speed = jnp.stack([sums[1], sums[2], sums[3] + 0.5 * force]) / density
    return (density, force, speed)


def collide(popul, heat, rates):
    flat = popul.reshape(27, -1)
    density, force, speed = flow_state(flat, heat.reshape(-1))
    along = jnp.dot(jnp.asarray(SUMMING[1:].T, jnp.float32), speed, precision=HIGHEST)
    square = jnp.sum(speed * speed, axis=0)
    balance = (
        density
        * jnp.asarray(LATTICE_WEIGHTS, jnp.float32)[:, None]
        * (1.0 + 3.0 * along + 4.5 * along * along - 1.5 * square)
    )
    scaled = (
        jnp.asarray(MOMENT_INVERSE, jnp.float32)
        * (rates * jnp.asarray(RELAXED, jnp.float32))[None, :]
    )
    relax = jnp.dot(scaled, jnp.asarray(MOMENT_MATRIX, jnp.float32), precision=HIGHEST)
    post = (
        flat
        - jnp.dot(relax, flat - balance, precision=HIGHEST)
        + jnp.asarray(MOMENT_INVERSE[:, 1], jnp.float32)[:, None] * force[None, :]
    )
    return post.reshape(popul.shape)


def flow_speed(popul, heat, solid):
    density, force, speed = flow_state(popul.reshape(27, -1), heat.reshape(-1))
    return jnp.where(solid[None] == 0, speed.reshape((3,) + solid.shape), 0.0)


def heat_collide(heat_pops, speed, relax_time):
    total = jnp.sum(heat_pops, axis=0)
    still = jnp.zeros_like(speed[0])
    along = jnp.stack([still, speed[0], -speed[0], speed[1], -speed[1], speed[2], -speed[2]])
    balance = (
        jnp.asarray(HEAT_WEIGHTS, jnp.float32)[:, None, None, None]
        * total[None]
        * (1.0 + 4.0 * along)
    )
    return heat_pops - (heat_pops - balance) / relax_time[None]


def relaxation(phase_ids, conductivity):
    levels = jnp.arange(conductivity.shape[0], dtype=jnp.int32)
    chosen = jnp.sum(
        jnp.where(
            phase_ids[None] == levels[:, None, None, None], conductivity[:, None, None, None], 0.0
        ),
        axis=0,
    )
    return 0.5 + 4.0 * chosen


def inner_window(padded, triple, sizes):
    return padded[
        1 - triple[0] : 1 - triple[0] + sizes[0],
        1 - triple[1] : 1 - triple[1] + sizes[1],
        1 - triple[2] : 1 - triple[2] + sizes[2],
    ]


def advance(grid, axis_number, send_up, send_down):
    space = 3 + axis_number
    length = grid.shape[space]
    rising = lax.index_in_dim(grid, 2, axis_number, keepdims=True)
    resting = lax.index_in_dim(grid, 1, axis_number, keepdims=True)
    falling = lax.index_in_dim(grid, 0, axis_number, keepdims=True)
    from_below = send_up(lax.slice_in_dim(rising, length - 1, length, axis=space))
    from_above = send_down(lax.slice_in_dim(falling, 0, 1, axis=space))
    rising = jnp.concatenate(
        [from_below, lax.slice_in_dim(rising, 0, length - 1, axis=space)], axis=space
    )
    falling = jnp.concatenate(
        [lax.slice_in_dim(falling, 1, length, axis=space), from_above], axis=space
    )
    return jnp.concatenate([falling, resting, rising], axis=axis_number)


def flow_arrivals(post):
    sizes = post.shape[1:]
    grid = post.reshape((3, 3, 3) + sizes)
    grid = advance(
        grid,
        0,
        lambda plane: from_behind(plane, "gx", 1),
        lambda plane: from_behind(plane, "gx", -1),
    )
    grid = advance(
        grid,
        1,
        lambda plane: from_behind(plane, "gy", 1),
        lambda plane: from_behind(plane, "gy", -1),
    )
    grid = advance(
        grid,
        2,
        lambda plane: from_behind(plane, "grp", 1),
        lambda plane: from_behind(plane, "grp", -1),
    )
    return grid.reshape(post.shape)


def stream_heat(post, grp_index, last_grp):
    length = post.shape[1]
    size_y = post.shape[2]
    eastward = post[1]
    westward = post[2]
    lower_first = from_behind(eastward, "grp", 1)
    lower_second = from_behind(lower_first, "gx", 1)
    entering = jnp.where(grp_index == 0, lower_second, lower_first)
    eastward = jnp.concatenate([entering, eastward[: length - 1]], axis=0)
    upper_first = from_behind(westward, "grp", -1)
    upper_second = from_behind(upper_first, "gx", -1)
    entering = jnp.where(grp_index == last_grp, upper_second, upper_first)
    westward = jnp.concatenate([westward[1:], entering], axis=0)
    sides = extended(post[3:5], (("gy", 2),), 1)
    northward = sides[0, :, 0:size_y]
    southward = sides[1, :, 2 : size_y + 2]
    upward = jnp.roll(post[5], 1, axis=2)
    downward = jnp.roll(post[6], -1, axis=2)
    return jnp.stack([post[0], eastward, westward, northward, southward, upward, downward])


def on_device(populations, thermal, velocity_prev, solid, phase_ids, conductivity, rates):
    padded_solid = extended(solid, (("grp", 2), ("gx", 0), ("gy", 1)), 1)
    sizes = solid.shape
    blocked = jnp.stack(
        [inner_window(padded_solid, OFFSET_TABLE[number], sizes) != 0 for number in range(27)]
    )
    fluid_cells = (solid == 0)[None]
    grp_index = lax.axis_index("grp")
    last_grp = lax.axis_size("grp") - 1
    relax_time = relaxation(phase_ids, conductivity)
    speed_brick = velocity_prev
    popul = populations
    heat_pops = thermal
    for window_number in range(WINDOWS):
        heat_brick = lax.all_to_all(
            jnp.sum(heat_pops, axis=0), "grp", split_axis=2, concat_axis=0, tiled=True
        )
        speed_column = lax.all_to_all(speed_brick, "grp", split_axis=1, concat_axis=3, tiled=True)
        for step_number in range(STEPS):
            post = collide(popul, heat_brick, rates)
            arrived = flow_arrivals(post)
            popul = jnp.where(fluid_cells, jnp.where(blocked, post[::-1], arrived), popul)
        for step_number in range(STEPS):
            heat_pops = stream_heat(
                heat_collide(heat_pops, speed_column, relax_time), grp_index, last_grp
            )
        if window_number + 1 < WINDOWS:
            speed_brick = flow_speed(popul, heat_brick, solid)
    return (popul, heat_pops)


SUBLANES = 8
LANES = 128
F32 = jnp.float32


class Slab:
    def __init__(self, mesh_shape, flow_block, heat_block):
        self.grp, self.gx, self.gy = (mesh_shape[name] for name in ("grp", "gx", "gy"))
        self.block_x, self.block_y, self.block_z = flow_block
        self.sub = self.gx * self.gy
        self.size_x = self.block_x * self.gx
        self.planes = self.block_z // self.sub
        self.deep = LANES // (self.size_x * self.gy) if self.size_x * self.gy <= LANES else 0
        self.fits = (
            self.block_y == SUBLANES
            and self.block_z == LANES
            and self.block_z % self.sub == 0
            and self.deep >= STEPS
            and self.deep * self.size_x * self.gy == LANES
            and self.planes == self.deep * self.gy
            and 2 * self.block_x == self.sub
            and self.size_x == self.sub
            and self.gx == 2
            and self.block_x == self.grp
            and heat_block == (1, SUBLANES, self.grp * LANES)
            and self.sub & (self.sub - 1) == 0
            and self.gy & (self.gy - 1) == 0
            and self.grp & (self.grp - 1) == 0
            and self.planes >= self.deep * WINDOWS
        )
        if self.fits:
            self.tiles = self.planes // self.deep
            self.margin = WINDOWS
            self.padded = self.tiles + 2 * self.margin
            self.snake = [
                x * self.gy + (y if x % 2 == 0 else self.gy - 1 - y)
                for x in range(self.gx)
                for y in range(self.gy)
            ]
            self.ring = [
                part * self.sub + self.snake[place if part % 2 == 0 else self.sub - 1 - place]
                for part in range(self.grp)
                for place in range(self.sub)
            ]

    def holder(self, place, part):
        return jnp.where(part % 2 == 0, self.snake[place], self.snake[self.sub - 1 - place])


def lane_index():
    return lax.broadcasted_iota(jnp.int32, (SUBLANES, LANES), 1)


def row_index():
    return lax.broadcasted_iota(jnp.int32, (SUBLANES, LANES), 0)


def lane_roll(value, amount):
    amount = amount % LANES
    return value if amount == 0 else pltpu.roll(value, amount, 1)


def swap_groups(values, group):
    count = len(values)
    lane = lane_index()
    values = list(values)
    bit = 1
    while bit < count:
        low = (lane // (group * bit)) % 2 == 0
        for first in range(count):
            if first & bit == 0:
                a, b = values[first], values[first | bit]
                values[first] = jnp.where(low, a, lane_roll(b, group * bit))
                values[first | bit] = jnp.where(low, lane_roll(a, -group * bit), b)
        bit *= 2
    return values


SENT_SPEED, SENT_SOLID, SENT_HEAT, SENT_RATE, SENT = 27, 30, 31, 38, 40
HEAT_AT, RATE_AT, SPEED_AT, SOLID_AT, ROWS = 27, 34, 35, 38, 39
MOVING = 34


def row_of(number):
    if number < SENT_SPEED:
        return number
    if number < SENT_SOLID:
        return SPEED_AT + number - SENT_SPEED
    if number == SENT_SOLID:
        return SOLID_AT
    return HEAT_AT + number - SENT_HEAT if number <= SENT_RATE else None


def offer_heat(slab, levels_hbm, heat_hbm, phase_hbm, *refs):
    outs, (levels_ref, heat_ref, phase_ref, sems) = refs[: slab.grp], refs[slab.grp :]
    copies = [
        pltpu.make_async_copy(heat_hbm, heat_ref, sems.at[0]),
        pltpu.make_async_copy(phase_hbm, phase_ref, sems.at[1]),
        pltpu.make_async_copy(levels_hbm, levels_ref, sems.at[2]),
    ]
    for copy in copies:
        copy.start()
    for copy in copies:
        copy.wait()
    mine = lax.axis_index("grp")
    for step in range(slab.grp):
        part = jnp.bitwise_xor(mine, step)
        span = pl.ds(pl.multiple_of(part * LANES, LANES), LANES)
        phase = phase_ref[0, :, span]
        chosen = jnp.zeros((SUBLANES, LANES), F32)
        for level in range(levels_ref.shape[0]):
            chosen = jnp.where(phase == level, levels_ref[level], chosen)
        for k in range(7):
            outs[step][k] = heat_ref[k, 0, :, span]
        outs[step][7] = 1.0 / (0.5 + 4.0 * chosen)


def pack_flow(
    slab, popul_hbm, speed_hbm, solid_hbm, sent, flags, popul_ref, speed_ref, solid_ref, sems
):
    half = 14
    copies = [
        pltpu.make_async_copy(popul_hbm.at[pl.ds(0, half)], popul_ref.at[pl.ds(0, half)], sems.at[0]),
        pltpu.make_async_copy(
            popul_hbm.at[pl.ds(half, 27 - half)], popul_ref.at[pl.ds(half, 27 - half)], sems.at[1]
        ),
        pltpu.make_async_copy(speed_hbm, speed_ref, sems.at[2]),
        pltpu.make_async_copy(solid_hbm, solid_ref, sems.at[3]),
    ]
    for copy in copies:
        copy.start()
    mine = lax.axis_index("grp")
    holders = [slab.holder(place, mine) for place in range(slab.sub)]

    def field(number, x):
        if number < SENT_SPEED:
            return popul_ref[number, x]
        return speed_ref[number - SENT_SPEED, x]

    copies[0].wait()
    for pair in range(SENT_SOLID // 2):
        if 2 * pair == half:
            copies[1].wait()
        if pair == SENT_SPEED // 2:
            copies[2].wait()
            copies[3].wait()
        sources = [field(2 * pair + h, x) for h in range(2) for x in range(slab.block_x)]
        for place, value in enumerate(swap_groups(sources, slab.planes)):
            sent[holders[place], pair] = value
    for x in range(slab.block_x):
        flags[x] = solid_ref[x].astype(F32)


def pack_heat(slab, sent_in, flags, *refs):
    parts, (sent, held, packed, sem) = refs[: slab.grp], refs[slab.grp :]
    mine = lax.axis_index("grp")
    holders = [slab.holder(place, mine) for place in range(slab.sub)]
    for step in range(slab.grp):
        held[jnp.bitwise_xor(mine, step)] = parts[step][...]
    zero = jnp.zeros((SUBLANES, LANES), F32)
    first = SENT_SOLID // 2

    def field(number, x):
        if number == SENT_SOLID:
            return flags[x]
        return held[x, number - SENT_HEAT] if number <= SENT_RATE else zero

    for pair in range(first, SENT // 2):
        sources = [field(2 * pair + h, x) for h in range(2) for x in range(slab.block_x)]
        for place, value in enumerate(swap_groups(sources, slab.planes)):
            packed[holders[place], pair - first] = value
    copy = pltpu.make_async_copy(packed, sent.at[:, pl.ds(first, SENT // 2 - first)], sem)
    copy.start()
    copy.wait()


def unpack_in(slab, came, state_out, low_out, high_out):
    half = slab.block_x * slab.planes
    first_half = lane_index() < half

    def put(row, by_gy):
        for tile, value in enumerate(swap_groups(by_gy, slab.deep)):
            state_out[row, tile] = value
            if tile < slab.margin:
                low_out[row, tile] = value
            if tile >= slab.tiles - slab.margin:
                high_out[row, tile - (slab.tiles - slab.margin)] = value

    for pair in range(SENT // 2):
        firsts, seconds = [], []
        for y in range(slab.gy):
            a, b = came[y, pair], came[slab.gy + y, pair]
            firsts.append(jnp.where(first_half, a, lane_roll(b, half)))
            seconds.append(jnp.where(first_half, lane_roll(a, half), b))
        put(row_of(2 * pair), firsts)
        if row_of(2 * pair + 1) is not None:
            put(row_of(2 * pair + 1), seconds)


def pack_out(slab, take, sent):
    half = slab.block_x * slab.planes
    first_half = lane_index() < half

    def by_gy(row):
        return swap_groups([take(row, tile) for tile in range(slab.tiles)], slab.deep)

    for pair in range(MOVING // 2):
        firsts, seconds = by_gy(2 * pair), by_gy(2 * pair + 1)
        for y in range(slab.gy):
            a, b = firsts[y], seconds[y]
            sent[y, pair] = jnp.where(first_half, a, lane_roll(b, half))
            sent[slab.gy + y, pair] = jnp.where(first_half, lane_roll(a, half), b)


def unpack_pair(slab, came, pair):
    mine = lax.axis_index("grp")
    sources = [came[slab.holder(place, mine), pair] for place in range(slab.sub)]
    for number, value in enumerate(swap_groups(sources, slab.planes)):
        yield 2 * pair + number // slab.block_x, number % slab.block_x, value


def return_heat(slab, came, *refs):
    outs, held = refs[: slab.grp], refs[slab.grp]
    for pair in range(HEAT_AT // 2, MOVING // 2):
        for row, x, value in unpack_pair(slab, came, pair):
            if row >= HEAT_AT:
                held[x, row - HEAT_AT] = value
    mine = lax.axis_index("grp")
    for step in range(slab.grp):
        outs[step][...] = held[jnp.bitwise_xor(mine, step)]


def unpack_flow(slab, came, popul_out):
    for pair in range((HEAT_AT + 1) // 2):
        for row, x, value in unpack_pair(slab, came, pair):
            if row < HEAT_AT:
                popul_out[row, x] = value


def join_heat(slab, *refs):
    parts, thermal_out = refs[: slab.grp], refs[slab.grp]
    mine = lax.axis_index("grp")
    for step in range(slab.grp):
        part = jnp.bitwise_xor(mine, step)
        span = pl.ds(pl.multiple_of(part * LANES, LANES), LANES)
        for k in range(7):
            thermal_out[k, 0, :, span] = parts[step][k]


def forward3(values):
    for stride in (9, 3, 1):
        out = [None] * 27
        for n in range(27):
            if n // stride % 3 == 0:
                a, b, c = values[n], values[n + stride], values[n + 2 * stride]
                both = a + c
                out[n], out[n + stride], out[n + 2 * stride] = both + b, c - a, both
        values = out
    return values


def backward3(values):
    for stride in (9, 3, 1):
        out = [None] * 27
        for n in range(27):
            if n // stride % 3 == 0:
                a, b, c = values[n], values[n + stride], values[n + 2 * stride]
                even, odd = 0.5 * c, 0.5 * b
                out[n], out[n + stride], out[n + 2 * stride] = even - odd, a - c, even + odd
        values = out
    return values


def collide_tile(values, force, rate):
    moments = forward3(values)
    density = moments[0]
    jx, jy, jz = moments[9], moments[3], moments[1] + 0.5 * force
    inverse = 1.0 / density
    flux = (jx, jy, jz)
    u = tuple(j * inverse for j in flux)
    third = 1.0 / 3.0
    base = {0: density}
    for k in (1, 2, 3):
        base[k] = density * third**k
    squares = [flux[d] * u[d] for d in range(3)]
    square_at = {}
    scaled = {}

    def scale(key, value, count):
        if count == 0:
            return value
        if (key, count) not in scaled:
            scaled[key, count] = value * third**count
        return scaled[key, count]

    cross = {(0, 1): jx * u[1], (0, 2): jx * u[2], (1, 2): jy * u[2]}
    out = [None] * 27
    for n in range(27):
        powers = (n // 9, n // 3 % 3, n % 3)
        if n in (0, 3, 9):
            out[n] = moments[n]
            continue
        if n == 1:
            out[n] = moments[n] + force
            continue
        odd = tuple(d for d in range(3) if powers[d] == 1)
        even = tuple(d for d in range(3) if powers[d] == 2)
        count = len(even)
        if len(odd) == 3:
            out[n] = moments[n] - rate(n) * moments[n]
            continue
        if len(odd) == 0:
            if even not in square_at:
                total = squares[even[0]]
                for d in even[1:]:
                    total = total + squares[d]
                square_at[even] = base[count] + (total * (3.0 * third**count) if count > 1 else total)
            level = square_at[even]
        elif len(odd) == 1:
            level = scale(odd, flux[odd[0]], count)
        else:
            level = scale(odd, cross[odd], count)
        out[n] = moments[n] - rate(n) * (moments[n] - level)
    return backward3(out)


def shifters(slab):
    lane, row = lane_index(), row_index()
    per_x = slab.gy * slab.deep
    in_z = lane % slab.deep
    in_y = (lane // slab.deep) % slab.gy
    z_edge = {1: in_z == 0, -1: in_z == slab.deep - 1}
    y_edge = {1: in_y == 0, -1: in_y == slab.gy - 1}
    row_edge = {1: row == 0, -1: row == SUBLANES - 1}

    def along_x(value, step):
        return lane_roll(value, step * per_x)

    def along_y(value, step):
        turned = pltpu.roll(value, step % SUBLANES, 0)
        near = lane_roll(turned, step * slab.deep)
        far = lane_roll(turned, step * (slab.deep - per_x))
        return jnp.where(row_edge[step], jnp.where(y_edge[step], far, near), turned)

    def along_z(value, beside, step):
        return jnp.where(z_edge[step], lane_roll(beside, step * (1 - slab.deep)), lane_roll(value, step))

    return along_x, along_y, along_z


HEAT_OFFSETS = [(0, 0, 0), (1, 0, 0), (-1, 0, 0), (0, 1, 0), (0, -1, 0), (0, 0, 1), (0, 0, -1)]


def run_steps(slab, rates_ref, state, post, force_ref, rate_ref, speed_ref, solid_ref, tiles):
    def collide_one(tile):
        values = [state[n, tile] for n in range(27)]
        solid = solid_ref[tile] != 0.0
        moved = collide_tile(values, force_ref[tile], lambda n: rates_ref[n])
        for n in range(27):
            post[n, tile] = jnp.where(solid, jnp.nan, moved[n])
        heat = [state[HEAT_AT + k, tile] for k in range(7)]
        total = heat[0]
        for k in range(1, 7):
            total = total + heat[k]
        omega = rate_ref[tile]
        side = 0.125 * total
        half = 0.5 * total
        for k in range(7):
            if k == 0:
                level = 0.25 * total
            else:
                drift = half * speed_ref[(k - 1) // 2, tile]
                level = side + drift if k % 2 == 1 else side - drift
            post[HEAT_AT + k, tile] = heat[k] - (heat[k] - level) * omega

    def stream_one(tile, shifts):
        along_x, along_y, along_z = shifts
        before, after = max(tile - 1, tiles[0]), min(tile + 1, tiles[-1])
        solid = solid_ref[tile] != 0.0

        def arrive(row, offset):
            value = post[row, tile]
            if offset[2] != 0:
                value = along_z(value, post[row, before if offset[2] == 1 else after], offset[2])
            if offset[1] != 0:
                value = along_y(value, offset[1])
            if offset[0] != 0:
                value = along_x(value, offset[0])
            return value

        for n in range(27):
            value = arrive(n, OFFSET_TABLE[n])
            value = jnp.where(value != value, post[26 - n, tile], value)
            state[n, tile] = jnp.where(solid, state[n, tile], value)
        for k in range(7):
            state[HEAT_AT + k, tile] = arrive(HEAT_AT + k, HEAT_OFFSETS[k])

    def step(number, _):
        shifts = shifters(slab)
        for tile in tiles:
            collide_one(tile)
            if tile > tiles[0]:
                stream_one(tile - 1, shifts)
        stream_one(tiles[-1], shifts)
        return 0

    lax.fori_loop(0, STEPS, step, 0)


def heat_force(state, tile):
    total = state[HEAT_AT, tile]
    for k in range(1, 7):
        total = total + state[HEAT_AT + k, tile]
    return BUOYANCY * (total - REFERENCE_HEAT)


def flow_speed_tile(state, tile, force):
    values = [state[n, tile] for n in range(27)]
    total = values[0]
    for n in range(1, 27):
        total = total + values[n]
    sums = []
    for d in range(3):
        plus, minus = None, None
        for n in range(27):
            part = OFFSET_TABLE[n][d]
            if part == 1:
                plus = values[n] if plus is None else plus + values[n]
            if part == -1:
                minus = values[n] if minus is None else minus + values[n]
        sums.append(plus - minus)
    sums[2] = sums[2] + 0.5 * force
    return [each / total for each in sums]


def both_windows(slab, rates_hbm, own_ref, low_ref, high_ref, *refs):
    sent, rates_ref, sem, state, post, speed, force, rate_ref, solid_ref = refs
    rates_copy = pltpu.make_async_copy(rates_hbm, rates_ref, sem)
    rates_copy.start()
    margin = slab.margin

    def gather(row, tile):
        if tile < margin:
            return low_ref[row, tile]
        if tile >= slab.padded - margin:
            return high_ref[row, tile - (slab.padded - margin)]
        return own_ref[row, tile - margin]

    for tile in range(slab.padded):
        for row in range(MOVING):
            state[row, tile] = gather(row, tile)
        for d in range(3):
            speed[d, tile] = gather(SPEED_AT + d, tile)
        rate_ref[tile] = gather(RATE_AT, tile)
        solid_ref[tile] = gather(SOLID_AT, tile)
        force[tile] = heat_force(state, tile)
    rates_copy.wait()
    for window in range(WINDOWS):
        tiles = list(range(window, slab.padded - window))
        if window > 0:
            for tile in tiles:
                solid = solid_ref[tile] != 0.0
                for d, each in enumerate(flow_speed_tile(state, tile, force[tile])):
                    speed[d, tile] = jnp.where(solid, 0.0, each)
                force[tile] = heat_force(state, tile)
        run_steps(slab, rates_ref, state, post, force, rate_ref, speed, solid_ref, tiles)
    pack_out(slab, lambda row, tile: state[row, tile + margin], sent)


def local_call(body, slab, arrays, outs, scratch=(), in_hbm=0, carried=False):
    def kernel(*refs):
        body(slab, *refs)

    return pl.pallas_call(
        kernel,
        out_shape=[jax.ShapeDtypeStruct(shape, F32) for shape in outs],
        in_specs=[
            pl.BlockSpec(
                memory_space=pltpu.HBM if i < in_hbm else pl.ANY if carried and i == 0 else pltpu.VMEM
            )
            for i in range(len(arrays))
        ],
        out_specs=[pl.BlockSpec(memory_space=pl.ANY if carried else pltpu.VMEM)] * len(outs),
        input_output_aliases={0: 0} if carried else {},
        scratch_shapes=[pltpu.VMEM(s, F32) if isinstance(s, tuple) else s for s in scratch],
        compiler_params=pltpu.CompilerParams(vmem_limit_bytes=24 * 1024 * 1024),
    )(
        *(
            pltpu.with_memory_space_constraint(array, pltpu.HBM) if i < in_hbm else array
            for i, array in enumerate(arrays)
        )
    )


RING = ("grp", "gx", "gy")


def exchange(slab, low, high):
    ring = slab.ring
    upward = [(ring[i - 1], ring[i]) for i in range(len(ring))]
    from_below = lax.ppermute(high, RING, upward)
    from_above = lax.ppermute(low, RING, [(b, a) for a, b in upward])
    return from_below, from_above


def across_planes(slab, parts):
    return [parts[0]] + [
        lax.ppermute(parts[step], "grp", [(i, i ^ step) for i in range(slab.grp)])
        for step in range(1, slab.grp)
    ]


def on_slabs(slab, populations, thermal, velocity_prev, solid, phase_ids, conductivity, rates):
    tile = (SUBLANES, LANES)

    def vmem_like(array):
        return pltpu.VMEM(array.shape, array.dtype)

    parts = local_call(
        offer_heat,
        slab,
        [conductivity, thermal, phase_ids],
        [(8,) + tile] * slab.grp,
        [
            pltpu.SMEM(conductivity.shape, F32),
            vmem_like(thermal),
            vmem_like(phase_ids),
            pltpu.SemaphoreType.DMA((3,)),
        ],
        in_hbm=3,
    )
    parts = across_planes(slab, parts)
    sent_shape = (slab.sub, SENT // 2) + tile
    sent, flags = local_call(
        pack_flow,
        slab,
        [populations, velocity_prev, solid],
        [sent_shape, solid.shape],
        [
            vmem_like(populations),
            vmem_like(velocity_prev),
            vmem_like(solid),
            pltpu.SemaphoreType.DMA((4,)),
        ],
        in_hbm=3,
    )
    (sent,) = local_call(
        pack_heat,
        slab,
        [sent, flags] + parts,
        [sent_shape],
        [
            (slab.grp, 8) + tile,
            (slab.sub, (SENT - SENT_SOLID) // 2) + tile,
            pltpu.SemaphoreType.DMA,
        ],
        carried=True,
    )
    came = lax.all_to_all(sent, ("gx", "gy"), split_axis=0, concat_axis=0, tiled=True)
    own, low, high = local_call(
        unpack_in,
        slab,
        [came],
        [(ROWS, slab.tiles) + tile, (ROWS, slab.margin) + tile, (ROWS, slab.margin) + tile],
    )
    below, above = exchange(slab, low, high)
    (sent,) = local_call(
        both_windows,
        slab,
        [rates, own, below, above],
        [(slab.sub, MOVING // 2) + tile],
        [
            pltpu.SMEM(rates.shape, F32),
            pltpu.SemaphoreType.DMA,
            (MOVING, slab.padded) + tile,
            (MOVING, slab.padded) + tile,
            (3, slab.padded) + tile,
            (slab.padded,) + tile,
            (slab.padded,) + tile,
            (slab.padded,) + tile,
        ],
        in_hbm=1,
    )
    came = lax.all_to_all(sent, ("gx", "gy"), split_axis=0, concat_axis=0, tiled=True)
    parts = local_call(
        return_heat, slab, [came], [(7,) + tile] * slab.grp, [(slab.grp, 7) + tile]
    )
    parts = across_planes(slab, parts)
    (populations_out,) = local_call(unpack_flow, slab, [came], [populations.shape])
    (thermal_out,) = local_call(join_heat, slab, parts, [thermal.shape])
    return populations_out, thermal_out


def solution(mesh):
    in_specs = (
        P(None, "gx", "gy", "grp"),
        P(None, ("gx", "grp"), "gy", None),
        P(None, "gx", "gy", "grp"),
        P("gx", "gy", "grp"),
        P(("gx", "grp"), "gy", None),
        P(),
        P(),
    )
    out_specs = (P(None, "gx", "gy", "grp"), P(None, ("gx", "grp"), "gy", None))

    def per_device(populations, thermal, *others):
        slab = Slab(mesh.shape, populations.shape[1:], thermal.shape[1:])
        plan = (lambda *arrays: on_slabs(slab, *arrays)) if slab.fits else on_device
        return plan(populations, thermal, *others)

    return jax.shard_map(
        per_device, mesh=mesh, in_specs=in_specs, out_specs=out_specs, check_vma=False
    )
```

```python
import jax
import jax.numpy as jnp
import numpy as np
from jax import lax
from jax.experimental import pallas as pl
from jax.experimental.pallas import tpu as pltpu
from jax.sharding import PartitionSpec as P

STEPS = 4
WINDOWS = 2


HIGHEST = lax.Precision.HIGHEST
BUOYANCY = 0.03
REFERENCE_HEAT = 1.0
OFFSET_TABLE = [(number // 9 - 1, number // 3 % 3 - 1, number % 3 - 1) for number in range(27)]
LATTICE_WEIGHTS = np.array(
    [
        np.prod([2.0 / 3.0 if component == 0 else 1.0 / 6.0 for component in triple])
        for triple in OFFSET_TABLE
    ]
)
VANDERMONDE = np.array([[1.0, 1.0, 1.0], [-1.0, 0.0, 1.0], [1.0, 0.0, 1.0]])
VANDER_INVERSE = np.array([[0.0, -0.5, 0.5], [1.0, 0.0, -1.0], [0.0, 0.5, 0.5]])
MOMENT_MATRIX = np.kron(np.kron(VANDERMONDE, VANDERMONDE), VANDERMONDE)
MOMENT_INVERSE = np.kron(np.kron(VANDER_INVERSE, VANDER_INVERSE), VANDER_INVERSE)
RELAXED = np.array([0.0 if number in (0, 1, 3, 9) else 1.0 for number in range(27)])
SUMMING = np.concatenate([np.ones((1, 27)), 1.0 * np.array(OFFSET_TABLE).T], axis=0)
HEAT_WEIGHTS = np.array([0.25] + [0.125] * 6)


def from_behind(value, axis, steps):
    count = lax.axis_size(axis)
    pairs = [(source, (source + steps) % count) for source in range(count)]
    return lax.ppermute(value, axis, pairs)


def extended(cells, sides, width):
    for axis, dim in sides:
        count = lax.axis_size(axis)
        head = lax.slice_in_dim(cells, 0, width, axis=dim)
        tail = lax.slice_in_dim(cells, cells.shape[dim] - width, cells.shape[dim], axis=dim)
        cells = jnp.concatenate(
            [
                lax.ppermute(tail, axis, [(i, (i + 1) % count) for i in range(count)]),
                cells,
                lax.ppermute(head, axis, [((i + 1) % count, i) for i in range(count)]),
            ],
            axis=dim,
        )
    return cells


def flow_state(flat, heat_flat):
    sums = jnp.dot(jnp.asarray(SUMMING, jnp.float32), flat, precision=HIGHEST)
    density = sums[0]
    force = BUOYANCY * (heat_flat - REFERENCE_HEAT)
    speed = jnp.stack([sums[1], sums[2], sums[3] + 0.5 * force]) / density
    return (density, force, speed)


def collide(popul, heat, rates):
    flat = popul.reshape(27, -1)
    density, force, speed = flow_state(flat, heat.reshape(-1))
    along = jnp.dot(jnp.asarray(SUMMING[1:].T, jnp.float32), speed, precision=HIGHEST)
    square = jnp.sum(speed * speed, axis=0)
    balance = (
        density
        * jnp.asarray(LATTICE_WEIGHTS, jnp.float32)[:, None]
        * (1.0 + 3.0 * along + 4.5 * along * along - 1.5 * square)
    )
    scaled = (
        jnp.asarray(MOMENT_INVERSE, jnp.float32)
        * (rates * jnp.asarray(RELAXED, jnp.float32))[None, :]
    )
    relax = jnp.dot(scaled, jnp.asarray(MOMENT_MATRIX, jnp.float32), precision=HIGHEST)
    post = (
        flat
        - jnp.dot(relax, flat - balance, precision=HIGHEST)
        + jnp.asarray(MOMENT_INVERSE[:, 1], jnp.float32)[:, None] * force[None, :]
    )
    return post.reshape(popul.shape)


def flow_speed(popul, heat, solid):
    density, force, speed = flow_state(popul.reshape(27, -1), heat.reshape(-1))
    return jnp.where(solid[None] == 0, speed.reshape((3,) + solid.shape), 0.0)


def heat_collide(heat_pops, speed, relax_time):
    total = jnp.sum(heat_pops, axis=0)
    still = jnp.zeros_like(speed[0])
    along = jnp.stack([still, speed[0], -speed[0], speed[1], -speed[1], speed[2], -speed[2]])
    balance = (
        jnp.asarray(HEAT_WEIGHTS, jnp.float32)[:, None, None, None]
        * total[None]
        * (1.0 + 4.0 * along)
    )
    return heat_pops - (heat_pops - balance) / relax_time[None]


def relaxation(phase_ids, conductivity):
    levels = jnp.arange(conductivity.shape[0], dtype=jnp.int32)
    chosen = jnp.sum(
        jnp.where(
            phase_ids[None] == levels[:, None, None, None], conductivity[:, None, None, None], 0.0
        ),
        axis=0,
    )
    return 0.5 + 4.0 * chosen


def inner_window(padded, triple, sizes):
    return padded[
        1 - triple[0] : 1 - triple[0] + sizes[0],
        1 - triple[1] : 1 - triple[1] + sizes[1],
        1 - triple[2] : 1 - triple[2] + sizes[2],
    ]


def advance(grid, axis_number, send_up, send_down):
    space = 3 + axis_number
    length = grid.shape[space]
    rising = lax.index_in_dim(grid, 2, axis_number, keepdims=True)
    resting = lax.index_in_dim(grid, 1, axis_number, keepdims=True)
    falling = lax.index_in_dim(grid, 0, axis_number, keepdims=True)
    from_below = send_up(lax.slice_in_dim(rising, length - 1, length, axis=space))
    from_above = send_down(lax.slice_in_dim(falling, 0, 1, axis=space))
    rising = jnp.concatenate(
        [from_below, lax.slice_in_dim(rising, 0, length - 1, axis=space)], axis=space
    )
    falling = jnp.concatenate(
        [lax.slice_in_dim(falling, 1, length, axis=space), from_above], axis=space
    )
    return jnp.concatenate([falling, resting, rising], axis=axis_number)


def flow_arrivals(post):
    sizes = post.shape[1:]
    grid = post.reshape((3, 3, 3) + sizes)
    grid = advance(
        grid,
        0,
        lambda plane: from_behind(plane, "gx", 1),
        lambda plane: from_behind(plane, "gx", -1),
    )
    grid = advance(
        grid,
        1,
        lambda plane: from_behind(plane, "gy", 1),
        lambda plane: from_behind(plane, "gy", -1),
    )
    grid = advance(
        grid,
        2,
        lambda plane: from_behind(plane, "grp", 1),
        lambda plane: from_behind(plane, "grp", -1),
    )
    return grid.reshape(post.shape)


def stream_heat(post, grp_index, last_grp):
    length = post.shape[1]
    size_y = post.shape[2]
    eastward = post[1]
    westward = post[2]
    lower_first = from_behind(eastward, "grp", 1)
    lower_second = from_behind(lower_first, "gx", 1)
    entering = jnp.where(grp_index == 0, lower_second, lower_first)
    eastward = jnp.concatenate([entering, eastward[: length - 1]], axis=0)
    upper_first = from_behind(westward, "grp", -1)
    upper_second = from_behind(upper_first, "gx", -1)
    entering = jnp.where(grp_index == last_grp, upper_second, upper_first)
    westward = jnp.concatenate([westward[1:], entering], axis=0)
    sides = extended(post[3:5], (("gy", 2),), 1)
    northward = sides[0, :, 0:size_y]
    southward = sides[1, :, 2 : size_y + 2]
    upward = jnp.roll(post[5], 1, axis=2)
    downward = jnp.roll(post[6], -1, axis=2)
    return jnp.stack([post[0], eastward, westward, northward, southward, upward, downward])


def on_device(populations, thermal, velocity_prev, solid, phase_ids, conductivity, rates):
    padded_solid = extended(solid, (("grp", 2), ("gx", 0), ("gy", 1)), 1)
    sizes = solid.shape
    blocked = jnp.stack(
        [inner_window(padded_solid, OFFSET_TABLE[number], sizes) != 0 for number in range(27)]
    )
    fluid_cells = (solid == 0)[None]
    grp_index = lax.axis_index("grp")
    last_grp = lax.axis_size("grp") - 1
    relax_time = relaxation(phase_ids, conductivity)
    speed_brick = velocity_prev
    popul = populations
    heat_pops = thermal
    for window_number in range(WINDOWS):
        heat_brick = lax.all_to_all(
            jnp.sum(heat_pops, axis=0), "grp", split_axis=2, concat_axis=0, tiled=True
        )
        speed_column = lax.all_to_all(speed_brick, "grp", split_axis=1, concat_axis=3, tiled=True)
        for step_number in range(STEPS):
            post = collide(popul, heat_brick, rates)
            arrived = flow_arrivals(post)
            popul = jnp.where(fluid_cells, jnp.where(blocked, post[::-1], arrived), popul)
        for step_number in range(STEPS):
            heat_pops = stream_heat(
                heat_collide(heat_pops, speed_column, relax_time), grp_index, last_grp
            )
        if window_number + 1 < WINDOWS:
            speed_brick = flow_speed(popul, heat_brick, solid)
    return (popul, heat_pops)


SUBLANES = 8
LANES = 128
F32 = jnp.float32


class Slab:
    def __init__(self, mesh_shape, flow_block, heat_block):
        self.grp, self.gx, self.gy = (mesh_shape[name] for name in ("grp", "gx", "gy"))
        self.block_x, self.block_y, self.block_z = flow_block
        self.sub = self.gx * self.gy
        self.size_x = self.block_x * self.gx
        self.planes = self.block_z // self.sub
        self.deep = LANES // (self.size_x * self.gy) if self.size_x * self.gy <= LANES else 0
        self.fits = (
            self.block_y == SUBLANES
            and self.block_z == LANES
            and self.block_z % self.sub == 0
            and self.deep >= STEPS
            and self.deep * self.size_x * self.gy == LANES
            and self.planes == self.deep * self.gy
            and 2 * self.block_x == self.sub
            and self.size_x == self.sub
            and self.gx == 2
            and self.block_x == self.grp
            and heat_block == (1, SUBLANES, self.grp * LANES)
            and self.sub & (self.sub - 1) == 0
            and self.gy & (self.gy - 1) == 0
            and self.grp & (self.grp - 1) == 0
            and self.planes >= self.deep * WINDOWS
        )
        if self.fits:
            self.tiles = self.planes // self.deep
            self.margin = WINDOWS
            self.padded = self.tiles + 2 * self.margin
            self.snake = [
                x * self.gy + (y if x % 2 == 0 else self.gy - 1 - y)
                for x in range(self.gx)
                for y in range(self.gy)
            ]
            self.ring = [
                part * self.sub + self.snake[place if part % 2 == 0 else self.sub - 1 - place]
                for part in range(self.grp)
                for place in range(self.sub)
            ]

    def holders(self):
        even = lax.axis_index("grp") % 2 == 0
        return [jnp.where(even, *pair) for pair in zip(self.snake, self.snake[::-1])]


def lane_index():
    return lax.broadcasted_iota(jnp.int32, (SUBLANES, LANES), 1)


def row_index():
    return lax.broadcasted_iota(jnp.int32, (SUBLANES, LANES), 0)


def lane_roll(value, amount):
    amount = amount % LANES
    return value if amount == 0 else pltpu.roll(value, amount, 1)


def swap_groups(values, group):
    count = len(values)
    lane = lane_index()
    values = list(values)
    bit = 1
    while bit < count:
        low = (lane // (group * bit)) % 2 == 0
        for first in range(count):
            if first & bit == 0:
                a, b = values[first], values[first | bit]
                values[first] = jnp.where(low, a, lane_roll(b, group * bit))
                values[first | bit] = jnp.where(low, lane_roll(a, -group * bit), b)
        bit *= 2
    return values


SPEED_AT, SOLID_AT, HEAT_AT, RATE_AT, ROWS = 27, 30, 31, 38, 40
MOVING = 34


def moving_row(number):
    return number + (HEAT_AT - SPEED_AT) * (number >= SPEED_AT)


def offer_heat(slab, levels_hbm, heat_hbm, phase_hbm, *refs):
    outs, (levels_ref, heat_ref, phase_ref, sems) = refs[: slab.grp], refs[slab.grp :]
    copies = [
        pltpu.make_async_copy(heat_hbm, heat_ref, sems.at[0]),
        pltpu.make_async_copy(phase_hbm, phase_ref, sems.at[1]),
        pltpu.make_async_copy(levels_hbm, levels_ref, sems.at[2]),
    ]
    for copy in copies:
        copy.start()
    for copy in copies:
        copy.wait()
    mine = lax.axis_index("grp")
    for step in range(slab.grp):
        part = jnp.bitwise_xor(mine, step)
        span = pl.ds(pl.multiple_of(part * LANES, LANES), LANES)
        phase = phase_ref[0, :, span]
        chosen = jnp.zeros((SUBLANES, LANES), F32)
        for level in range(levels_ref.shape[0]):
            chosen = jnp.where(phase == level, levels_ref[level], chosen)
        for k in range(7):
            outs[step][k] = heat_ref[k, 0, :, span]
        outs[step][7] = 1.0 / (0.5 + 4.0 * chosen)


def pack_flow(slab, popul_hbm, speed_hbm, solid_hbm, sent, flags, fields, solid_ref, sems):
    copies = [
        pltpu.make_async_copy(popul_hbm, fields.at[pl.ds(0, SPEED_AT)], sems.at[0]),
        pltpu.make_async_copy(speed_hbm, fields.at[pl.ds(SPEED_AT, 3)], sems.at[1]),
        pltpu.make_async_copy(solid_hbm, solid_ref, sems.at[2]),
    ]
    for copy in copies:
        copy.start()
    for copy in copies:
        copy.wait()
    holders = slab.holders()

    def one(pair, _):
        pack_pair(slab, fields, pair, sent, pair, holders)
        return 0

    lax.fori_loop(0, SOLID_AT // 2, one, 0)
    flags[...] = solid_ref[...].astype(F32)


def pack_pair(slab, fields, source, sent, target, holders):
    sources = [fields[2 * source + h, x] for h in range(2) for x in range(slab.block_x)]
    for place, value in enumerate(swap_groups(sources, slab.planes)):
        sent[holders[place], target] = value


def pack_heat(slab, sent_in, flags, *refs):
    parts, (sent, held, packed, sem) = refs[: slab.grp], refs[slab.grp :]
    mine = lax.axis_index("grp")
    holders = slab.holders()
    held[0] = flags[...]
    held[9] = jnp.zeros(flags.shape, F32)
    for step in range(slab.grp):
        held[pl.ds(1, 8), jnp.bitwise_xor(mine, step)] = parts[step][...]
    first, count = SOLID_AT // 2, (ROWS - SOLID_AT) // 2

    def one(pair, _):
        pack_pair(slab, held, pair, packed, pair, holders)
        return 0

    lax.fori_loop(0, count, one, 0)
    copy = pltpu.make_async_copy(packed, sent.at[:, pl.ds(first, count)], sem)
    copy.start()
    copy.wait()


def unpack_in(slab, came, state_out, low_out, high_out):
    half = slab.block_x * slab.planes

    def put(row, by_gy):
        for tile, value in enumerate(swap_groups(by_gy, slab.deep)):
            state_out[row, tile] = value
            if tile < slab.margin:
                low_out[row, tile] = value
            if tile >= slab.tiles - slab.margin:
                high_out[row, tile - (slab.tiles - slab.margin)] = value

    def one(pair, _):
        first_half = lane_index() < half
        firsts, seconds = [], []
        for y in range(slab.gy):
            a, b = came[y, pair], came[slab.gy + y, pair]
            firsts.append(jnp.where(first_half, a, lane_roll(b, half)))
            seconds.append(jnp.where(first_half, lane_roll(a, half), b))
        put(2 * pair, firsts)
        put(2 * pair + 1, seconds)
        return 0

    lax.fori_loop(0, ROWS // 2, one, 0)


def pack_out(slab, take, sent):
    half = slab.block_x * slab.planes

    def by_gy(row):
        return swap_groups([take(row, tile) for tile in range(slab.tiles)], slab.deep)

    def one(pair, _):
        first_half = lane_index() < half
        firsts, seconds = by_gy(moving_row(2 * pair)), by_gy(moving_row(2 * pair + 1))
        for y in range(slab.gy):
            a, b = firsts[y], seconds[y]
            sent[y, pair] = jnp.where(first_half, a, lane_roll(b, half))
            sent[slab.gy + y, pair] = jnp.where(first_half, lane_roll(a, half), b)
        return 0

    lax.fori_loop(0, MOVING // 2, one, 0)


def unpack_pair(slab, came, pair, holders):
    sources = [came[holders[place], pair] for place in range(slab.sub)]
    values = swap_groups(sources, slab.planes)
    return [values[: slab.block_x], values[slab.block_x :]]


def return_heat(slab, came, *refs):
    outs, held = refs[: slab.grp], refs[slab.grp]
    holders = slab.holders()
    _, values = unpack_pair(slab, came, SPEED_AT // 2, holders)
    for x in range(slab.block_x):
        held[x, 0] = values[x]

    def one(pair, _):
        for h, values in enumerate(unpack_pair(slab, came, SPEED_AT // 2 + 1 + pair, holders)):
            for x in range(slab.block_x):
                held[x, 2 * pair + 1 + h] = values[x]
        return 0

    lax.fori_loop(0, 3, one, 0)
    mine = lax.axis_index("grp")
    for step in range(slab.grp):
        outs[step][...] = held[jnp.bitwise_xor(mine, step)]


def unpack_flow(slab, came, popul_out):
    holders = slab.holders()

    def one(pair, _):
        for h, values in enumerate(unpack_pair(slab, came, pair, holders)):
            for x in range(slab.block_x):
                popul_out[2 * pair + h, x] = values[x]
        return 0

    lax.fori_loop(0, SPEED_AT // 2, one, 0)
    values, _ = unpack_pair(slab, came, SPEED_AT // 2, holders)
    for x in range(slab.block_x):
        popul_out[SPEED_AT - 1, x] = values[x]


def join_heat(slab, *refs):
    parts, thermal_out = refs[: slab.grp], refs[slab.grp]
    mine = lax.axis_index("grp")
    for step in range(slab.grp):
        part = jnp.bitwise_xor(mine, step)
        span = pl.ds(pl.multiple_of(part * LANES, LANES), LANES)
        for k in range(7):
            thermal_out[k, 0, :, span] = parts[step][k]


def forward3(values):
    for stride in (9, 3, 1):
        out = [None] * 27
        for n in range(27):
            if n // stride % 3 == 0:
                a, b, c = values[n], values[n + stride], values[n + 2 * stride]
                both = a + c
                out[n], out[n + stride], out[n + 2 * stride] = both + b, c - a, both
        values = out
    return values


def backward3(values):
    for stride in (9, 3, 1):
        out = [None] * 27
        for n in range(27):
            if n // stride % 3 == 0:
                a, b, c = values[n], values[n + stride], values[n + 2 * stride]
                even, odd = 0.5 * c, 0.5 * b
                out[n], out[n + stride], out[n + 2 * stride] = even - odd, a - c, even + odd
        values = out
    return values


def collide_tile(values, force, rate):
    moments = forward3(values)
    density = moments[0]
    jx, jy, jz = moments[9], moments[3], moments[1] + 0.5 * force
    inverse = 1.0 / density
    flux = (jx, jy, jz)
    u = tuple(j * inverse for j in flux)
    third = 1.0 / 3.0
    base = {0: density}
    for k in (1, 2, 3):
        base[k] = density * third**k
    squares = [flux[d] * u[d] for d in range(3)]
    square_at = {}
    scaled = {}

    def scale(key, value, count):
        if count == 0:
            return value
        if (key, count) not in scaled:
            scaled[key, count] = value * third**count
        return scaled[key, count]

    cross = {(0, 1): jx * u[1], (0, 2): jx * u[2], (1, 2): jy * u[2]}
    out = [None] * 27
    for n in range(27):
        powers = (n // 9, n // 3 % 3, n % 3)
        if n in (0, 3, 9):
            out[n] = moments[n]
            continue
        if n == 1:
            out[n] = moments[n] + force
            continue
        odd = tuple(d for d in range(3) if powers[d] == 1)
        even = tuple(d for d in range(3) if powers[d] == 2)
        count = len(even)
        if len(odd) == 3:
            out[n] = moments[n] - rate(n) * moments[n]
            continue
        if len(odd) == 0:
            if even not in square_at:
                total = squares[even[0]]
                for d in even[1:]:
                    total = total + squares[d]
                square_at[even] = base[count] + (total * (3.0 * third**count) if count > 1 else total)
            level = square_at[even]
        elif len(odd) == 1:
            level = scale(odd, flux[odd[0]], count)
        else:
            level = scale(odd, cross[odd], count)
        out[n] = moments[n] - rate(n) * (moments[n] - level)
    return backward3(out)


def shifters(slab):
    lane, row = lane_index(), row_index()
    per_x = slab.gy * slab.deep
    in_z = lane % slab.deep
    in_y = (lane // slab.deep) % slab.gy
    z_edge = {1: in_z == 0, -1: in_z == slab.deep - 1}
    y_edge = {1: in_y == 0, -1: in_y == slab.gy - 1}
    row_edge = {1: row == 0, -1: row == SUBLANES - 1}

    def along_x(value, step):
        return lane_roll(value, step * per_x)

    def along_y(value, step):
        turned = pltpu.roll(value, step % SUBLANES, 0)
        near = lane_roll(turned, step * slab.deep)
        far = lane_roll(turned, step * (slab.deep - per_x))
        return jnp.where(row_edge[step], jnp.where(y_edge[step], far, near), turned)

    def along_z(value, beside, step):
        return jnp.where(z_edge[step], lane_roll(beside, step * (1 - slab.deep)), lane_roll(value, step))

    return along_x, along_y, along_z


HEAT_OFFSETS = [(0, 0, 0), (1, 0, 0), (-1, 0, 0), (0, 1, 0), (0, -1, 0), (0, 0, 1), (0, 0, -1)]


def run_steps(slab, rates_ref, state, post, force_ref, start, end):
    def collide_one(tile, _):
        values = [state[n, tile] for n in range(27)]
        solid = state[SOLID_AT, tile] != 0.0
        moved = collide_tile(values, force_ref[tile], lambda n: rates_ref[n])
        for n in range(27):
            post[n, tile] = jnp.where(solid, jnp.nan, moved[n])
        heat = [state[HEAT_AT + k, tile] for k in range(7)]
        total = heat[0]
        for k in range(1, 7):
            total = total + heat[k]
        omega = state[RATE_AT, tile]
        side = 0.125 * total
        half = 0.5 * total
        for k in range(7):
            if k == 0:
                level = 0.25 * total
            else:
                drift = half * state[SPEED_AT + (k - 1) // 2, tile]
                level = side + drift if k % 2 == 1 else side - drift
            post[SPEED_AT + k, tile] = heat[k] - (heat[k] - level) * omega
        return 0

    def stream_one(tile, _):
        along_x, along_y, along_z = shifters(slab)
        before, after = jnp.maximum(tile - 1, start), jnp.minimum(tile + 1, end - 1)
        solid = state[SOLID_AT, tile] != 0.0

        def arrive(row, offset):
            value = post[row, tile]
            if offset[2] != 0:
                value = along_z(value, post[row, before if offset[2] == 1 else after], offset[2])
            if offset[1] != 0:
                value = along_y(value, offset[1])
            if offset[0] != 0:
                value = along_x(value, offset[0])
            return value

        for n in range(27):
            value = arrive(n, OFFSET_TABLE[n])
            value = jnp.where(value != value, post[26 - n, tile], value)
            state[n, tile] = jnp.where(solid, state[n, tile], value)
        for k in range(7):
            state[HEAT_AT + k, tile] = arrive(SPEED_AT + k, HEAT_OFFSETS[k])
        return 0

    def step(number, _):
        lax.fori_loop(start, end, collide_one, 0)
        lax.fori_loop(start, end, stream_one, 0)
        return 0

    lax.fori_loop(0, STEPS, step, 0)


def heat_force(state, tile):
    total = state[HEAT_AT, tile]
    for k in range(1, 7):
        total = total + state[HEAT_AT + k, tile]
    return BUOYANCY * (total - REFERENCE_HEAT)


def flow_speed_tile(state, tile, force):
    values = [state[n, tile] for n in range(27)]
    total = values[0]
    for n in range(1, 27):
        total = total + values[n]
    sums = []
    for d in range(3):
        plus, minus = None, None
        for n in range(27):
            part = OFFSET_TABLE[n][d]
            if part == 1:
                plus = values[n] if plus is None else plus + values[n]
            if part == -1:
                minus = values[n] if minus is None else minus + values[n]
        sums.append(plus - minus)
    sums[2] = sums[2] + 0.5 * force
    return [each / total for each in sums]


def both_windows(slab, rates_hbm, own_ref, low_ref, high_ref, *refs):
    sent, rates_ref, sem, state, post, force = refs
    rates_copy = pltpu.make_async_copy(rates_hbm, rates_ref, sem)
    rates_copy.start()
    margin = slab.margin

    def gather(row, _):
        state[row, pl.ds(0, margin)] = low_ref[row]
        state[row, pl.ds(margin, slab.tiles)] = own_ref[row]
        state[row, pl.ds(slab.padded - margin, margin)] = high_ref[row]
        return 0

    lax.fori_loop(0, ROWS, gather, 0)

    def first_force(tile, _):
        force[tile] = heat_force(state, tile)
        return 0

    lax.fori_loop(0, slab.padded, first_force, 0)
    rates_copy.wait()

    def next_speed(tile, _):
        solid = state[SOLID_AT, tile] != 0.0
        for d, each in enumerate(flow_speed_tile(state, tile, force[tile])):
            state[SPEED_AT + d, tile] = jnp.where(solid, 0.0, each)
        force[tile] = heat_force(state, tile)
        return 0

    def one_window(window, _):
        run_steps(slab, rates_ref, state, post, force, window, slab.padded - window)

        @pl.when(window + 1 < WINDOWS)
        def _():
            lax.fori_loop(window + 1, slab.padded - window - 1, next_speed, 0)

        return 0

    lax.fori_loop(0, WINDOWS, one_window, 0)
    pack_out(slab, lambda row, tile: state[row, tile + margin], sent)


def local_call(body, slab, arrays, outs, scratch=(), in_hbm=0, carried=False):
    def kernel(*refs):
        body(slab, *refs)

    return pl.pallas_call(
        kernel,
        out_shape=[jax.ShapeDtypeStruct(shape, F32) for shape in outs],
        in_specs=[
            pl.BlockSpec(
                memory_space=pltpu.HBM if i < in_hbm else pl.ANY if carried and i == 0 else pltpu.VMEM
            )
            for i in range(len(arrays))
        ],
        out_specs=[pl.BlockSpec(memory_space=pl.ANY if carried else pltpu.VMEM)] * len(outs),
        input_output_aliases={0: 0} if carried else {},
        scratch_shapes=[pltpu.VMEM(s, F32) if isinstance(s, tuple) else s for s in scratch],
        compiler_params=pltpu.CompilerParams(vmem_limit_bytes=24 * 1024 * 1024),
    )(
        *(
            pltpu.with_memory_space_constraint(array, pltpu.HBM) if i < in_hbm else array
            for i, array in enumerate(arrays)
        )
    )


RING = ("grp", "gx", "gy")


def exchange(slab, low, high):
    ring = slab.ring
    upward = [(ring[i - 1], ring[i]) for i in range(len(ring))]
    from_below = lax.ppermute(high, RING, upward)
    from_above = lax.ppermute(low, RING, [(b, a) for a, b in upward])
    return from_below, from_above


def across_planes(slab, parts):
    return [parts[0]] + [
        lax.ppermute(parts[step], "grp", [(i, i ^ step) for i in range(slab.grp)])
        for step in range(1, slab.grp)
    ]


def on_slabs(slab, populations, thermal, velocity_prev, solid, phase_ids, conductivity, rates):
    tile = (SUBLANES, LANES)

    def vmem_like(array):
        return pltpu.VMEM(array.shape, array.dtype)

    parts = local_call(
        offer_heat,
        slab,
        [conductivity, thermal, phase_ids],
        [(8,) + tile] * slab.grp,
        [
            pltpu.SMEM(conductivity.shape, F32),
            vmem_like(thermal),
            vmem_like(phase_ids),
            pltpu.SemaphoreType.DMA((3,)),
        ],
        in_hbm=3,
    )
    parts = across_planes(slab, parts)
    sent_shape = (slab.sub, ROWS // 2) + tile
    sent, flags = local_call(
        pack_flow,
        slab,
        [populations, velocity_prev, solid],
        [sent_shape, solid.shape],
        [
            (SOLID_AT,) + solid.shape,
            pltpu.VMEM(solid.shape, solid.dtype),
            pltpu.SemaphoreType.DMA((3,)),
        ],
        in_hbm=3,
    )
    (sent,) = local_call(
        pack_heat,
        slab,
        [sent, flags] + parts,
        [sent_shape],
        [
            (ROWS - SOLID_AT,) + solid.shape,
            (slab.sub, (ROWS - SOLID_AT) // 2) + tile,
            pltpu.SemaphoreType.DMA,
        ],
        carried=True,
    )
    came = lax.all_to_all(sent, ("gx", "gy"), split_axis=0, concat_axis=0, tiled=True)
    own, low, high = local_call(
        unpack_in,
        slab,
        [came],
        [(ROWS, slab.tiles) + tile, (ROWS, slab.margin) + tile, (ROWS, slab.margin) + tile],
    )
    below, above = exchange(slab, low, high)
    (sent,) = local_call(
        both_windows,
        slab,
        [rates, own, below, above],
        [(slab.sub, MOVING // 2) + tile],
        [
            pltpu.SMEM(rates.shape, F32),
            pltpu.SemaphoreType.DMA,
            (ROWS, slab.padded) + tile,
            (MOVING, slab.padded) + tile,
            (slab.padded,) + tile,
        ],
        in_hbm=1,
    )
    came = lax.all_to_all(sent, ("gx", "gy"), split_axis=0, concat_axis=0, tiled=True)
    parts = local_call(
        return_heat, slab, [came], [(7,) + tile] * slab.grp, [(slab.grp, 7) + tile]
    )
    parts = across_planes(slab, parts)
    (populations_out,) = local_call(unpack_flow, slab, [came], [populations.shape])
    (thermal_out,) = local_call(join_heat, slab, parts, [thermal.shape])
    return populations_out, thermal_out


def solution(mesh):
    in_specs = (
        P(None, "gx", "gy", "grp"),
        P(None, ("gx", "grp"), "gy", None),
        P(None, "gx", "gy", "grp"),
        P("gx", "gy", "grp"),
        P(("gx", "grp"), "gy", None),
        P(),
        P(),
    )
    out_specs = (P(None, "gx", "gy", "grp"), P(None, ("gx", "grp"), "gy", None))

    def per_device(populations, thermal, *others):
        slab = Slab(mesh.shape, populations.shape[1:], thermal.shape[1:])
        plan = (lambda *arrays: on_slabs(slab, *arrays)) if slab.fits else on_device
        return plan(populations, thermal, *others)

    return jax.shard_map(
        per_device, mesh=mesh, in_specs=in_specs, out_specs=out_specs, check_vma=False
    )
```

```python
import jax
import jax.numpy as jnp
import numpy as np
from jax import lax
from jax.experimental import pallas as pl
from jax.experimental.pallas import tpu as pltpu
from jax.sharding import PartitionSpec as P

STEPS = 4
WINDOWS = 2


HIGHEST = lax.Precision.HIGHEST
BUOYANCY = 0.03
REFERENCE_HEAT = 1.0
OFFSET_TABLE = [(number // 9 - 1, number // 3 % 3 - 1, number % 3 - 1) for number in range(27)]
LATTICE_WEIGHTS = np.array(
    [
        np.prod([2.0 / 3.0 if component == 0 else 1.0 / 6.0 for component in triple])
        for triple in OFFSET_TABLE
    ]
)
VANDERMONDE = np.array([[1.0, 1.0, 1.0], [-1.0, 0.0, 1.0], [1.0, 0.0, 1.0]])
VANDER_INVERSE = np.array([[0.0, -0.5, 0.5], [1.0, 0.0, -1.0], [0.0, 0.5, 0.5]])
MOMENT_MATRIX = np.kron(np.kron(VANDERMONDE, VANDERMONDE), VANDERMONDE)
MOMENT_INVERSE = np.kron(np.kron(VANDER_INVERSE, VANDER_INVERSE), VANDER_INVERSE)
RELAXED = np.array([0.0 if number in (0, 1, 3, 9) else 1.0 for number in range(27)])
SUMMING = np.concatenate([np.ones((1, 27)), 1.0 * np.array(OFFSET_TABLE).T], axis=0)
HEAT_WEIGHTS = np.array([0.25] + [0.125] * 6)


def from_behind(value, axis, steps):
    count = lax.axis_size(axis)
    pairs = [(source, (source + steps) % count) for source in range(count)]
    return lax.ppermute(value, axis, pairs)


def extended(cells, sides, width):
    for axis, dim in sides:
        count = lax.axis_size(axis)
        head = lax.slice_in_dim(cells, 0, width, axis=dim)
        tail = lax.slice_in_dim(cells, cells.shape[dim] - width, cells.shape[dim], axis=dim)
        cells = jnp.concatenate(
            [
                lax.ppermute(tail, axis, [(i, (i + 1) % count) for i in range(count)]),
                cells,
                lax.ppermute(head, axis, [((i + 1) % count, i) for i in range(count)]),
            ],
            axis=dim,
        )
    return cells


def flow_state(flat, heat_flat):
    sums = jnp.dot(jnp.asarray(SUMMING, jnp.float32), flat, precision=HIGHEST)
    density = sums[0]
    force = BUOYANCY * (heat_flat - REFERENCE_HEAT)
    speed = jnp.stack([sums[1], sums[2], sums[3] + 0.5 * force]) / density
    return (density, force, speed)


def collide(popul, heat, rates):
    flat = popul.reshape(27, -1)
    density, force, speed = flow_state(flat, heat.reshape(-1))
    along = jnp.dot(jnp.asarray(SUMMING[1:].T, jnp.float32), speed, precision=HIGHEST)
    square = jnp.sum(speed * speed, axis=0)
    balance = (
        density
        * jnp.asarray(LATTICE_WEIGHTS, jnp.float32)[:, None]
        * (1.0 + 3.0 * along + 4.5 * along * along - 1.5 * square)
    )
    scaled = (
        jnp.asarray(MOMENT_INVERSE, jnp.float32)
        * (rates * jnp.asarray(RELAXED, jnp.float32))[None, :]
    )
    relax = jnp.dot(scaled, jnp.asarray(MOMENT_MATRIX, jnp.float32), precision=HIGHEST)
    post = (
        flat
        - jnp.dot(relax, flat - balance, precision=HIGHEST)
        + jnp.asarray(MOMENT_INVERSE[:, 1], jnp.float32)[:, None] * force[None, :]
    )
    return post.reshape(popul.shape)


def flow_speed(popul, heat, solid):
    density, force, speed = flow_state(popul.reshape(27, -1), heat.reshape(-1))
    return jnp.where(solid[None] == 0, speed.reshape((3,) + solid.shape), 0.0)


def heat_collide(heat_pops, speed, relax_time):
    total = jnp.sum(heat_pops, axis=0)
    still = jnp.zeros_like(speed[0])
    along = jnp.stack([still, speed[0], -speed[0], speed[1], -speed[1], speed[2], -speed[2]])
    balance = (
        jnp.asarray(HEAT_WEIGHTS, jnp.float32)[:, None, None, None]
        * total[None]
        * (1.0 + 4.0 * along)
    )
    return heat_pops - (heat_pops - balance) / relax_time[None]


def relaxation(phase_ids, conductivity):
    levels = jnp.arange(conductivity.shape[0], dtype=jnp.int32)
    chosen = jnp.sum(
        jnp.where(
            phase_ids[None] == levels[:, None, None, None], conductivity[:, None, None, None], 0.0
        ),
        axis=0,
    )
    return 0.5 + 4.0 * chosen


def inner_window(padded, triple, sizes):
    return padded[
        1 - triple[0] : 1 - triple[0] + sizes[0],
        1 - triple[1] : 1 - triple[1] + sizes[1],
        1 - triple[2] : 1 - triple[2] + sizes[2],
    ]


def advance(grid, axis_number, send_up, send_down):
    space = 3 + axis_number
    length = grid.shape[space]
    rising = lax.index_in_dim(grid, 2, axis_number, keepdims=True)
    resting = lax.index_in_dim(grid, 1, axis_number, keepdims=True)
    falling = lax.index_in_dim(grid, 0, axis_number, keepdims=True)
    from_below = send_up(lax.slice_in_dim(rising, length - 1, length, axis=space))
    from_above = send_down(lax.slice_in_dim(falling, 0, 1, axis=space))
    rising = jnp.concatenate(
        [from_below, lax.slice_in_dim(rising, 0, length - 1, axis=space)], axis=space
    )
    falling = jnp.concatenate(
        [lax.slice_in_dim(falling, 1, length, axis=space), from_above], axis=space
    )
    return jnp.concatenate([falling, resting, rising], axis=axis_number)


def flow_arrivals(post):
    sizes = post.shape[1:]
    grid = post.reshape((3, 3, 3) + sizes)
    grid = advance(
        grid,
        0,
        lambda plane: from_behind(plane, "gx", 1),
        lambda plane: from_behind(plane, "gx", -1),
    )
    grid = advance(
        grid,
        1,
        lambda plane: from_behind(plane, "gy", 1),
        lambda plane: from_behind(plane, "gy", -1),
    )
    grid = advance(
        grid,
        2,
        lambda plane: from_behind(plane, "grp", 1),
        lambda plane: from_behind(plane, "grp", -1),
    )
    return grid.reshape(post.shape)


def stream_heat(post, grp_index, last_grp):
    length = post.shape[1]
    size_y = post.shape[2]
    eastward = post[1]
    westward = post[2]
    lower_first = from_behind(eastward, "grp", 1)
    lower_second = from_behind(lower_first, "gx", 1)
    entering = jnp.where(grp_index == 0, lower_second, lower_first)
    eastward = jnp.concatenate([entering, eastward[: length - 1]], axis=0)
    upper_first = from_behind(westward, "grp", -1)
    upper_second = from_behind(upper_first, "gx", -1)
    entering = jnp.where(grp_index == last_grp, upper_second, upper_first)
    westward = jnp.concatenate([westward[1:], entering], axis=0)
    sides = extended(post[3:5], (("gy", 2),), 1)
    northward = sides[0, :, 0:size_y]
    southward = sides[1, :, 2 : size_y + 2]
    upward = jnp.roll(post[5], 1, axis=2)
    downward = jnp.roll(post[6], -1, axis=2)
    return jnp.stack([post[0], eastward, westward, northward, southward, upward, downward])


def on_device(populations, thermal, velocity_prev, solid, phase_ids, conductivity, rates):
    padded_solid = extended(solid, (("grp", 2), ("gx", 0), ("gy", 1)), 1)
    sizes = solid.shape
    blocked = jnp.stack(
        [inner_window(padded_solid, OFFSET_TABLE[number], sizes) != 0 for number in range(27)]
    )
    fluid_cells = (solid == 0)[None]
    grp_index = lax.axis_index("grp")
    last_grp = lax.axis_size("grp") - 1
    relax_time = relaxation(phase_ids, conductivity)
    speed_brick = velocity_prev
    popul = populations
    heat_pops = thermal
    for window_number in range(WINDOWS):
        heat_brick = lax.all_to_all(
            jnp.sum(heat_pops, axis=0), "grp", split_axis=2, concat_axis=0, tiled=True
        )
        speed_column = lax.all_to_all(speed_brick, "grp", split_axis=1, concat_axis=3, tiled=True)
        for step_number in range(STEPS):
            post = collide(popul, heat_brick, rates)
            arrived = flow_arrivals(post)
            popul = jnp.where(fluid_cells, jnp.where(blocked, post[::-1], arrived), popul)
        for step_number in range(STEPS):
            heat_pops = stream_heat(
                heat_collide(heat_pops, speed_column, relax_time), grp_index, last_grp
            )
        if window_number + 1 < WINDOWS:
            speed_brick = flow_speed(popul, heat_brick, solid)
    return (popul, heat_pops)


SUBLANES = 8
LANES = 128
F32 = jnp.float32


class Slab:
    def __init__(self, mesh_shape, flow_block, heat_block):
        self.grp, self.gx, self.gy = (mesh_shape[name] for name in ("grp", "gx", "gy"))
        self.block_x, self.block_y, self.block_z = flow_block
        self.sub = self.gx * self.gy
        self.size_x = self.block_x * self.gx
        self.planes = self.block_z // self.sub
        self.deep = LANES // (self.size_x * self.gy) if self.size_x * self.gy <= LANES else 0
        self.fits = (
            self.block_y == SUBLANES
            and self.block_z == LANES
            and self.block_z % self.sub == 0
            and self.deep >= STEPS
            and self.deep * self.size_x * self.gy == LANES
            and self.planes == self.deep * self.gy
            and 2 * self.block_x == self.sub
            and self.size_x == self.sub
            and self.gx == 2
            and self.block_x == self.grp
            and heat_block == (1, SUBLANES, self.grp * LANES)
            and self.sub & (self.sub - 1) == 0
            and self.gy & (self.gy - 1) == 0
            and self.grp & (self.grp - 1) == 0
            and self.planes >= self.deep * WINDOWS
            and self.planes % (2 * self.deep) == 0
        )
        if self.fits:
            self.tiles = self.planes // self.deep
            self.margin = WINDOWS
            self.padded = self.tiles + 2 * self.margin
            self.snake = [
                x * self.gy + (y if x % 2 == 0 else self.gy - 1 - y)
                for x in range(self.gx)
                for y in range(self.gy)
            ]
            self.ring = [
                part * self.sub + self.snake[place if part % 2 == 0 else self.sub - 1 - place]
                for part in range(self.grp)
                for place in range(self.sub)
            ]

    def holders(self):
        even = lax.axis_index("grp") % 2 == 0
        return [jnp.where(even, *pair) for pair in zip(self.snake, self.snake[::-1])]


def lane_index():
    return lax.broadcasted_iota(jnp.int32, (SUBLANES, LANES), 1)


def row_index():
    return lax.broadcasted_iota(jnp.int32, (SUBLANES, LANES), 0)


def lane_roll(value, amount):
    amount = amount % LANES
    return value if amount == 0 else pltpu.roll(value, amount, 1)


def swap_groups(values, group):
    count = len(values)
    lane = lane_index()
    values = list(values)
    bit = 1
    while bit < count:
        low = (lane // (group * bit)) % 2 == 0
        for first in range(count):
            if first & bit == 0:
                a, b = values[first], values[first | bit]
                values[first] = jnp.where(low, a, lane_roll(b, group * bit))
                values[first | bit] = jnp.where(low, lane_roll(a, -group * bit), b)
        bit *= 2
    return values


SPEED_AT, SOLID_AT, HEAT_AT, RATE_AT, ROWS = 27, 30, 31, 38, 40
MOVING = 34


def moving_row(number):
    return number + (HEAT_AT - SPEED_AT) * (number >= SPEED_AT)


def offer_heat(slab, levels_hbm, heat_hbm, phase_hbm, *refs):
    outs, (levels_ref, heat_ref, phase_ref, sems) = refs[: slab.grp], refs[slab.grp :]
    copies = [
        pltpu.make_async_copy(heat_hbm, heat_ref, sems.at[0]),
        pltpu.make_async_copy(phase_hbm, phase_ref, sems.at[1]),
        pltpu.make_async_copy(levels_hbm, levels_ref, sems.at[2]),
    ]
    for copy in copies:
        copy.start()
    for copy in copies:
        copy.wait()
    mine = lax.axis_index("grp")
    for step in range(slab.grp):
        part = jnp.bitwise_xor(mine, step)
        span = pl.ds(pl.multiple_of(part * LANES, LANES), LANES)
        phase = phase_ref[0, :, span]
        chosen = jnp.zeros((SUBLANES, LANES), F32)
        for level in range(levels_ref.shape[0]):
            chosen = jnp.where(phase == level, levels_ref[level], chosen)
        for k in range(7):
            outs[step][k] = heat_ref[k, 0, :, span]
        outs[step][7] = 1.0 / (0.5 + 4.0 * chosen)


def for_each(count, body):
    for number in range(count):
        body(number)


def pack_flow(slab, popul_hbm, speed_hbm, solid_hbm, sent, flags, fields, solid_ref, sems):
    copies = [
        pltpu.make_async_copy(popul_hbm, fields.at[pl.ds(0, SPEED_AT)], sems.at[0]),
        pltpu.make_async_copy(speed_hbm, fields.at[pl.ds(SPEED_AT, 3)], sems.at[1]),
        pltpu.make_async_copy(solid_hbm, solid_ref, sems.at[2]),
    ]
    for copy in copies:
        copy.start()
    for copy in copies:
        copy.wait()
    holders = slab.holders()

    def one(pair):
        pack_pair(slab, fields, pair, sent, pair, holders)

    for_each(SOLID_AT // 2, one)
    flags[...] = solid_ref[...].astype(F32)


def pack_pair(slab, fields, source, sent, target, holders):
    sources = [fields[2 * source + h, x] for h in range(2) for x in range(slab.block_x)]
    for place, value in enumerate(swap_groups(sources, slab.planes)):
        sent[holders[place], target] = value


def pack_heat(slab, sent_in, flags, *refs):
    parts, (sent, held, packed, sem) = refs[: slab.grp], refs[slab.grp :]
    mine = lax.axis_index("grp")
    holders = slab.holders()
    held[0] = flags[...]
    held[9] = jnp.zeros(flags.shape, F32)
    for step in range(slab.grp):
        held[pl.ds(1, 8), jnp.bitwise_xor(mine, step)] = parts[step][...]
    first, count = SOLID_AT // 2, (ROWS - SOLID_AT) // 2

    def one(pair):
        pack_pair(slab, held, pair, packed, pair, holders)

    for_each(count, one)
    copy = pltpu.make_async_copy(packed, sent.at[:, pl.ds(first, count)], sem)
    copy.start()
    copy.wait()


def unpack_in(slab, came, state_out, low_out, high_out):
    half = slab.block_x * slab.planes

    def put(row, by_gy):
        for tile, value in enumerate(swap_groups(by_gy, slab.deep)):
            state_out[row, tile] = value
            if tile < slab.margin:
                low_out[row, tile] = value
            if tile >= slab.tiles - slab.margin:
                high_out[row, tile - (slab.tiles - slab.margin)] = value

    def one(pair):
        first_half = lane_index() < half
        firsts, seconds = [], []
        for y in range(slab.gy):
            a, b = came[y, pair], came[slab.gy + y, pair]
            firsts.append(jnp.where(first_half, a, lane_roll(b, half)))
            seconds.append(jnp.where(first_half, lane_roll(a, half), b))
        put(2 * pair, firsts)
        put(2 * pair + 1, seconds)

    for_each(ROWS // 2, one)


def pack_out(slab, take, sent):
    half = slab.block_x * slab.planes

    def by_gy(row):
        return swap_groups([take(row, tile) for tile in range(slab.tiles)], slab.deep)

    def one(pair):
        first_half = lane_index() < half
        firsts, seconds = by_gy(moving_row(2 * pair)), by_gy(moving_row(2 * pair + 1))
        for y in range(slab.gy):
            a, b = firsts[y], seconds[y]
            sent[y, pair] = jnp.where(first_half, a, lane_roll(b, half))
            sent[slab.gy + y, pair] = jnp.where(first_half, lane_roll(a, half), b)

    for_each(MOVING // 2, one)


def unpack_pair(slab, came, pair, holders):
    sources = [came[holders[place], pair] for place in range(slab.sub)]
    values = swap_groups(sources, slab.planes)
    return [values[: slab.block_x], values[slab.block_x :]]


def return_heat(slab, came, *refs):
    outs, held = refs[: slab.grp], refs[slab.grp]
    holders = slab.holders()
    _, values = unpack_pair(slab, came, SPEED_AT // 2, holders)
    for x in range(slab.block_x):
        held[x, 0] = values[x]

    def one(pair):
        for h, values in enumerate(unpack_pair(slab, came, SPEED_AT // 2 + 1 + pair, holders)):
            for x in range(slab.block_x):
                held[x, 2 * pair + 1 + h] = values[x]

    for_each(3, one)
    mine = lax.axis_index("grp")
    for step in range(slab.grp):
        outs[step][...] = held[jnp.bitwise_xor(mine, step)]


def unpack_flow(slab, came, popul_out):
    holders = slab.holders()

    def one(pair):
        for h, values in enumerate(unpack_pair(slab, came, pair, holders)):
            for x in range(slab.block_x):
                popul_out[2 * pair + h, x] = values[x]

    for_each(SPEED_AT // 2, one)
    values, _ = unpack_pair(slab, came, SPEED_AT // 2, holders)
    for x in range(slab.block_x):
        popul_out[SPEED_AT - 1, x] = values[x]


def join_heat(slab, *refs):
    parts, thermal_out = refs[: slab.grp], refs[slab.grp]
    mine = lax.axis_index("grp")
    for step in range(slab.grp):
        part = jnp.bitwise_xor(mine, step)
        span = pl.ds(pl.multiple_of(part * LANES, LANES), LANES)
        for k in range(7):
            thermal_out[k, 0, :, span] = parts[step][k]


def forward3(values):
    for stride in (9, 3, 1):
        out = [None] * 27
        for n in range(27):
            if n // stride % 3 == 0:
                a, b, c = values[n], values[n + stride], values[n + 2 * stride]
                both = a + c
                out[n], out[n + stride], out[n + 2 * stride] = both + b, c - a, both
        values = out
    return values


def backward3(values):
    for stride in (9, 3, 1):
        out = [None] * 27
        for n in range(27):
            if n // stride % 3 == 0:
                a, b, c = values[n], values[n + stride], values[n + 2 * stride]
                even, odd = 0.5 * c, 0.5 * b
                out[n], out[n + stride], out[n + 2 * stride] = even - odd, a - c, even + odd
        values = out
    return values


def collide_tile(values, force, rate):
    moments = forward3(values)
    density = moments[0]
    jx, jy, jz = moments[9], moments[3], moments[1] + 0.5 * force
    inverse = 1.0 / density
    flux = (jx, jy, jz)
    u = tuple(j * inverse for j in flux)
    third = 1.0 / 3.0
    base = {0: density}
    for k in (1, 2, 3):
        base[k] = density * third**k
    squares = [flux[d] * u[d] for d in range(3)]
    square_at = {}
    scaled = {}

    def scale(key, value, count):
        if count == 0:
            return value
        if (key, count) not in scaled:
            scaled[key, count] = value * third**count
        return scaled[key, count]

    cross = {(0, 1): jx * u[1], (0, 2): jx * u[2], (1, 2): jy * u[2]}
    out = [None] * 27
    for n in range(27):
        powers = (n // 9, n // 3 % 3, n % 3)
        if n in (0, 3, 9):
            out[n] = moments[n]
            continue
        if n == 1:
            out[n] = moments[n] + force
            continue
        odd = tuple(d for d in range(3) if powers[d] == 1)
        even = tuple(d for d in range(3) if powers[d] == 2)
        count = len(even)
        if len(odd) == 3:
            out[n] = moments[n] - rate(n) * moments[n]
            continue
        if len(odd) == 0:
            if even not in square_at:
                total = squares[even[0]]
                for d in even[1:]:
                    total = total + squares[d]
                square_at[even] = base[count] + (total * (3.0 * third**count) if count > 1 else total)
            level = square_at[even]
        elif len(odd) == 1:
            level = scale(odd, flux[odd[0]], count)
        else:
            level = scale(odd, cross[odd], count)
        out[n] = moments[n] - rate(n) * (moments[n] - level)
    return backward3(out)


def shifters(slab):
    lane, row = lane_index(), row_index()
    per_x = slab.gy * slab.deep
    in_z = lane % slab.deep
    in_y = (lane // slab.deep) % slab.gy
    z_edge = {1: in_z == 0, -1: in_z == slab.deep - 1}
    y_edge = {1: in_y == 0, -1: in_y == slab.gy - 1}
    row_edge = {1: row == 0, -1: row == SUBLANES - 1}

    def along_x(value, step):
        return lane_roll(value, step * per_x)

    def along_y(value, step):
        turned = pltpu.roll(value, step % SUBLANES, 0)
        near = lane_roll(turned, step * slab.deep)
        far = lane_roll(turned, step * (slab.deep - per_x))
        return jnp.where(row_edge[step], jnp.where(y_edge[step], far, near), turned)

    def along_z(value, beside, step):
        return jnp.where(z_edge[step], lane_roll(beside, step * (1 - slab.deep)), lane_roll(value, step))

    return along_x, along_y, along_z


HEAT_OFFSETS = [(0, 0, 0), (1, 0, 0), (-1, 0, 0), (0, 1, 0), (0, -1, 0), (0, 0, 1), (0, 0, -1)]


def run_steps(slab, rates_ref, state, post, force_ref, start, end):
    def collide_one(tile, _):
        values = [state[n, tile] for n in range(27)]
        solid = state[SOLID_AT, tile] != 0.0
        moved = collide_tile(values, force_ref[tile], lambda n: rates_ref[n])
        for n in range(27):
            post[n, tile] = jnp.where(solid, jnp.nan, moved[n])
        heat = [state[HEAT_AT + k, tile] for k in range(7)]
        total = heat[0]
        for k in range(1, 7):
            total = total + heat[k]
        omega = state[RATE_AT, tile]
        side = 0.125 * total
        half = 0.5 * total
        for k in range(7):
            if k == 0:
                level = 0.25 * total
            else:
                drift = half * state[SPEED_AT + (k - 1) // 2, tile]
                level = side + drift if k % 2 == 1 else side - drift
            post[SPEED_AT + k, tile] = heat[k] - (heat[k] - level) * omega
        return 0

    def stream_one(tile, _):
        along_x, along_y, along_z = shifters(slab)
        before, after = jnp.maximum(tile - 1, start), jnp.minimum(tile + 1, end - 1)
        fluid = state[SOLID_AT, tile] == 0.0

        def arrive(row, offset):
            value = post[row, tile]
            if offset[2] != 0:
                value = along_z(value, post[row, before if offset[2] == 1 else after], offset[2])
            if offset[1] != 0:
                value = along_y(value, offset[1])
            if offset[0] != 0:
                value = along_x(value, offset[0])
            return value

        for n in range(27):
            value = arrive(n, OFFSET_TABLE[n])
            value = jnp.where(value != value, post[26 - n, tile], value)
            pltpu.store(state.at[n, tile], value, mask=fluid)
        for k in range(7):
            state[HEAT_AT + k, tile] = arrive(SPEED_AT + k, HEAT_OFFSETS[k])
        return 0

    def in_pairs(body):
        def two(pair, _):
            body(start + 2 * pair, 0)
            body(start + 2 * pair + 1, 0)
            return 0

        lax.fori_loop(0, (end - start) // 2, two, 0)

    def step(number, _):
        in_pairs(collide_one)
        in_pairs(stream_one)
        return 0

    lax.fori_loop(0, STEPS, step, 0)


def heat_force(state, tile):
    total = state[HEAT_AT, tile]
    for k in range(1, 7):
        total = total + state[HEAT_AT + k, tile]
    return BUOYANCY * (total - REFERENCE_HEAT)


def flow_speed_tile(state, tile, force):
    values = [state[n, tile] for n in range(27)]
    total = values[0]
    for n in range(1, 27):
        total = total + values[n]
    sums = []
    for d in range(3):
        plus, minus = None, None
        for n in range(27):
            part = OFFSET_TABLE[n][d]
            if part == 1:
                plus = values[n] if plus is None else plus + values[n]
            if part == -1:
                minus = values[n] if minus is None else minus + values[n]
        sums.append(plus - minus)
    sums[2] = sums[2] + 0.5 * force
    return [each / total for each in sums]


def both_windows(slab, rates_hbm, own_ref, low_ref, high_ref, *refs):
    sent, rates_ref, sem, state, post, force = refs
    rates_copy = pltpu.make_async_copy(rates_hbm, rates_ref, sem)
    rates_copy.start()
    margin = slab.margin

    def gather(row, _):
        state[row, pl.ds(0, margin)] = low_ref[row]
        state[row, pl.ds(margin, slab.tiles)] = own_ref[row]
        state[row, pl.ds(slab.padded - margin, margin)] = high_ref[row]
        return 0

    lax.fori_loop(0, ROWS, gather, 0, unroll=4)

    def first_force(tile, _):
        force[tile] = heat_force(state, tile)
        return 0

    lax.fori_loop(0, slab.padded, first_force, 0)
    rates_copy.wait()

    def next_speed(tile, _):
        solid = state[SOLID_AT, tile] != 0.0
        for d, each in enumerate(flow_speed_tile(state, tile, force[tile])):
            state[SPEED_AT + d, tile] = jnp.where(solid, 0.0, each)
        force[tile] = heat_force(state, tile)
        return 0

    def one_window(window, _):
        run_steps(slab, rates_ref, state, post, force, window, slab.padded - window)

        @pl.when(window + 1 < WINDOWS)
        def _():
            lax.fori_loop(window + 1, slab.padded - window - 1, next_speed, 0)

        return 0

    lax.fori_loop(0, WINDOWS, one_window, 0)
    pack_out(slab, lambda row, tile: state[row, tile + margin], sent)


def local_call(body, slab, arrays, outs, scratch=(), in_hbm=0, carried=False):
    def kernel(*refs):
        body(slab, *refs)

    return pl.pallas_call(
        kernel,
        out_shape=[jax.ShapeDtypeStruct(shape, F32) for shape in outs],
        in_specs=[
            pl.BlockSpec(
                memory_space=pltpu.HBM if i < in_hbm else pl.ANY if carried and i == 0 else pltpu.VMEM
            )
            for i in range(len(arrays))
        ],
        out_specs=[pl.BlockSpec(memory_space=pl.ANY if carried else pltpu.VMEM)] * len(outs),
        input_output_aliases={0: 0} if carried else {},
        scratch_shapes=[pltpu.VMEM(s, F32) if isinstance(s, tuple) else s for s in scratch],
        compiler_params=pltpu.CompilerParams(vmem_limit_bytes=24 * 1024 * 1024),
    )(
        *(
            pltpu.with_memory_space_constraint(array, pltpu.HBM) if i < in_hbm else array
            for i, array in enumerate(arrays)
        )
    )


RING = ("grp", "gx", "gy")


def exchange(slab, low, high):
    ring = slab.ring
    upward = [(ring[i - 1], ring[i]) for i in range(len(ring))]
    from_below = lax.ppermute(high, RING, upward)
    from_above = lax.ppermute(low, RING, [(b, a) for a, b in upward])
    return from_below, from_above


def across_planes(slab, parts):
    return [parts[0]] + [
        lax.ppermute(parts[step], "grp", [(i, i ^ step) for i in range(slab.grp)])
        for step in range(1, slab.grp)
    ]


def on_slabs(slab, populations, thermal, velocity_prev, solid, phase_ids, conductivity, rates):
    tile = (SUBLANES, LANES)

    def vmem_like(array):
        return pltpu.VMEM(array.shape, array.dtype)

    parts = local_call(
        offer_heat,
        slab,
        [conductivity, thermal, phase_ids],
        [(8,) + tile] * slab.grp,
        [
            pltpu.SMEM(conductivity.shape, F32),
            vmem_like(thermal),
            vmem_like(phase_ids),
            pltpu.SemaphoreType.DMA((3,)),
        ],
        in_hbm=3,
    )
    parts = across_planes(slab, parts)
    sent_shape = (slab.sub, ROWS // 2) + tile
    sent, flags = local_call(
        pack_flow,
        slab,
        [populations, velocity_prev, solid],
        [sent_shape, solid.shape],
        [
            (SOLID_AT,) + solid.shape,
            pltpu.VMEM(solid.shape, solid.dtype),
            pltpu.SemaphoreType.DMA((3,)),
        ],
        in_hbm=3,
    )
    (sent,) = local_call(
        pack_heat,
        slab,
        [sent, flags] + parts,
        [sent_shape],
        [
            (ROWS - SOLID_AT,) + solid.shape,
            (slab.sub, (ROWS - SOLID_AT) // 2) + tile,
            pltpu.SemaphoreType.DMA,
        ],
        carried=True,
    )
    came = lax.all_to_all(sent, ("gx", "gy"), split_axis=0, concat_axis=0, tiled=True)
    own, low, high = local_call(
        unpack_in,
        slab,
        [came],
        [(ROWS, slab.tiles) + tile, (ROWS, slab.margin) + tile, (ROWS, slab.margin) + tile],
    )
    below, above = exchange(slab, low, high)
    (sent,) = local_call(
        both_windows,
        slab,
        [rates, own, below, above],
        [(slab.sub, MOVING // 2) + tile],
        [
            pltpu.SMEM(rates.shape, F32),
            pltpu.SemaphoreType.DMA,
            (ROWS, slab.padded) + tile,
            (MOVING, slab.padded) + tile,
            (slab.padded,) + tile,
        ],
        in_hbm=1,
    )
    came = lax.all_to_all(sent, ("gx", "gy"), split_axis=0, concat_axis=0, tiled=True)
    parts = local_call(
        return_heat, slab, [came], [(7,) + tile] * slab.grp, [(slab.grp, 7) + tile]
    )
    parts = across_planes(slab, parts)
    (populations_out,) = local_call(unpack_flow, slab, [came], [populations.shape])
    (thermal_out,) = local_call(join_heat, slab, parts, [thermal.shape])
    return populations_out, thermal_out


def solution(mesh):
    in_specs = (
        P(None, "gx", "gy", "grp"),
        P(None, ("gx", "grp"), "gy", None),
        P(None, "gx", "gy", "grp"),
        P("gx", "gy", "grp"),
        P(("gx", "grp"), "gy", None),
        P(),
        P(),
    )
    out_specs = (P(None, "gx", "gy", "grp"), P(None, ("gx", "grp"), "gy", None))

    def per_device(populations, thermal, *others):
        slab = Slab(mesh.shape, populations.shape[1:], thermal.shape[1:])
        plan = (lambda *arrays: on_slabs(slab, *arrays)) if slab.fits else on_device
        return plan(populations, thermal, *others)

    return jax.shard_map(
        per_device, mesh=mesh, in_specs=in_specs, out_specs=out_specs, check_vma=False
    )
```

```python
import jax
import jax.numpy as jnp
import numpy as np
from jax import lax
from jax.experimental import pallas as pl
from jax.experimental.pallas import tpu as pltpu
from jax.sharding import PartitionSpec as P

STEPS = 4
WINDOWS = 2


HIGHEST = lax.Precision.HIGHEST
BUOYANCY = 0.03
REFERENCE_HEAT = 1.0
OFFSET_TABLE = [(number // 9 - 1, number // 3 % 3 - 1, number % 3 - 1) for number in range(27)]
LATTICE_WEIGHTS = np.array(
    [
        np.prod([2.0 / 3.0 if component == 0 else 1.0 / 6.0 for component in triple])
        for triple in OFFSET_TABLE
    ]
)
VANDERMONDE = np.array([[1.0, 1.0, 1.0], [-1.0, 0.0, 1.0], [1.0, 0.0, 1.0]])
VANDER_INVERSE = np.array([[0.0, -0.5, 0.5], [1.0, 0.0, -1.0], [0.0, 0.5, 0.5]])
MOMENT_MATRIX = np.kron(np.kron(VANDERMONDE, VANDERMONDE), VANDERMONDE)
MOMENT_INVERSE = np.kron(np.kron(VANDER_INVERSE, VANDER_INVERSE), VANDER_INVERSE)
RELAXED = np.array([0.0 if number in (0, 1, 3, 9) else 1.0 for number in range(27)])
SUMMING = np.concatenate([np.ones((1, 27)), 1.0 * np.array(OFFSET_TABLE).T], axis=0)
HEAT_WEIGHTS = np.array([0.25] + [0.125] * 6)


def from_behind(value, axis, steps):
    count = lax.axis_size(axis)
    pairs = [(source, (source + steps) % count) for source in range(count)]
    return lax.ppermute(value, axis, pairs)


def extended(cells, sides, width):
    for axis, dim in sides:
        count = lax.axis_size(axis)
        head = lax.slice_in_dim(cells, 0, width, axis=dim)
        tail = lax.slice_in_dim(cells, cells.shape[dim] - width, cells.shape[dim], axis=dim)
        cells = jnp.concatenate(
            [
                lax.ppermute(tail, axis, [(i, (i + 1) % count) for i in range(count)]),
                cells,
                lax.ppermute(head, axis, [((i + 1) % count, i) for i in range(count)]),
            ],
            axis=dim,
        )
    return cells


def flow_state(flat, heat_flat):
    sums = jnp.dot(jnp.asarray(SUMMING, jnp.float32), flat, precision=HIGHEST)
    density = sums[0]
    force = BUOYANCY * (heat_flat - REFERENCE_HEAT)
    speed = jnp.stack([sums[1], sums[2], sums[3] + 0.5 * force]) / density
    return (density, force, speed)


def collide(popul, heat, rates):
    flat = popul.reshape(27, -1)
    density, force, speed = flow_state(flat, heat.reshape(-1))
    along = jnp.dot(jnp.asarray(SUMMING[1:].T, jnp.float32), speed, precision=HIGHEST)
    square = jnp.sum(speed * speed, axis=0)
    balance = (
        density
        * jnp.asarray(LATTICE_WEIGHTS, jnp.float32)[:, None]
        * (1.0 + 3.0 * along + 4.5 * along * along - 1.5 * square)
    )
    scaled = (
        jnp.asarray(MOMENT_INVERSE, jnp.float32)
        * (rates * jnp.asarray(RELAXED, jnp.float32))[None, :]
    )
    relax = jnp.dot(scaled, jnp.asarray(MOMENT_MATRIX, jnp.float32), precision=HIGHEST)
    post = (
        flat
        - jnp.dot(relax, flat - balance, precision=HIGHEST)
        + jnp.asarray(MOMENT_INVERSE[:, 1], jnp.float32)[:, None] * force[None, :]
    )
    return post.reshape(popul.shape)


def flow_speed(popul, heat, solid):
    density, force, speed = flow_state(popul.reshape(27, -1), heat.reshape(-1))
    return jnp.where(solid[None] == 0, speed.reshape((3,) + solid.shape), 0.0)


def heat_collide(heat_pops, speed, relax_time):
    total = jnp.sum(heat_pops, axis=0)
    still = jnp.zeros_like(speed[0])
    along = jnp.stack([still, speed[0], -speed[0], speed[1], -speed[1], speed[2], -speed[2]])
    balance = (
        jnp.asarray(HEAT_WEIGHTS, jnp.float32)[:, None, None, None]
        * total[None]
        * (1.0 + 4.0 * along)
    )
    return heat_pops - (heat_pops - balance) / relax_time[None]


def relaxation(phase_ids, conductivity):
    levels = jnp.arange(conductivity.shape[0], dtype=jnp.int32)
    chosen = jnp.sum(
        jnp.where(
            phase_ids[None] == levels[:, None, None, None], conductivity[:, None, None, None], 0.0
        ),
        axis=0,
    )
    return 0.5 + 4.0 * chosen


def inner_window(padded, triple, sizes):
    return padded[
        1 - triple[0] : 1 - triple[0] + sizes[0],
        1 - triple[1] : 1 - triple[1] + sizes[1],
        1 - triple[2] : 1 - triple[2] + sizes[2],
    ]


def advance(grid, axis_number, send_up, send_down):
    space = 3 + axis_number
    length = grid.shape[space]
    rising = lax.index_in_dim(grid, 2, axis_number, keepdims=True)
    resting = lax.index_in_dim(grid, 1, axis_number, keepdims=True)
    falling = lax.index_in_dim(grid, 0, axis_number, keepdims=True)
    from_below = send_up(lax.slice_in_dim(rising, length - 1, length, axis=space))
    from_above = send_down(lax.slice_in_dim(falling, 0, 1, axis=space))
    rising = jnp.concatenate(
        [from_below, lax.slice_in_dim(rising, 0, length - 1, axis=space)], axis=space
    )
    falling = jnp.concatenate(
        [lax.slice_in_dim(falling, 1, length, axis=space), from_above], axis=space
    )
    return jnp.concatenate([falling, resting, rising], axis=axis_number)


def flow_arrivals(post):
    sizes = post.shape[1:]
    grid = post.reshape((3, 3, 3) + sizes)
    grid = advance(
        grid,
        0,
        lambda plane: from_behind(plane, "gx", 1),
        lambda plane: from_behind(plane, "gx", -1),
    )
    grid = advance(
        grid,
        1,
        lambda plane: from_behind(plane, "gy", 1),
        lambda plane: from_behind(plane, "gy", -1),
    )
    grid = advance(
        grid,
        2,
        lambda plane: from_behind(plane, "grp", 1),
        lambda plane: from_behind(plane, "grp", -1),
    )
    return grid.reshape(post.shape)


def stream_heat(post, grp_index, last_grp):
    length = post.shape[1]
    size_y = post.shape[2]
    eastward = post[1]
    westward = post[2]
    lower_first = from_behind(eastward, "grp", 1)
    lower_second = from_behind(lower_first, "gx", 1)
    entering = jnp.where(grp_index == 0, lower_second, lower_first)
    eastward = jnp.concatenate([entering, eastward[: length - 1]], axis=0)
    upper_first = from_behind(westward, "grp", -1)
    upper_second = from_behind(upper_first, "gx", -1)
    entering = jnp.where(grp_index == last_grp, upper_second, upper_first)
    westward = jnp.concatenate([westward[1:], entering], axis=0)
    sides = extended(post[3:5], (("gy", 2),), 1)
    northward = sides[0, :, 0:size_y]
    southward = sides[1, :, 2 : size_y + 2]
    upward = jnp.roll(post[5], 1, axis=2)
    downward = jnp.roll(post[6], -1, axis=2)
    return jnp.stack([post[0], eastward, westward, northward, southward, upward, downward])


def on_device(populations, thermal, velocity_prev, solid, phase_ids, conductivity, rates):
    padded_solid = extended(solid, (("grp", 2), ("gx", 0), ("gy", 1)), 1)
    sizes = solid.shape
    blocked = jnp.stack(
        [inner_window(padded_solid, OFFSET_TABLE[number], sizes) != 0 for number in range(27)]
    )
    fluid_cells = (solid == 0)[None]
    grp_index = lax.axis_index("grp")
    last_grp = lax.axis_size("grp") - 1
    relax_time = relaxation(phase_ids, conductivity)
    speed_brick = velocity_prev
    popul = populations
    heat_pops = thermal
    for window_number in range(WINDOWS):
        heat_brick = lax.all_to_all(
            jnp.sum(heat_pops, axis=0), "grp", split_axis=2, concat_axis=0, tiled=True
        )
        speed_column = lax.all_to_all(speed_brick, "grp", split_axis=1, concat_axis=3, tiled=True)
        for step_number in range(STEPS):
            post = collide(popul, heat_brick, rates)
            arrived = flow_arrivals(post)
            popul = jnp.where(fluid_cells, jnp.where(blocked, post[::-1], arrived), popul)
        for step_number in range(STEPS):
            heat_pops = stream_heat(
                heat_collide(heat_pops, speed_column, relax_time), grp_index, last_grp
            )
        if window_number + 1 < WINDOWS:
            speed_brick = flow_speed(popul, heat_brick, solid)
    return (popul, heat_pops)


SUBLANES = 8
LANES = 128
F32 = jnp.float32


class Slab:
    def __init__(self, mesh_shape, flow_block, heat_block):
        self.grp, self.gx, self.gy = (mesh_shape[name] for name in ("grp", "gx", "gy"))
        self.block_x, self.block_y, self.block_z = flow_block
        self.sub = self.gx * self.gy
        self.planes = self.block_z // self.sub
        self.halo = self.planes // 2
        self.fits = (
            self.block_y == SUBLANES
            and self.block_z == LANES
            and self.planes * self.sub == LANES
            and self.halo * 2 == self.planes
            and self.halo == STEPS * WINDOWS
            and 2 * self.block_x == self.sub
            and self.block_x == self.grp
            and heat_block == (1, SUBLANES, self.grp * LANES)
            and self.sub & (self.sub - 1) == 0
            and self.grp & (self.grp - 1) == 0
            and self.gy % 2 == 0
        )
        if self.fits:
            self.snake = [
                x * self.gy + (y if x % 2 == 0 else self.gy - 1 - y)
                for x in range(self.gx)
                for y in range(self.gy)
            ]
            self.ring = [
                part * self.sub + self.snake[place if part % 2 == 0 else self.sub - 1 - place]
                for part in range(self.grp)
                for place in range(self.sub)
            ]

    def holders(self):
        even = lax.axis_index("grp") % 2 == 0
        return [jnp.where(even, *pair) for pair in zip(self.snake, self.snake[::-1])]


def lane_index():
    return lax.broadcasted_iota(jnp.int32, (SUBLANES, LANES), 1)


def row_index():
    return lax.broadcasted_iota(jnp.int32, (SUBLANES, LANES), 0)


def lane_roll(value, amount):
    amount = amount % LANES
    return value if amount == 0 else pltpu.roll(value, amount, 1)


def swap_groups(values, group):
    count = len(values)
    lane = lane_index()
    values = list(values)
    bit = 1
    while bit < count:
        low = (lane // (group * bit)) % 2 == 0
        for first in range(count):
            if first & bit == 0:
                a, b = values[first], values[first | bit]
                values[first] = jnp.where(low, a, lane_roll(b, group * bit))
                values[first | bit] = jnp.where(low, lane_roll(a, -group * bit), b)
        bit *= 2
    return values


SPEED_AT, SOLID_AT, HEAT_AT, RATE_AT, ROWS = 27, 30, 31, 38, 40
MOVING = 34


def moving_row(number):
    return number + (HEAT_AT - SPEED_AT) * (number >= SPEED_AT)


def offer_heat(slab, levels_hbm, heat_hbm, phase_hbm, *refs):
    outs, (levels_ref, heat_ref, phase_ref, sems) = refs[: slab.grp], refs[slab.grp :]
    copies = [
        pltpu.make_async_copy(heat_hbm, heat_ref, sems.at[0]),
        pltpu.make_async_copy(phase_hbm, phase_ref, sems.at[1]),
        pltpu.make_async_copy(levels_hbm, levels_ref, sems.at[2]),
    ]
    for copy in copies:
        copy.start()
    for copy in copies:
        copy.wait()
    mine = lax.axis_index("grp")
    for step in range(slab.grp):
        part = jnp.bitwise_xor(mine, step)
        span = pl.ds(pl.multiple_of(part * LANES, LANES), LANES)
        phase = phase_ref[0, :, span]
        chosen = jnp.zeros((SUBLANES, LANES), F32)
        for level in range(levels_ref.shape[0]):
            chosen = jnp.where(phase == level, levels_ref[level], chosen)
        for k in range(7):
            outs[step][k] = heat_ref[k, 0, :, span]
        outs[step][7] = 1.0 / (0.5 + 4.0 * chosen)


def for_each(count, body):
    for number in range(count):
        body(number)


def pack_flow(slab, popul_hbm, speed_hbm, solid_hbm, sent, flags, fields, solid_ref, sems):
    copies = [
        pltpu.make_async_copy(popul_hbm, fields.at[pl.ds(0, SPEED_AT)], sems.at[0]),
        pltpu.make_async_copy(speed_hbm, fields.at[pl.ds(SPEED_AT, 3)], sems.at[1]),
        pltpu.make_async_copy(solid_hbm, solid_ref, sems.at[2]),
    ]
    for copy in copies:
        copy.start()
    for copy in copies:
        copy.wait()
    holders = slab.holders()

    def one(pair):
        pack_pair(slab, fields, pair, sent, pair, holders)

    for_each(SOLID_AT // 2, one)
    flags[...] = solid_ref[...].astype(F32)


def pack_pair(slab, fields, source, sent, target, holders):
    sources = [fields[2 * source + h, x] for x in range(slab.block_x) for h in range(2)]
    for place, value in enumerate(swap_groups(sources, slab.planes)):
        sent[holders[place], target] = value


def pack_heat(slab, sent_in, flags, *refs):
    parts, (sent, held, packed, sem) = refs[: slab.grp], refs[slab.grp :]
    mine = lax.axis_index("grp")
    holders = slab.holders()
    held[0] = flags[...]
    held[9] = jnp.zeros(flags.shape, F32)
    for step in range(slab.grp):
        held[pl.ds(1, 8), jnp.bitwise_xor(mine, step)] = parts[step][...]
    first, count = SOLID_AT // 2, (ROWS - SOLID_AT) // 2

    def one(pair):
        pack_pair(slab, held, pair, packed, pair, holders)

    for_each(count, one)
    copy = pltpu.make_async_copy(packed, sent.at[:, pl.ds(first, count)], sem)
    copy.start()
    copy.wait()


def in_first_half(slab):
    return lane_index() % slab.planes < slab.halo


def offer_halo(slab, came, low_out, high_out):
    def one(number, _):
        tile = 2 * number
        first = in_first_half(slab)
        for pair in range(ROWS // 2):
            a, b = came[tile, pair], came[tile + 1, pair]
            low_out[number, pair] = jnp.where(first, a, lane_roll(b, slab.halo))
            high_out[number, pair] = jnp.where(first, lane_roll(b, -slab.halo), a)
        return 0

    lax.fori_loop(0, slab.sub // 2, one, 0)


def make_tiles(slab, came, below_ref, above_ref, state):
    def one(number, _):
        first = in_first_half(slab)
        even = (lane_index() // slab.planes) % 2 == 0
        back = 2 * slab.planes
        for pair in range(ROWS // 2):
            below, above = below_ref[number, pair], above_ref[number, pair]
            beside = (
                jnp.where(first, above, lane_roll(below, -back)),
                jnp.where(first, lane_roll(above, -slab.halo), lane_roll(below, slab.halo - back)),
            )
            for which in range(2):
                tile = 2 * number + which
                own, halo = came[tile, pair], beside[which]
                state[2 * pair, tile] = jnp.where(even, own, lane_roll(halo, slab.planes))
                state[2 * pair + 1, tile] = jnp.where(even, lane_roll(own, -slab.planes), halo)
        return 0

    lax.fori_loop(0, slab.sub // 2, one, 0)


def pack_out(slab, came, state, sent):
    def one(tile, _):
        even = (lane_index() // slab.planes) % 2 == 0
        flags = came[tile, SOLID_AT // 2]
        solid = jnp.where(even, flags, lane_roll(flags, slab.planes)) != 0.0
        for pair in range(MOVING // 2):
            first, second = (state[moving_row(2 * pair + h), tile] for h in range(2))
            value = jnp.where(even, first, lane_roll(second, slab.planes))
            if 2 * pair + 1 < SPEED_AT:
                value = jnp.where(solid, came[tile, pair], value)
            elif 2 * pair < SPEED_AT:
                value = jnp.where(jnp.logical_and(solid, even), came[tile, pair], value)
            sent[tile, pair] = value
        return 0

    lax.fori_loop(0, slab.sub, one, 0)


def unpack_pair(slab, came, pair, holders):
    sources = [came[holders[place], pair] for place in range(slab.sub)]
    values = swap_groups(sources, slab.planes)
    return [values[0::2], values[1::2]]


def return_heat(slab, came, *refs):
    outs, held = refs[: slab.grp], refs[slab.grp]
    holders = slab.holders()
    _, values = unpack_pair(slab, came, SPEED_AT // 2, holders)
    for x in range(slab.block_x):
        held[x, 0] = values[x]

    def one(pair):
        for h, values in enumerate(unpack_pair(slab, came, SPEED_AT // 2 + 1 + pair, holders)):
            for x in range(slab.block_x):
                held[x, 2 * pair + 1 + h] = values[x]

    for_each(3, one)
    mine = lax.axis_index("grp")
    for step in range(slab.grp):
        outs[step][...] = held[jnp.bitwise_xor(mine, step)]


def unpack_flow(slab, came, popul_out):
    holders = slab.holders()

    def one(pair):
        for h, values in enumerate(unpack_pair(slab, came, pair, holders)):
            for x in range(slab.block_x):
                popul_out[2 * pair + h, x] = values[x]

    for_each(SPEED_AT // 2, one)
    values, _ = unpack_pair(slab, came, SPEED_AT // 2, holders)
    for x in range(slab.block_x):
        popul_out[SPEED_AT - 1, x] = values[x]


def join_heat(slab, *refs):
    parts, thermal_out = refs[: slab.grp], refs[slab.grp]
    mine = lax.axis_index("grp")
    for step in range(slab.grp):
        part = jnp.bitwise_xor(mine, step)
        span = pl.ds(pl.multiple_of(part * LANES, LANES), LANES)
        for k in range(7):
            thermal_out[k, 0, :, span] = parts[step][k]


def forward3(values):
    for stride in (9, 3, 1):
        out = [None] * 27
        for n in range(27):
            if n // stride % 3 == 0:
                a, b, c = values[n], values[n + stride], values[n + 2 * stride]
                both = a + c
                out[n], out[n + stride], out[n + 2 * stride] = both + b, c - a, both
        values = out
    return values


def backward3(values):
    for stride in (9, 3, 1):
        out = [None] * 27
        for n in range(27):
            if n // stride % 3 == 0:
                a, b, c = values[n], values[n + stride], values[n + 2 * stride]
                even, odd = 0.5 * c, 0.5 * b
                out[n], out[n + stride], out[n + 2 * stride] = even - odd, a - c, even + odd
        values = out
    return values


def collide_tile(values, force, rate):
    moments = forward3(values)
    density = moments[0]
    jx, jy, jz = moments[9], moments[3], moments[1] + 0.5 * force
    inverse = 1.0 / density
    flux = (jx, jy, jz)
    u = tuple(j * inverse for j in flux)
    third = 1.0 / 3.0
    base = {0: density}
    for k in (1, 2, 3):
        base[k] = density * third**k
    squares = [flux[d] * u[d] for d in range(3)]
    square_at = {}
    scaled = {}

    def scale(key, value, count):
        if count == 0:
            return value
        if (key, count) not in scaled:
            scaled[key, count] = value * third**count
        return scaled[key, count]

    cross = {(0, 1): jx * u[1], (0, 2): jx * u[2], (1, 2): jy * u[2]}
    out = [None] * 27
    for n in range(27):
        powers = (n // 9, n // 3 % 3, n % 3)
        if n in (0, 3, 9):
            out[n] = moments[n]
            continue
        if n == 1:
            out[n] = moments[n] + force
            continue
        odd = tuple(d for d in range(3) if powers[d] == 1)
        even = tuple(d for d in range(3) if powers[d] == 2)
        count = len(even)
        if len(odd) == 3:
            out[n] = moments[n] - rate(n) * moments[n]
            continue
        if len(odd) == 0:
            if even not in square_at:
                total = squares[even[0]]
                for d in even[1:]:
                    total = total + squares[d]
                square_at[even] = base[count] + (total * (3.0 * third**count) if count > 1 else total)
            level = square_at[even]
        elif len(odd) == 1:
            level = scale(odd, flux[odd[0]], count)
        else:
            level = scale(odd, cross[odd], count)
        out[n] = moments[n] - rate(n) * (moments[n] - level)
    return backward3(out)


HEAT_OFFSETS = [(0, 0, 0), (1, 0, 0), (-1, 0, 0), (0, 1, 0), (0, -1, 0), (0, 0, 1), (0, 0, -1)]


def run_steps(slab, rates_ref, state, post, force_ref):
    def collide_one(tile, _):
        values = [state[n, tile] for n in range(27)]
        solid = state[SOLID_AT, tile] != 0.0
        moved = collide_tile(values, force_ref[tile], lambda n: rates_ref[n])
        for n in range(27):
            post[n, tile] = jnp.where(solid, jnp.nan, moved[n])
        heat = [state[HEAT_AT + k, tile] for k in range(7)]
        total = heat[0]
        for k in range(1, 7):
            total = total + heat[k]
        omega = state[RATE_AT, tile]
        side = 0.125 * total
        half = 0.5 * total
        for k in range(7):
            if k == 0:
                level = 0.25 * total
            else:
                drift = half * state[SPEED_AT + (k - 1) // 2, tile]
                level = side + drift if k % 2 == 1 else side - drift
            post[SPEED_AT + k, tile] = heat[k] - (heat[k] - level) * omega
        return 0

    def stream_one(tile, _):
        block_x, block_y = tile // slab.gy, tile % slab.gy
        x_of = {a: lax.rem(block_x + slab.gx - a, slab.gx) for a in (-1, 0, 1)}
        y_of = {b: lax.rem(block_y + slab.gy - b, slab.gy) for b in (-1, 0, 1)}
        row = row_index()
        per_x = 2 * slab.planes
        in_x = (lane_index() + slab.halo) % LANES // per_x
        last_x = {1: in_x == slab.block_x - 1, -1: in_x == 0}
        last_y = {1: row == SUBLANES - 1, -1: row == 0}

        def arrive(number, offset):
            a, b, c = offset

            def take(x):
                value = post[number, x_of[x] * slab.gy + block_y]
                if b != 0:
                    other = post[number, x_of[x] * slab.gy + y_of[b]]
                    value = jnp.where(last_y[b], other, value)
                return value

            value = take(0)
            if a != 0:
                value = jnp.where(last_x[a], take(a), value)
            if b != 0:
                value = pltpu.roll(value, b % SUBLANES, 0)
            return lane_roll(value, a * per_x + c)

        for n in range(27):
            value = arrive(n, OFFSET_TABLE[n])
            state[n, tile] = jnp.where(value != value, post[26 - n, tile], value)
        for k in range(7):
            state[HEAT_AT + k, tile] = arrive(SPEED_AT + k, HEAT_OFFSETS[k])
        return 0

    def step(number, _):
        lax.fori_loop(0, slab.sub, collide_one, 0)
        lax.fori_loop(0, slab.sub, stream_one, 0)
        return 0

    lax.fori_loop(0, STEPS, step, 0)


def heat_force(state, tile):
    total = state[HEAT_AT, tile]
    for k in range(1, 7):
        total = total + state[HEAT_AT + k, tile]
    return BUOYANCY * (total - REFERENCE_HEAT)


def flow_speed_tile(state, tile, force):
    values = [state[n, tile] for n in range(27)]
    total = values[0]
    for n in range(1, 27):
        total = total + values[n]
    sums = []
    for d in range(3):
        plus, minus = None, None
        for n in range(27):
            part = OFFSET_TABLE[n][d]
            if part == 1:
                plus = values[n] if plus is None else plus + values[n]
            if part == -1:
                minus = values[n] if minus is None else minus + values[n]
        sums.append(plus - minus)
    sums[2] = sums[2] + 0.5 * force
    return [each / total for each in sums]


def both_windows(slab, rates_hbm, came, below_ref, above_ref, *refs):
    sent, rates_ref, sem, state, post, force = refs
    rates_copy = pltpu.make_async_copy(rates_hbm, rates_ref, sem)
    rates_copy.start()
    make_tiles(slab, came, below_ref, above_ref, state)

    def first_force(tile, _):
        force[tile] = heat_force(state, tile)
        return 0

    lax.fori_loop(0, slab.sub, first_force, 0)
    rates_copy.wait()

    def next_speed(tile, _):
        solid = state[SOLID_AT, tile] != 0.0
        for d, each in enumerate(flow_speed_tile(state, tile, force[tile])):
            state[SPEED_AT + d, tile] = jnp.where(solid, 0.0, each)
        force[tile] = heat_force(state, tile)
        return 0

    def one_window(window, _):
        run_steps(slab, rates_ref, state, post, force)

        @pl.when(window + 1 < WINDOWS)
        def _():
            lax.fori_loop(0, slab.sub, next_speed, 0)

        return 0

    lax.fori_loop(0, WINDOWS, one_window, 0)
    pack_out(slab, came, state, sent)


def local_call(body, slab, arrays, outs, scratch=(), in_hbm=0, carried=False):
    def kernel(*refs):
        body(slab, *refs)

    return pl.pallas_call(
        kernel,
        out_shape=[jax.ShapeDtypeStruct(shape, F32) for shape in outs],
        in_specs=[
            pl.BlockSpec(
                memory_space=pltpu.HBM if i < in_hbm else pl.ANY if carried and i == 0 else pltpu.VMEM
            )
            for i in range(len(arrays))
        ],
        out_specs=[pl.BlockSpec(memory_space=pl.ANY if carried else pltpu.VMEM)] * len(outs),
        input_output_aliases={0: 0} if carried else {},
        scratch_shapes=[pltpu.VMEM(s, F32) if isinstance(s, tuple) else s for s in scratch],
        compiler_params=pltpu.CompilerParams(vmem_limit_bytes=24 * 1024 * 1024),
    )(
        *(
            pltpu.with_memory_space_constraint(array, pltpu.HBM) if i < in_hbm else array
            for i, array in enumerate(arrays)
        )
    )


RING = ("grp", "gx", "gy")


def exchange(slab, low, high):
    ring = slab.ring
    upward = [(ring[i - 1], ring[i]) for i in range(len(ring))]
    from_below = lax.ppermute(high, RING, upward)
    from_above = lax.ppermute(low, RING, [(b, a) for a, b in upward])
    return from_below, from_above


def across_planes(slab, parts):
    return [parts[0]] + [
        lax.ppermute(parts[step], "grp", [(i, i ^ step) for i in range(slab.grp)])
        for step in range(1, slab.grp)
    ]


def on_slabs(slab, populations, thermal, velocity_prev, solid, phase_ids, conductivity, rates):
    tile = (SUBLANES, LANES)

    def vmem_like(array):
        return pltpu.VMEM(array.shape, array.dtype)

    parts = local_call(
        offer_heat,
        slab,
        [conductivity, thermal, phase_ids],
        [(8,) + tile] * slab.grp,
        [
            pltpu.SMEM(conductivity.shape, F32),
            vmem_like(thermal),
            vmem_like(phase_ids),
            pltpu.SemaphoreType.DMA((3,)),
        ],
        in_hbm=3,
    )
    parts = across_planes(slab, parts)
    sent_shape = (slab.sub, ROWS // 2) + tile
    sent, flags = local_call(
        pack_flow,
        slab,
        [populations, velocity_prev, solid],
        [sent_shape, solid.shape],
        [
            (SOLID_AT,) + solid.shape,
            pltpu.VMEM(solid.shape, solid.dtype),
            pltpu.SemaphoreType.DMA((3,)),
        ],
        in_hbm=3,
    )
    (sent,) = local_call(
        pack_heat,
        slab,
        [sent, flags] + parts,
        [sent_shape],
        [
            (ROWS - SOLID_AT,) + solid.shape,
            (slab.sub, (ROWS - SOLID_AT) // 2) + tile,
            pltpu.SemaphoreType.DMA,
        ],
        carried=True,
    )
    came = lax.all_to_all(sent, ("gx", "gy"), split_axis=0, concat_axis=0, tiled=True)
    halo_shape = (slab.sub // 2, ROWS // 2) + tile
    low, high = local_call(offer_halo, slab, [came], [halo_shape, halo_shape])
    below, above = exchange(slab, low, high)
    (sent,) = local_call(
        both_windows,
        slab,
        [rates, came, below, above],
        [(slab.sub, MOVING // 2) + tile],
        [
            pltpu.SMEM(rates.shape, F32),
            pltpu.SemaphoreType.DMA,
            (ROWS, slab.sub) + tile,
            (MOVING, slab.sub) + tile,
            (slab.sub,) + tile,
        ],
        in_hbm=1,
    )
    came = lax.all_to_all(sent, ("gx", "gy"), split_axis=0, concat_axis=0, tiled=True)
    parts = local_call(
        return_heat, slab, [came], [(7,) + tile] * slab.grp, [(slab.grp, 7) + tile]
    )
    parts = across_planes(slab, parts)
    (populations_out,) = local_call(unpack_flow, slab, [came], [populations.shape])
    (thermal_out,) = local_call(join_heat, slab, parts, [thermal.shape])
    return populations_out, thermal_out


def solution(mesh):
    in_specs = (
        P(None, "gx", "gy", "grp"),
        P(None, ("gx", "grp"), "gy", None),
        P(None, "gx", "gy", "grp"),
        P("gx", "gy", "grp"),
        P(("gx", "grp"), "gy", None),
        P(),
        P(),
    )
    out_specs = (P(None, "gx", "gy", "grp"), P(None, ("gx", "grp"), "gy", None))

    def per_device(populations, thermal, *others):
        slab = Slab(mesh.shape, populations.shape[1:], thermal.shape[1:])
        plan = (lambda *arrays: on_slabs(slab, *arrays)) if slab.fits else on_device
        return plan(populations, thermal, *others)

    return jax.shard_map(
        per_device, mesh=mesh, in_specs=in_specs, out_specs=out_specs, check_vma=False
    )
```

```python
import jax
import jax.numpy as jnp
import numpy as np
from jax import lax
from jax.experimental import pallas as pl
from jax.experimental.pallas import tpu as pltpu
from jax.sharding import PartitionSpec as P

STEPS = 4
WINDOWS = 2


HIGHEST = lax.Precision.HIGHEST
BUOYANCY = 0.03
REFERENCE_HEAT = 1.0
OFFSET_TABLE = [(number // 9 - 1, number // 3 % 3 - 1, number % 3 - 1) for number in range(27)]
LATTICE_WEIGHTS = np.array(
    [
        np.prod([2.0 / 3.0 if component == 0 else 1.0 / 6.0 for component in triple])
        for triple in OFFSET_TABLE
    ]
)
VANDERMONDE = np.array([[1.0, 1.0, 1.0], [-1.0, 0.0, 1.0], [1.0, 0.0, 1.0]])
VANDER_INVERSE = np.array([[0.0, -0.5, 0.5], [1.0, 0.0, -1.0], [0.0, 0.5, 0.5]])
MOMENT_MATRIX = np.kron(np.kron(VANDERMONDE, VANDERMONDE), VANDERMONDE)
MOMENT_INVERSE = np.kron(np.kron(VANDER_INVERSE, VANDER_INVERSE), VANDER_INVERSE)
RELAXED = np.array([0.0 if number in (0, 1, 3, 9) else 1.0 for number in range(27)])
SUMMING = np.concatenate([np.ones((1, 27)), 1.0 * np.array(OFFSET_TABLE).T], axis=0)
HEAT_WEIGHTS = np.array([0.25] + [0.125] * 6)


def from_behind(value, axis, steps):
    count = lax.axis_size(axis)
    pairs = [(source, (source + steps) % count) for source in range(count)]
    return lax.ppermute(value, axis, pairs)


def extended(cells, sides, width):
    for axis, dim in sides:
        count = lax.axis_size(axis)
        head = lax.slice_in_dim(cells, 0, width, axis=dim)
        tail = lax.slice_in_dim(cells, cells.shape[dim] - width, cells.shape[dim], axis=dim)
        cells = jnp.concatenate(
            [
                lax.ppermute(tail, axis, [(i, (i + 1) % count) for i in range(count)]),
                cells,
                lax.ppermute(head, axis, [((i + 1) % count, i) for i in range(count)]),
            ],
            axis=dim,
        )
    return cells


def flow_state(flat, heat_flat):
    sums = jnp.dot(jnp.asarray(SUMMING, jnp.float32), flat, precision=HIGHEST)
    density = sums[0]
    force = BUOYANCY * (heat_flat - REFERENCE_HEAT)
    speed = jnp.stack([sums[1], sums[2], sums[3] + 0.5 * force]) / density
    return (density, force, speed)


def collide(popul, heat, rates):
    flat = popul.reshape(27, -1)
    density, force, speed = flow_state(flat, heat.reshape(-1))
    along = jnp.dot(jnp.asarray(SUMMING[1:].T, jnp.float32), speed, precision=HIGHEST)
    square = jnp.sum(speed * speed, axis=0)
    balance = (
        density
        * jnp.asarray(LATTICE_WEIGHTS, jnp.float32)[:, None]
        * (1.0 + 3.0 * along + 4.5 * along * along - 1.5 * square)
    )
    scaled = (
        jnp.asarray(MOMENT_INVERSE, jnp.float32)
        * (rates * jnp.asarray(RELAXED, jnp.float32))[None, :]
    )
    relax = jnp.dot(scaled, jnp.asarray(MOMENT_MATRIX, jnp.float32), precision=HIGHEST)
    post = (
        flat
        - jnp.dot(relax, flat - balance, precision=HIGHEST)
        + jnp.asarray(MOMENT_INVERSE[:, 1], jnp.float32)[:, None] * force[None, :]
    )
    return post.reshape(popul.shape)


def flow_speed(popul, heat, solid):
    density, force, speed = flow_state(popul.reshape(27, -1), heat.reshape(-1))
    return jnp.where(solid[None] == 0, speed.reshape((3,) + solid.shape), 0.0)


def heat_collide(heat_pops, speed, relax_time):
    total = jnp.sum(heat_pops, axis=0)
    still = jnp.zeros_like(speed[0])
    along = jnp.stack([still, speed[0], -speed[0], speed[1], -speed[1], speed[2], -speed[2]])
    balance = (
        jnp.asarray(HEAT_WEIGHTS, jnp.float32)[:, None, None, None]
        * total[None]
        * (1.0 + 4.0 * along)
    )
    return heat_pops - (heat_pops - balance) / relax_time[None]


def relaxation(phase_ids, conductivity):
    levels = jnp.arange(conductivity.shape[0], dtype=jnp.int32)
    chosen = jnp.sum(
        jnp.where(
            phase_ids[None] == levels[:, None, None, None], conductivity[:, None, None, None], 0.0
        ),
        axis=0,
    )
    return 0.5 + 4.0 * chosen


def inner_window(padded, triple, sizes):
    return padded[
        1 - triple[0] : 1 - triple[0] + sizes[0],
        1 - triple[1] : 1 - triple[1] + sizes[1],
        1 - triple[2] : 1 - triple[2] + sizes[2],
    ]


def advance(grid, axis_number, send_up, send_down):
    space = 3 + axis_number
    length = grid.shape[space]
    rising = lax.index_in_dim(grid, 2, axis_number, keepdims=True)
    resting = lax.index_in_dim(grid, 1, axis_number, keepdims=True)
    falling = lax.index_in_dim(grid, 0, axis_number, keepdims=True)
    from_below = send_up(lax.slice_in_dim(rising, length - 1, length, axis=space))
    from_above = send_down(lax.slice_in_dim(falling, 0, 1, axis=space))
    rising = jnp.concatenate(
        [from_below, lax.slice_in_dim(rising, 0, length - 1, axis=space)], axis=space
    )
    falling = jnp.concatenate(
        [lax.slice_in_dim(falling, 1, length, axis=space), from_above], axis=space
    )
    return jnp.concatenate([falling, resting, rising], axis=axis_number)


def flow_arrivals(post):
    sizes = post.shape[1:]
    grid = post.reshape((3, 3, 3) + sizes)
    grid = advance(
        grid,
        0,
        lambda plane: from_behind(plane, "gx", 1),
        lambda plane: from_behind(plane, "gx", -1),
    )
    grid = advance(
        grid,
        1,
        lambda plane: from_behind(plane, "gy", 1),
        lambda plane: from_behind(plane, "gy", -1),
    )
    grid = advance(
        grid,
        2,
        lambda plane: from_behind(plane, "grp", 1),
        lambda plane: from_behind(plane, "grp", -1),
    )
    return grid.reshape(post.shape)


def stream_heat(post, grp_index, last_grp):
    length = post.shape[1]
    size_y = post.shape[2]
    eastward = post[1]
    westward = post[2]
    lower_first = from_behind(eastward, "grp", 1)
    lower_second = from_behind(lower_first, "gx", 1)
    entering = jnp.where(grp_index == 0, lower_second, lower_first)
    eastward = jnp.concatenate([entering, eastward[: length - 1]], axis=0)
    upper_first = from_behind(westward, "grp", -1)
    upper_second = from_behind(upper_first, "gx", -1)
    entering = jnp.where(grp_index == last_grp, upper_second, upper_first)
    westward = jnp.concatenate([westward[1:], entering], axis=0)
    sides = extended(post[3:5], (("gy", 2),), 1)
    northward = sides[0, :, 0:size_y]
    southward = sides[1, :, 2 : size_y + 2]
    upward = jnp.roll(post[5], 1, axis=2)
    downward = jnp.roll(post[6], -1, axis=2)
    return jnp.stack([post[0], eastward, westward, northward, southward, upward, downward])


def on_device(populations, thermal, velocity_prev, solid, phase_ids, conductivity, rates):
    padded_solid = extended(solid, (("grp", 2), ("gx", 0), ("gy", 1)), 1)
    sizes = solid.shape
    blocked = jnp.stack(
        [inner_window(padded_solid, OFFSET_TABLE[number], sizes) != 0 for number in range(27)]
    )
    fluid_cells = (solid == 0)[None]
    grp_index = lax.axis_index("grp")
    last_grp = lax.axis_size("grp") - 1
    relax_time = relaxation(phase_ids, conductivity)
    speed_brick = velocity_prev
    popul = populations
    heat_pops = thermal
    for window_number in range(WINDOWS):
        heat_brick = lax.all_to_all(
            jnp.sum(heat_pops, axis=0), "grp", split_axis=2, concat_axis=0, tiled=True
        )
        speed_column = lax.all_to_all(speed_brick, "grp", split_axis=1, concat_axis=3, tiled=True)
        for step_number in range(STEPS):
            post = collide(popul, heat_brick, rates)
            arrived = flow_arrivals(post)
            popul = jnp.where(fluid_cells, jnp.where(blocked, post[::-1], arrived), popul)
        for step_number in range(STEPS):
            heat_pops = stream_heat(
                heat_collide(heat_pops, speed_column, relax_time), grp_index, last_grp
            )
        if window_number + 1 < WINDOWS:
            speed_brick = flow_speed(popul, heat_brick, solid)
    return (popul, heat_pops)


SUBLANES = 8
LANES = 128
F32 = jnp.float32


class Slab:
    def __init__(self, mesh_shape, flow_block, heat_block):
        self.grp, self.gx, self.gy = (mesh_shape[name] for name in ("grp", "gx", "gy"))
        self.block_x, self.block_y, self.block_z = flow_block
        self.sub = self.gx * self.gy
        self.planes = self.block_z // self.sub
        self.halo = self.planes // 2
        self.fits = (
            self.block_y == SUBLANES
            and self.block_z == LANES
            and self.planes * self.sub == LANES
            and self.halo * 2 == self.planes
            and self.halo == STEPS * WINDOWS
            and 2 * self.block_x == self.sub
            and self.block_x == self.grp
            and heat_block == (1, SUBLANES, self.grp * LANES)
            and self.sub & (self.sub - 1) == 0
            and self.grp & (self.grp - 1) == 0
            and self.gy % 2 == 0
        )
        if self.fits:
            self.snake = [
                x * self.gy + (y if x % 2 == 0 else self.gy - 1 - y)
                for x in range(self.gx)
                for y in range(self.gy)
            ]
            self.ring = [
                part * self.sub + self.snake[place if part % 2 == 0 else self.sub - 1 - place]
                for part in range(self.grp)
                for place in range(self.sub)
            ]

    def holders(self):
        even = lax.axis_index("grp") % 2 == 0
        mine = self.place_in_plane()
        return [
            jnp.bitwise_xor(jnp.where(even, *pair), mine)
            for pair in zip(self.snake, self.snake[::-1])
        ]

    def place_in_plane(self):
        return lax.axis_index("gx") * self.gy + lax.axis_index("gy")


def lane_index():
    return lax.broadcasted_iota(jnp.int32, (SUBLANES, LANES), 1)


def row_index():
    return lax.broadcasted_iota(jnp.int32, (SUBLANES, LANES), 0)


def lane_roll(value, amount):
    amount = amount % LANES
    return value if amount == 0 else pltpu.roll(value, amount, 1)


def swap_groups(values, group):
    count = len(values)
    lane = lane_index()
    values = list(values)
    bit = 1
    while bit < count:
        low = (lane // (group * bit)) % 2 == 0
        for first in range(count):
            if first & bit == 0:
                a, b = values[first], values[first | bit]
                values[first] = jnp.where(low, a, lane_roll(b, group * bit))
                values[first | bit] = jnp.where(low, lane_roll(a, -group * bit), b)
        bit *= 2
    return values


SPEED_AT, SOLID_AT, HEAT_AT, RATE_AT, ROWS = 27, 30, 31, 38, 40
MOVING = 34


def moving_row(number):
    return number + (HEAT_AT - SPEED_AT) * (number >= SPEED_AT)


def offer_heat(slab, levels_hbm, heat_hbm, phase_hbm, *refs):
    outs, (levels_ref, heat_ref, phase_ref, sems) = refs[: slab.grp], refs[slab.grp :]
    copies = [
        pltpu.make_async_copy(heat_hbm, heat_ref, sems.at[0]),
        pltpu.make_async_copy(phase_hbm, phase_ref, sems.at[1]),
        pltpu.make_async_copy(levels_hbm, levels_ref, sems.at[2]),
    ]
    for copy in copies:
        copy.start()
    for copy in copies:
        copy.wait()
    mine = lax.axis_index("grp")
    for step in range(slab.grp):
        part = jnp.bitwise_xor(mine, step)
        span = pl.ds(pl.multiple_of(part * LANES, LANES), LANES)
        phase = phase_ref[0, :, span]
        chosen = jnp.zeros((SUBLANES, LANES), F32)
        for level in range(levels_ref.shape[0]):
            chosen = jnp.where(phase == level, levels_ref[level], chosen)
        for k in range(7):
            outs[step][k] = heat_ref[k, 0, :, span]
        outs[step][7] = 1.0 / (0.5 + 4.0 * chosen)


def for_each(count, body):
    for number in range(count):
        body(number)


def pack_flow(slab, popul_hbm, speed_hbm, solid_hbm, sent, flags, fields, solid_ref, sems):
    copies = [
        pltpu.make_async_copy(popul_hbm, fields.at[pl.ds(0, SPEED_AT)], sems.at[0]),
        pltpu.make_async_copy(speed_hbm, fields.at[pl.ds(SPEED_AT, 3)], sems.at[1]),
        pltpu.make_async_copy(solid_hbm, solid_ref, sems.at[2]),
    ]
    for copy in copies:
        copy.start()
    for copy in copies:
        copy.wait()
    holders = slab.holders()

    def one(pair):
        pack_pair(slab, fields, pair, sent, pair, holders)

    for_each(SOLID_AT // 2, one)
    flags[...] = solid_ref[...].astype(F32)


def pack_pair(slab, fields, source, sent, target, holders):
    sources = [fields[2 * source + h, x] for x in range(slab.block_x) for h in range(2)]
    for place, value in enumerate(swap_groups(sources, slab.planes)):
        sent[holders[place], target] = value


def pack_heat(slab, sent_in, flags, *refs):
    parts, (sent, held, packed, sem) = refs[: slab.grp], refs[slab.grp :]
    mine = lax.axis_index("grp")
    holders = slab.holders()
    held[0] = flags[...]
    held[9] = jnp.zeros(flags.shape, F32)
    for step in range(slab.grp):
        held[pl.ds(1, 8), jnp.bitwise_xor(mine, step)] = parts[step][...]
    first, count = SOLID_AT // 2, (ROWS - SOLID_AT) // 2

    def one(pair):
        pack_pair(slab, held, pair, packed, pair, holders)

    for_each(count, one)
    copy = pltpu.make_async_copy(packed, sent.at[:, pl.ds(first, count)], sem)
    copy.start()
    copy.wait()


def in_first_half(slab):
    return lane_index() % slab.planes < slab.halo


def collect(slab, parts, came):
    mine = slab.place_in_plane()
    for step in range(slab.sub):
        came[jnp.bitwise_xor(mine, step)] = parts[step][...]


def offer_halo(slab, *refs):
    parts, (came, low_out, high_out) = refs[: slab.sub], refs[slab.sub :]
    collect(slab, parts, came)

    def one(number, _):
        tile = 2 * number
        first = in_first_half(slab)
        for pair in range(ROWS // 2):
            a, b = came[tile, pair], came[tile + 1, pair]
            low_out[number, pair] = jnp.where(first, a, lane_roll(b, slab.halo))
            high_out[number, pair] = jnp.where(first, lane_roll(b, -slab.halo), a)
        return 0

    lax.fori_loop(0, slab.sub // 2, one, 0)


def make_tiles(slab, came, below_ref, above_ref, state):
    def one(number, _):
        first = in_first_half(slab)
        even = (lane_index() // slab.planes) % 2 == 0
        back = 2 * slab.planes
        for pair in range(ROWS // 2):
            below, above = below_ref[number, pair], above_ref[number, pair]
            beside = (
                jnp.where(first, above, lane_roll(below, -back)),
                jnp.where(first, lane_roll(above, -slab.halo), lane_roll(below, slab.halo - back)),
            )
            for which in range(2):
                tile = 2 * number + which
                own, halo = came[tile, pair], beside[which]
                state[2 * pair, tile] = jnp.where(even, own, lane_roll(halo, slab.planes))
                state[2 * pair + 1, tile] = jnp.where(even, lane_roll(own, -slab.planes), halo)
        return 0

    lax.fori_loop(0, slab.sub // 2, one, 0)


def pack_out(slab, came, state, sent):
    def one(tile, _):
        even = (lane_index() // slab.planes) % 2 == 0
        partner = jnp.bitwise_xor(tile, slab.place_in_plane())
        flags = came[tile, SOLID_AT // 2]
        solid = jnp.where(even, flags, lane_roll(flags, slab.planes)) != 0.0
        for pair in range(MOVING // 2):
            first, second = (state[moving_row(2 * pair + h), tile] for h in range(2))
            value = jnp.where(even, first, lane_roll(second, slab.planes))
            if 2 * pair + 1 < SPEED_AT:
                value = jnp.where(solid, came[tile, pair], value)
            elif 2 * pair < SPEED_AT:
                value = jnp.where(jnp.logical_and(solid, even), came[tile, pair], value)
            sent[partner, pair] = value
        return 0

    lax.fori_loop(0, slab.sub, one, 0)


def unpack_pair(slab, came, pair, holders):
    sources = [came[holders[place], pair] for place in range(slab.sub)]
    values = swap_groups(sources, slab.planes)
    return [values[0::2], values[1::2]]


def return_heat(slab, *refs):
    parts, came, outs, held = (
        refs[: slab.sub],
        refs[slab.sub],
        refs[slab.sub + 1 : slab.sub + 1 + slab.grp],
        refs[-1],
    )
    for step in range(slab.sub):
        came[step] = parts[step][...]
    holders = slab.holders()
    _, values = unpack_pair(slab, came, SPEED_AT // 2, holders)
    for x in range(slab.block_x):
        held[x, 0] = values[x]

    def one(pair):
        for h, values in enumerate(unpack_pair(slab, came, SPEED_AT // 2 + 1 + pair, holders)):
            for x in range(slab.block_x):
                held[x, 2 * pair + 1 + h] = values[x]

    for_each(3, one)
    mine = lax.axis_index("grp")
    for step in range(slab.grp):
        outs[step][...] = held[jnp.bitwise_xor(mine, step)]


def unpack_flow(slab, came, popul_out):
    holders = slab.holders()

    def one(pair):
        for h, values in enumerate(unpack_pair(slab, came, pair, holders)):
            for x in range(slab.block_x):
                popul_out[2 * pair + h, x] = values[x]

    for_each(SPEED_AT // 2, one)
    values, _ = unpack_pair(slab, came, SPEED_AT // 2, holders)
    for x in range(slab.block_x):
        popul_out[SPEED_AT - 1, x] = values[x]


def join_heat(slab, *refs):
    parts, thermal_out = refs[: slab.grp], refs[slab.grp]
    mine = lax.axis_index("grp")
    for step in range(slab.grp):
        part = jnp.bitwise_xor(mine, step)
        span = pl.ds(pl.multiple_of(part * LANES, LANES), LANES)
        for k in range(7):
            thermal_out[k, 0, :, span] = parts[step][k]


def forward3(values):
    for stride in (9, 3, 1):
        out = [None] * 27
        for n in range(27):
            if n // stride % 3 == 0:
                a, b, c = values[n], values[n + stride], values[n + 2 * stride]
                both = a + c
                out[n], out[n + stride], out[n + 2 * stride] = both + b, c - a, both
        values = out
    return values


def backward3(values):
    for stride in (9, 3, 1):
        out = [None] * 27
        for n in range(27):
            if n // stride % 3 == 0:
                a, b, c = values[n], values[n + stride], values[n + 2 * stride]
                even, odd = 0.5 * c, 0.5 * b
                out[n], out[n + stride], out[n + 2 * stride] = even - odd, a - c, even + odd
        values = out
    return values


def collide_tile(values, force, rate):
    moments = forward3(values)
    density = moments[0]
    jx, jy, jz = moments[9], moments[3], moments[1] + 0.5 * force
    inverse = 1.0 / density
    flux = (jx, jy, jz)
    u = tuple(j * inverse for j in flux)
    third = 1.0 / 3.0
    base = {0: density}
    for k in (1, 2, 3):
        base[k] = density * third**k
    squares = [flux[d] * u[d] for d in range(3)]
    square_at = {}
    scaled = {}

    def scale(key, value, count):
        if count == 0:
            return value
        if (key, count) not in scaled:
            scaled[key, count] = value * third**count
        return scaled[key, count]

    cross = {(0, 1): jx * u[1], (0, 2): jx * u[2], (1, 2): jy * u[2]}
    out = [None] * 27
    for n in range(27):
        powers = (n // 9, n // 3 % 3, n % 3)
        if n in (0, 3, 9):
            out[n] = moments[n]
            continue
        if n == 1:
            out[n] = moments[n] + force
            continue
        odd = tuple(d for d in range(3) if powers[d] == 1)
        even = tuple(d for d in range(3) if powers[d] == 2)
        count = len(even)
        if len(odd) == 3:
            out[n] = moments[n] - rate(n) * moments[n]
            continue
        if len(odd) == 0:
            if even not in square_at:
                total = squares[even[0]]
                for d in even[1:]:
                    total = total + squares[d]
                square_at[even] = base[count] + (total * (3.0 * third**count) if count > 1 else total)
            level = square_at[even]
        elif len(odd) == 1:
            level = scale(odd, flux[odd[0]], count)
        else:
            level = scale(odd, cross[odd], count)
        out[n] = moments[n] - rate(n) * (moments[n] - level)
    return backward3(out)


HEAT_OFFSETS = [(0, 0, 0), (1, 0, 0), (-1, 0, 0), (0, 1, 0), (0, -1, 0), (0, 0, 1), (0, 0, -1)]


def run_steps(slab, rates_ref, state, post, force_ref):
    def collide_one(tile, _):
        values = [state[n, tile] for n in range(27)]
        solid = state[SOLID_AT, tile] != 0.0
        moved = collide_tile(values, force_ref[tile], lambda n: rates_ref[n])
        for n in range(27):
            post[n, tile] = jnp.where(solid, jnp.nan, moved[n])
        heat = [state[HEAT_AT + k, tile] for k in range(7)]
        total = heat[0]
        for k in range(1, 7):
            total = total + heat[k]
        omega = state[RATE_AT, tile]
        side = 0.125 * total
        half = 0.5 * total
        for k in range(7):
            if k == 0:
                level = 0.25 * total
            else:
                drift = half * state[SPEED_AT + (k - 1) // 2, tile]
                level = side + drift if k % 2 == 1 else side - drift
            post[SPEED_AT + k, tile] = heat[k] - (heat[k] - level) * omega
        return 0

    def stream_one(tile, _):
        block_x, block_y = tile // slab.gy, tile % slab.gy
        x_of = {a: lax.rem(block_x + slab.gx - a, slab.gx) for a in (-1, 0, 1)}
        y_of = {b: lax.rem(block_y + slab.gy - b, slab.gy) for b in (-1, 0, 1)}
        row = row_index()
        per_x = 2 * slab.planes
        in_x = (lane_index() + slab.halo) % LANES // per_x
        last_x = {1: in_x == slab.block_x - 1, -1: in_x == 0}
        last_y = {1: row == SUBLANES - 1, -1: row == 0}

        def arrive(number, offset):
            a, b, c = offset

            def take(x):
                value = post[number, x_of[x] * slab.gy + block_y]
                if b != 0:
                    other = post[number, x_of[x] * slab.gy + y_of[b]]
                    value = jnp.where(last_y[b], other, value)
                return value

            value = take(0)
            if a != 0:
                value = jnp.where(last_x[a], take(a), value)
            if b != 0:
                value = pltpu.roll(value, b % SUBLANES, 0)
            return lane_roll(value, a * per_x + c)

        for n in range(27):
            value = arrive(n, OFFSET_TABLE[n])
            state[n, tile] = jnp.where(value != value, post[26 - n, tile], value)
        for k in range(7):
            state[HEAT_AT + k, tile] = arrive(SPEED_AT + k, HEAT_OFFSETS[k])
        return 0

    def step(number, _):
        lax.fori_loop(0, slab.sub, collide_one, 0)
        lax.fori_loop(0, slab.sub, stream_one, 0)
        return 0

    lax.fori_loop(0, STEPS, step, 0)


def heat_force(state, tile):
    total = state[HEAT_AT, tile]
    for k in range(1, 7):
        total = total + state[HEAT_AT + k, tile]
    return BUOYANCY * (total - REFERENCE_HEAT)


def flow_speed_tile(state, tile, force):
    values = [state[n, tile] for n in range(27)]
    total = values[0]
    for n in range(1, 27):
        total = total + values[n]
    sums = []
    for d in range(3):
        plus, minus = None, None
        for n in range(27):
            part = OFFSET_TABLE[n][d]
            if part == 1:
                plus = values[n] if plus is None else plus + values[n]
            if part == -1:
                minus = values[n] if minus is None else minus + values[n]
        sums.append(plus - minus)
    sums[2] = sums[2] + 0.5 * force
    return [each / total for each in sums]


def both_windows(slab, rates_hbm, came, below_ref, above_ref, *refs):
    sent, rates_ref, sem, state, post, force = refs
    rates_copy = pltpu.make_async_copy(rates_hbm, rates_ref, sem)
    rates_copy.start()
    make_tiles(slab, came, below_ref, above_ref, state)

    def first_force(tile, _):
        force[tile] = heat_force(state, tile)
        return 0

    lax.fori_loop(0, slab.sub, first_force, 0)
    rates_copy.wait()

    def next_speed(tile, _):
        solid = state[SOLID_AT, tile] != 0.0
        for d, each in enumerate(flow_speed_tile(state, tile, force[tile])):
            state[SPEED_AT + d, tile] = jnp.where(solid, 0.0, each)
        force[tile] = heat_force(state, tile)
        return 0

    def one_window(window, _):
        run_steps(slab, rates_ref, state, post, force)

        @pl.when(window + 1 < WINDOWS)
        def _():
            lax.fori_loop(0, slab.sub, next_speed, 0)

        return 0

    lax.fori_loop(0, WINDOWS, one_window, 0)
    pack_out(slab, came, state, sent)


def local_call(body, slab, arrays, outs, scratch=(), in_hbm=0, carried=False):
    def kernel(*refs):
        body(slab, *refs)

    return pl.pallas_call(
        kernel,
        out_shape=[jax.ShapeDtypeStruct(shape, F32) for shape in outs],
        in_specs=[
            pl.BlockSpec(
                memory_space=pltpu.HBM if i < in_hbm else pl.ANY if carried and i == 0 else pltpu.VMEM
            )
            for i in range(len(arrays))
        ],
        out_specs=[pl.BlockSpec(memory_space=pl.ANY if carried else pltpu.VMEM)] * len(outs),
        input_output_aliases={0: 0} if carried else {},
        scratch_shapes=[pltpu.VMEM(s, F32) if isinstance(s, tuple) else s for s in scratch],
        compiler_params=pltpu.CompilerParams(vmem_limit_bytes=24 * 1024 * 1024),
    )(
        *(
            pltpu.with_memory_space_constraint(array, pltpu.HBM) if i < in_hbm else array
            for i, array in enumerate(arrays)
        )
    )


RING = ("grp", "gx", "gy")


def exchange(slab, low, high):
    ring = slab.ring
    upward = [(ring[i - 1], ring[i]) for i in range(len(ring))]
    from_below = lax.ppermute(high, RING, upward)
    from_above = lax.ppermute(low, RING, [(b, a) for a, b in upward])
    return from_below, from_above


def across_plane(slab, sent):
    came = {0: sent[0]}
    for step in sorted(range(1, slab.sub), key=lambda step: -bin(step >> 1).count("1")):
        pairs = [(i, i ^ step) for i in range(slab.sub)]
        came[step] = lax.ppermute(sent[step], ("gx", "gy"), pairs)
    return [came[step] for step in range(slab.sub)]


def across_planes(slab, parts):
    return [parts[0]] + [
        lax.ppermute(parts[step], "grp", [(i, i ^ step) for i in range(slab.grp)])
        for step in range(1, slab.grp)
    ]


def on_slabs(slab, populations, thermal, velocity_prev, solid, phase_ids, conductivity, rates):
    tile = (SUBLANES, LANES)

    def vmem_like(array):
        return pltpu.VMEM(array.shape, array.dtype)

    parts = local_call(
        offer_heat,
        slab,
        [conductivity, thermal, phase_ids],
        [(8,) + tile] * slab.grp,
        [
            pltpu.SMEM(conductivity.shape, F32),
            vmem_like(thermal),
            vmem_like(phase_ids),
            pltpu.SemaphoreType.DMA((3,)),
        ],
        in_hbm=3,
    )
    parts = across_planes(slab, parts)
    sent_shape = (slab.sub, ROWS // 2) + tile
    sent, flags = local_call(
        pack_flow,
        slab,
        [populations, velocity_prev, solid],
        [sent_shape, solid.shape],
        [
            (SOLID_AT,) + solid.shape,
            pltpu.VMEM(solid.shape, solid.dtype),
            pltpu.SemaphoreType.DMA((3,)),
        ],
        in_hbm=3,
    )
    (sent,) = local_call(
        pack_heat,
        slab,
        [sent, flags] + parts,
        [sent_shape],
        [
            (ROWS - SOLID_AT,) + solid.shape,
            (slab.sub, (ROWS - SOLID_AT) // 2) + tile,
            pltpu.SemaphoreType.DMA,
        ],
        carried=True,
    )
    halo_shape = (slab.sub // 2, ROWS // 2) + tile
    came, low, high = local_call(
        offer_halo, slab, across_plane(slab, sent), [sent_shape, halo_shape, halo_shape]
    )
    below, above = exchange(slab, low, high)
    (sent,) = local_call(
        both_windows,
        slab,
        [rates, came, below, above],
        [(slab.sub, MOVING // 2) + tile],
        [
            pltpu.SMEM(rates.shape, F32),
            pltpu.SemaphoreType.DMA,
            (ROWS, slab.sub) + tile,
            (MOVING, slab.sub) + tile,
            (slab.sub,) + tile,
        ],
        in_hbm=1,
    )
    came, *parts = local_call(
        return_heat,
        slab,
        across_plane(slab, sent),
        [sent.shape] + [(7,) + tile] * slab.grp,
        [(slab.grp, 7) + tile],
    )
    parts = across_planes(slab, parts)
    (populations_out,) = local_call(unpack_flow, slab, [came], [populations.shape])
    (thermal_out,) = local_call(join_heat, slab, parts, [thermal.shape])
    return populations_out, thermal_out


def solution(mesh):
    in_specs = (
        P(None, "gx", "gy", "grp"),
        P(None, ("gx", "grp"), "gy", None),
        P(None, "gx", "gy", "grp"),
        P("gx", "gy", "grp"),
        P(("gx", "grp"), "gy", None),
        P(),
        P(),
    )
    out_specs = (P(None, "gx", "gy", "grp"), P(None, ("gx", "grp"), "gy", None))

    def per_device(populations, thermal, *others):
        slab = Slab(mesh.shape, populations.shape[1:], thermal.shape[1:])
        plan = (lambda *arrays: on_slabs(slab, *arrays)) if slab.fits else on_device
        return plan(populations, thermal, *others)

    return jax.shard_map(
        per_device, mesh=mesh, in_specs=in_specs, out_specs=out_specs, check_vma=False
    )
```

```python
import jax
import jax.numpy as jnp
import numpy as np
from jax import lax
from jax.experimental import pallas as pl
from jax.experimental.pallas import tpu as pltpu
from jax.sharding import PartitionSpec as P

STEPS = 4
WINDOWS = 2


HIGHEST = lax.Precision.HIGHEST
BUOYANCY = 0.03
REFERENCE_HEAT = 1.0
OFFSET_TABLE = [(number // 9 - 1, number // 3 % 3 - 1, number % 3 - 1) for number in range(27)]
LATTICE_WEIGHTS = np.array(
    [
        np.prod([2.0 / 3.0 if component == 0 else 1.0 / 6.0 for component in triple])
        for triple in OFFSET_TABLE
    ]
)
VANDERMONDE = np.array([[1.0, 1.0, 1.0], [-1.0, 0.0, 1.0], [1.0, 0.0, 1.0]])
VANDER_INVERSE = np.array([[0.0, -0.5, 0.5], [1.0, 0.0, -1.0], [0.0, 0.5, 0.5]])
MOMENT_MATRIX = np.kron(np.kron(VANDERMONDE, VANDERMONDE), VANDERMONDE)
MOMENT_INVERSE = np.kron(np.kron(VANDER_INVERSE, VANDER_INVERSE), VANDER_INVERSE)
RELAXED = np.array([0.0 if number in (0, 1, 3, 9) else 1.0 for number in range(27)])
SUMMING = np.concatenate([np.ones((1, 27)), 1.0 * np.array(OFFSET_TABLE).T], axis=0)
HEAT_WEIGHTS = np.array([0.25] + [0.125] * 6)


def from_behind(value, axis, steps):
    count = lax.axis_size(axis)
    pairs = [(source, (source + steps) % count) for source in range(count)]
    return lax.ppermute(value, axis, pairs)


def extended(cells, sides, width):
    for axis, dim in sides:
        count = lax.axis_size(axis)
        head = lax.slice_in_dim(cells, 0, width, axis=dim)
        tail = lax.slice_in_dim(cells, cells.shape[dim] - width, cells.shape[dim], axis=dim)
        cells = jnp.concatenate(
            [
                lax.ppermute(tail, axis, [(i, (i + 1) % count) for i in range(count)]),
                cells,
                lax.ppermute(head, axis, [((i + 1) % count, i) for i in range(count)]),
            ],
            axis=dim,
        )
    return cells


def flow_state(flat, heat_flat):
    sums = jnp.dot(jnp.asarray(SUMMING, jnp.float32), flat, precision=HIGHEST)
    density = sums[0]
    force = BUOYANCY * (heat_flat - REFERENCE_HEAT)
    speed = jnp.stack([sums[1], sums[2], sums[3] + 0.5 * force]) / density
    return (density, force, speed)


def collide(popul, heat, rates):
    flat = popul.reshape(27, -1)
    density, force, speed = flow_state(flat, heat.reshape(-1))
    along = jnp.dot(jnp.asarray(SUMMING[1:].T, jnp.float32), speed, precision=HIGHEST)
    square = jnp.sum(speed * speed, axis=0)
    balance = (
        density
        * jnp.asarray(LATTICE_WEIGHTS, jnp.float32)[:, None]
        * (1.0 + 3.0 * along + 4.5 * along * along - 1.5 * square)
    )
    scaled = (
        jnp.asarray(MOMENT_INVERSE, jnp.float32)
        * (rates * jnp.asarray(RELAXED, jnp.float32))[None, :]
    )
    relax = jnp.dot(scaled, jnp.asarray(MOMENT_MATRIX, jnp.float32), precision=HIGHEST)
    post = (
        flat
        - jnp.dot(relax, flat - balance, precision=HIGHEST)
        + jnp.asarray(MOMENT_INVERSE[:, 1], jnp.float32)[:, None] * force[None, :]
    )
    return post.reshape(popul.shape)


def flow_speed(popul, heat, solid):
    density, force, speed = flow_state(popul.reshape(27, -1), heat.reshape(-1))
    return jnp.where(solid[None] == 0, speed.reshape((3,) + solid.shape), 0.0)


def heat_collide(heat_pops, speed, relax_time):
    total = jnp.sum(heat_pops, axis=0)
    still = jnp.zeros_like(speed[0])
    along = jnp.stack([still, speed[0], -speed[0], speed[1], -speed[1], speed[2], -speed[2]])
    balance = (
        jnp.asarray(HEAT_WEIGHTS, jnp.float32)[:, None, None, None]
        * total[None]
        * (1.0 + 4.0 * along)
    )
    return heat_pops - (heat_pops - balance) / relax_time[None]


def relaxation(phase_ids, conductivity):
    levels = jnp.arange(conductivity.shape[0], dtype=jnp.int32)
    chosen = jnp.sum(
        jnp.where(
            phase_ids[None] == levels[:, None, None, None], conductivity[:, None, None, None], 0.0
        ),
        axis=0,
    )
    return 0.5 + 4.0 * chosen


def inner_window(padded, triple, sizes):
    return padded[
        1 - triple[0] : 1 - triple[0] + sizes[0],
        1 - triple[1] : 1 - triple[1] + sizes[1],
        1 - triple[2] : 1 - triple[2] + sizes[2],
    ]


def advance(grid, axis_number, send_up, send_down):
    space = 3 + axis_number
    length = grid.shape[space]
    rising = lax.index_in_dim(grid, 2, axis_number, keepdims=True)
    resting = lax.index_in_dim(grid, 1, axis_number, keepdims=True)
    falling = lax.index_in_dim(grid, 0, axis_number, keepdims=True)
    from_below = send_up(lax.slice_in_dim(rising, length - 1, length, axis=space))
    from_above = send_down(lax.slice_in_dim(falling, 0, 1, axis=space))
    rising = jnp.concatenate(
        [from_below, lax.slice_in_dim(rising, 0, length - 1, axis=space)], axis=space
    )
    falling = jnp.concatenate(
        [lax.slice_in_dim(falling, 1, length, axis=space), from_above], axis=space
    )
    return jnp.concatenate([falling, resting, rising], axis=axis_number)


def flow_arrivals(post):
    sizes = post.shape[1:]
    grid = post.reshape((3, 3, 3) + sizes)
    grid = advance(
        grid,
        0,
        lambda plane: from_behind(plane, "gx", 1),
        lambda plane: from_behind(plane, "gx", -1),
    )
    grid = advance(
        grid,
        1,
        lambda plane: from_behind(plane, "gy", 1),
        lambda plane: from_behind(plane, "gy", -1),
    )
    grid = advance(
        grid,
        2,
        lambda plane: from_behind(plane, "grp", 1),
        lambda plane: from_behind(plane, "grp", -1),
    )
    return grid.reshape(post.shape)


def stream_heat(post, grp_index, last_grp):
    length = post.shape[1]
    size_y = post.shape[2]
    eastward = post[1]
    westward = post[2]
    lower_first = from_behind(eastward, "grp", 1)
    lower_second = from_behind(lower_first, "gx", 1)
    entering = jnp.where(grp_index == 0, lower_second, lower_first)
    eastward = jnp.concatenate([entering, eastward[: length - 1]], axis=0)
    upper_first = from_behind(westward, "grp", -1)
    upper_second = from_behind(upper_first, "gx", -1)
    entering = jnp.where(grp_index == last_grp, upper_second, upper_first)
    westward = jnp.concatenate([westward[1:], entering], axis=0)
    sides = extended(post[3:5], (("gy", 2),), 1)
    northward = sides[0, :, 0:size_y]
    southward = sides[1, :, 2 : size_y + 2]
    upward = jnp.roll(post[5], 1, axis=2)
    downward = jnp.roll(post[6], -1, axis=2)
    return jnp.stack([post[0], eastward, westward, northward, southward, upward, downward])


def on_device(populations, thermal, velocity_prev, solid, phase_ids, conductivity, rates):
    padded_solid = extended(solid, (("grp", 2), ("gx", 0), ("gy", 1)), 1)
    sizes = solid.shape
    blocked = jnp.stack(
        [inner_window(padded_solid, OFFSET_TABLE[number], sizes) != 0 for number in range(27)]
    )
    fluid_cells = (solid == 0)[None]
    grp_index = lax.axis_index("grp")
    last_grp = lax.axis_size("grp") - 1
    relax_time = relaxation(phase_ids, conductivity)
    speed_brick = velocity_prev
    popul = populations
    heat_pops = thermal
    for window_number in range(WINDOWS):
        heat_brick = lax.all_to_all(
            jnp.sum(heat_pops, axis=0), "grp", split_axis=2, concat_axis=0, tiled=True
        )
        speed_column = lax.all_to_all(speed_brick, "grp", split_axis=1, concat_axis=3, tiled=True)
        for step_number in range(STEPS):
            post = collide(popul, heat_brick, rates)
            arrived = flow_arrivals(post)
            popul = jnp.where(fluid_cells, jnp.where(blocked, post[::-1], arrived), popul)
        for step_number in range(STEPS):
            heat_pops = stream_heat(
                heat_collide(heat_pops, speed_column, relax_time), grp_index, last_grp
            )
        if window_number + 1 < WINDOWS:
            speed_brick = flow_speed(popul, heat_brick, solid)
    return (popul, heat_pops)


SUBLANES = 8
LANES = 128
F32 = jnp.float32


class Slab:
    def __init__(self, mesh_shape, flow_block, heat_block):
        self.grp, self.gx, self.gy = (mesh_shape[name] for name in ("grp", "gx", "gy"))
        self.block_x, self.block_y, self.block_z = flow_block
        self.sub = self.gx * self.gy
        self.planes = self.block_z // self.sub
        self.halo = self.planes // 2
        self.fits = (
            self.block_y == SUBLANES
            and self.block_z == LANES
            and self.planes * self.sub == LANES
            and self.halo * 2 == self.planes
            and self.halo == STEPS * WINDOWS
            and 2 * self.block_x == self.sub
            and self.block_x == self.grp
            and heat_block == (1, SUBLANES, self.grp * LANES)
            and self.sub & (self.sub - 1) == 0
            and self.grp & (self.grp - 1) == 0
            and self.gy % 2 == 0
            and self.sub % self.grp == 0
        )
        if self.fits:
            self.turn = self.sub // self.grp
            self.ring = [
                part * self.sub + self.round_plane((place - self.turn * part) % self.sub)
                for part in range(self.grp)
                for place in range(self.sub)
            ]

    def round_plane(self, number):
        x, y = number // self.gy, number % self.gy
        back = x % 2
        return x * self.gy + y + back * (self.gy - 1 - 2 * y)

    def holders(self):
        begin = self.sub * self.grp - self.turn * lax.axis_index("grp")
        mine = self.place_in_plane()
        return [
            jnp.bitwise_xor(self.round_plane(lax.rem(begin + place, self.sub)), mine)
            for place in range(self.sub)
        ]

    def place_in_plane(self):
        return lax.axis_index("gx") * self.gy + lax.axis_index("gy")


def lane_index():
    return lax.broadcasted_iota(jnp.int32, (SUBLANES, LANES), 1)


def row_index():
    return lax.broadcasted_iota(jnp.int32, (SUBLANES, LANES), 0)


def lane_roll(value, amount):
    amount = amount % LANES
    return value if amount == 0 else pltpu.roll(value, amount, 1)


def swap_groups(values, group):
    count = len(values)
    lane = lane_index()
    values = list(values)
    bit = 1
    while bit < count:
        low = (lane // (group * bit)) % 2 == 0
        for first in range(count):
            if first & bit == 0:
                a, b = values[first], values[first | bit]
                values[first] = jnp.where(low, a, lane_roll(b, group * bit))
                values[first | bit] = jnp.where(low, lane_roll(a, -group * bit), b)
        bit *= 2
    return values


SPEED_AT, SOLID_AT, HEAT_AT, RATE_AT, ROWS = 27, 30, 31, 38, 40
MOVING = 34


def moving_row(number):
    return number + (HEAT_AT - SPEED_AT) * (number >= SPEED_AT)


def offer_heat(slab, levels_hbm, heat_hbm, phase_hbm, *refs):
    outs, (levels_ref, heat_ref, phase_ref, sems) = refs[: slab.grp], refs[slab.grp :]
    copies = [
        pltpu.make_async_copy(heat_hbm, heat_ref, sems.at[0]),
        pltpu.make_async_copy(phase_hbm, phase_ref, sems.at[1]),
        pltpu.make_async_copy(levels_hbm, levels_ref, sems.at[2]),
    ]
    for copy in copies:
        copy.start()
    for copy in copies:
        copy.wait()
    mine = lax.axis_index("grp")
    for step in range(slab.grp):
        part = jnp.bitwise_xor(mine, step)
        span = pl.ds(pl.multiple_of(part * LANES, LANES), LANES)
        phase = phase_ref[0, :, span]
        chosen = jnp.zeros((SUBLANES, LANES), F32)
        for level in range(levels_ref.shape[0]):
            chosen = jnp.where(phase == level, levels_ref[level], chosen)
        for k in range(7):
            outs[step][k] = heat_ref[k, 0, :, span]
        outs[step][7] = 1.0 / (0.5 + 4.0 * chosen)


def for_each(count, body):
    for number in range(count):
        body(number)


def pack_flow(slab, popul_hbm, speed_hbm, solid_hbm, sent, flags, fields, solid_ref, sems):
    copies = [
        pltpu.make_async_copy(popul_hbm, fields.at[pl.ds(0, SPEED_AT)], sems.at[0]),
        pltpu.make_async_copy(speed_hbm, fields.at[pl.ds(SPEED_AT, 3)], sems.at[1]),
        pltpu.make_async_copy(solid_hbm, solid_ref, sems.at[2]),
    ]
    for copy in copies:
        copy.start()
    for copy in copies:
        copy.wait()
    holders = slab.holders()

    def one(pair):
        pack_pair(slab, fields, pair, sent, pair, holders)

    for_each(SOLID_AT // 2, one)
    flags[...] = solid_ref[...].astype(F32)


def pack_pair(slab, fields, source, sent, target, holders):
    sources = [fields[2 * source + h, x] for x in range(slab.block_x) for h in range(2)]
    for place, value in enumerate(swap_groups(sources, slab.planes)):
        sent[holders[place], target] = value


def pack_heat(slab, sent_in, flags, *refs):
    parts, (sent, held, packed, sem) = refs[: slab.grp], refs[slab.grp :]
    mine = lax.axis_index("grp")
    holders = slab.holders()
    held[0] = flags[...]
    held[9] = jnp.zeros(flags.shape, F32)
    for step in range(slab.grp):
        held[pl.ds(1, 8), jnp.bitwise_xor(mine, step)] = parts[step][...]
    first, count = SOLID_AT // 2, (ROWS - SOLID_AT) // 2

    def one(pair):
        pack_pair(slab, held, pair, packed, pair, holders)

    for_each(count, one)
    copy = pltpu.make_async_copy(packed, sent.at[:, pl.ds(first, count)], sem)
    copy.start()
    copy.wait()


def in_first_half(slab):
    return lane_index() % slab.planes < slab.halo


def collect(slab, parts, came):
    mine = slab.place_in_plane()
    for step in range(slab.sub):
        came[jnp.bitwise_xor(mine, step)] = parts[step][...]


def offer_halo(slab, *refs):
    parts, (came, low_out, high_out) = refs[: slab.sub], refs[slab.sub :]
    collect(slab, parts, came)

    def one(number, _):
        tile = 2 * number
        first = in_first_half(slab)
        for pair in range(ROWS // 2):
            a, b = came[tile, pair], came[tile + 1, pair]
            low_out[number, pair] = jnp.where(first, a, lane_roll(b, slab.halo))
            high_out[number, pair] = jnp.where(first, lane_roll(b, -slab.halo), a)
        return 0

    lax.fori_loop(0, slab.sub // 2, one, 0)


def make_tiles(slab, came, below_ref, above_ref, state):
    def one(number, _):
        first = in_first_half(slab)
        even = (lane_index() // slab.planes) % 2 == 0
        back = 2 * slab.planes
        for pair in range(ROWS // 2):
            below, above = below_ref[number, pair], above_ref[number, pair]
            beside = (
                jnp.where(first, above, lane_roll(below, -back)),
                jnp.where(first, lane_roll(above, -slab.halo), lane_roll(below, slab.halo - back)),
            )
            for which in range(2):
                tile = 2 * number + which
                own, halo = came[tile, pair], beside[which]
                state[2 * pair, tile] = jnp.where(even, own, lane_roll(halo, slab.planes))
                state[2 * pair + 1, tile] = jnp.where(even, lane_roll(own, -slab.planes), halo)
        return 0

    lax.fori_loop(0, slab.sub // 2, one, 0)


def pack_out(slab, came, state, sent):
    def one(tile, _):
        even = (lane_index() // slab.planes) % 2 == 0
        partner = jnp.bitwise_xor(tile, slab.place_in_plane())
        flags = came[tile, SOLID_AT // 2]
        solid = jnp.where(even, flags, lane_roll(flags, slab.planes)) != 0.0
        for pair in range(MOVING // 2):
            first, second = (state[moving_row(2 * pair + h), tile] for h in range(2))
            value = jnp.where(even, first, lane_roll(second, slab.planes))
            if 2 * pair + 1 < SPEED_AT:
                value = jnp.where(solid, came[tile, pair], value)
            elif 2 * pair < SPEED_AT:
                value = jnp.where(jnp.logical_and(solid, even), came[tile, pair], value)
            sent[partner, pair] = value
        return 0

    lax.fori_loop(0, slab.sub, one, 0)


def unpack_pair(slab, came, pair, holders):
    sources = [came[holders[place], pair] for place in range(slab.sub)]
    values = swap_groups(sources, slab.planes)
    return [values[0::2], values[1::2]]


def return_heat(slab, *refs):
    parts, came, outs, held = (
        refs[: slab.sub],
        refs[slab.sub],
        refs[slab.sub + 1 : slab.sub + 1 + slab.grp],
        refs[-1],
    )
    for step in range(slab.sub):
        came[step] = parts[step][...]
    holders = slab.holders()
    _, values = unpack_pair(slab, came, SPEED_AT // 2, holders)
    for x in range(slab.block_x):
        held[x, 0] = values[x]

    def one(pair):
        for h, values in enumerate(unpack_pair(slab, came, SPEED_AT // 2 + 1 + pair, holders)):
            for x in range(slab.block_x):
                held[x, 2 * pair + 1 + h] = values[x]

    for_each(3, one)
    mine = lax.axis_index("grp")
    for step in range(slab.grp):
        outs[step][...] = held[jnp.bitwise_xor(mine, step)]


def unpack_flow(slab, came, popul_out):
    holders = slab.holders()

    def one(pair):
        for h, values in enumerate(unpack_pair(slab, came, pair, holders)):
            for x in range(slab.block_x):
                popul_out[2 * pair + h, x] = values[x]

    for_each(SPEED_AT // 2, one)
    values, _ = unpack_pair(slab, came, SPEED_AT // 2, holders)
    for x in range(slab.block_x):
        popul_out[SPEED_AT - 1, x] = values[x]


def join_heat(slab, *refs):
    parts, thermal_out = refs[: slab.grp], refs[slab.grp]
    mine = lax.axis_index("grp")
    for step in range(slab.grp):
        part = jnp.bitwise_xor(mine, step)
        span = pl.ds(pl.multiple_of(part * LANES, LANES), LANES)
        for k in range(7):
            thermal_out[k, 0, :, span] = parts[step][k]


def forward3(values):
    for stride in (9, 3, 1):
        out = [None] * 27
        for n in range(27):
            if n // stride % 3 == 0:
                a, b, c = values[n], values[n + stride], values[n + 2 * stride]
                both = a + c
                out[n], out[n + stride], out[n + 2 * stride] = both + b, c - a, both
        values = out
    return values


def backward3(values):
    for stride in (9, 3, 1):
        out = [None] * 27
        for n in range(27):
            if n // stride % 3 == 0:
                a, b, c = values[n], values[n + stride], values[n + 2 * stride]
                even, odd = 0.5 * c, 0.5 * b
                out[n], out[n + stride], out[n + 2 * stride] = even - odd, a - c, even + odd
        values = out
    return values


def collide_tile(values, force, rate):
    moments = forward3(values)
    density = moments[0]
    jx, jy, jz = moments[9], moments[3], moments[1] + 0.5 * force
    inverse = 1.0 / density
    flux = (jx, jy, jz)
    u = tuple(j * inverse for j in flux)
    third = 1.0 / 3.0
    base = {0: density}
    for k in (1, 2, 3):
        base[k] = density * third**k
    squares = [flux[d] * u[d] for d in range(3)]
    square_at = {}
    scaled = {}

    def scale(key, value, count):
        if count == 0:
            return value
        if (key, count) not in scaled:
            scaled[key, count] = value * third**count
        return scaled[key, count]

    cross = {(0, 1): jx * u[1], (0, 2): jx * u[2], (1, 2): jy * u[2]}
    out = [None] * 27
    for n in range(27):
        powers = (n // 9, n // 3 % 3, n % 3)
        if n in (0, 3, 9):
            out[n] = moments[n]
            continue
        if n == 1:
            out[n] = moments[n] + force
            continue
        odd = tuple(d for d in range(3) if powers[d] == 1)
        even = tuple(d for d in range(3) if powers[d] == 2)
        count = len(even)
        if len(odd) == 3:
            out[n] = moments[n] - rate(n) * moments[n]
            continue
        if len(odd) == 0:
            if even not in square_at:
                total = squares[even[0]]
                for d in even[1:]:
                    total = total + squares[d]
                square_at[even] = base[count] + (total * (3.0 * third**count) if count > 1 else total)
            level = square_at[even]
        elif len(odd) == 1:
            level = scale(odd, flux[odd[0]], count)
        else:
            level = scale(odd, cross[odd], count)
        out[n] = moments[n] - rate(n) * (moments[n] - level)
    return backward3(out)


HEAT_OFFSETS = [(0, 0, 0), (1, 0, 0), (-1, 0, 0), (0, 1, 0), (0, -1, 0), (0, 0, 1), (0, 0, -1)]


class Lattices:
    def __init__(self, slab, rates_ref, state, post, force_ref):
        self.slab, self.rates_ref = slab, rates_ref
        self.state, self.post, self.force_ref = state, post, force_ref

    def speeds(self, tile):
        return [self.state[SPEED_AT + d, tile] for d in range(3)]

    def held(self, tile):
        flow = [self.state[n, tile] for n in range(27)]
        return flow, [self.state[HEAT_AT + k, tile] for k in range(7)]

    def collide(self, tile, flow, heat, force, speeds, target):
        state, post = self.state, self.post
        solid = state[SOLID_AT, tile] != 0.0
        moved = collide_tile(flow, force, lambda n: self.rates_ref[n])
        for n in range(27):
            post[target, n, tile] = jnp.where(solid, jnp.nan, moved[n])
        total = heat[0]
        for k in range(1, 7):
            total = total + heat[k]
        omega = state[RATE_AT, tile]
        side = 0.125 * total
        half = 0.5 * total
        for k in range(7):
            if k == 0:
                level = 0.25 * total
            else:
                drift = half * speeds[(k - 1) // 2]
                level = side + drift if k % 2 == 1 else side - drift
            post[target, SPEED_AT + k, tile] = heat[k] - (heat[k] - level) * omega

    def stream(self, tile, source):
        slab, post = self.slab, self.post
        block_x, block_y = tile // slab.gy, tile % slab.gy
        x_of = {a: lax.rem(block_x + slab.gx - a, slab.gx) for a in (-1, 0, 1)}
        y_of = {b: lax.rem(block_y + slab.gy - b, slab.gy) for b in (-1, 0, 1)}
        row = row_index()
        per_x = 2 * slab.planes
        in_x = (lane_index() + slab.halo) % LANES // per_x
        last_x = {1: in_x == slab.block_x - 1, -1: in_x == 0}
        last_y = {1: row == SUBLANES - 1, -1: row == 0}

        def arrive(number, offset):
            a, b, c = offset

            def take(x):
                value = post[source, number, x_of[x] * slab.gy + block_y]
                if b != 0:
                    other = post[source, number, x_of[x] * slab.gy + y_of[b]]
                    value = jnp.where(last_y[b], other, value)
                return value

            value = take(0)
            if a != 0:
                value = jnp.where(last_x[a], take(a), value)
            if b != 0:
                value = pltpu.roll(value, b % SUBLANES, 0)
            return lane_roll(value, a * per_x + c)

        flow = []
        for n in range(27):
            value = arrive(n, OFFSET_TABLE[n])
            flow.append(jnp.where(value != value, post[source, 26 - n, tile], value))
        return flow, [arrive(SPEED_AT + k, HEAT_OFFSETS[k]) for k in range(7)]


def run_windows(slab, rates_ref, state, post, force_ref):
    lattices = Lattices(slab, rates_ref, state, post, force_ref)

    def over_tiles(body):
        def one(tile, _):
            body(tile)
            return 0

        lax.fori_loop(0, slab.sub, one, 0)

    def begin(tile):
        flow, heat = lattices.held(tile)
        force = heat_force(heat)
        force_ref[tile] = force
        lattices.collide(tile, flow, heat, force, lattices.speeds(tile), 0)

    over_tiles(begin)

    def one_window(window, _):
        def step(number, _):
            source = lax.rem(window * STEPS + number, 2)

            def go_on(tile):
                flow, heat = lattices.stream(tile, source)
                lattices.collide(
                    tile, flow, heat, force_ref[tile], lattices.speeds(tile), 1 - source
                )

            over_tiles(go_on)
            return 0

        lax.fori_loop(0, STEPS - 1, step, 0)
        source = lax.rem(window * STEPS + STEPS - 1, 2)

        @pl.when(window + 1 < WINDOWS)
        def _():
            def next_window(tile):
                flow, heat = lattices.stream(tile, source)
                solid = state[SOLID_AT, tile] != 0.0
                speeds = [
                    jnp.where(solid, 0.0, each) for each in flow_speed_tile(flow, force_ref[tile])
                ]
                for d in range(3):
                    state[SPEED_AT + d, tile] = speeds[d]
                force = heat_force(heat)
                force_ref[tile] = force
                lattices.collide(tile, flow, heat, force, speeds, 1 - source)

            over_tiles(next_window)

        @pl.when(window + 1 == WINDOWS)
        def _():
            def end(tile):
                flow, heat = lattices.stream(tile, source)
                for n in range(27):
                    state[n, tile] = flow[n]
                for k in range(7):
                    state[HEAT_AT + k, tile] = heat[k]

            over_tiles(end)

        return 0

    lax.fori_loop(0, WINDOWS, one_window, 0)


def heat_force(heat):
    total = heat[0]
    for k in range(1, 7):
        total = total + heat[k]
    return BUOYANCY * (total - REFERENCE_HEAT)


def flow_speed_tile(values, force):
    total = values[0]
    for n in range(1, 27):
        total = total + values[n]
    sums = []
    for d in range(3):
        plus, minus = None, None
        for n in range(27):
            part = OFFSET_TABLE[n][d]
            if part == 1:
                plus = values[n] if plus is None else plus + values[n]
            if part == -1:
                minus = values[n] if minus is None else minus + values[n]
        sums.append(plus - minus)
    sums[2] = sums[2] + 0.5 * force
    return [each / total for each in sums]


def both_windows(slab, rates_hbm, came, below_ref, above_ref, *refs):
    sent, rates_ref, sem, state, post, force = refs
    rates_copy = pltpu.make_async_copy(rates_hbm, rates_ref, sem)
    rates_copy.start()
    make_tiles(slab, came, below_ref, above_ref, state)
    rates_copy.wait()
    run_windows(slab, rates_ref, state, post, force)
    pack_out(slab, came, state, sent)


def local_call(body, slab, arrays, outs, scratch=(), in_hbm=0, carried=False):
    def kernel(*refs):
        body(slab, *refs)

    return pl.pallas_call(
        kernel,
        out_shape=[jax.ShapeDtypeStruct(shape, F32) for shape in outs],
        in_specs=[
            pl.BlockSpec(
                memory_space=pltpu.HBM if i < in_hbm else pl.ANY if carried and i == 0 else pltpu.VMEM
            )
            for i in range(len(arrays))
        ],
        out_specs=[pl.BlockSpec(memory_space=pl.ANY if carried else pltpu.VMEM)] * len(outs),
        input_output_aliases={0: 0} if carried else {},
        scratch_shapes=[pltpu.VMEM(s, F32) if isinstance(s, tuple) else s for s in scratch],
        compiler_params=pltpu.CompilerParams(vmem_limit_bytes=24 * 1024 * 1024),
    )(
        *(
            pltpu.with_memory_space_constraint(array, pltpu.HBM) if i < in_hbm else array
            for i, array in enumerate(arrays)
        )
    )


RING = ("grp", "gx", "gy")


def exchange(slab, low, high):
    ring = slab.ring
    upward = [(ring[i - 1], ring[i]) for i in range(len(ring))]
    from_below = lax.ppermute(high, RING, upward)
    from_above = lax.ppermute(low, RING, [(b, a) for a, b in upward])
    return from_below, from_above


def across_plane(slab, sent):
    came = {0: sent[0]}
    far_first = [step for k in range(2) for step in range(2 + k, slab.sub, 2)] + [1]
    far_first.sort(key=lambda step: -bin(step >> 1).count("1"))
    for step in far_first:
        pairs = [(i, i ^ step) for i in range(slab.sub)]
        came[step] = lax.ppermute(sent[step], ("gx", "gy"), pairs)
    return [came[step] for step in range(slab.sub)]


def across_planes(slab, parts):
    return [parts[0]] + [
        lax.ppermute(parts[step], "grp", [(i, i ^ step) for i in range(slab.grp)])
        for step in range(1, slab.grp)
    ]


def on_slabs(slab, populations, thermal, velocity_prev, solid, phase_ids, conductivity, rates):
    tile = (SUBLANES, LANES)

    def vmem_like(array):
        return pltpu.VMEM(array.shape, array.dtype)

    parts = local_call(
        offer_heat,
        slab,
        [conductivity, thermal, phase_ids],
        [(8,) + tile] * slab.grp,
        [
            pltpu.SMEM(conductivity.shape, F32),
            vmem_like(thermal),
            vmem_like(phase_ids),
            pltpu.SemaphoreType.DMA((3,)),
        ],
        in_hbm=3,
    )
    parts = across_planes(slab, parts)
    sent_shape = (slab.sub, ROWS // 2) + tile
    sent, flags = local_call(
        pack_flow,
        slab,
        [populations, velocity_prev, solid],
        [sent_shape, solid.shape],
        [
            (SOLID_AT,) + solid.shape,
            pltpu.VMEM(solid.shape, solid.dtype),
            pltpu.SemaphoreType.DMA((3,)),
        ],
        in_hbm=3,
    )
    (sent,) = local_call(
        pack_heat,
        slab,
        [sent, flags] + parts,
        [sent_shape],
        [
            (ROWS - SOLID_AT,) + solid.shape,
            (slab.sub, (ROWS - SOLID_AT) // 2) + tile,
            pltpu.SemaphoreType.DMA,
        ],
        carried=True,
    )
    halo_shape = (slab.sub // 2, ROWS // 2) + tile
    came, low, high = local_call(
        offer_halo, slab, across_plane(slab, sent), [sent_shape, halo_shape, halo_shape]
    )
    below, above = exchange(slab, low, high)
    (sent,) = local_call(
        both_windows,
        slab,
        [rates, came, below, above],
        [(slab.sub, MOVING // 2) + tile],
        [
            pltpu.SMEM(rates.shape, F32),
            pltpu.SemaphoreType.DMA,
            (ROWS, slab.sub) + tile,
            (2, MOVING, slab.sub) + tile,
            (slab.sub,) + tile,
        ],
        in_hbm=1,
    )
    came, *parts = local_call(
        return_heat,
        slab,
        across_plane(slab, sent),
        [sent.shape] + [(7,) + tile] * slab.grp,
        [(slab.grp, 7) + tile],
    )
    parts = across_planes(slab, parts)
    (populations_out,) = local_call(unpack_flow, slab, [came], [populations.shape])
    (thermal_out,) = local_call(join_heat, slab, parts, [thermal.shape])
    return populations_out, thermal_out


def solution(mesh):
    in_specs = (
        P(None, "gx", "gy", "grp"),
        P(None, ("gx", "grp"), "gy", None),
        P(None, "gx", "gy", "grp"),
        P("gx", "gy", "grp"),
        P(("gx", "grp"), "gy", None),
        P(),
        P(),
    )
    out_specs = (P(None, "gx", "gy", "grp"), P(None, ("gx", "grp"), "gy", None))

    def per_device(populations, thermal, *others):
        slab = Slab(mesh.shape, populations.shape[1:], thermal.shape[1:])
        plan = (lambda *arrays: on_slabs(slab, *arrays)) if slab.fits else on_device
        return plan(populations, thermal, *others)

    return jax.shard_map(
        per_device, mesh=mesh, in_specs=in_specs, out_specs=out_specs, check_vma=False
    )
```

```python
import jax
import jax.numpy as jnp
import numpy as np
from jax import lax
from jax.experimental import pallas as pl
from jax.experimental.pallas import tpu as pltpu
from jax.sharding import PartitionSpec as P

STEPS = 4
WINDOWS = 2


HIGHEST = lax.Precision.HIGHEST
BUOYANCY = 0.03
REFERENCE_HEAT = 1.0
OFFSET_TABLE = [(number // 9 - 1, number // 3 % 3 - 1, number % 3 - 1) for number in range(27)]
LATTICE_WEIGHTS = np.array(
    [
        np.prod([2.0 / 3.0 if component == 0 else 1.0 / 6.0 for component in triple])
        for triple in OFFSET_TABLE
    ]
)
VANDERMONDE = np.array([[1.0, 1.0, 1.0], [-1.0, 0.0, 1.0], [1.0, 0.0, 1.0]])
VANDER_INVERSE = np.array([[0.0, -0.5, 0.5], [1.0, 0.0, -1.0], [0.0, 0.5, 0.5]])
MOMENT_MATRIX = np.kron(np.kron(VANDERMONDE, VANDERMONDE), VANDERMONDE)
MOMENT_INVERSE = np.kron(np.kron(VANDER_INVERSE, VANDER_INVERSE), VANDER_INVERSE)
RELAXED = np.array([0.0 if number in (0, 1, 3, 9) else 1.0 for number in range(27)])
SUMMING = np.concatenate([np.ones((1, 27)), 1.0 * np.array(OFFSET_TABLE).T], axis=0)
HEAT_WEIGHTS = np.array([0.25] + [0.125] * 6)


def from_behind(value, axis, steps):
    count = lax.axis_size(axis)
    pairs = [(source, (source + steps) % count) for source in range(count)]
    return lax.ppermute(value, axis, pairs)


def extended(cells, sides, width):
    for axis, dim in sides:
        count = lax.axis_size(axis)
        head = lax.slice_in_dim(cells, 0, width, axis=dim)
        tail = lax.slice_in_dim(cells, cells.shape[dim] - width, cells.shape[dim], axis=dim)
        cells = jnp.concatenate(
            [
                lax.ppermute(tail, axis, [(i, (i + 1) % count) for i in range(count)]),
                cells,
                lax.ppermute(head, axis, [((i + 1) % count, i) for i in range(count)]),
            ],
            axis=dim,
        )
    return cells


def flow_state(flat, heat_flat):
    sums = jnp.dot(jnp.asarray(SUMMING, jnp.float32), flat, precision=HIGHEST)
    density = sums[0]
    force = BUOYANCY * (heat_flat - REFERENCE_HEAT)
    speed = jnp.stack([sums[1], sums[2], sums[3] + 0.5 * force]) / density
    return (density, force, speed)


def collide(popul, heat, rates):
    flat = popul.reshape(27, -1)
    density, force, speed = flow_state(flat, heat.reshape(-1))
    along = jnp.dot(jnp.asarray(SUMMING[1:].T, jnp.float32), speed, precision=HIGHEST)
    square = jnp.sum(speed * speed, axis=0)
    balance = (
        density
        * jnp.asarray(LATTICE_WEIGHTS, jnp.float32)[:, None]
        * (1.0 + 3.0 * along + 4.5 * along * along - 1.5 * square)
    )
    scaled = (
        jnp.asarray(MOMENT_INVERSE, jnp.float32)
        * (rates * jnp.asarray(RELAXED, jnp.float32))[None, :]
    )
    relax = jnp.dot(scaled, jnp.asarray(MOMENT_MATRIX, jnp.float32), precision=HIGHEST)
    post = (
        flat
        - jnp.dot(relax, flat - balance, precision=HIGHEST)
        + jnp.asarray(MOMENT_INVERSE[:, 1], jnp.float32)[:, None] * force[None, :]
    )
    return post.reshape(popul.shape)


def flow_speed(popul, heat, solid):
    density, force, speed = flow_state(popul.reshape(27, -1), heat.reshape(-1))
    return jnp.where(solid[None] == 0, speed.reshape((3,) + solid.shape), 0.0)


def heat_collide(heat_pops, speed, relax_time):
    total = jnp.sum(heat_pops, axis=0)
    still = jnp.zeros_like(speed[0])
    along = jnp.stack([still, speed[0], -speed[0], speed[1], -speed[1], speed[2], -speed[2]])
    balance = (
        jnp.asarray(HEAT_WEIGHTS, jnp.float32)[:, None, None, None]
        * total[None]
        * (1.0 + 4.0 * along)
    )
    return heat_pops - (heat_pops - balance) / relax_time[None]


def relaxation(phase_ids, conductivity):
    levels = jnp.arange(conductivity.shape[0], dtype=jnp.int32)
    chosen = jnp.sum(
        jnp.where(
            phase_ids[None] == levels[:, None, None, None], conductivity[:, None, None, None], 0.0
        ),
        axis=0,
    )
    return 0.5 + 4.0 * chosen


def inner_window(padded, triple, sizes):
    return padded[
        1 - triple[0] : 1 - triple[0] + sizes[0],
        1 - triple[1] : 1 - triple[1] + sizes[1],
        1 - triple[2] : 1 - triple[2] + sizes[2],
    ]


def advance(grid, axis_number, send_up, send_down):
    space = 3 + axis_number
    length = grid.shape[space]
    rising = lax.index_in_dim(grid, 2, axis_number, keepdims=True)
    resting = lax.index_in_dim(grid, 1, axis_number, keepdims=True)
    falling = lax.index_in_dim(grid, 0, axis_number, keepdims=True)
    from_below = send_up(lax.slice_in_dim(rising, length - 1, length, axis=space))
    from_above = send_down(lax.slice_in_dim(falling, 0, 1, axis=space))
    rising = jnp.concatenate(
        [from_below, lax.slice_in_dim(rising, 0, length - 1, axis=space)], axis=space
    )
    falling = jnp.concatenate(
        [lax.slice_in_dim(falling, 1, length, axis=space), from_above], axis=space
    )
    return jnp.concatenate([falling, resting, rising], axis=axis_number)


def flow_arrivals(post):
    sizes = post.shape[1:]
    grid = post.reshape((3, 3, 3) + sizes)
    grid = advance(
        grid,
        0,
        lambda plane: from_behind(plane, "gx", 1),
        lambda plane: from_behind(plane, "gx", -1),
    )
    grid = advance(
        grid,
        1,
        lambda plane: from_behind(plane, "gy", 1),
        lambda plane: from_behind(plane, "gy", -1),
    )
    grid = advance(
        grid,
        2,
        lambda plane: from_behind(plane, "grp", 1),
        lambda plane: from_behind(plane, "grp", -1),
    )
    return grid.reshape(post.shape)


def stream_heat(post, grp_index, last_grp):
    length = post.shape[1]
    size_y = post.shape[2]
    eastward = post[1]
    westward = post[2]
    lower_first = from_behind(eastward, "grp", 1)
    lower_second = from_behind(lower_first, "gx", 1)
    entering = jnp.where(grp_index == 0, lower_second, lower_first)
    eastward = jnp.concatenate([entering, eastward[: length - 1]], axis=0)
    upper_first = from_behind(westward, "grp", -1)
    upper_second = from_behind(upper_first, "gx", -1)
    entering = jnp.where(grp_index == last_grp, upper_second, upper_first)
    westward = jnp.concatenate([westward[1:], entering], axis=0)
    sides = extended(post[3:5], (("gy", 2),), 1)
    northward = sides[0, :, 0:size_y]
    southward = sides[1, :, 2 : size_y + 2]
    upward = jnp.roll(post[5], 1, axis=2)
    downward = jnp.roll(post[6], -1, axis=2)
    return jnp.stack([post[0], eastward, westward, northward, southward, upward, downward])


def on_device(populations, thermal, velocity_prev, solid, phase_ids, conductivity, rates):
    padded_solid = extended(solid, (("grp", 2), ("gx", 0), ("gy", 1)), 1)
    sizes = solid.shape
    blocked = jnp.stack(
        [inner_window(padded_solid, OFFSET_TABLE[number], sizes) != 0 for number in range(27)]
    )
    fluid_cells = (solid == 0)[None]
    grp_index = lax.axis_index("grp")
    last_grp = lax.axis_size("grp") - 1
    relax_time = relaxation(phase_ids, conductivity)
    speed_brick = velocity_prev
    popul = populations
    heat_pops = thermal
    for window_number in range(WINDOWS):
        heat_brick = lax.all_to_all(
            jnp.sum(heat_pops, axis=0), "grp", split_axis=2, concat_axis=0, tiled=True
        )
        speed_column = lax.all_to_all(speed_brick, "grp", split_axis=1, concat_axis=3, tiled=True)
        for step_number in range(STEPS):
            post = collide(popul, heat_brick, rates)
            arrived = flow_arrivals(post)
            popul = jnp.where(fluid_cells, jnp.where(blocked, post[::-1], arrived), popul)
        for step_number in range(STEPS):
            heat_pops = stream_heat(
                heat_collide(heat_pops, speed_column, relax_time), grp_index, last_grp
            )
        if window_number + 1 < WINDOWS:
            speed_brick = flow_speed(popul, heat_brick, solid)
    return (popul, heat_pops)


SUBLANES = 8
LANES = 128
F32 = jnp.float32


class Slab:
    def __init__(self, mesh_shape, flow_block, heat_block):
        self.grp, self.gx, self.gy = (mesh_shape[name] for name in ("grp", "gx", "gy"))
        self.block_x, self.block_y, self.block_z = flow_block
        self.sub = self.gx * self.gy
        self.planes = self.block_z // self.sub
        self.halo = self.planes // 2
        self.fits = (
            self.block_y == SUBLANES
            and self.block_z == LANES
            and self.planes * self.sub == LANES
            and self.halo * 2 == self.planes
            and WINDOWS == 2
            and self.halo == STEPS * WINDOWS
            and self.sub >= 8
            and 2 * self.block_x == self.sub
            and self.block_x == self.grp
            and heat_block == (1, SUBLANES, self.grp * LANES)
            and self.sub & (self.sub - 1) == 0
            and self.grp & (self.grp - 1) == 0
            and self.gy % 2 == 0
            and self.sub % self.grp == 0
        )
        if self.fits:
            self.turn = self.sub // self.grp
            self.ring = [
                part * self.sub + self.round_plane((place - self.turn * part) % self.sub)
                for part in range(self.grp)
                for place in range(self.sub)
            ]

    def round_plane(self, number):
        x, y = number // self.gy, number % self.gy
        back = x % 2
        return x * self.gy + y + back * (self.gy - 1 - 2 * y)

    def holders(self, part):
        begin = self.sub * self.grp - self.turn * part
        mine = self.place_in_plane()
        return [
            jnp.bitwise_xor(self.round_plane(lax.rem(begin + place, self.sub)), mine)
            for place in range(self.sub)
        ]

    def place_in_plane(self):
        return lax.axis_index("gx") * self.gy + lax.axis_index("gy")


def lane_index():
    return lax.broadcasted_iota(jnp.int32, (SUBLANES, LANES), 1)


def row_index():
    return lax.broadcasted_iota(jnp.int32, (SUBLANES, LANES), 0)


def lane_roll(value, amount):
    amount = amount % LANES
    return value if amount == 0 else pltpu.roll(value, amount, 1)


def swap_groups(values, group):
    count = len(values)
    lane = lane_index()
    values = list(values)
    bit = 1
    while bit < count:
        low = (lane // (group * bit)) % 2 == 0
        for first in range(count):
            if first & bit == 0:
                a, b = values[first], values[first | bit]
                values[first] = jnp.where(low, a, lane_roll(b, group * bit))
                values[first | bit] = jnp.where(low, lane_roll(a, -group * bit), b)
        bit *= 2
    return values


SPEED_AT, SOLID_AT, HEAT_AT, RATE_AT, ROWS = 27, 30, 31, 38, 40
FLOW_PAIRS = 14


def offer_heat(slab, levels_hbm, heat_hbm, phase_hbm, *refs):
    outs, (levels_ref, heat_ref, phase_ref, sems) = refs[: slab.grp], refs[slab.grp :]
    copies = [
        pltpu.make_async_copy(heat_hbm, heat_ref, sems.at[0]),
        pltpu.make_async_copy(phase_hbm, phase_ref, sems.at[1]),
        pltpu.make_async_copy(levels_hbm, levels_ref, sems.at[2]),
    ]
    for copy in copies:
        copy.start()
    for copy in copies:
        copy.wait()
    mine = lax.axis_index("grp")
    for step in range(slab.grp):
        part = jnp.bitwise_xor(mine, step)
        span = pl.ds(pl.multiple_of(part * LANES, LANES), LANES)
        phase = phase_ref[0, :, span]
        chosen = jnp.zeros((SUBLANES, LANES), F32)
        for level in range(levels_ref.shape[0]):
            chosen = jnp.where(phase == level, levels_ref[level], chosen)
        for k in range(7):
            outs[step][k] = heat_ref[k, 0, :, span]
        outs[step][7] = 1.0 / (0.5 + 4.0 * chosen)


def for_each(count, body):
    for number in range(count):
        body(number)


def pack_flow(slab, popul_hbm, speed_hbm, solid_hbm, sent, flags, fields, solid_ref, sems):
    copies = [
        pltpu.make_async_copy(popul_hbm, fields.at[pl.ds(0, SPEED_AT)], sems.at[0]),
        pltpu.make_async_copy(speed_hbm, fields.at[pl.ds(SPEED_AT, 3)], sems.at[1]),
        pltpu.make_async_copy(solid_hbm, solid_ref, sems.at[2]),
    ]
    for copy in copies:
        copy.start()
    for copy in copies:
        copy.wait()
    holders = slab.holders(lax.axis_index("grp"))

    def one(pair):
        pack_pair(slab, fields, pair, sent, pair, holders)

    for_each(SOLID_AT // 2, one)
    flags[...] = solid_ref[...].astype(F32)


def pack_pair(slab, fields, source, sent, target, holders):
    sources = [fields[2 * source + h, x] for x in range(slab.block_x) for h in range(2)]
    for place, value in enumerate(swap_groups(sources, slab.planes)):
        sent[holders[place], target] = value


def pack_heat(slab, sent_in, flags, *refs):
    parts, (sent, held, packed, sem) = refs[: slab.grp], refs[slab.grp :]
    mine = lax.axis_index("grp")
    holders = slab.holders(lax.axis_index("grp"))
    held[0] = flags[...]
    held[9] = jnp.zeros(flags.shape, F32)
    for step in range(slab.grp):
        held[pl.ds(1, 8), jnp.bitwise_xor(mine, step)] = parts[step][...]
    first, count = SOLID_AT // 2, (ROWS - SOLID_AT) // 2

    def one(pair):
        pack_pair(slab, held, pair, packed, pair, holders)

    for_each(count, one)
    copy = pltpu.make_async_copy(packed, sent.at[:, pl.ds(first, count)], sem)
    copy.start()
    copy.wait()


def in_first_half(slab):
    return lane_index() % slab.planes < slab.halo


def collect(slab, parts, came):
    mine = slab.place_in_plane()
    for step in range(slab.sub):
        came[jnp.bitwise_xor(mine, step)] = parts[step][...]


def offer_halo(slab, *refs):
    parts, (came, low_out, high_out) = refs[: slab.sub], refs[slab.sub :]
    collect(slab, parts, came)

    def one(number, _):
        tile = 2 * number
        first = in_first_half(slab)
        for pair in range(ROWS // 2):
            a, b = came[tile, pair], came[tile + 1, pair]
            low_out[number, pair] = jnp.where(first, a, lane_roll(b, slab.halo))
            high_out[number, pair] = jnp.where(first, lane_roll(b, -slab.halo), a)
        return 0

    lax.fori_loop(0, slab.sub // 2, one, 0)


def make_tiles(slab, came, below_ref, above_ref, state):
    def one(number, _):
        first = in_first_half(slab)
        even = (lane_index() // slab.planes) % 2 == 0
        back = 2 * slab.planes
        for pair in range(ROWS // 2):
            below, above = below_ref[number, pair], above_ref[number, pair]
            beside = (
                jnp.where(first, above, lane_roll(below, -back)),
                jnp.where(first, lane_roll(above, -slab.halo), lane_roll(below, slab.halo - back)),
            )
            for which in range(2):
                tile = 2 * number + which
                own, halo = came[tile, pair], beside[which]
                state[2 * pair, tile] = jnp.where(even, own, lane_roll(halo, slab.planes))
                state[2 * pair + 1, tile] = jnp.where(even, lane_roll(own, -slab.planes), halo)
        return 0

    lax.fori_loop(0, slab.sub // 2, one, 0)


def pack_out(slab, flow, came, tile, sent):
    even = (lane_index() // slab.planes) % 2 == 0
    flags = came[tile, SOLID_AT // 2]
    solid = jnp.where(even, flags, lane_roll(flags, slab.planes)) != 0.0
    partner = jnp.bitwise_xor(tile, slab.place_in_plane())
    for pair in range(FLOW_PAIRS):
        value = flow[2 * pair]
        if 2 * pair + 1 < len(flow):
            value = jnp.where(even, value, lane_roll(flow[2 * pair + 1], slab.planes))
        sent[partner, pair] = jnp.where(solid, came[tile, pair], value)


def add_heat(slab, sent_in, *refs):
    parts, (sent, packed, sem) = refs[: slab.grp], refs[slab.grp :]
    mine = slab.place_in_plane()
    for tile in range(slab.sub):
        for step in range(slab.grp):
            packed[jnp.bitwise_xor(mine, tile), step] = parts[step][tile]
    copy = pltpu.make_async_copy(packed, sent.at[:, pl.ds(FLOW_PAIRS, slab.grp)], sem)
    copy.start()
    copy.wait()


def unpack_out(slab, *refs):
    parts, (popul_out, thermal_out, came) = refs[: slab.sub], refs[slab.sub :]
    for step in range(slab.sub):
        came[step] = parts[step][...]
    mine = lax.axis_index("grp")
    holders = slab.holders(mine)
    for pair in range(FLOW_PAIRS):
        sources = [came[holders[place], pair] for place in range(slab.sub)]
        for number, value in enumerate(swap_groups(sources, slab.planes)):
            if 2 * pair + number % 2 < 27:
                popul_out[2 * pair + number % 2, number // 2] = value
    for step in range(slab.grp):
        part = jnp.bitwise_xor(mine, step)
        holders = slab.holders(part)
        span = pl.ds(pl.multiple_of(part * LANES, LANES), LANES)
        sources = [came[holders[place], FLOW_PAIRS + step] for place in range(slab.sub)]
        for k, value in enumerate(swap_groups(sources, slab.planes)[:7]):
            thermal_out[k, 0, :, span] = value


def forward3(values):
    for stride in (9, 3, 1):
        out = [None] * 27
        for n in range(27):
            if n // stride % 3 == 0:
                a, b, c = values[n], values[n + stride], values[n + 2 * stride]
                both = a + c
                out[n], out[n + stride], out[n + 2 * stride] = both + b, c - a, both
        values = out
    return values


def backward3(values):
    for stride in (9, 3, 1):
        out = [None] * 27
        for n in range(27):
            if n // stride % 3 == 0:
                a, b, c = values[n], values[n + stride], values[n + 2 * stride]
                even, odd = 0.5 * c, 0.5 * b
                out[n], out[n + stride], out[n + 2 * stride] = even - odd, a - c, even + odd
        values = out
    return values


def collide_tile(values, force, rate, solid):
    moments = forward3(values)
    density = moments[0]
    jx, jy, jz = moments[9], moments[3], moments[1] + 0.5 * force
    inverse = 1.0 / density
    flux = (jx, jy, jz)
    u = tuple(j * inverse for j in flux)
    third = 1.0 / 3.0
    base = {0: density}
    for k in (1, 2, 3):
        base[k] = density * third**k
    squares = [flux[d] * u[d] for d in range(3)]
    square_at = {}
    scaled = {}

    def scale(key, value, count):
        if count == 0:
            return value
        if (key, count) not in scaled:
            scaled[key, count] = value * third**count
        return scaled[key, count]

    cross = {(0, 1): jx * u[1], (0, 2): jx * u[2], (1, 2): jy * u[2]}
    out = [None] * 27
    for n in range(27):
        powers = (n // 9, n // 3 % 3, n % 3)
        if n in (0, 3, 9):
            out[n] = moments[n]
            continue
        if n == 1:
            out[n] = moments[n] + force
            continue
        odd = tuple(d for d in range(3) if powers[d] == 1)
        even = tuple(d for d in range(3) if powers[d] == 2)
        count = len(even)
        if len(odd) == 3:
            out[n] = moments[n] - rate(n) * moments[n]
            continue
        if len(odd) == 0:
            if even not in square_at:
                total = squares[even[0]]
                for d in even[1:]:
                    total = total + squares[d]
                square_at[even] = base[count] + (total * (3.0 * third**count) if count > 1 else total)
            level = square_at[even]
        elif len(odd) == 1:
            level = scale(odd, flux[odd[0]], count)
        else:
            level = scale(odd, cross[odd], count)
        out[n] = moments[n] - rate(n) * (moments[n] - level)
    out[26] = jnp.where(solid, jnp.nan, out[26])
    return backward3(out)


HEAT_OFFSETS = [(0, 0, 0), (1, 0, 0), (-1, 0, 0), (0, 1, 0), (0, -1, 0), (0, 0, 1), (0, 0, -1)]


def collide_flow(rates_ref, flow, force, solid, target, tile):
    for n, value in enumerate(collide_tile(flow, force, lambda n: rates_ref[n], solid)):
        target[n, tile] = value


def collide_heat(heat, omega, speeds, target, tile):
    total = heat[0]
    for k in range(1, 7):
        total = total + heat[k]
    side = 0.125 * total
    half = 0.5 * total
    for k in range(7):
        if k == 0:
            level = 0.25 * total
        else:
            drift = half * speeds[(k - 1) // 2]
            level = side + drift if k % 2 == 1 else side - drift
        target[k, tile] = heat[k] - (heat[k] - level) * omega


def stream(slab, post, tile, offsets):
    block_x, block_y = tile // slab.gy, tile % slab.gy
    x_of = {a: lax.rem(block_x + slab.gx - a, slab.gx) for a in (-1, 0, 1)}
    y_of = {b: lax.rem(block_y + slab.gy - b, slab.gy) for b in (-1, 0, 1)}
    row = row_index()
    per_x = 2 * slab.planes
    in_x = (lane_index() + slab.halo) % LANES // per_x
    last_x = {1: in_x == slab.block_x - 1, -1: in_x == 0}
    last_y = {1: row == SUBLANES - 1, -1: row == 0}

    def arrive(number, offset):
        a, b, c = offset

        def take(x):
            value = post[number, x_of[x] * slab.gy + block_y]
            if b != 0:
                other = post[number, x_of[x] * slab.gy + y_of[b]]
                value = jnp.where(last_y[b], other, value)
            return value

        value = take(0)
        if a != 0:
            value = jnp.where(last_x[a], take(a), value)
        if b != 0:
            value = pltpu.roll(value, b % SUBLANES, 0)
        return lane_roll(value, a * per_x + c)

    return [arrive(number, offset) for number, offset in enumerate(offsets)]


def stream_flow(slab, post, tile):
    return [
        jnp.where(value != value, post[26 - n, tile], value)
        for n, value in enumerate(stream(slab, post, tile, OFFSET_TABLE))
    ]


def over_tiles(slab, body, unroll=1):
    def one(tile, _):
        body(tile)
        return 0

    lax.fori_loop(0, slab.sub, one, 0, unroll=unroll)


def over_steps(count, body):
    def one(number, _):
        body(number)
        return 0

    lax.fori_loop(0, count, one, 0)


def first_window(slab, rates_hbm, came, below_ref, above_ref, *refs):
    flow_out, keep_out, heat_outs = refs[0], refs[1], refs[2 : 2 + slab.grp]
    rates_ref, sem, state, flow_post, heat_post, held = refs[2 + slab.grp :]
    rates_copy = pltpu.make_async_copy(rates_hbm, rates_ref, sem)
    rates_copy.start()
    make_tiles(slab, came, below_ref, above_ref, state)
    rates_copy.wait()

    def speeds_of(tile):
        return [state[SPEED_AT + d, tile] for d in range(3)]

    def begin(tile):
        solid = state[SOLID_AT, tile]
        heat = [state[HEAT_AT + k, tile] for k in range(7)]
        force = heat_force(heat)
        keep_out[0, tile] = force
        keep_out[1, tile] = solid
        flow = [state[n, tile] for n in range(27)]
        collide_flow(rates_ref, flow, force, solid != 0.0, flow_post.at[0], tile)
        collide_heat(heat, state[RATE_AT, tile], speeds_of(tile), heat_post.at[0], tile)

    over_tiles(slab, begin)

    def step(number):
        source = lax.rem(number, 2)

        def go_on(tile):
            flow = stream_flow(slab, flow_post.at[source], tile)
            solid = state[SOLID_AT, tile] != 0.0
            collide_flow(rates_ref, flow, keep_out[0, tile], solid, flow_post.at[1 - source], tile)
            heat = stream(slab, heat_post.at[source], tile, HEAT_OFFSETS)
            omega = state[RATE_AT, tile]
            collide_heat(heat, omega, speeds_of(tile), heat_post.at[1 - source], tile)

        over_tiles(slab, go_on)

    over_steps(STEPS - 1, step)
    source = (STEPS - 1) % 2

    def next_window(tile):
        flow = stream_flow(slab, flow_post.at[source], tile)
        heat = stream(slab, heat_post.at[source], tile, HEAT_OFFSETS)
        solid = state[SOLID_AT, tile] != 0.0
        speeds = [
            jnp.where(solid, 0.0, each) for each in flow_speed_tile(flow, keep_out[0, tile])
        ]
        for d in range(3):
            state[SPEED_AT + d, tile] = speeds[d]
        force = heat_force(heat)
        keep_out[0, tile] = force
        collide_flow(rates_ref, flow, force, solid, flow_out, tile)
        collide_heat(heat, state[RATE_AT, tile], speeds, heat_post.at[1 - source], tile)

    over_tiles(slab, next_window)

    def heat_step(number):
        source = lax.rem(number + STEPS, 2)

        def go_on(tile):
            heat = stream(slab, heat_post.at[source], tile, HEAT_OFFSETS)
            omega = state[RATE_AT, tile]
            collide_heat(heat, omega, speeds_of(tile), heat_post.at[1 - source], tile)

        over_tiles(slab, go_on, unroll=2)

    over_steps(STEPS - 1, heat_step)
    zero = jnp.zeros((SUBLANES, LANES), F32)

    def end_heat(tile):
        heat = stream(slab, heat_post.at[(2 * STEPS - 1) % 2], tile, HEAT_OFFSETS)
        heat += [zero] * (slab.sub - 7)
        for x, value in enumerate(swap_groups(heat, slab.planes)[0::2]):
            held[x, tile] = value

    over_tiles(slab, end_heat, unroll=2)
    mine = lax.axis_index("grp")
    for step_number in range(slab.grp):
        heat_outs[step_number][...] = held[jnp.bitwise_xor(mine, step_number)]


def last_window(slab, rates_hbm, came, flow_in, keep_ref, sent, rates_ref, sem, flow_post):
    rates_copy = pltpu.make_async_copy(rates_hbm, rates_ref, sem)
    rates_copy.start()

    def copy(n, _):
        flow_post[0, n] = flow_in[n]
        return 0

    lax.fori_loop(0, 27, copy, 0, unroll=3)
    rates_copy.wait()

    def step(number):
        source = lax.rem(number, 2)

        def go_on(tile):
            flow = stream_flow(slab, flow_post.at[source], tile)
            solid = keep_ref[1, tile] != 0.0
            collide_flow(rates_ref, flow, keep_ref[0, tile], solid, flow_post.at[1 - source], tile)

        over_tiles(slab, go_on)

    over_steps(STEPS - 1, step)

    def end(tile):
        flow = stream_flow(slab, flow_post.at[(STEPS - 1) % 2], tile)
        pack_out(slab, flow, came, tile, sent)

    over_tiles(slab, end)


def heat_force(heat):
    total = heat[0]
    for k in range(1, 7):
        total = total + heat[k]
    return BUOYANCY * (total - REFERENCE_HEAT)


def flow_speed_tile(values, force):
    total = values[0]
    for n in range(1, 27):
        total = total + values[n]
    sums = []
    for d in range(3):
        plus, minus = None, None
        for n in range(27):
            part = OFFSET_TABLE[n][d]
            if part == 1:
                plus = values[n] if plus is None else plus + values[n]
            if part == -1:
                minus = values[n] if minus is None else minus + values[n]
        sums.append(plus - minus)
    sums[2] = sums[2] + 0.5 * force
    return [each / total for each in sums]


def local_call(body, slab, arrays, outs, scratch=(), in_hbm=0, carried=False):
    def kernel(*refs):
        body(slab, *refs)

    return pl.pallas_call(
        kernel,
        out_shape=[jax.ShapeDtypeStruct(shape, F32) for shape in outs],
        in_specs=[
            pl.BlockSpec(
                memory_space=pltpu.HBM if i < in_hbm else pl.ANY if carried and i == 0 else pltpu.VMEM
            )
            for i in range(len(arrays))
        ],
        out_specs=[pl.BlockSpec(memory_space=pl.ANY if carried else pltpu.VMEM)] * len(outs),
        input_output_aliases={0: 0} if carried else {},
        scratch_shapes=[pltpu.VMEM(s, F32) if isinstance(s, tuple) else s for s in scratch],
        compiler_params=pltpu.CompilerParams(vmem_limit_bytes=24 * 1024 * 1024),
    )(
        *(
            pltpu.with_memory_space_constraint(array, pltpu.HBM) if i < in_hbm else array
            for i, array in enumerate(arrays)
        )
    )


RING = ("grp", "gx", "gy")


def exchange(slab, low, high):
    ring = slab.ring
    upward = [(ring[i - 1], ring[i]) for i in range(len(ring))]
    from_below = lax.ppermute(high, RING, upward)
    from_above = lax.ppermute(low, RING, [(b, a) for a, b in upward])
    return from_below, from_above


def across_plane(slab, sent):
    came = {0: sent[0]}
    far_first = [step for k in range(2) for step in range(2 + k, slab.sub, 2)] + [1]
    far_first.sort(key=lambda step: -bin(step >> 1).count("1"))
    for step in far_first:
        pairs = [(i, i ^ step) for i in range(slab.sub)]
        came[step] = lax.ppermute(sent[step], ("gx", "gy"), pairs)
    return [came[step] for step in range(slab.sub)]


def across_planes(slab, parts):
    return [parts[0]] + [
        lax.ppermute(parts[step], "grp", [(i, i ^ step) for i in range(slab.grp)])
        for step in range(1, slab.grp)
    ]


def on_slabs(slab, populations, thermal, velocity_prev, solid, phase_ids, conductivity, rates):
    tile = (SUBLANES, LANES)

    def vmem_like(array):
        return pltpu.VMEM(array.shape, array.dtype)

    parts = local_call(
        offer_heat,
        slab,
        [conductivity, thermal, phase_ids],
        [(8,) + tile] * slab.grp,
        [
            pltpu.SMEM(conductivity.shape, F32),
            vmem_like(thermal),
            vmem_like(phase_ids),
            pltpu.SemaphoreType.DMA((3,)),
        ],
        in_hbm=3,
    )
    parts = across_planes(slab, parts)
    sent_shape = (slab.sub, ROWS // 2) + tile
    sent, flags = local_call(
        pack_flow,
        slab,
        [populations, velocity_prev, solid],
        [sent_shape, solid.shape],
        [
            (SOLID_AT,) + solid.shape,
            pltpu.VMEM(solid.shape, solid.dtype),
            pltpu.SemaphoreType.DMA((3,)),
        ],
        in_hbm=3,
    )
    (sent,) = local_call(
        pack_heat,
        slab,
        [sent, flags] + parts,
        [sent_shape],
        [
            (ROWS - SOLID_AT,) + solid.shape,
            (slab.sub, (ROWS - SOLID_AT) // 2) + tile,
            pltpu.SemaphoreType.DMA,
        ],
        carried=True,
    )
    halo_shape = (slab.sub // 2, ROWS // 2) + tile
    came, low, high = local_call(
        offer_halo, slab, across_plane(slab, sent), [sent_shape, halo_shape, halo_shape]
    )
    below, above = exchange(slab, low, high)
    plane = (slab.sub,) + tile
    scalars = [pltpu.SMEM(rates.shape, F32), pltpu.SemaphoreType.DMA]
    flow, keep, *parts = local_call(
        first_window,
        slab,
        [rates, came, below, above],
        [(27,) + plane, (2,) + plane] + [plane] * slab.grp,
        scalars + [(ROWS,) + plane, (2, 27) + plane, (2, 7) + plane, (slab.grp,) + plane],
        in_hbm=1,
    )
    parts = across_planes(slab, parts)
    last_shape = (slab.sub, FLOW_PAIRS + slab.grp) + tile
    (sent,) = local_call(
        last_window,
        slab,
        [rates, came, flow, keep],
        [last_shape],
        scalars + [(2, 27) + plane],
        in_hbm=1,
    )
    (sent,) = local_call(
        add_heat,
        slab,
        [sent] + parts,
        [last_shape],
        [(slab.sub, slab.grp) + tile, pltpu.SemaphoreType.DMA],
        carried=True,
    )
    return tuple(
        local_call(
            unpack_out,
            slab,
            across_plane(slab, sent),
            [populations.shape, thermal.shape],
            [last_shape],
        )
    )


def solution(mesh):
    in_specs = (
        P(None, "gx", "gy", "grp"),
        P(None, ("gx", "grp"), "gy", None),
        P(None, "gx", "gy", "grp"),
        P("gx", "gy", "grp"),
        P(("gx", "grp"), "gy", None),
        P(),
        P(),
    )
    out_specs = (P(None, "gx", "gy", "grp"), P(None, ("gx", "grp"), "gy", None))

    def per_device(populations, thermal, *others):
        slab = Slab(mesh.shape, populations.shape[1:], thermal.shape[1:])
        plan = (lambda *arrays: on_slabs(slab, *arrays)) if slab.fits else on_device
        return plan(populations, thermal, *others)

    return jax.shard_map(
        per_device, mesh=mesh, in_specs=in_specs, out_specs=out_specs, check_vma=False
    )
```

```python
import jax
import jax.numpy as jnp
import numpy as np
from jax import lax
from jax.experimental import pallas as pl
from jax.experimental.pallas import tpu as pltpu
from jax.sharding import PartitionSpec as P

STEPS = 4
WINDOWS = 2


HIGHEST = lax.Precision.HIGHEST
BUOYANCY = 0.03
REFERENCE_HEAT = 1.0
OFFSET_TABLE = [(number // 9 - 1, number // 3 % 3 - 1, number % 3 - 1) for number in range(27)]
LATTICE_WEIGHTS = np.array(
    [
        np.prod([2.0 / 3.0 if component == 0 else 1.0 / 6.0 for component in triple])
        for triple in OFFSET_TABLE
    ]
)
VANDERMONDE = np.array([[1.0, 1.0, 1.0], [-1.0, 0.0, 1.0], [1.0, 0.0, 1.0]])
VANDER_INVERSE = np.array([[0.0, -0.5, 0.5], [1.0, 0.0, -1.0], [0.0, 0.5, 0.5]])
MOMENT_MATRIX = np.kron(np.kron(VANDERMONDE, VANDERMONDE), VANDERMONDE)
MOMENT_INVERSE = np.kron(np.kron(VANDER_INVERSE, VANDER_INVERSE), VANDER_INVERSE)
RELAXED = np.array([0.0 if number in (0, 1, 3, 9) else 1.0 for number in range(27)])
SUMMING = np.concatenate([np.ones((1, 27)), 1.0 * np.array(OFFSET_TABLE).T], axis=0)
HEAT_WEIGHTS = np.array([0.25] + [0.125] * 6)


def from_behind(value, axis, steps):
    count = lax.axis_size(axis)
    pairs = [(source, (source + steps) % count) for source in range(count)]
    return lax.ppermute(value, axis, pairs)


def extended(cells, sides, width):
    for axis, dim in sides:
        count = lax.axis_size(axis)
        head = lax.slice_in_dim(cells, 0, width, axis=dim)
        tail = lax.slice_in_dim(cells, cells.shape[dim] - width, cells.shape[dim], axis=dim)
        cells = jnp.concatenate(
            [
                lax.ppermute(tail, axis, [(i, (i + 1) % count) for i in range(count)]),
                cells,
                lax.ppermute(head, axis, [((i + 1) % count, i) for i in range(count)]),
            ],
            axis=dim,
        )
    return cells


def flow_state(flat, heat_flat):
    sums = jnp.dot(jnp.asarray(SUMMING, jnp.float32), flat, precision=HIGHEST)
    density = sums[0]
    force = BUOYANCY * (heat_flat - REFERENCE_HEAT)
    speed = jnp.stack([sums[1], sums[2], sums[3] + 0.5 * force]) / density
    return (density, force, speed)


def collide(popul, heat, rates):
    flat = popul.reshape(27, -1)
    density, force, speed = flow_state(flat, heat.reshape(-1))
    along = jnp.dot(jnp.asarray(SUMMING[1:].T, jnp.float32), speed, precision=HIGHEST)
    square = jnp.sum(speed * speed, axis=0)
    balance = (
        density
        * jnp.asarray(LATTICE_WEIGHTS, jnp.float32)[:, None]
        * (1.0 + 3.0 * along + 4.5 * along * along - 1.5 * square)
    )
    scaled = (
        jnp.asarray(MOMENT_INVERSE, jnp.float32)
        * (rates * jnp.asarray(RELAXED, jnp.float32))[None, :]
    )
    relax = jnp.dot(scaled, jnp.asarray(MOMENT_MATRIX, jnp.float32), precision=HIGHEST)
    post = (
        flat
        - jnp.dot(relax, flat - balance, precision=HIGHEST)
        + jnp.asarray(MOMENT_INVERSE[:, 1], jnp.float32)[:, None] * force[None, :]
    )
    return post.reshape(popul.shape)


def flow_speed(popul, heat, solid):
    density, force, speed = flow_state(popul.reshape(27, -1), heat.reshape(-1))
    return jnp.where(solid[None] == 0, speed.reshape((3,) + solid.shape), 0.0)


def heat_collide(heat_pops, speed, relax_time):
    total = jnp.sum(heat_pops, axis=0)
    still = jnp.zeros_like(speed[0])
    along = jnp.stack([still, speed[0], -speed[0], speed[1], -speed[1], speed[2], -speed[2]])
    balance = (
        jnp.asarray(HEAT_WEIGHTS, jnp.float32)[:, None, None, None]
        * total[None]
        * (1.0 + 4.0 * along)
    )
    return heat_pops - (heat_pops - balance) / relax_time[None]


def relaxation(phase_ids, conductivity):
    levels = jnp.arange(conductivity.shape[0], dtype=jnp.int32)
    chosen = jnp.sum(
        jnp.where(
            phase_ids[None] == levels[:, None, None, None], conductivity[:, None, None, None], 0.0
        ),
        axis=0,
    )
    return 0.5 + 4.0 * chosen


def inner_window(padded, triple, sizes):
    return padded[
        1 - triple[0] : 1 - triple[0] + sizes[0],
        1 - triple[1] : 1 - triple[1] + sizes[1],
        1 - triple[2] : 1 - triple[2] + sizes[2],
    ]


def advance(grid, axis_number, send_up, send_down):
    space = 3 + axis_number
    length = grid.shape[space]
    rising = lax.index_in_dim(grid, 2, axis_number, keepdims=True)
    resting = lax.index_in_dim(grid, 1, axis_number, keepdims=True)
    falling = lax.index_in_dim(grid, 0, axis_number, keepdims=True)
    from_below = send_up(lax.slice_in_dim(rising, length - 1, length, axis=space))
    from_above = send_down(lax.slice_in_dim(falling, 0, 1, axis=space))
    rising = jnp.concatenate(
        [from_below, lax.slice_in_dim(rising, 0, length - 1, axis=space)], axis=space
    )
    falling = jnp.concatenate(
        [lax.slice_in_dim(falling, 1, length, axis=space), from_above], axis=space
    )
    return jnp.concatenate([falling, resting, rising], axis=axis_number)


def flow_arrivals(post):
    sizes = post.shape[1:]
    grid = post.reshape((3, 3, 3) + sizes)
    grid = advance(
        grid,
        0,
        lambda plane: from_behind(plane, "gx", 1),
        lambda plane: from_behind(plane, "gx", -1),
    )
    grid = advance(
        grid,
        1,
        lambda plane: from_behind(plane, "gy", 1),
        lambda plane: from_behind(plane, "gy", -1),
    )
    grid = advance(
        grid,
        2,
        lambda plane: from_behind(plane, "grp", 1),
        lambda plane: from_behind(plane, "grp", -1),
    )
    return grid.reshape(post.shape)


def stream_heat(post, grp_index, last_grp):
    length = post.shape[1]
    size_y = post.shape[2]
    eastward = post[1]
    westward = post[2]
    lower_first = from_behind(eastward, "grp", 1)
    lower_second = from_behind(lower_first, "gx", 1)
    entering = jnp.where(grp_index == 0, lower_second, lower_first)
    eastward = jnp.concatenate([entering, eastward[: length - 1]], axis=0)
    upper_first = from_behind(westward, "grp", -1)
    upper_second = from_behind(upper_first, "gx", -1)
    entering = jnp.where(grp_index == last_grp, upper_second, upper_first)
    westward = jnp.concatenate([westward[1:], entering], axis=0)
    sides = extended(post[3:5], (("gy", 2),), 1)
    northward = sides[0, :, 0:size_y]
    southward = sides[1, :, 2 : size_y + 2]
    upward = jnp.roll(post[5], 1, axis=2)
    downward = jnp.roll(post[6], -1, axis=2)
    return jnp.stack([post[0], eastward, westward, northward, southward, upward, downward])


def on_device(populations, thermal, velocity_prev, solid, phase_ids, conductivity, rates):
    padded_solid = extended(solid, (("grp", 2), ("gx", 0), ("gy", 1)), 1)
    sizes = solid.shape
    blocked = jnp.stack(
        [inner_window(padded_solid, OFFSET_TABLE[number], sizes) != 0 for number in range(27)]
    )
    fluid_cells = (solid == 0)[None]
    grp_index = lax.axis_index("grp")
    last_grp = lax.axis_size("grp") - 1
    relax_time = relaxation(phase_ids, conductivity)
    speed_brick = velocity_prev
    popul = populations
    heat_pops = thermal
    for window_number in range(WINDOWS):
        heat_brick = lax.all_to_all(
            jnp.sum(heat_pops, axis=0), "grp", split_axis=2, concat_axis=0, tiled=True
        )
        speed_column = lax.all_to_all(speed_brick, "grp", split_axis=1, concat_axis=3, tiled=True)
        for step_number in range(STEPS):
            post = collide(popul, heat_brick, rates)
            arrived = flow_arrivals(post)
            popul = jnp.where(fluid_cells, jnp.where(blocked, post[::-1], arrived), popul)
        for step_number in range(STEPS):
            heat_pops = stream_heat(
                heat_collide(heat_pops, speed_column, relax_time), grp_index, last_grp
            )
        if window_number + 1 < WINDOWS:
            speed_brick = flow_speed(popul, heat_brick, solid)
    return (popul, heat_pops)


SUBLANES = 8
LANES = 128
F32 = jnp.float32


class Slab:
    def __init__(self, mesh_shape, flow_block, heat_block):
        self.grp, self.gx, self.gy = (mesh_shape[name] for name in ("grp", "gx", "gy"))
        self.block_x, self.block_y, self.block_z = flow_block
        self.sub = self.gx * self.gy
        self.planes = self.block_z // self.sub
        self.halo = self.planes // 2
        self.fits = (
            self.block_y == SUBLANES
            and self.block_z == LANES
            and self.planes * self.sub == LANES
            and self.halo * 2 == self.planes
            and WINDOWS == 2
            and self.halo == STEPS * WINDOWS
            and self.sub >= 8
            and 2 * self.block_x == self.sub
            and self.block_x == self.grp
            and heat_block == (1, SUBLANES, self.grp * LANES)
            and self.sub & (self.sub - 1) == 0
            and self.grp & (self.grp - 1) == 0
            and self.gy % 2 == 0
            and self.sub % self.grp == 0
        )
        if self.fits:
            self.turn = self.sub // self.grp
            partners = [step for k in (1, 0) for step in range(self.sub - 2 + k, 1, -2)]
            partners.sort(key=lambda step: bin(step >> 1).count("1"))
            self.steps = [0, 1] + partners
            self.ring = [
                part * self.sub + self.round_plane((place - self.turn * part) % self.sub)
                for part in range(self.grp)
                for place in range(self.sub)
            ]

    def round_plane(self, number):
        x, y = number // self.gy, number % self.gy
        back = x % 2
        return x * self.gy + y + back * (self.gy - 1 - 2 * y)

    def holders(self, part):
        begin = self.sub * self.grp - self.turn * part
        mine = self.place_in_plane()
        return [
            jnp.bitwise_xor(self.round_plane(lax.rem(begin + place, self.sub)), mine)
            for place in range(self.sub)
        ]

    def place_in_plane(self):
        return lax.axis_index("gx") * self.gy + lax.axis_index("gy")


def lane_index():
    return lax.broadcasted_iota(jnp.int32, (SUBLANES, LANES), 1)


def row_index():
    return lax.broadcasted_iota(jnp.int32, (SUBLANES, LANES), 0)


def lane_roll(value, amount):
    amount = amount % LANES
    return value if amount == 0 else pltpu.roll(value, amount, 1)


def swap_groups(values, group):
    count = len(values)
    lane = lane_index()
    values = list(values)
    bit = 1
    while bit < count:
        low = (lane // (group * bit)) % 2 == 0
        for first in range(count):
            if first & bit == 0:
                a, b = values[first], values[first | bit]
                values[first] = jnp.where(low, a, lane_roll(b, group * bit))
                values[first | bit] = jnp.where(low, lane_roll(a, -group * bit), b)
        bit *= 2
    return values


SPEED_AT, SOLID_AT, HEAT_AT, RATE_AT, ROWS = 27, 30, 31, 38, 40
FLOW_PAIRS = 14


def offer_heat(slab, levels_hbm, heat_hbm, phase_hbm, *refs):
    outs, (levels_ref, heat_ref, phase_ref, sems) = refs[: slab.grp], refs[slab.grp :]
    copies = [
        pltpu.make_async_copy(heat_hbm, heat_ref, sems.at[0]),
        pltpu.make_async_copy(phase_hbm, phase_ref, sems.at[1]),
        pltpu.make_async_copy(levels_hbm, levels_ref, sems.at[2]),
    ]
    for copy in copies:
        copy.start()
    for copy in copies:
        copy.wait()
    mine = lax.axis_index("grp")
    for step in range(slab.grp):
        part = jnp.bitwise_xor(mine, step)
        span = pl.ds(pl.multiple_of(part * LANES, LANES), LANES)
        phase = phase_ref[0, :, span]
        chosen = jnp.zeros((SUBLANES, LANES), F32)
        for level in range(levels_ref.shape[0]):
            chosen = jnp.where(phase == level, levels_ref[level], chosen)
        for k in range(7):
            outs[step][k] = heat_ref[k, 0, :, span]
        outs[step][7] = 1.0 / (0.5 + 4.0 * chosen)


def for_each(count, body):
    for number in range(count):
        body(number)


def pack_flow(slab, popul_hbm, speed_hbm, solid_hbm, sent, flags, fields, solid_ref, sems):
    copies = [
        pltpu.make_async_copy(popul_hbm, fields.at[pl.ds(0, SPEED_AT)], sems.at[0]),
        pltpu.make_async_copy(speed_hbm, fields.at[pl.ds(SPEED_AT, 3)], sems.at[1]),
        pltpu.make_async_copy(solid_hbm, solid_ref, sems.at[2]),
    ]
    for copy in copies:
        copy.start()
    for copy in copies:
        copy.wait()
    holders = slab.holders(lax.axis_index("grp"))

    def one(pair):
        pack_pair(slab, fields, pair, sent, pair, holders)

    for_each(SOLID_AT // 2, one)
    flags[...] = solid_ref[...].astype(F32)


def pack_pair(slab, fields, source, sent, target, holders):
    sources = [fields[2 * source + h, x] for x in range(slab.block_x) for h in range(2)]
    for place, value in enumerate(swap_groups(sources, slab.planes)):
        sent[holders[place], target] = value


def pack_heat(slab, sent_in, flags, *refs):
    parts, (sent, held, packed, sem) = refs[: slab.grp], refs[slab.grp :]
    mine = lax.axis_index("grp")
    holders = slab.holders(lax.axis_index("grp"))
    held[0] = flags[...]
    held[9] = jnp.zeros(flags.shape, F32)
    for step in range(slab.grp):
        held[pl.ds(1, 8), jnp.bitwise_xor(mine, step)] = parts[step][...]
    first, count = SOLID_AT // 2, (ROWS - SOLID_AT) // 2

    def one(pair):
        pack_pair(slab, held, pair, packed, pair, holders)

    for_each(count, one)
    copy = pltpu.make_async_copy(packed, sent.at[:, pl.ds(first, count)], sem)
    copy.start()
    copy.wait()


def in_first_half(slab):
    return lane_index() % slab.planes < slab.halo


def collect(slab, parts, came):
    mine = slab.place_in_plane()
    for part, step in zip(parts, slab.steps):
        came[jnp.bitwise_xor(mine, step)] = part[...]


def offer_halo(slab, *refs):
    parts, (came, low_out, high_out) = refs[: slab.sub], refs[slab.sub :]
    collect(slab, parts, came)

    def one(number, _):
        tile = 2 * number
        first = in_first_half(slab)
        for pair in range(ROWS // 2):
            a, b = came[tile, pair], came[tile + 1, pair]
            low_out[number, pair] = jnp.where(first, a, lane_roll(b, slab.halo))
            high_out[number, pair] = jnp.where(first, lane_roll(b, -slab.halo), a)
        return 0

    lax.fori_loop(0, slab.sub // 2, one, 0)


def make_tiles(slab, came, below_ref, above_ref, state):
    def one(number, _):
        first = in_first_half(slab)
        even = (lane_index() // slab.planes) % 2 == 0
        back = 2 * slab.planes
        for pair in range(ROWS // 2):
            below, above = below_ref[number, pair], above_ref[number, pair]
            beside = (
                jnp.where(first, above, lane_roll(below, -back)),
                jnp.where(first, lane_roll(above, -slab.halo), lane_roll(below, slab.halo - back)),
            )
            for which in range(2):
                tile = 2 * number + which
                own, halo = came[tile, pair], beside[which]
                state[2 * pair, tile] = jnp.where(even, own, lane_roll(halo, slab.planes))
                state[2 * pair + 1, tile] = jnp.where(even, lane_roll(own, -slab.planes), halo)
        return 0

    lax.fori_loop(0, slab.sub // 2, one, 0)


def pack_out(slab, flow, came, tile, sent):
    even = (lane_index() // slab.planes) % 2 == 0
    flags = came[tile, SOLID_AT // 2]
    solid = jnp.where(even, flags, lane_roll(flags, slab.planes)) != 0.0
    partner = jnp.bitwise_xor(tile, slab.place_in_plane())
    for pair in range(FLOW_PAIRS):
        value = flow[2 * pair]
        if 2 * pair + 1 < len(flow):
            value = jnp.where(even, value, lane_roll(flow[2 * pair + 1], slab.planes))
        sent[partner, pair] = jnp.where(solid, came[tile, pair], value)


def add_heat(slab, sent_in, *refs):
    parts, (sent, packed, sem) = refs[: slab.grp], refs[slab.grp :]
    mine = slab.place_in_plane()
    for tile in range(slab.sub):
        for step in range(slab.grp):
            packed[jnp.bitwise_xor(mine, tile), step] = parts[step][tile]
    copy = pltpu.make_async_copy(packed, sent.at[:, pl.ds(FLOW_PAIRS, slab.grp)], sem)
    copy.start()
    copy.wait()


def unpack_out(slab, *refs):
    parts, (popul_hbm, thermal_hbm, came, popul, thermal, sems) = refs[: slab.sub], refs[slab.sub :]
    for part, step in zip(parts, slab.steps):
        came[step] = part[...]
    mine = lax.axis_index("grp")
    for step in range(slab.grp):
        part = jnp.bitwise_xor(mine, step)
        holders = slab.holders(part)
        span = pl.ds(pl.multiple_of(part * LANES, LANES), LANES)
        sources = [came[holders[place], FLOW_PAIRS + step] for place in range(slab.sub)]
        for k, value in enumerate(swap_groups(sources, slab.planes)[:7]):
            thermal[k, 0, :, span] = value
    copies = [pltpu.make_async_copy(thermal, thermal_hbm, sems.at[0])]
    copies[0].start()
    holders = slab.holders(mine)
    begin = 0
    for pair in range(FLOW_PAIRS):
        sources = [came[holders[place], pair] for place in range(slab.sub)]
        for number, value in enumerate(swap_groups(sources, slab.planes)):
            if 2 * pair + number % 2 < 27:
                popul[2 * pair + number % 2, number // 2] = value
        end = min(2 * pair + 2, 27)
        if pair % 4 == 3 or end == 27:
            rows = pl.ds(begin, end - begin)
            sem = sems.at[len(copies)]
            copies.append(pltpu.make_async_copy(popul.at[rows], popul_hbm.at[rows], sem))
            copies[-1].start()
            begin = end
    for copy in copies:
        copy.wait()


def forward3(values):
    for stride in (9, 3, 1):
        out = [None] * 27
        for n in range(27):
            if n // stride % 3 == 0:
                a, b, c = values[n], values[n + stride], values[n + 2 * stride]
                both = a + c
                out[n], out[n + stride], out[n + 2 * stride] = both + b, c - a, both
        values = out
    return values


def backward3(values):
    for stride in (9, 3, 1):
        out = [None] * 27
        for n in range(27):
            if n // stride % 3 == 0:
                a, b, c = values[n], values[n + stride], values[n + 2 * stride]
                even, odd = 0.5 * c, 0.5 * b
                out[n], out[n + stride], out[n + 2 * stride] = even - odd, a - c, even + odd
        values = out
    return values


def collide_tile(values, force, rate, solid):
    moments = forward3(values)
    density = moments[0]
    jx, jy, jz = moments[9], moments[3], moments[1] + 0.5 * force
    inverse = 1.0 / density
    flux = (jx, jy, jz)
    u = tuple(j * inverse for j in flux)
    third = 1.0 / 3.0
    base = {0: density}
    for k in (1, 2, 3):
        base[k] = density * third**k
    squares = [flux[d] * u[d] for d in range(3)]
    square_at = {}
    scaled = {}

    def scale(key, value, count):
        if count == 0:
            return value
        if (key, count) not in scaled:
            scaled[key, count] = value * third**count
        return scaled[key, count]

    cross = {(0, 1): jx * u[1], (0, 2): jx * u[2], (1, 2): jy * u[2]}
    out = [None] * 27
    for n in range(27):
        powers = (n // 9, n // 3 % 3, n % 3)
        if n in (0, 3, 9):
            out[n] = moments[n]
            continue
        if n == 1:
            out[n] = moments[n] + force
            continue
        odd = tuple(d for d in range(3) if powers[d] == 1)
        even = tuple(d for d in range(3) if powers[d] == 2)
        count = len(even)
        if len(odd) == 3:
            out[n] = moments[n] - rate(n) * moments[n]
            continue
        if len(odd) == 0:
            if even not in square_at:
                total = squares[even[0]]
                for d in even[1:]:
                    total = total + squares[d]
                square_at[even] = base[count] + (total * (3.0 * third**count) if count > 1 else total)
            level = square_at[even]
        elif len(odd) == 1:
            level = scale(odd, flux[odd[0]], count)
        else:
            level = scale(odd, cross[odd], count)
        out[n] = moments[n] - rate(n) * (moments[n] - level)
    out[26] = jnp.where(solid, jnp.nan, out[26])
    return backward3(out)


HEAT_OFFSETS = [(0, 0, 0), (1, 0, 0), (-1, 0, 0), (0, 1, 0), (0, -1, 0), (0, 0, 1), (0, 0, -1)]


def collide_flow(rates_ref, flow, force, solid, target, tile):
    for n, value in enumerate(collide_tile(flow, force, lambda n: rates_ref[n], solid)):
        target[n, tile] = value


def collide_heat(heat, omega, speeds, target, tile):
    total = heat[0]
    for k in range(1, 7):
        total = total + heat[k]
    side = 0.125 * total
    half = 0.5 * total
    for k in range(7):
        if k == 0:
            level = 0.25 * total
        else:
            drift = half * speeds[(k - 1) // 2]
            level = side + drift if k % 2 == 1 else side - drift
        target[k, tile] = heat[k] - (heat[k] - level) * omega


def stream(slab, post, tile, offsets):
    block_x, block_y = lax.div(tile, slab.gy), lax.rem(tile, slab.gy)
    x_of = {a: lax.rem(block_x + slab.gx - a, slab.gx) for a in (-1, 0, 1)}
    y_of = {b: lax.rem(block_y + slab.gy - b, slab.gy) for b in (-1, 0, 1)}
    row = row_index()
    per_x = 2 * slab.planes
    in_x = (lane_index() + slab.halo) % LANES // per_x
    last_x = {1: in_x == slab.block_x - 1, -1: in_x == 0}
    last_y = {1: row == SUBLANES - 1, -1: row == 0}

    def arrive(number, offset):
        a, b, c = offset

        def take(x):
            value = post[number, x_of[x] * slab.gy + block_y]
            if b != 0:
                other = post[number, x_of[x] * slab.gy + y_of[b]]
                value = jnp.where(last_y[b], other, value)
            return value

        value = take(0)
        if a != 0:
            value = jnp.where(last_x[a], take(a), value)
        if b != 0:
            value = pltpu.roll(value, b % SUBLANES, 0)
        return lane_roll(value, a * per_x + c)

    return [arrive(number, offset) for number, offset in enumerate(offsets)]


def stream_flow(slab, post, tile):
    return [
        jnp.where(value != value, post[26 - n, tile], value)
        for n, value in enumerate(stream(slab, post, tile, OFFSET_TABLE))
    ]


def over_tiles(slab, body, unroll=1):
    def one(tile, _):
        body(tile)
        return 0

    lax.fori_loop(0, slab.sub, one, 0, unroll=unroll)


def over_steps(count, body):
    def one(number, _):
        body(number)
        return 0

    lax.fori_loop(0, count, one, 0)


def first_window(slab, rates_hbm, came, below_ref, above_ref, *refs):
    flow_out, keep_out, heat_outs = refs[0], refs[1], refs[2 : 2 + slab.grp]
    rates_ref, sem, state, flow_post, heat_post, heat_a, heat_b, held = refs[2 + slab.grp :]
    rates_copy = pltpu.make_async_copy(rates_hbm, rates_ref, sem)
    rates_copy.start()
    make_tiles(slab, came, below_ref, above_ref, state)
    rates_copy.wait()

    def speeds_of(tile):
        return [state[SPEED_AT + d, tile] for d in range(3)]

    def begin(tile):
        solid = state[SOLID_AT, tile]
        heat = [state[HEAT_AT + k, tile] for k in range(7)]
        force = heat_force(heat)
        keep_out[0, tile] = force
        keep_out[1, tile] = solid
        flow = [state[n, tile] for n in range(27)]
        collide_flow(rates_ref, flow, force, solid != 0.0, flow_post.at[0], tile)
        collide_heat(heat, state[RATE_AT, tile], speeds_of(tile), heat_post.at[0], tile)

    over_tiles(slab, begin)

    def step(number):
        source = lax.rem(number, 2)

        def go_on(tile):
            flow = stream_flow(slab, flow_post.at[source], tile)
            solid = state[SOLID_AT, tile] != 0.0
            collide_flow(rates_ref, flow, keep_out[0, tile], solid, flow_post.at[1 - source], tile)
            heat = stream(slab, heat_post.at[source], tile, HEAT_OFFSETS)
            omega = state[RATE_AT, tile]
            collide_heat(heat, omega, speeds_of(tile), heat_post.at[1 - source], tile)

        over_tiles(slab, go_on)

    over_steps(STEPS - 1, step)
    source = (STEPS - 1) % 2

    def next_window(tile):
        flow = stream_flow(slab, flow_post.at[source], tile)
        heat = stream(slab, heat_post.at[source], tile, HEAT_OFFSETS)
        solid = state[SOLID_AT, tile] != 0.0
        speeds = [
            jnp.where(solid, 0.0, each) for each in flow_speed_tile(flow, keep_out[0, tile])
        ]
        for d in range(3):
            state[SPEED_AT + d, tile] = speeds[d]
        force = heat_force(heat)
        keep_out[0, tile] = force
        collide_flow(rates_ref, flow, force, solid, flow_out, tile)
        collide_heat(heat, state[RATE_AT, tile], speeds, heat_a, tile)

    over_tiles(slab, next_window)
    here, there = heat_a, heat_b
    for _ in range(STEPS - 1):

        def heat_alone(tile, here=here, there=there):
            heat = stream(slab, here, tile, HEAT_OFFSETS)
            collide_heat(heat, state[RATE_AT, tile], speeds_of(tile), there, tile)

        over_tiles(slab, heat_alone, unroll=4)
        here, there = there, here
    zero = jnp.zeros((SUBLANES, LANES), F32)

    def end_heat(tile):
        heat = stream(slab, here, tile, HEAT_OFFSETS)
        heat += [zero] * (slab.sub - 7)
        for x, value in enumerate(swap_groups(heat, slab.planes)[0::2]):
            held[x, tile] = value

    over_tiles(slab, end_heat, unroll=2)
    mine = lax.axis_index("grp")
    for step_number in range(slab.grp):
        heat_outs[step_number][...] = held[jnp.bitwise_xor(mine, step_number)]


def last_window(slab, rates_hbm, came, flow_in, keep_ref, sent, rates_ref, sem, flow_post):
    rates_copy = pltpu.make_async_copy(rates_hbm, rates_ref, sem)
    rates_copy.start()

    def copy(n, _):
        flow_post[0, n] = flow_in[n]
        return 0

    lax.fori_loop(0, 27, copy, 0, unroll=3)
    rates_copy.wait()

    def step(number):
        source = lax.rem(number, 2)

        def go_on(tile):
            flow = stream_flow(slab, flow_post.at[source], tile)
            solid = keep_ref[1, tile] != 0.0
            collide_flow(rates_ref, flow, keep_ref[0, tile], solid, flow_post.at[1 - source], tile)

        over_tiles(slab, go_on)

    over_steps(STEPS - 1, step)

    def end(tile):
        flow = stream_flow(slab, flow_post.at[(STEPS - 1) % 2], tile)
        pack_out(slab, flow, came, tile, sent)

    over_tiles(slab, end)


def heat_force(heat):
    total = heat[0]
    for k in range(1, 7):
        total = total + heat[k]
    return BUOYANCY * (total - REFERENCE_HEAT)


def flow_speed_tile(values, force):
    total = values[0]
    for n in range(1, 27):
        total = total + values[n]
    sums = []
    for d in range(3):
        plus, minus = None, None
        for n in range(27):
            part = OFFSET_TABLE[n][d]
            if part == 1:
                plus = values[n] if plus is None else plus + values[n]
            if part == -1:
                minus = values[n] if minus is None else minus + values[n]
        sums.append(plus - minus)
    sums[2] = sums[2] + 0.5 * force
    return [each / total for each in sums]


def local_call(body, slab, arrays, outs, scratch=(), in_hbm=0, carried=False, outs_in_hbm=False):
    def kernel(*refs):
        body(slab, *refs)

    return pl.pallas_call(
        kernel,
        out_shape=[jax.ShapeDtypeStruct(shape, F32) for shape in outs],
        in_specs=[
            pl.BlockSpec(
                memory_space=pltpu.HBM if i < in_hbm else pl.ANY if carried and i == 0 else pltpu.VMEM
            )
            for i in range(len(arrays))
        ],
        out_specs=[
            pl.BlockSpec(memory_space=pl.ANY if carried or outs_in_hbm else pltpu.VMEM)
        ]
        * len(outs),
        input_output_aliases={0: 0} if carried else {},
        scratch_shapes=[pltpu.VMEM(s, F32) if isinstance(s, tuple) else s for s in scratch],
        compiler_params=pltpu.CompilerParams(vmem_limit_bytes=24 * 1024 * 1024),
    )(
        *(
            pltpu.with_memory_space_constraint(array, pltpu.HBM) if i < in_hbm else array
            for i, array in enumerate(arrays)
        )
    )


RING = ("grp", "gx", "gy")


def exchange(slab, low, high):
    ring = slab.ring
    upward = [(ring[i - 1], ring[i]) for i in range(len(ring))]
    from_below = lax.ppermute(high, RING, upward)
    from_above = lax.ppermute(low, RING, [(b, a) for a, b in upward])
    return from_below, from_above


def across_plane(slab, sent):
    came = {0: sent[0]}
    for step in slab.steps[1:]:
        pairs = [(i, i ^ step) for i in range(slab.sub)]
        came[step] = lax.ppermute(sent[step], ("gx", "gy"), pairs)
    return [came[step] for step in slab.steps]


def across_planes(slab, parts):
    return [parts[0]] + [
        lax.ppermute(parts[step], "grp", [(i, i ^ step) for i in range(slab.grp)])
        for step in range(1, slab.grp)
    ]


def on_slabs(slab, populations, thermal, velocity_prev, solid, phase_ids, conductivity, rates):
    tile = (SUBLANES, LANES)

    def vmem_like(array):
        return pltpu.VMEM(array.shape, array.dtype)

    parts = local_call(
        offer_heat,
        slab,
        [conductivity, thermal, phase_ids],
        [(8,) + tile] * slab.grp,
        [
            pltpu.SMEM(conductivity.shape, F32),
            vmem_like(thermal),
            vmem_like(phase_ids),
            pltpu.SemaphoreType.DMA((3,)),
        ],
        in_hbm=3,
    )
    parts = across_planes(slab, parts)
    sent_shape = (slab.sub, ROWS // 2) + tile
    sent, flags = local_call(
        pack_flow,
        slab,
        [populations, velocity_prev, solid],
        [sent_shape, solid.shape],
        [
            (SOLID_AT,) + solid.shape,
            pltpu.VMEM(solid.shape, solid.dtype),
            pltpu.SemaphoreType.DMA((3,)),
        ],
        in_hbm=3,
    )
    (sent,) = local_call(
        pack_heat,
        slab,
        [sent, flags] + parts,
        [sent_shape],
        [
            (ROWS - SOLID_AT,) + solid.shape,
            (slab.sub, (ROWS - SOLID_AT) // 2) + tile,
            pltpu.SemaphoreType.DMA,
        ],
        carried=True,
    )
    halo_shape = (slab.sub // 2, ROWS // 2) + tile
    came, low, high = local_call(
        offer_halo, slab, across_plane(slab, sent), [sent_shape, halo_shape, halo_shape]
    )
    below, above = exchange(slab, low, high)
    plane = (slab.sub,) + tile
    scalars = [pltpu.SMEM(rates.shape, F32), pltpu.SemaphoreType.DMA]
    flow, keep, *parts = local_call(
        first_window,
        slab,
        [rates, came, below, above],
        [(27,) + plane, (2,) + plane] + [plane] * slab.grp,
        scalars + [(ROWS,) + plane, (2, 27) + plane, (2, 7) + plane] + [(7,) + plane] * 2 + [(slab.grp,) + plane],
        in_hbm=1,
    )
    parts = across_planes(slab, parts)
    last_shape = (slab.sub, FLOW_PAIRS + slab.grp) + tile
    (sent,) = local_call(
        last_window,
        slab,
        [rates, came, flow, keep],
        [last_shape],
        scalars + [(2, 27) + plane],
        in_hbm=1,
    )
    (sent,) = local_call(
        add_heat,
        slab,
        [sent] + parts,
        [last_shape],
        [(slab.sub, slab.grp) + tile, pltpu.SemaphoreType.DMA],
        carried=True,
    )
    return tuple(
        local_call(
            unpack_out,
            slab,
            across_plane(slab, sent),
            [populations.shape, thermal.shape],
            [
                last_shape,
                populations.shape,
                thermal.shape,
                pltpu.SemaphoreType.DMA((1 + -(-FLOW_PAIRS // 4),)),
            ],
            outs_in_hbm=True,
        )
    )


def solution(mesh):
    in_specs = (
        P(None, "gx", "gy", "grp"),
        P(None, ("gx", "grp"), "gy", None),
        P(None, "gx", "gy", "grp"),
        P("gx", "gy", "grp"),
        P(("gx", "grp"), "gy", None),
        P(),
        P(),
    )
    out_specs = (P(None, "gx", "gy", "grp"), P(None, ("gx", "grp"), "gy", None))

    def per_device(populations, thermal, *others):
        slab = Slab(mesh.shape, populations.shape[1:], thermal.shape[1:])
        plan = (lambda *arrays: on_slabs(slab, *arrays)) if slab.fits else on_device
        return plan(populations, thermal, *others)

    return jax.shard_map(
        per_device, mesh=mesh, in_specs=in_specs, out_specs=out_specs, check_vma=False
    )
```

```python
import jax
import jax.numpy as jnp
import numpy as np
from jax import lax
from jax.experimental import pallas as pl
from jax.experimental.pallas import tpu as pltpu
from jax.sharding import PartitionSpec as P

STEPS = 4
WINDOWS = 2


HIGHEST = lax.Precision.HIGHEST
BUOYANCY = 0.03
REFERENCE_HEAT = 1.0
OFFSET_TABLE = [(number // 9 - 1, number // 3 % 3 - 1, number % 3 - 1) for number in range(27)]
LATTICE_WEIGHTS = np.array(
    [
        np.prod([2.0 / 3.0 if component == 0 else 1.0 / 6.0 for component in triple])
        for triple in OFFSET_TABLE
    ]
)
VANDERMONDE = np.array([[1.0, 1.0, 1.0], [-1.0, 0.0, 1.0], [1.0, 0.0, 1.0]])
VANDER_INVERSE = np.array([[0.0, -0.5, 0.5], [1.0, 0.0, -1.0], [0.0, 0.5, 0.5]])
MOMENT_MATRIX = np.kron(np.kron(VANDERMONDE, VANDERMONDE), VANDERMONDE)
MOMENT_INVERSE = np.kron(np.kron(VANDER_INVERSE, VANDER_INVERSE), VANDER_INVERSE)
RELAXED = np.array([0.0 if number in (0, 1, 3, 9) else 1.0 for number in range(27)])
SUMMING = np.concatenate([np.ones((1, 27)), 1.0 * np.array(OFFSET_TABLE).T], axis=0)
HEAT_WEIGHTS = np.array([0.25] + [0.125] * 6)


def from_behind(value, axis, steps):
    count = lax.axis_size(axis)
    pairs = [(source, (source + steps) % count) for source in range(count)]
    return lax.ppermute(value, axis, pairs)


def extended(cells, sides, width):
    for axis, dim in sides:
        count = lax.axis_size(axis)
        head = lax.slice_in_dim(cells, 0, width, axis=dim)
        tail = lax.slice_in_dim(cells, cells.shape[dim] - width, cells.shape[dim], axis=dim)
        cells = jnp.concatenate(
            [
                lax.ppermute(tail, axis, [(i, (i + 1) % count) for i in range(count)]),
                cells,
                lax.ppermute(head, axis, [((i + 1) % count, i) for i in range(count)]),
            ],
            axis=dim,
        )
    return cells


def flow_state(flat, heat_flat):
    sums = jnp.dot(jnp.asarray(SUMMING, jnp.float32), flat, precision=HIGHEST)
    density = sums[0]
    force = BUOYANCY * (heat_flat - REFERENCE_HEAT)
    speed = jnp.stack([sums[1], sums[2], sums[3] + 0.5 * force]) / density
    return (density, force, speed)


def collide(popul, heat, rates):
    flat = popul.reshape(27, -1)
    density, force, speed = flow_state(flat, heat.reshape(-1))
    along = jnp.dot(jnp.asarray(SUMMING[1:].T, jnp.float32), speed, precision=HIGHEST)
    square = jnp.sum(speed * speed, axis=0)
    balance = (
        density
        * jnp.asarray(LATTICE_WEIGHTS, jnp.float32)[:, None]
        * (1.0 + 3.0 * along + 4.5 * along * along - 1.5 * square)
    )
    scaled = (
        jnp.asarray(MOMENT_INVERSE, jnp.float32)
        * (rates * jnp.asarray(RELAXED, jnp.float32))[None, :]
    )
    relax = jnp.dot(scaled, jnp.asarray(MOMENT_MATRIX, jnp.float32), precision=HIGHEST)
    post = (
        flat
        - jnp.dot(relax, flat - balance, precision=HIGHEST)
        + jnp.asarray(MOMENT_INVERSE[:, 1], jnp.float32)[:, None] * force[None, :]
    )
    return post.reshape(popul.shape)


def flow_speed(popul, heat, solid):
    density, force, speed = flow_state(popul.reshape(27, -1), heat.reshape(-1))
    return jnp.where(solid[None] == 0, speed.reshape((3,) + solid.shape), 0.0)


def heat_collide(heat_pops, speed, relax_time):
    total = jnp.sum(heat_pops, axis=0)
    still = jnp.zeros_like(speed[0])
    along = jnp.stack([still, speed[0], -speed[0], speed[1], -speed[1], speed[2], -speed[2]])
    balance = (
        jnp.asarray(HEAT_WEIGHTS, jnp.float32)[:, None, None, None]
        * total[None]
        * (1.0 + 4.0 * along)
    )
    return heat_pops - (heat_pops - balance) / relax_time[None]


def relaxation(phase_ids, conductivity):
    levels = jnp.arange(conductivity.shape[0], dtype=jnp.int32)
    chosen = jnp.sum(
        jnp.where(
            phase_ids[None] == levels[:, None, None, None], conductivity[:, None, None, None], 0.0
        ),
        axis=0,
    )
    return 0.5 + 4.0 * chosen


def inner_window(padded, triple, sizes):
    return padded[
        1 - triple[0] : 1 - triple[0] + sizes[0],
        1 - triple[1] : 1 - triple[1] + sizes[1],
        1 - triple[2] : 1 - triple[2] + sizes[2],
    ]


def advance(grid, axis_number, send_up, send_down):
    space = 3 + axis_number
    length = grid.shape[space]
    rising = lax.index_in_dim(grid, 2, axis_number, keepdims=True)
    resting = lax.index_in_dim(grid, 1, axis_number, keepdims=True)
    falling = lax.index_in_dim(grid, 0, axis_number, keepdims=True)
    from_below = send_up(lax.slice_in_dim(rising, length - 1, length, axis=space))
    from_above = send_down(lax.slice_in_dim(falling, 0, 1, axis=space))
    rising = jnp.concatenate(
        [from_below, lax.slice_in_dim(rising, 0, length - 1, axis=space)], axis=space
    )
    falling = jnp.concatenate(
        [lax.slice_in_dim(falling, 1, length, axis=space), from_above], axis=space
    )
    return jnp.concatenate([falling, resting, rising], axis=axis_number)


def flow_arrivals(post):
    sizes = post.shape[1:]
    grid = post.reshape((3, 3, 3) + sizes)
    grid = advance(
        grid,
        0,
        lambda plane: from_behind(plane, "gx", 1),
        lambda plane: from_behind(plane, "gx", -1),
    )
    grid = advance(
        grid,
        1,
        lambda plane: from_behind(plane, "gy", 1),
        lambda plane: from_behind(plane, "gy", -1),
    )
    grid = advance(
        grid,
        2,
        lambda plane: from_behind(plane, "grp", 1),
        lambda plane: from_behind(plane, "grp", -1),
    )
    return grid.reshape(post.shape)


def stream_heat(post, grp_index, last_grp):
    length = post.shape[1]
    size_y = post.shape[2]
    eastward = post[1]
    westward = post[2]
    lower_first = from_behind(eastward, "grp", 1)
    lower_second = from_behind(lower_first, "gx", 1)
    entering = jnp.where(grp_index == 0, lower_second, lower_first)
    eastward = jnp.concatenate([entering, eastward[: length - 1]], axis=0)
    upper_first = from_behind(westward, "grp", -1)
    upper_second = from_behind(upper_first, "gx", -1)
    entering = jnp.where(grp_index == last_grp, upper_second, upper_first)
    westward = jnp.concatenate([westward[1:], entering], axis=0)
    sides = extended(post[3:5], (("gy", 2),), 1)
    northward = sides[0, :, 0:size_y]
    southward = sides[1, :, 2 : size_y + 2]
    upward = jnp.roll(post[5], 1, axis=2)
    downward = jnp.roll(post[6], -1, axis=2)
    return jnp.stack([post[0], eastward, westward, northward, southward, upward, downward])


def on_device(populations, thermal, velocity_prev, solid, phase_ids, conductivity, rates):
    padded_solid = extended(solid, (("grp", 2), ("gx", 0), ("gy", 1)), 1)
    sizes = solid.shape
    blocked = jnp.stack(
        [inner_window(padded_solid, OFFSET_TABLE[number], sizes) != 0 for number in range(27)]
    )
    fluid_cells = (solid == 0)[None]
    grp_index = lax.axis_index("grp")
    last_grp = lax.axis_size("grp") - 1
    relax_time = relaxation(phase_ids, conductivity)
    speed_brick = velocity_prev
    popul = populations
    heat_pops = thermal
    for window_number in range(WINDOWS):
        heat_brick = lax.all_to_all(
            jnp.sum(heat_pops, axis=0), "grp", split_axis=2, concat_axis=0, tiled=True
        )
        speed_column = lax.all_to_all(speed_brick, "grp", split_axis=1, concat_axis=3, tiled=True)
        for step_number in range(STEPS):
            post = collide(popul, heat_brick, rates)
            arrived = flow_arrivals(post)
            popul = jnp.where(fluid_cells, jnp.where(blocked, post[::-1], arrived), popul)
        for step_number in range(STEPS):
            heat_pops = stream_heat(
                heat_collide(heat_pops, speed_column, relax_time), grp_index, last_grp
            )
        if window_number + 1 < WINDOWS:
            speed_brick = flow_speed(popul, heat_brick, solid)
    return (popul, heat_pops)


SUBLANES = 8
LANES = 128
F32 = jnp.float32


class Slab:
    def __init__(self, mesh_shape, flow_block, heat_block):
        self.grp, self.gx, self.gy = (mesh_shape[name] for name in ("grp", "gx", "gy"))
        self.block_x, self.block_y, self.block_z = flow_block
        self.sub = self.gx * self.gy
        self.planes = self.block_z // self.sub
        self.halo = self.planes // 2
        self.fits = (
            self.block_y == SUBLANES
            and self.block_z == LANES
            and self.planes * self.sub == LANES
            and self.halo * 2 == self.planes
            and WINDOWS == 2
            and self.halo == STEPS * WINDOWS
            and self.sub >= 8
            and 2 * self.block_x == self.sub
            and self.block_x == self.grp
            and heat_block == (1, SUBLANES, self.grp * LANES)
            and self.sub & (self.sub - 1) == 0
            and self.grp & (self.grp - 1) == 0
            and self.gy % 2 == 0
            and self.sub % self.grp == 0
        )
        if self.fits:
            self.turn = self.sub // self.grp
            partners = [step for k in (1, 0) for step in range(self.sub - 2 + k, 1, -2)]
            partners.sort(key=lambda step: bin(step >> 1).count("1"))
            self.steps = [0, 1] + partners
            self.ring = [
                part * self.sub + self.round_plane((place - self.turn * part) % self.sub)
                for part in range(self.grp)
                for place in range(self.sub)
            ]

    def round_plane(self, number):
        x, y = number // self.gy, number % self.gy
        back = x % 2
        return x * self.gy + y + back * (self.gy - 1 - 2 * y)

    def holders(self, part):
        begin = self.sub * self.grp - self.turn * part
        mine = self.place_in_plane()
        return [
            jnp.bitwise_xor(self.round_plane(lax.rem(begin + place, self.sub)), mine)
            for place in range(self.sub)
        ]

    def place_in_plane(self):
        return lax.axis_index("gx") * self.gy + lax.axis_index("gy")


def lane_index():
    return lax.broadcasted_iota(jnp.int32, (SUBLANES, LANES), 1)


def row_index():
    return lax.broadcasted_iota(jnp.int32, (SUBLANES, LANES), 0)


def lane_roll(value, amount):
    amount = amount % LANES
    return value if amount == 0 else pltpu.roll(value, amount, 1)


def swap_groups(values, group):
    count = len(values)
    lane = lane_index()
    values = list(values)
    bit = 1
    while bit < count:
        low = (lane // (group * bit)) % 2 == 0
        for first in range(count):
            if first & bit == 0:
                a, b = values[first], values[first | bit]
                values[first] = jnp.where(low, a, lane_roll(b, group * bit))
                values[first | bit] = jnp.where(low, lane_roll(a, -group * bit), b)
        bit *= 2
    return values


SPEED_AT, SOLID_AT, HEAT_AT, RATE_AT, ROWS = 27, 30, 32, 39, 40
IN_PAIRS = 16
FLOW_PAIRS = 14


def pack_in(
    slab, levels_hbm, popul_hbm, speed_hbm, solid_hbm, heat_hbm, phase_hbm, sent, *scratch
):
    levels_ref, fields, solid_ref, heat_ref, phase_ref, sems = scratch
    copies = [
        pltpu.make_async_copy(source, target, sems.at[number])
        for number, (source, target) in enumerate(
            [
                (heat_hbm, heat_ref),
                (phase_hbm, phase_ref),
                (levels_hbm, levels_ref),
                (speed_hbm, fields.at[pl.ds(SPEED_AT, 3)]),
                (solid_hbm, solid_ref),
                (popul_hbm, fields.at[pl.ds(0, SPEED_AT)]),
            ]
        )
    ]
    for copy in copies:
        copy.start()
    for copy in copies[:3]:
        copy.wait()
    lane = lane_index()
    first = in_first_half(slab)
    columns = []
    for part in range(slab.grp):
        span = pl.ds(part * LANES, LANES)
        phase = phase_ref[0, :, span]
        chosen = jnp.zeros((SUBLANES, LANES), F32)
        for level in range(levels_ref.shape[0]):
            chosen = jnp.where(phase == level, levels_ref[level], chosen)
        columns.append([heat_ref[k, 0, :, span] for k in range(7)] + [1.0 / (0.5 + 4.0 * chosen)])
    for part in range(slab.grp):
        own, after = columns[part], columns[(part + 1) % slab.grp]
        before = columns[part - 1]
        beside = []
        for k in range(8):
            above = jnp.where(lane < slab.planes, after[k], own[k])
            below = jnp.where(lane >= LANES - slab.planes, before[k], own[k])
            beside.append(
                jnp.where(first, lane_roll(above, -slab.planes), lane_roll(below, slab.planes))
            )
        holders = slab.holders(part)
        for which, sources in enumerate((own, beside)):
            for place, value in enumerate(swap_groups(sources, slab.planes)):
                sent[holders[place], IN_PAIRS + 2 * part + which] = value
    for copy in copies[3:]:
        copy.wait()
    fields[SOLID_AT] = solid_ref[...].astype(F32)
    fields[SOLID_AT + 1] = jnp.zeros(solid_ref.shape, F32)
    holders = slab.holders(lax.axis_index("grp"))
    for pair in range(IN_PAIRS):
        sources = [fields[2 * pair + h, x] for x in range(slab.block_x) for h in range(2)]
        for place, value in enumerate(swap_groups(sources, slab.planes)):
            sent[holders[place], pair] = value


def in_first_half(slab):
    return lane_index() % slab.planes < slab.halo


def collect(slab, parts, came):
    mine = slab.place_in_plane()
    for part, step in zip(parts, slab.steps):
        came[jnp.bitwise_xor(mine, step)] = part[...]


def offer_halo(slab, *refs):
    parts, (came, low_out, high_out, *heat_outs) = refs[: slab.sub], refs[slab.sub :]
    collect(slab, parts, came)
    mine = lax.axis_index("grp")
    for step, heat_out in enumerate(heat_outs):
        slots = pl.ds(IN_PAIRS + 2 * jnp.bitwise_xor(mine, step), 2)
        for tile in range(slab.sub):
            heat_out[tile] = came[tile, slots]

    def one(number, _):
        tile = 2 * number
        first = in_first_half(slab)
        for pair in range(IN_PAIRS):
            a, b = came[tile, pair], came[tile + 1, pair]
            low_out[number, pair] = jnp.where(first, a, lane_roll(b, slab.halo))
            high_out[number, pair] = jnp.where(first, lane_roll(b, -slab.halo), a)
        return 0

    lax.fori_loop(0, slab.sub // 2, one, 0)


def make_heat_tiles(slab, parts, held, state):
    mine = lax.axis_index("grp")
    for step, part in enumerate(parts):
        held[jnp.bitwise_xor(mine, step)] = part[...]
    first = in_first_half(slab)
    for tile in range(slab.sub):
        sources = []
        for x in range(slab.block_x):
            after = held[(x + 1) % slab.block_x, tile, 1]
            sources += [held[x, tile, 0], jnp.where(first, held[x, tile, 1], after)]
        for k, value in enumerate(swap_groups(sources, slab.planes)):
            state[HEAT_AT + k, tile] = value


def make_tiles(slab, came, below_ref, above_ref, state):
    def one(number, _):
        first = in_first_half(slab)
        even = (lane_index() // slab.planes) % 2 == 0
        back = 2 * slab.planes
        for pair in range(IN_PAIRS):
            below, above = below_ref[number, pair], above_ref[number, pair]
            beside = (
                jnp.where(first, above, lane_roll(below, -back)),
                jnp.where(first, lane_roll(above, -slab.halo), lane_roll(below, slab.halo - back)),
            )
            for which in range(2):
                tile = 2 * number + which
                own, halo = came[tile, pair], beside[which]
                state[2 * pair, tile] = jnp.where(even, own, lane_roll(halo, slab.planes))
                state[2 * pair + 1, tile] = jnp.where(even, lane_roll(own, -slab.planes), halo)
        return 0

    lax.fori_loop(0, slab.sub // 2, one, 0)


def pack_out(slab, flow, came, tile, sent):
    even = (lane_index() // slab.planes) % 2 == 0
    flags = came[tile, SOLID_AT // 2]
    solid = jnp.where(even, flags, lane_roll(flags, slab.planes)) != 0.0
    partner = jnp.bitwise_xor(tile, slab.place_in_plane())
    for pair in range(FLOW_PAIRS):
        value = flow[2 * pair]
        if 2 * pair + 1 < len(flow):
            value = jnp.where(even, value, lane_roll(flow[2 * pair + 1], slab.planes))
        sent[partner, pair] = jnp.where(solid, came[tile, pair], value)


def add_heat(slab, sent_in, *refs):
    parts, (sent, packed, sem) = refs[: slab.grp], refs[slab.grp :]
    mine = slab.place_in_plane()
    for tile in range(slab.sub):
        for step in range(slab.grp):
            packed[jnp.bitwise_xor(mine, tile), step] = parts[step][tile]
    copy = pltpu.make_async_copy(packed, sent.at[:, pl.ds(FLOW_PAIRS, slab.grp)], sem)
    copy.start()
    copy.wait()


def unpack_out(slab, *refs):
    parts, (popul_hbm, thermal_hbm, came, popul, thermal, sems) = refs[: slab.sub], refs[slab.sub :]
    for part, step in zip(parts, slab.steps):
        came[step] = part[...]
    mine = lax.axis_index("grp")
    for step in range(slab.grp):
        part = jnp.bitwise_xor(mine, step)
        holders = slab.holders(part)
        span = pl.ds(pl.multiple_of(part * LANES, LANES), LANES)
        sources = [came[holders[place], FLOW_PAIRS + step] for place in range(slab.sub)]
        for k, value in enumerate(swap_groups(sources, slab.planes)[:7]):
            thermal[k, 0, :, span] = value
    copies = [pltpu.make_async_copy(thermal, thermal_hbm, sems.at[0])]
    copies[0].start()
    holders = slab.holders(mine)
    begin = 0
    for pair in range(FLOW_PAIRS):
        sources = [came[holders[place], pair] for place in range(slab.sub)]
        for number, value in enumerate(swap_groups(sources, slab.planes)):
            if 2 * pair + number % 2 < 27:
                popul[2 * pair + number % 2, number // 2] = value
        end = min(2 * pair + 2, 27)
        if pair % 4 == 3 or end == 27:
            rows = pl.ds(begin, end - begin)
            sem = sems.at[len(copies)]
            copies.append(pltpu.make_async_copy(popul.at[rows], popul_hbm.at[rows], sem))
            copies[-1].start()
            begin = end
    for copy in copies:
        copy.wait()


def forward3(values):
    for stride in (9, 3, 1):
        out = [None] * 27
        for n in range(27):
            if n // stride % 3 == 0:
                a, b, c = values[n], values[n + stride], values[n + 2 * stride]
                both = a + c
                out[n], out[n + stride], out[n + 2 * stride] = both + b, c - a, both
        values = out
    return values


def backward3(values):
    for stride in (9, 3, 1):
        out = [None] * 27
        for n in range(27):
            if n // stride % 3 == 0:
                a, b, c = values[n], values[n + stride], values[n + 2 * stride]
                even, odd = 0.5 * c, 0.5 * b
                out[n], out[n + stride], out[n + 2 * stride] = even - odd, a - c, even + odd
        values = out
    return values


def collide_tile(values, force, rate, solid):
    moments = forward3(values)
    density = moments[0]
    jx, jy, jz = moments[9], moments[3], moments[1] + 0.5 * force
    inverse = 1.0 / density
    flux = (jx, jy, jz)
    u = tuple(j * inverse for j in flux)
    third = 1.0 / 3.0
    base = {0: density}
    for k in (1, 2, 3):
        base[k] = density * third**k
    squares = [flux[d] * u[d] for d in range(3)]
    square_at = {}
    scaled = {}

    def scale(key, value, count):
        if count == 0:
            return value
        if (key, count) not in scaled:
            scaled[key, count] = value * third**count
        return scaled[key, count]

    cross = {(0, 1): jx * u[1], (0, 2): jx * u[2], (1, 2): jy * u[2]}
    out = [None] * 27
    for n in range(27):
        powers = (n // 9, n // 3 % 3, n % 3)
        if n in (0, 3, 9):
            out[n] = moments[n]
            continue
        if n == 1:
            out[n] = moments[n] + force
            continue
        odd = tuple(d for d in range(3) if powers[d] == 1)
        even = tuple(d for d in range(3) if powers[d] == 2)
        count = len(even)
        if len(odd) == 3:
            out[n] = moments[n] - rate(n) * moments[n]
            continue
        if len(odd) == 0:
            if even not in square_at:
                total = squares[even[0]]
                for d in even[1:]:
                    total = total + squares[d]
                square_at[even] = base[count] + (total * (3.0 * third**count) if count > 1 else total)
            level = square_at[even]
        elif len(odd) == 1:
            level = scale(odd, flux[odd[0]], count)
        else:
            level = scale(odd, cross[odd], count)
        out[n] = moments[n] - rate(n) * (moments[n] - level)
    out[26] = jnp.where(solid, jnp.nan, out[26])
    return backward3(out)


HEAT_OFFSETS = [(0, 0, 0), (1, 0, 0), (-1, 0, 0), (0, 1, 0), (0, -1, 0), (0, 0, 1), (0, 0, -1)]


def collide_flow(rates_ref, flow, force, solid, target, tile):
    for n, value in enumerate(collide_tile(flow, force, lambda n: rates_ref[n], solid)):
        target[n, tile] = value


def collide_heat(heat, omega, speeds, target, tile):
    total = heat[0]
    for k in range(1, 7):
        total = total + heat[k]
    side = 0.125 * total
    half = 0.5 * total
    for k in range(7):
        if k == 0:
            level = 0.25 * total
        else:
            drift = half * speeds[(k - 1) // 2]
            level = side + drift if k % 2 == 1 else side - drift
        target[k, tile] = heat[k] - (heat[k] - level) * omega


def stream(slab, post, tile, offsets):
    block_x, block_y = lax.div(tile, slab.gy), lax.rem(tile, slab.gy)
    x_of = {a: lax.rem(block_x + slab.gx - a, slab.gx) for a in (-1, 0, 1)}
    y_of = {b: lax.rem(block_y + slab.gy - b, slab.gy) for b in (-1, 0, 1)}
    row = row_index()
    per_x = 2 * slab.planes
    in_x = (lane_index() + slab.halo) % LANES // per_x
    last_x = {1: in_x == slab.block_x - 1, -1: in_x == 0}
    last_y = {1: row == SUBLANES - 1, -1: row == 0}

    def arrive(number, offset):
        a, b, c = offset

        def take(x):
            value = post[number, x_of[x] * slab.gy + block_y]
            if b != 0:
                other = post[number, x_of[x] * slab.gy + y_of[b]]
                value = jnp.where(last_y[b], other, value)
            return value

        value = take(0)
        if a != 0:
            value = jnp.where(last_x[a], take(a), value)
        if b != 0:
            value = pltpu.roll(value, b % SUBLANES, 0)
        return lane_roll(value, a * per_x + c)

    return [arrive(number, offset) for number, offset in enumerate(offsets)]


def stream_flow(slab, post, tile):
    return [
        jnp.where(value != value, post[26 - n, tile], value)
        for n, value in enumerate(stream(slab, post, tile, OFFSET_TABLE))
    ]


def over_tiles(slab, body, unroll=1):
    def one(tile, _):
        body(tile)
        return 0

    lax.fori_loop(0, slab.sub, one, 0, unroll=unroll)


def over_steps(count, body):
    def one(number, _):
        body(number)
        return 0

    lax.fori_loop(0, count, one, 0)


def first_window(slab, rates_hbm, came, below_ref, above_ref, *refs):
    heat_parts, refs = refs[: slab.grp], refs[slab.grp :]
    flow_out, keep_out, heat_outs = refs[0], refs[1], refs[2 : 2 + slab.grp]
    rates_ref, sem, state, flow_post, heat_post, heat_a, heat_b, held, came_heat = refs[
        2 + slab.grp :
    ]
    rates_copy = pltpu.make_async_copy(rates_hbm, rates_ref, sem)
    rates_copy.start()
    make_tiles(slab, came, below_ref, above_ref, state)
    make_heat_tiles(slab, heat_parts, came_heat, state)
    rates_copy.wait()

    def speeds_of(tile):
        return [state[SPEED_AT + d, tile] for d in range(3)]

    def begin(tile):
        solid = state[SOLID_AT, tile]
        heat = [state[HEAT_AT + k, tile] for k in range(7)]
        force = heat_force(heat)
        keep_out[0, tile] = force
        keep_out[1, tile] = solid
        flow = [state[n, tile] for n in range(27)]
        collide_flow(rates_ref, flow, force, solid != 0.0, flow_post.at[0], tile)
        collide_heat(heat, state[RATE_AT, tile], speeds_of(tile), heat_post.at[0], tile)

    over_tiles(slab, begin)

    def step(number):
        source = lax.rem(number, 2)

        def go_on(tile):
            flow = stream_flow(slab, flow_post.at[source], tile)
            solid = state[SOLID_AT, tile] != 0.0
            collide_flow(rates_ref, flow, keep_out[0, tile], solid, flow_post.at[1 - source], tile)
            heat = stream(slab, heat_post.at[source], tile, HEAT_OFFSETS)
            omega = state[RATE_AT, tile]
            collide_heat(heat, omega, speeds_of(tile), heat_post.at[1 - source], tile)

        over_tiles(slab, go_on)

    over_steps(STEPS - 1, step)
    source = (STEPS - 1) % 2

    def next_window(tile):
        flow = stream_flow(slab, flow_post.at[source], tile)
        heat = stream(slab, heat_post.at[source], tile, HEAT_OFFSETS)
        solid = state[SOLID_AT, tile] != 0.0
        speeds = [
            jnp.where(solid, 0.0, each) for each in flow_speed_tile(flow, keep_out[0, tile])
        ]
        for d in range(3):
            state[SPEED_AT + d, tile] = speeds[d]
        force = heat_force(heat)
        keep_out[0, tile] = force
        collide_flow(rates_ref, flow, force, solid, flow_out, tile)
        collide_heat(heat, state[RATE_AT, tile], speeds, heat_a, tile)

    over_tiles(slab, next_window)
    here, there = heat_a, heat_b
    for _ in range(STEPS - 1):

        def heat_alone(tile, here=here, there=there):
            heat = stream(slab, here, tile, HEAT_OFFSETS)
            collide_heat(heat, state[RATE_AT, tile], speeds_of(tile), there, tile)

        over_tiles(slab, heat_alone, unroll=4)
        here, there = there, here
    zero = jnp.zeros((SUBLANES, LANES), F32)

    def end_heat(tile):
        heat = stream(slab, here, tile, HEAT_OFFSETS)
        heat += [zero] * (slab.sub - 7)
        for x, value in enumerate(swap_groups(heat, slab.planes)[0::2]):
            held[x, tile] = value

    over_tiles(slab, end_heat, unroll=2)
    mine = lax.axis_index("grp")
    for step_number in range(slab.grp):
        heat_outs[step_number][...] = held[jnp.bitwise_xor(mine, step_number)]


def last_window(slab, rates_hbm, came, flow_in, keep_ref, sent, rates_ref, sem, flow_post):
    rates_copy = pltpu.make_async_copy(rates_hbm, rates_ref, sem)
    rates_copy.start()

    def copy(n, _):
        flow_post[0, n] = flow_in[n]
        return 0

    lax.fori_loop(0, 27, copy, 0, unroll=3)
    rates_copy.wait()

    def step(number):
        source = lax.rem(number, 2)

        def go_on(tile):
            flow = stream_flow(slab, flow_post.at[source], tile)
            solid = keep_ref[1, tile] != 0.0
            collide_flow(rates_ref, flow, keep_ref[0, tile], solid, flow_post.at[1 - source], tile)

        over_tiles(slab, go_on)

    over_steps(STEPS - 1, step)

    def end(tile):
        flow = stream_flow(slab, flow_post.at[(STEPS - 1) % 2], tile)
        pack_out(slab, flow, came, tile, sent)

    over_tiles(slab, end)


def heat_force(heat):
    total = heat[0]
    for k in range(1, 7):
        total = total + heat[k]
    return BUOYANCY * (total - REFERENCE_HEAT)


def flow_speed_tile(values, force):
    total = values[0]
    for n in range(1, 27):
        total = total + values[n]
    sums = []
    for d in range(3):
        plus, minus = None, None
        for n in range(27):
            part = OFFSET_TABLE[n][d]
            if part == 1:
                plus = values[n] if plus is None else plus + values[n]
            if part == -1:
                minus = values[n] if minus is None else minus + values[n]
        sums.append(plus - minus)
    sums[2] = sums[2] + 0.5 * force
    return [each / total for each in sums]


def local_call(body, slab, arrays, outs, scratch=(), in_hbm=0, carried=False, outs_in_hbm=False):
    def kernel(*refs):
        body(slab, *refs)

    return pl.pallas_call(
        kernel,
        out_shape=[jax.ShapeDtypeStruct(shape, F32) for shape in outs],
        in_specs=[
            pl.BlockSpec(
                memory_space=pltpu.HBM if i < in_hbm else pl.ANY if carried and i == 0 else pltpu.VMEM
            )
            for i in range(len(arrays))
        ],
        out_specs=[
            pl.BlockSpec(memory_space=pl.ANY if carried or outs_in_hbm else pltpu.VMEM)
        ]
        * len(outs),
        input_output_aliases={0: 0} if carried else {},
        scratch_shapes=[pltpu.VMEM(s, F32) if isinstance(s, tuple) else s for s in scratch],
        compiler_params=pltpu.CompilerParams(vmem_limit_bytes=24 * 1024 * 1024),
    )(
        *(
            pltpu.with_memory_space_constraint(array, pltpu.HBM) if i < in_hbm else array
            for i, array in enumerate(arrays)
        )
    )


RING = ("grp", "gx", "gy")


def exchange(slab, low, high):
    ring = slab.ring
    upward = [(ring[i - 1], ring[i]) for i in range(len(ring))]
    from_below = lax.ppermute(high, RING, upward)
    from_above = lax.ppermute(low, RING, [(b, a) for a, b in upward])
    return from_below, from_above


def across_plane(slab, sent):
    came = {0: sent[0]}
    for step in slab.steps[1:]:
        pairs = [(i, i ^ step) for i in range(slab.sub)]
        came[step] = lax.ppermute(sent[step], ("gx", "gy"), pairs)
    return [came[step] for step in slab.steps]


def across_planes(slab, parts):
    return [parts[0]] + [
        lax.ppermute(parts[step], "grp", [(i, i ^ step) for i in range(slab.grp)])
        for step in range(1, slab.grp)
    ]


def on_slabs(slab, populations, thermal, velocity_prev, solid, phase_ids, conductivity, rates):
    tile = (SUBLANES, LANES)

    def vmem_like(array):
        return pltpu.VMEM(array.shape, array.dtype)

    sent_shape = (slab.sub, IN_PAIRS + 2 * slab.grp) + tile
    (sent,) = local_call(
        pack_in,
        slab,
        [conductivity, populations, velocity_prev, solid, thermal, phase_ids],
        [sent_shape],
        [
            pltpu.SMEM(conductivity.shape, F32),
            (2 * IN_PAIRS,) + solid.shape,
            vmem_like(solid),
            vmem_like(thermal),
            vmem_like(phase_ids),
            pltpu.SemaphoreType.DMA((6,)),
        ],
        in_hbm=6,
    )
    plane = (slab.sub,) + tile
    halo_shape = (slab.sub // 2, IN_PAIRS) + tile
    heat_shape = (slab.sub, 2) + tile
    came, low, high, *parts = local_call(
        offer_halo,
        slab,
        across_plane(slab, sent),
        [sent_shape, halo_shape, halo_shape] + [heat_shape] * slab.grp,
    )
    below, above = exchange(slab, low, high)
    parts = across_planes(slab, parts)
    scalars = [pltpu.SMEM(rates.shape, F32), pltpu.SemaphoreType.DMA]
    flow, keep, *parts = local_call(
        first_window,
        slab,
        [rates, came, below, above] + parts,
        [(27,) + plane, (2,) + plane] + [plane] * slab.grp,
        scalars
        + [(ROWS,) + plane, (2, 27) + plane, (2, 7) + plane]
        + [(7,) + plane] * 2
        + [(slab.grp,) + plane, (slab.grp,) + heat_shape],
        in_hbm=1,
    )
    parts = across_planes(slab, parts)
    last_shape = (slab.sub, FLOW_PAIRS + slab.grp) + tile
    (sent,) = local_call(
        last_window,
        slab,
        [rates, came, flow, keep],
        [last_shape],
        scalars + [(2, 27) + plane],
        in_hbm=1,
    )
    (sent,) = local_call(
        add_heat,
        slab,
        [sent] + parts,
        [last_shape],
        [(slab.sub, slab.grp) + tile, pltpu.SemaphoreType.DMA],
        carried=True,
    )
    return tuple(
        local_call(
            unpack_out,
            slab,
            across_plane(slab, sent),
            [populations.shape, thermal.shape],
            [
                last_shape,
                populations.shape,
                thermal.shape,
                pltpu.SemaphoreType.DMA((1 + -(-FLOW_PAIRS // 4),)),
            ],
            outs_in_hbm=True,
        )
    )


def solution(mesh):
    in_specs = (
        P(None, "gx", "gy", "grp"),
        P(None, ("gx", "grp"), "gy", None),
        P(None, "gx", "gy", "grp"),
        P("gx", "gy", "grp"),
        P(("gx", "grp"), "gy", None),
        P(),
        P(),
    )
    out_specs = (P(None, "gx", "gy", "grp"), P(None, ("gx", "grp"), "gy", None))

    def per_device(populations, thermal, *others):
        slab = Slab(mesh.shape, populations.shape[1:], thermal.shape[1:])
        plan = (lambda *arrays: on_slabs(slab, *arrays)) if slab.fits else on_device
        return plan(populations, thermal, *others)

    return jax.shard_map(
        per_device, mesh=mesh, in_specs=in_specs, out_specs=out_specs, check_vma=False
    )
```

```python
import jax
import jax.numpy as jnp
import numpy as np
from jax import lax
from jax.experimental import pallas as pl
from jax.experimental.pallas import tpu as pltpu
from jax.sharding import PartitionSpec as P

STEPS = 4
WINDOWS = 2


HIGHEST = lax.Precision.HIGHEST
BUOYANCY = 0.03
REFERENCE_HEAT = 1.0
OFFSET_TABLE = [(number // 9 - 1, number // 3 % 3 - 1, number % 3 - 1) for number in range(27)]
LATTICE_WEIGHTS = np.array(
    [
        np.prod([2.0 / 3.0 if component == 0 else 1.0 / 6.0 for component in triple])
        for triple in OFFSET_TABLE
    ]
)
VANDERMONDE = np.array([[1.0, 1.0, 1.0], [-1.0, 0.0, 1.0], [1.0, 0.0, 1.0]])
VANDER_INVERSE = np.array([[0.0, -0.5, 0.5], [1.0, 0.0, -1.0], [0.0, 0.5, 0.5]])
MOMENT_MATRIX = np.kron(np.kron(VANDERMONDE, VANDERMONDE), VANDERMONDE)
MOMENT_INVERSE = np.kron(np.kron(VANDER_INVERSE, VANDER_INVERSE), VANDER_INVERSE)
RELAXED = np.array([0.0 if number in (0, 1, 3, 9) else 1.0 for number in range(27)])
SUMMING = np.concatenate([np.ones((1, 27)), 1.0 * np.array(OFFSET_TABLE).T], axis=0)
HEAT_WEIGHTS = np.array([0.25] + [0.125] * 6)


def from_behind(value, axis, steps):
    count = lax.axis_size(axis)
    pairs = [(source, (source + steps) % count) for source in range(count)]
    return lax.ppermute(value, axis, pairs)


def extended(cells, sides, width):
    for axis, dim in sides:
        count = lax.axis_size(axis)
        head = lax.slice_in_dim(cells, 0, width, axis=dim)
        tail = lax.slice_in_dim(cells, cells.shape[dim] - width, cells.shape[dim], axis=dim)
        cells = jnp.concatenate(
            [
                lax.ppermute(tail, axis, [(i, (i + 1) % count) for i in range(count)]),
                cells,
                lax.ppermute(head, axis, [((i + 1) % count, i) for i in range(count)]),
            ],
            axis=dim,
        )
    return cells


def flow_state(flat, heat_flat):
    sums = jnp.dot(jnp.asarray(SUMMING, jnp.float32), flat, precision=HIGHEST)
    density = sums[0]
    force = BUOYANCY * (heat_flat - REFERENCE_HEAT)
    speed = jnp.stack([sums[1], sums[2], sums[3] + 0.5 * force]) / density
    return (density, force, speed)


def collide(popul, heat, rates):
    flat = popul.reshape(27, -1)
    density, force, speed = flow_state(flat, heat.reshape(-1))
    along = jnp.dot(jnp.asarray(SUMMING[1:].T, jnp.float32), speed, precision=HIGHEST)
    square = jnp.sum(speed * speed, axis=0)
    balance = (
        density
        * jnp.asarray(LATTICE_WEIGHTS, jnp.float32)[:, None]
        * (1.0 + 3.0 * along + 4.5 * along * along - 1.5 * square)
    )
    scaled = (
        jnp.asarray(MOMENT_INVERSE, jnp.float32)
        * (rates * jnp.asarray(RELAXED, jnp.float32))[None, :]
    )
    relax = jnp.dot(scaled, jnp.asarray(MOMENT_MATRIX, jnp.float32), precision=HIGHEST)
    post = (
        flat
        - jnp.dot(relax, flat - balance, precision=HIGHEST)
        + jnp.asarray(MOMENT_INVERSE[:, 1], jnp.float32)[:, None] * force[None, :]
    )
    return post.reshape(popul.shape)


def flow_speed(popul, heat, solid):
    density, force, speed = flow_state(popul.reshape(27, -1), heat.reshape(-1))
    return jnp.where(solid[None] == 0, speed.reshape((3,) + solid.shape), 0.0)


def heat_collide(heat_pops, speed, relax_time):
    total = jnp.sum(heat_pops, axis=0)
    still = jnp.zeros_like(speed[0])
    along = jnp.stack([still, speed[0], -speed[0], speed[1], -speed[1], speed[2], -speed[2]])
    balance = (
        jnp.asarray(HEAT_WEIGHTS, jnp.float32)[:, None, None, None]
        * total[None]
        * (1.0 + 4.0 * along)
    )
    return heat_pops - (heat_pops - balance) / relax_time[None]


def relaxation(phase_ids, conductivity):
    levels = jnp.arange(conductivity.shape[0], dtype=jnp.int32)
    chosen = jnp.sum(
        jnp.where(
            phase_ids[None] == levels[:, None, None, None], conductivity[:, None, None, None], 0.0
        ),
        axis=0,
    )
    return 0.5 + 4.0 * chosen


def inner_window(padded, triple, sizes):
    return padded[
        1 - triple[0] : 1 - triple[0] + sizes[0],
        1 - triple[1] : 1 - triple[1] + sizes[1],
        1 - triple[2] : 1 - triple[2] + sizes[2],
    ]


def advance(grid, axis_number, send_up, send_down):
    space = 3 + axis_number
    length = grid.shape[space]
    rising = lax.index_in_dim(grid, 2, axis_number, keepdims=True)
    resting = lax.index_in_dim(grid, 1, axis_number, keepdims=True)
    falling = lax.index_in_dim(grid, 0, axis_number, keepdims=True)
    from_below = send_up(lax.slice_in_dim(rising, length - 1, length, axis=space))
    from_above = send_down(lax.slice_in_dim(falling, 0, 1, axis=space))
    rising = jnp.concatenate(
        [from_below, lax.slice_in_dim(rising, 0, length - 1, axis=space)], axis=space
    )
    falling = jnp.concatenate(
        [lax.slice_in_dim(falling, 1, length, axis=space), from_above], axis=space
    )
    return jnp.concatenate([falling, resting, rising], axis=axis_number)


def flow_arrivals(post):
    sizes = post.shape[1:]
    grid = post.reshape((3, 3, 3) + sizes)
    grid = advance(
        grid,
        0,
        lambda plane: from_behind(plane, "gx", 1),
        lambda plane: from_behind(plane, "gx", -1),
    )
    grid = advance(
        grid,
        1,
        lambda plane: from_behind(plane, "gy", 1),
        lambda plane: from_behind(plane, "gy", -1),
    )
    grid = advance(
        grid,
        2,
        lambda plane: from_behind(plane, "grp", 1),
        lambda plane: from_behind(plane, "grp", -1),
    )
    return grid.reshape(post.shape)


def stream_heat(post, grp_index, last_grp):
    length = post.shape[1]
    size_y = post.shape[2]
    eastward = post[1]
    westward = post[2]
    lower_first = from_behind(eastward, "grp", 1)
    lower_second = from_behind(lower_first, "gx", 1)
    entering = jnp.where(grp_index == 0, lower_second, lower_first)
    eastward = jnp.concatenate([entering, eastward[: length - 1]], axis=0)
    upper_first = from_behind(westward, "grp", -1)
    upper_second = from_behind(upper_first, "gx", -1)
    entering = jnp.where(grp_index == last_grp, upper_second, upper_first)
    westward = jnp.concatenate([westward[1:], entering], axis=0)
    sides = extended(post[3:5], (("gy", 2),), 1)
    northward = sides[0, :, 0:size_y]
    southward = sides[1, :, 2 : size_y + 2]
    upward = jnp.roll(post[5], 1, axis=2)
    downward = jnp.roll(post[6], -1, axis=2)
    return jnp.stack([post[0], eastward, westward, northward, southward, upward, downward])


def on_device(populations, thermal, velocity_prev, solid, phase_ids, conductivity, rates):
    padded_solid = extended(solid, (("grp", 2), ("gx", 0), ("gy", 1)), 1)
    sizes = solid.shape
    blocked = jnp.stack(
        [inner_window(padded_solid, OFFSET_TABLE[number], sizes) != 0 for number in range(27)]
    )
    fluid_cells = (solid == 0)[None]
    grp_index = lax.axis_index("grp")
    last_grp = lax.axis_size("grp") - 1
    relax_time = relaxation(phase_ids, conductivity)
    speed_brick = velocity_prev
    popul = populations
    heat_pops = thermal
    for window_number in range(WINDOWS):
        heat_brick = lax.all_to_all(
            jnp.sum(heat_pops, axis=0), "grp", split_axis=2, concat_axis=0, tiled=True
        )
        speed_column = lax.all_to_all(speed_brick, "grp", split_axis=1, concat_axis=3, tiled=True)
        for step_number in range(STEPS):
            post = collide(popul, heat_brick, rates)
            arrived = flow_arrivals(post)
            popul = jnp.where(fluid_cells, jnp.where(blocked, post[::-1], arrived), popul)
        for step_number in range(STEPS):
            heat_pops = stream_heat(
                heat_collide(heat_pops, speed_column, relax_time), grp_index, last_grp
            )
        if window_number + 1 < WINDOWS:
            speed_brick = flow_speed(popul, heat_brick, solid)
    return (popul, heat_pops)


SUBLANES = 8
LANES = 128
F32 = jnp.float32


class Slab:
    def __init__(self, mesh_shape, flow_block, heat_block):
        self.grp, self.gx, self.gy = (mesh_shape[name] for name in ("grp", "gx", "gy"))
        self.block_x, self.block_y, self.block_z = flow_block
        self.sub = self.gx * self.gy
        self.planes = self.block_z // self.sub
        self.halo = self.planes // 2
        self.fits = (
            self.block_y == SUBLANES
            and self.block_z == LANES
            and self.planes * self.sub == LANES
            and self.halo * 2 == self.planes
            and WINDOWS == 2
            and self.halo == STEPS * WINDOWS
            and self.sub >= 8
            and 2 * self.block_x == self.sub
            and self.block_x == self.grp
            and heat_block == (1, SUBLANES, self.grp * LANES)
            and self.sub & (self.sub - 1) == 0
            and self.grp & (self.grp - 1) == 0
            and self.gy % 2 == 0
            and self.sub % self.grp == 0
        )
        if self.fits:
            self.turn = self.sub // self.grp
            partners = [step for k in (1, 0) for step in range(self.sub - 2 + k, 1, -2)]
            partners.sort(key=lambda step: bin(step >> 1).count("1"))
            self.steps = [0, 1] + partners
            self.ring = [
                part * self.sub + self.round_plane((place - self.turn * part) % self.sub)
                for part in range(self.grp)
                for place in range(self.sub)
            ]

    def round_plane(self, number):
        x, y = number // self.gy, number % self.gy
        back = x % 2
        return x * self.gy + y + back * (self.gy - 1 - 2 * y)

    def holders(self, part):
        begin = self.sub * self.grp - self.turn * part
        mine = self.place_in_plane()
        return [
            jnp.bitwise_xor(self.round_plane(lax.rem(begin + place, self.sub)), mine)
            for place in range(self.sub)
        ]

    def place_in_plane(self):
        return lax.axis_index("gx") * self.gy + lax.axis_index("gy")


def lane_index():
    return lax.broadcasted_iota(jnp.int32, (SUBLANES, LANES), 1)


def row_index():
    return lax.broadcasted_iota(jnp.int32, (SUBLANES, LANES), 0)


def lane_roll(value, amount):
    amount = amount % LANES
    return value if amount == 0 else pltpu.roll(value, amount, 1)


def swap_groups(values, group):
    count = len(values)
    lane = lane_index()
    values = list(values)
    bit = 1
    while bit < count:
        low = (lane // (group * bit)) % 2 == 0
        for first in range(count):
            if first & bit == 0:
                a, b = values[first], values[first | bit]
                if 2 * group * bit == LANES:
                    crossed = lane_roll(jnp.where(low, b, a), group * bit)
                    values[first] = jnp.where(low, a, crossed)
                    values[first | bit] = jnp.where(low, crossed, b)
                    continue
                values[first] = jnp.where(low, a, lane_roll(b, group * bit))
                values[first | bit] = jnp.where(low, lane_roll(a, -group * bit), b)
        bit *= 2
    return values


SPEED_AT, SOLID_AT = 27, 30
IN_PAIRS = 16
FLOW_PAIRS = 14


def pack_in(
    slab, levels_hbm, popul_hbm, speed_hbm, solid_hbm, heat_hbm, phase_hbm, sent, *scratch
):
    levels_ref, fields, solid_ref, heat_ref, phase_ref, sems = scratch
    copies = [
        pltpu.make_async_copy(source, target, sems.at[number])
        for number, (source, target) in enumerate(
            [
                (heat_hbm, heat_ref),
                (phase_hbm, phase_ref),
                (levels_hbm, levels_ref),
                (speed_hbm, fields.at[pl.ds(SPEED_AT, 3)]),
                (solid_hbm, solid_ref),
                (popul_hbm, fields.at[pl.ds(0, SPEED_AT)]),
            ]
        )
    ]
    for copy in copies:
        copy.start()
    for copy in copies[:3]:
        copy.wait()
    lane = lane_index()
    first = in_first_half(slab)
    columns = []
    for part in range(slab.grp):
        span = pl.ds(part * LANES, LANES)
        phase = phase_ref[0, :, span]
        chosen = jnp.zeros((SUBLANES, LANES), F32)
        for level in range(levels_ref.shape[0]):
            chosen = jnp.where(phase == level, levels_ref[level], chosen)
        columns.append([heat_ref[k, 0, :, span] for k in range(7)] + [1.0 / (0.5 + 4.0 * chosen)])
    for part in range(slab.grp):
        own, after = columns[part], columns[(part + 1) % slab.grp]
        before = columns[part - 1]
        beside = []
        for k in range(8):
            above = jnp.where(lane < slab.planes, after[k], own[k])
            below = jnp.where(lane >= LANES - slab.planes, before[k], own[k])
            beside.append(
                jnp.where(first, lane_roll(above, -slab.planes), lane_roll(below, slab.planes))
            )
        holders = slab.holders(part)
        for which, sources in enumerate((own, beside)):
            for place, value in enumerate(swap_groups(sources, slab.planes)):
                sent[holders[place], IN_PAIRS + 2 * part + which] = value
    for copy in copies[3:]:
        copy.wait()
    fields[SOLID_AT] = solid_ref[...].astype(F32)
    fields[SOLID_AT + 1] = jnp.zeros(solid_ref.shape, F32)
    holders = slab.holders(lax.axis_index("grp"))
    for pair in range(IN_PAIRS):
        sources = [fields[2 * pair + h, x] for x in range(slab.block_x) for h in range(2)]
        for place, value in enumerate(swap_groups(sources, slab.planes)):
            sent[holders[place], pair] = value


def in_first_half(slab):
    return lane_index() % slab.planes < slab.halo


def collect(slab, parts, came):
    mine = slab.place_in_plane()
    for part, step in zip(parts, slab.steps):
        came[jnp.bitwise_xor(mine, step)] = part[...]


def offer_halo(slab, *refs):
    parts, (came, low_out, high_out, *heat_outs) = refs[: slab.sub], refs[slab.sub :]
    collect(slab, parts, came)
    mine = lax.axis_index("grp")
    for step, heat_out in enumerate(heat_outs):
        slots = pl.ds(IN_PAIRS + 2 * jnp.bitwise_xor(mine, step), 2)
        for tile in range(slab.sub):
            heat_out[tile] = came[tile, slots]

    def one(number, _):
        tile = 2 * number
        first = in_first_half(slab)
        for pair in range(IN_PAIRS):
            a, b = came[tile, pair], came[tile + 1, pair]
            low_out[number, pair] = jnp.where(first, a, lane_roll(b, slab.halo))
            high_out[number, pair] = jnp.where(first, lane_roll(b, -slab.halo), a)
        return 0

    lax.fori_loop(0, slab.sub // 2, one, 0)


def make_heat_tiles(slab, parts, held, heat_tiles):
    mine = lax.axis_index("grp")
    for step, part in enumerate(parts):
        held[jnp.bitwise_xor(mine, step)] = part[...]
    first = in_first_half(slab)
    for tile in range(slab.sub):
        sources = []
        for x in range(slab.block_x):
            after = held[(x + 1) % slab.block_x, tile, 1]
            sources += [held[x, tile, 0], jnp.where(first, held[x, tile, 1], after)]
        for k, value in enumerate(swap_groups(sources, slab.planes)):
            heat_tiles[k, tile] = value


def make_tiles(slab, came, below_ref, above_ref, state):
    def one(number, _):
        first = in_first_half(slab)
        even = (lane_index() // slab.planes) % 2 == 0
        back = 2 * slab.planes
        for pair in range(IN_PAIRS):
            below, above = below_ref[number, pair], above_ref[number, pair]
            beside = (
                jnp.where(first, above, lane_roll(below, -back)),
                jnp.where(first, lane_roll(above, -slab.halo), lane_roll(below, slab.halo - back)),
            )
            for which in range(2):
                tile = 2 * number + which
                own, halo = came[tile, pair], beside[which]
                state[2 * pair, tile] = jnp.where(even, own, lane_roll(halo, slab.planes))
                state[2 * pair + 1, tile] = jnp.where(even, lane_roll(own, -slab.planes), halo)
        return 0

    lax.fori_loop(0, slab.sub // 2, one, 0)


def pack_out(slab, flow, came, tile, sent):
    even = (lane_index() // slab.planes) % 2 == 0
    flags = came[tile, SOLID_AT // 2]
    solid = jnp.where(even, flags, lane_roll(flags, slab.planes)) != 0.0
    partner = jnp.bitwise_xor(tile, slab.place_in_plane())
    for pair in range(FLOW_PAIRS):
        value = flow[2 * pair]
        if 2 * pair + 1 < len(flow):
            value = jnp.where(even, value, lane_roll(flow[2 * pair + 1], slab.planes))
        sent[partner, pair] = jnp.where(solid, came[tile, pair], value)


def add_heat(slab, sent_in, *refs):
    parts, (sent, packed, sem) = refs[: slab.grp], refs[slab.grp :]
    mine = slab.place_in_plane()
    for tile in range(slab.sub):
        for step in range(slab.grp):
            packed[jnp.bitwise_xor(mine, tile), step] = parts[step][tile]
    copy = pltpu.make_async_copy(packed, sent.at[:, pl.ds(FLOW_PAIRS, slab.grp)], sem)
    copy.start()
    copy.wait()


def unpack_out(slab, *refs):
    parts, (popul_hbm, thermal_hbm, came, popul, thermal, sems) = refs[: slab.sub], refs[slab.sub :]
    for part, step in zip(parts, slab.steps):
        came[step] = part[...]
    mine = lax.axis_index("grp")
    for step in range(slab.grp):
        part = jnp.bitwise_xor(mine, step)
        holders = slab.holders(part)
        span = pl.ds(pl.multiple_of(part * LANES, LANES), LANES)
        sources = [came[holders[place], FLOW_PAIRS + step] for place in range(slab.sub)]
        for k, value in enumerate(swap_groups(sources, slab.planes)[:7]):
            thermal[k, 0, :, span] = value
    copies = [pltpu.make_async_copy(thermal, thermal_hbm, sems.at[0])]
    copies[0].start()
    holders = slab.holders(mine)
    begin = 0
    for pair in range(FLOW_PAIRS):
        sources = [came[holders[place], pair] for place in range(slab.sub)]
        for number, value in enumerate(swap_groups(sources, slab.planes)):
            if 2 * pair + number % 2 < 27:
                popul[2 * pair + number % 2, number // 2] = value
        end = min(2 * pair + 2, 27)
        if pair % 4 == 3 or end == 27:
            rows = pl.ds(begin, end - begin)
            sem = sems.at[len(copies)]
            copies.append(pltpu.make_async_copy(popul.at[rows], popul_hbm.at[rows], sem))
            copies[-1].start()
            begin = end
    for copy in copies:
        copy.wait()


def forward3(values):
    for stride in (9, 3, 1):
        out = [None] * 27
        for n in range(27):
            if n // stride % 3 == 0:
                a, b, c = values[n], values[n + stride], values[n + 2 * stride]
                both = a + c
                out[n], out[n + stride], out[n + 2 * stride] = both + b, c - a, both
        values = out
    return values


def backward3(values):
    for stride in (9, 3, 1):
        out = [None] * 27
        for n in range(27):
            if n // stride % 3 == 0:
                a, b, c = values[n], values[n + stride], values[n + 2 * stride]
                even, odd = 0.5 * c, 0.5 * b
                out[n], out[n + stride], out[n + 2 * stride] = even - odd, a - c, even + odd
        values = out
    return values


def collide_tile(values, force, rate, solid):
    moments = forward3(values)
    density = moments[0]
    jx, jy, jz = moments[9], moments[3], moments[1] + 0.5 * force
    inverse = 1.0 / density
    flux = (jx, jy, jz)
    u = tuple(j * inverse for j in flux)
    third = 1.0 / 3.0
    base = {0: density}
    for k in (1, 2, 3):
        base[k] = density * third**k
    squares = [flux[d] * u[d] for d in range(3)]
    square_at = {}
    scaled = {}

    def scale(key, value, count):
        if count == 0:
            return value
        if (key, count) not in scaled:
            scaled[key, count] = value * third**count
        return scaled[key, count]

    cross = {(0, 1): jx * u[1], (0, 2): jx * u[2], (1, 2): jy * u[2]}
    out = [None] * 27
    for n in range(27):
        powers = (n // 9, n // 3 % 3, n % 3)
        if n in (0, 3, 9):
            out[n] = moments[n]
            continue
        if n == 1:
            out[n] = moments[n] + force
            continue
        odd = tuple(d for d in range(3) if powers[d] == 1)
        even = tuple(d for d in range(3) if powers[d] == 2)
        count = len(even)
        if len(odd) == 3:
            out[n] = moments[n] - rate(n) * moments[n]
            continue
        if len(odd) == 0:
            if even not in square_at:
                total = squares[even[0]]
                for d in even[1:]:
                    total = total + squares[d]
                square_at[even] = base[count] + (total * (3.0 * third**count) if count > 1 else total)
            level = square_at[even]
        elif len(odd) == 1:
            level = scale(odd, flux[odd[0]], count)
        else:
            level = scale(odd, cross[odd], count)
        out[n] = moments[n] - rate(n) * (moments[n] - level)
    out[26] = jnp.where(solid, jnp.nan, out[26])
    return backward3(out)


HEAT_OFFSETS = [(0, 0, 0), (1, 0, 0), (-1, 0, 0), (0, 1, 0), (0, -1, 0), (0, 0, 1), (0, 0, -1)]


def collide_flow(rates_ref, flow, force, solid, target, tile):
    for n, value in enumerate(collide_tile(flow, force, lambda n: rates_ref[n], solid)):
        target[n, tile] = value


def collide_heat(heat, omega, speeds, target, tile):
    total = heat[0]
    for k in range(1, 7):
        total = total + heat[k]
    side = 0.125 * total
    half = 0.5 * total
    for k in range(7):
        if k == 0:
            level = 0.25 * total
        else:
            drift = half * speeds[(k - 1) // 2]
            level = side + drift if k % 2 == 1 else side - drift
        target[k, tile] = heat[k] - (heat[k] - level) * omega


def stream(slab, post, tile, offsets):
    block_x, block_y = lax.div(tile, slab.gy), lax.rem(tile, slab.gy)
    x_of = {a: lax.rem(block_x + slab.gx - a, slab.gx) for a in (-1, 0, 1)}
    y_of = {b: lax.rem(block_y + slab.gy - b, slab.gy) for b in (-1, 0, 1)}
    row = row_index()
    per_x = 2 * slab.planes
    in_x = (lane_index() + slab.halo) % LANES // per_x
    last_x = {1: in_x == slab.block_x - 1, -1: in_x == 0}
    last_y = {1: row == SUBLANES - 1, -1: row == 0}

    def arrive(number, offset):
        a, b, c = offset

        def take(x):
            value = post[number, x_of[x] * slab.gy + block_y]
            if b != 0:
                other = post[number, x_of[x] * slab.gy + y_of[b]]
                value = jnp.where(last_y[b], other, value)
            return value

        value = take(0)
        if a != 0:
            value = jnp.where(last_x[a], take(a), value)
        if b != 0:
            value = pltpu.roll(value, b % SUBLANES, 0)
        return lane_roll(value, a * per_x + c)

    return [arrive(number, offset) for number, offset in enumerate(offsets)]


def stream_flow(slab, post, tile):
    return [
        jnp.where(value != value, post[26 - n, tile], value)
        for n, value in enumerate(stream(slab, post, tile, OFFSET_TABLE))
    ]


def over_tiles(slab, body, unroll=1):
    def one(tile, _):
        body(tile)
        return 0

    lax.fori_loop(0, slab.sub, one, 0, unroll=unroll)


def over_steps(count, body):
    def one(number, _):
        body(number)
        return 0

    lax.fori_loop(0, count, one, 0)


def first_window(slab, rates_hbm, state, *refs):
    heat_parts, refs = refs[: slab.grp], refs[slab.grp :]
    flow_out, keep_out, heat_outs = refs[0], refs[1], refs[2 : 2 + slab.grp]
    (rates_ref, sem, speed, heat_tiles, flow_post, heat_post, heat_a, heat_b, held, came_heat) = refs[
        2 + slab.grp :
    ]
    rates_copy = pltpu.make_async_copy(rates_hbm, rates_ref, sem)
    rates_copy.start()
    make_heat_tiles(slab, heat_parts, came_heat, heat_tiles)
    rates_copy.wait()

    def speeds_of(tile):
        return [speed[d, tile] for d in range(3)]

    def begin(tile):
        solid = state[SOLID_AT, tile]
        heat = [heat_tiles[k, tile] for k in range(7)]
        for d in range(3):
            speed[d, tile] = state[SPEED_AT + d, tile]
        force = heat_force(heat)
        keep_out[0, tile] = force
        keep_out[1, tile] = solid
        flow = [state[n, tile] for n in range(27)]
        collide_flow(rates_ref, flow, force, solid != 0.0, flow_post.at[0], tile)
        collide_heat(heat, heat_tiles[7, tile], speeds_of(tile), heat_post.at[0], tile)

    over_tiles(slab, begin)

    def step(number):
        source = lax.rem(number, 2)

        def go_on(tile):
            flow = stream_flow(slab, flow_post.at[source], tile)
            solid = state[SOLID_AT, tile] != 0.0
            collide_flow(rates_ref, flow, keep_out[0, tile], solid, flow_post.at[1 - source], tile)
            heat = stream(slab, heat_post.at[source], tile, HEAT_OFFSETS)
            omega = heat_tiles[7, tile]
            collide_heat(heat, omega, speeds_of(tile), heat_post.at[1 - source], tile)

        over_tiles(slab, go_on)

    over_steps(STEPS - 1, step)
    source = (STEPS - 1) % 2

    def next_window(tile):
        flow = stream_flow(slab, flow_post.at[source], tile)
        heat = stream(slab, heat_post.at[source], tile, HEAT_OFFSETS)
        solid = state[SOLID_AT, tile] != 0.0
        speeds = [
            jnp.where(solid, 0.0, each) for each in flow_speed_tile(flow, keep_out[0, tile])
        ]
        for d in range(3):
            speed[d, tile] = speeds[d]
        force = heat_force(heat)
        keep_out[0, tile] = force
        collide_flow(rates_ref, flow, force, solid, flow_out, tile)
        collide_heat(heat, heat_tiles[7, tile], speeds, heat_a, tile)

    over_tiles(slab, next_window)
    here, there = heat_a, heat_b
    for _ in range(STEPS - 1):

        def heat_alone(tile, here=here, there=there):
            heat = stream(slab, here, tile, HEAT_OFFSETS)
            collide_heat(heat, heat_tiles[7, tile], speeds_of(tile), there, tile)

        over_tiles(slab, heat_alone, unroll=4)
        here, there = there, here
    zero = jnp.zeros((SUBLANES, LANES), F32)

    def end_heat(tile):
        heat = stream(slab, here, tile, HEAT_OFFSETS)
        heat += [zero] * (slab.sub - 7)
        for x, value in enumerate(swap_groups(heat, slab.planes)[0::2]):
            held[x, tile] = value

    over_tiles(slab, end_heat, unroll=2)
    mine = lax.axis_index("grp")
    for step_number in range(slab.grp):
        heat_outs[step_number][...] = held[jnp.bitwise_xor(mine, step_number)]


def last_window(slab, rates_hbm, came, flow_in, keep_ref, sent, rates_ref, sem, flow_post):
    rates_copy = pltpu.make_async_copy(rates_hbm, rates_ref, sem)
    rates_copy.start()

    def copy(n, _):
        flow_post[0, n] = flow_in[n]
        return 0

    lax.fori_loop(0, 27, copy, 0, unroll=3)
    rates_copy.wait()

    def step(number):
        source = lax.rem(number, 2)

        def go_on(tile):
            flow = stream_flow(slab, flow_post.at[source], tile)
            solid = keep_ref[1, tile] != 0.0
            collide_flow(rates_ref, flow, keep_ref[0, tile], solid, flow_post.at[1 - source], tile)

        over_tiles(slab, go_on)

    over_steps(STEPS - 1, step)

    def end(tile):
        flow = stream_flow(slab, flow_post.at[(STEPS - 1) % 2], tile)
        pack_out(slab, flow, came, tile, sent)

    over_tiles(slab, end)


def heat_force(heat):
    total = heat[0]
    for k in range(1, 7):
        total = total + heat[k]
    return BUOYANCY * (total - REFERENCE_HEAT)


def flow_speed_tile(values, force):
    total = values[0]
    for n in range(1, 27):
        total = total + values[n]
    sums = []
    for d in range(3):
        plus, minus = None, None
        for n in range(27):
            part = OFFSET_TABLE[n][d]
            if part == 1:
                plus = values[n] if plus is None else plus + values[n]
            if part == -1:
                minus = values[n] if minus is None else minus + values[n]
        sums.append(plus - minus)
    sums[2] = sums[2] + 0.5 * force
    return [each / total for each in sums]


def local_call(body, slab, arrays, outs, scratch=(), in_hbm=0, carried=False, outs_in_hbm=False):
    def kernel(*refs):
        body(slab, *refs)

    return pl.pallas_call(
        kernel,
        out_shape=[jax.ShapeDtypeStruct(shape, F32) for shape in outs],
        in_specs=[
            pl.BlockSpec(
                memory_space=pltpu.HBM if i < in_hbm else pl.ANY if carried and i == 0 else pltpu.VMEM
            )
            for i in range(len(arrays))
        ],
        out_specs=[
            pl.BlockSpec(memory_space=pl.ANY if carried or outs_in_hbm else pltpu.VMEM)
        ]
        * len(outs),
        input_output_aliases={0: 0} if carried else {},
        scratch_shapes=[pltpu.VMEM(s, F32) if isinstance(s, tuple) else s for s in scratch],
        compiler_params=pltpu.CompilerParams(vmem_limit_bytes=24 * 1024 * 1024),
    )(
        *(
            pltpu.with_memory_space_constraint(array, pltpu.HBM) if i < in_hbm else array
            for i, array in enumerate(arrays)
        )
    )


RING = ("grp", "gx", "gy")


def exchange(slab, low, high):
    ring = slab.ring
    upward = [(ring[i - 1], ring[i]) for i in range(len(ring))]
    from_below = lax.ppermute(high, RING, upward)
    from_above = lax.ppermute(low, RING, [(b, a) for a, b in upward])
    return from_below, from_above


def across_plane(slab, sent):
    came = {0: sent[0]}
    for step in slab.steps[1:]:
        pairs = [(i, i ^ step) for i in range(slab.sub)]
        came[step] = lax.ppermute(sent[step], ("gx", "gy"), pairs)
    return [came[step] for step in slab.steps]


def across_planes(slab, parts):
    return [parts[0]] + [
        lax.ppermute(parts[step], "grp", [(i, i ^ step) for i in range(slab.grp)])
        for step in range(1, slab.grp)
    ]


def on_slabs(slab, populations, thermal, velocity_prev, solid, phase_ids, conductivity, rates):
    tile = (SUBLANES, LANES)

    def vmem_like(array):
        return pltpu.VMEM(array.shape, array.dtype)

    sent_shape = (slab.sub, IN_PAIRS + 2 * slab.grp) + tile
    (sent,) = local_call(
        pack_in,
        slab,
        [conductivity, populations, velocity_prev, solid, thermal, phase_ids],
        [sent_shape],
        [
            pltpu.SMEM(conductivity.shape, F32),
            (2 * IN_PAIRS,) + solid.shape,
            vmem_like(solid),
            vmem_like(thermal),
            vmem_like(phase_ids),
            pltpu.SemaphoreType.DMA((6,)),
        ],
        in_hbm=6,
    )
    plane = (slab.sub,) + tile
    halo_shape = (slab.sub // 2, IN_PAIRS) + tile
    heat_shape = (slab.sub, 2) + tile
    came, low, high, *parts = local_call(
        offer_halo,
        slab,
        across_plane(slab, sent),
        [sent_shape, halo_shape, halo_shape] + [heat_shape] * slab.grp,
    )
    below, above = exchange(slab, low, high)
    parts = across_planes(slab, parts)
    (state,) = local_call(make_tiles, slab, [came, below, above], [(2 * IN_PAIRS,) + plane])
    scalars = [pltpu.SMEM(rates.shape, F32), pltpu.SemaphoreType.DMA]
    flow, keep, *parts = local_call(
        first_window,
        slab,
        [rates, state] + parts,
        [(27,) + plane, (2,) + plane] + [plane] * slab.grp,
        scalars
        + [(3,) + plane, (8,) + plane, (2, 27) + plane, (2, 7) + plane]
        + [(7,) + plane] * 2
        + [(slab.grp,) + plane, (slab.grp,) + heat_shape],
        in_hbm=1,
    )
    parts = across_planes(slab, parts)
    last_shape = (slab.sub, FLOW_PAIRS + slab.grp) + tile
    (sent,) = local_call(
        last_window,
        slab,
        [rates, came, flow, keep],
        [last_shape],
        scalars + [(2, 27) + plane],
        in_hbm=1,
    )
    (sent,) = local_call(
        add_heat,
        slab,
        [sent] + parts,
        [last_shape],
        [(slab.sub, slab.grp) + tile, pltpu.SemaphoreType.DMA],
        carried=True,
    )
    return tuple(
        local_call(
            unpack_out,
            slab,
            across_plane(slab, sent),
            [populations.shape, thermal.shape],
            [
                last_shape,
                populations.shape,
                thermal.shape,
                pltpu.SemaphoreType.DMA((1 + -(-FLOW_PAIRS // 4),)),
            ],
            outs_in_hbm=True,
        )
    )


def solution(mesh):
    in_specs = (
        P(None, "gx", "gy", "grp"),
        P(None, ("gx", "grp"), "gy", None),
        P(None, "gx", "gy", "grp"),
        P("gx", "gy", "grp"),
        P(("gx", "grp"), "gy", None),
        P(),
        P(),
    )
    out_specs = (P(None, "gx", "gy", "grp"), P(None, ("gx", "grp"), "gy", None))

    def per_device(populations, thermal, *others):
        slab = Slab(mesh.shape, populations.shape[1:], thermal.shape[1:])
        plan = (lambda *arrays: on_slabs(slab, *arrays)) if slab.fits else on_device
        return plan(populations, thermal, *others)

    return jax.shard_map(
        per_device, mesh=mesh, in_specs=in_specs, out_specs=out_specs, check_vma=False
    )
```

```python
import jax
import jax.numpy as jnp
import numpy as np
from jax import lax
from jax.experimental import pallas as pl
from jax.experimental.pallas import tpu as pltpu
from jax.sharding import PartitionSpec as P

STEPS = 4
WINDOWS = 2


HIGHEST = lax.Precision.HIGHEST
BUOYANCY = 0.03
REFERENCE_HEAT = 1.0
OFFSET_TABLE = [(number // 9 - 1, number // 3 % 3 - 1, number % 3 - 1) for number in range(27)]
LATTICE_WEIGHTS = np.array(
    [
        np.prod([2.0 / 3.0 if component == 0 else 1.0 / 6.0 for component in triple])
        for triple in OFFSET_TABLE
    ]
)
VANDERMONDE = np.array([[1.0, 1.0, 1.0], [-1.0, 0.0, 1.0], [1.0, 0.0, 1.0]])
VANDER_INVERSE = np.array([[0.0, -0.5, 0.5], [1.0, 0.0, -1.0], [0.0, 0.5, 0.5]])
MOMENT_MATRIX = np.kron(np.kron(VANDERMONDE, VANDERMONDE), VANDERMONDE)
MOMENT_INVERSE = np.kron(np.kron(VANDER_INVERSE, VANDER_INVERSE), VANDER_INVERSE)
RELAXED = np.array([0.0 if number in (0, 1, 3, 9) else 1.0 for number in range(27)])
SUMMING = np.concatenate([np.ones((1, 27)), 1.0 * np.array(OFFSET_TABLE).T], axis=0)
HEAT_WEIGHTS = np.array([0.25] + [0.125] * 6)


def from_behind(value, axis, steps):
    count = lax.axis_size(axis)
    pairs = [(source, (source + steps) % count) for source in range(count)]
    return lax.ppermute(value, axis, pairs)


def extended(cells, sides, width):
    for axis, dim in sides:
        count = lax.axis_size(axis)
        head = lax.slice_in_dim(cells, 0, width, axis=dim)
        tail = lax.slice_in_dim(cells, cells.shape[dim] - width, cells.shape[dim], axis=dim)
        cells = jnp.concatenate(
            [
                lax.ppermute(tail, axis, [(i, (i + 1) % count) for i in range(count)]),
                cells,
                lax.ppermute(head, axis, [((i + 1) % count, i) for i in range(count)]),
            ],
            axis=dim,
        )
    return cells


def flow_state(flat, heat_flat):
    sums = jnp.dot(jnp.asarray(SUMMING, jnp.float32), flat, precision=HIGHEST)
    density = sums[0]
    force = BUOYANCY * (heat_flat - REFERENCE_HEAT)
    speed = jnp.stack([sums[1], sums[2], sums[3] + 0.5 * force]) / density
    return (density, force, speed)


def collide(popul, heat, rates):
    flat = popul.reshape(27, -1)
    density, force, speed = flow_state(flat, heat.reshape(-1))
    along = jnp.dot(jnp.asarray(SUMMING[1:].T, jnp.float32), speed, precision=HIGHEST)
    square = jnp.sum(speed * speed, axis=0)
    balance = (
        density
        * jnp.asarray(LATTICE_WEIGHTS, jnp.float32)[:, None]
        * (1.0 + 3.0 * along + 4.5 * along * along - 1.5 * square)
    )
    scaled = (
        jnp.asarray(MOMENT_INVERSE, jnp.float32)
        * (rates * jnp.asarray(RELAXED, jnp.float32))[None, :]
    )
    relax = jnp.dot(scaled, jnp.asarray(MOMENT_MATRIX, jnp.float32), precision=HIGHEST)
    post = (
        flat
        - jnp.dot(relax, flat - balance, precision=HIGHEST)
        + jnp.asarray(MOMENT_INVERSE[:, 1], jnp.float32)[:, None] * force[None, :]
    )
    return post.reshape(popul.shape)


def flow_speed(popul, heat, solid):
    density, force, speed = flow_state(popul.reshape(27, -1), heat.reshape(-1))
    return jnp.where(solid[None] == 0, speed.reshape((3,) + solid.shape), 0.0)


def heat_collide(heat_pops, speed, relax_time):
    total = jnp.sum(heat_pops, axis=0)
    still = jnp.zeros_like(speed[0])
    along = jnp.stack([still, speed[0], -speed[0], speed[1], -speed[1], speed[2], -speed[2]])
    balance = (
        jnp.asarray(HEAT_WEIGHTS, jnp.float32)[:, None, None, None]
        * total[None]
        * (1.0 + 4.0 * along)
    )
    return heat_pops - (heat_pops - balance) / relax_time[None]


def relaxation(phase_ids, conductivity):
    levels = jnp.arange(conductivity.shape[0], dtype=jnp.int32)
    chosen = jnp.sum(
        jnp.where(
            phase_ids[None] == levels[:, None, None, None], conductivity[:, None, None, None], 0.0
        ),
        axis=0,
    )
    return 0.5 + 4.0 * chosen


def inner_window(padded, triple, sizes):
    return padded[
        1 - triple[0] : 1 - triple[0] + sizes[0],
        1 - triple[1] : 1 - triple[1] + sizes[1],
        1 - triple[2] : 1 - triple[2] + sizes[2],
    ]


def advance(grid, axis_number, send_up, send_down):
    space = 3 + axis_number
    length = grid.shape[space]
    rising = lax.index_in_dim(grid, 2, axis_number, keepdims=True)
    resting = lax.index_in_dim(grid, 1, axis_number, keepdims=True)
    falling = lax.index_in_dim(grid, 0, axis_number, keepdims=True)
    from_below = send_up(lax.slice_in_dim(rising, length - 1, length, axis=space))
    from_above = send_down(lax.slice_in_dim(falling, 0, 1, axis=space))
    rising = jnp.concatenate(
        [from_below, lax.slice_in_dim(rising, 0, length - 1, axis=space)], axis=space
    )
    falling = jnp.concatenate(
        [lax.slice_in_dim(falling, 1, length, axis=space), from_above], axis=space
    )
    return jnp.concatenate([falling, resting, rising], axis=axis_number)


def flow_arrivals(post):
    sizes = post.shape[1:]
    grid = post.reshape((3, 3, 3) + sizes)
    grid = advance(
        grid,
        0,
        lambda plane: from_behind(plane, "gx", 1),
        lambda plane: from_behind(plane, "gx", -1),
    )
    grid = advance(
        grid,
        1,
        lambda plane: from_behind(plane, "gy", 1),
        lambda plane: from_behind(plane, "gy", -1),
    )
    grid = advance(
        grid,
        2,
        lambda plane: from_behind(plane, "grp", 1),
        lambda plane: from_behind(plane, "grp", -1),
    )
    return grid.reshape(post.shape)


def stream_heat(post, grp_index, last_grp):
    length = post.shape[1]
    size_y = post.shape[2]
    eastward = post[1]
    westward = post[2]
    lower_first = from_behind(eastward, "grp", 1)
    lower_second = from_behind(lower_first, "gx", 1)
    entering = jnp.where(grp_index == 0, lower_second, lower_first)
    eastward = jnp.concatenate([entering, eastward[: length - 1]], axis=0)
    upper_first = from_behind(westward, "grp", -1)
    upper_second = from_behind(upper_first, "gx", -1)
    entering = jnp.where(grp_index == last_grp, upper_second, upper_first)
    westward = jnp.concatenate([westward[1:], entering], axis=0)
    sides = extended(post[3:5], (("gy", 2),), 1)
    northward = sides[0, :, 0:size_y]
    southward = sides[1, :, 2 : size_y + 2]
    upward = jnp.roll(post[5], 1, axis=2)
    downward = jnp.roll(post[6], -1, axis=2)
    return jnp.stack([post[0], eastward, westward, northward, southward, upward, downward])


def on_device(populations, thermal, velocity_prev, solid, phase_ids, conductivity, rates):
    padded_solid = extended(solid, (("grp", 2), ("gx", 0), ("gy", 1)), 1)
    sizes = solid.shape
    blocked = jnp.stack(
        [inner_window(padded_solid, OFFSET_TABLE[number], sizes) != 0 for number in range(27)]
    )
    fluid_cells = (solid == 0)[None]
    grp_index = lax.axis_index("grp")
    last_grp = lax.axis_size("grp") - 1
    relax_time = relaxation(phase_ids, conductivity)
    speed_brick = velocity_prev
    popul = populations
    heat_pops = thermal
    for window_number in range(WINDOWS):
        heat_brick = lax.all_to_all(
            jnp.sum(heat_pops, axis=0), "grp", split_axis=2, concat_axis=0, tiled=True
        )
        speed_column = lax.all_to_all(speed_brick, "grp", split_axis=1, concat_axis=3, tiled=True)
        for step_number in range(STEPS):
            post = collide(popul, heat_brick, rates)
            arrived = flow_arrivals(post)
            popul = jnp.where(fluid_cells, jnp.where(blocked, post[::-1], arrived), popul)
        for step_number in range(STEPS):
            heat_pops = stream_heat(
                heat_collide(heat_pops, speed_column, relax_time), grp_index, last_grp
            )
        if window_number + 1 < WINDOWS:
            speed_brick = flow_speed(popul, heat_brick, solid)
    return (popul, heat_pops)


SUBLANES = 8
LANES = 128
F32 = jnp.float32


class Slab:
    def __init__(self, mesh_shape, flow_block, heat_block):
        self.grp, self.gx, self.gy = (mesh_shape[name] for name in ("grp", "gx", "gy"))
        self.block_x, self.block_y, self.block_z = flow_block
        self.sub = self.gx * self.gy
        self.planes = self.block_z // self.sub
        self.halo = self.planes // 2
        self.fits = (
            self.block_y == SUBLANES
            and self.block_z == LANES
            and self.planes * self.sub == LANES
            and self.halo * 2 == self.planes
            and WINDOWS == 2
            and self.halo == STEPS * WINDOWS
            and self.sub >= 8
            and 2 * self.block_x == self.sub
            and self.block_x == self.grp
            and heat_block == (1, SUBLANES, self.grp * LANES)
            and self.sub & (self.sub - 1) == 0
            and self.grp & (self.grp - 1) == 0
            and self.gy % 2 == 0
            and self.sub % self.grp == 0
        )
        if self.fits:
            self.turn = self.sub // self.grp
            partners = [step for k in (1, 0) for step in range(self.sub - 2 + k, 1, -2)]
            partners.sort(key=lambda step: bin(step >> 1).count("1"))
            self.steps = [0, 1] + partners
            self.ring = [
                part * self.sub + self.round_plane((place - self.turn * part) % self.sub)
                for part in range(self.grp)
                for place in range(self.sub)
            ]

    def round_plane(self, number):
        x, y = number // self.gy, number % self.gy
        back = x % 2
        return x * self.gy + y + back * (self.gy - 1 - 2 * y)

    def holders(self, part):
        begin = self.sub * self.grp - self.turn * part
        mine = self.place_in_plane()
        return [
            jnp.bitwise_xor(self.round_plane(lax.rem(begin + place, self.sub)), mine)
            for place in range(self.sub)
        ]

    def place_in_plane(self):
        return lax.axis_index("gx") * self.gy + lax.axis_index("gy")


def lane_index():
    return lax.broadcasted_iota(jnp.int32, (SUBLANES, LANES), 1)


def row_index():
    return lax.broadcasted_iota(jnp.int32, (SUBLANES, LANES), 0)


def lane_roll(value, amount):
    amount = amount % LANES
    return value if amount == 0 else pltpu.roll(value, amount, 1)


def swap_groups(values, group):
    count = len(values)
    lane = lane_index()
    values = list(values)
    bit = 1
    while bit < count:
        low = (lane // (group * bit)) % 2 == 0
        for first in range(count):
            if first & bit == 0:
                a, b = values[first], values[first | bit]
                if 2 * group * bit == LANES:
                    crossed = lane_roll(jnp.where(low, b, a), group * bit)
                    values[first] = jnp.where(low, a, crossed)
                    values[first | bit] = jnp.where(low, crossed, b)
                    continue
                values[first] = jnp.where(low, a, lane_roll(b, group * bit))
                values[first | bit] = jnp.where(low, lane_roll(a, -group * bit), b)
        bit *= 2
    return values


SPEED_AT, SOLID_AT = 27, 30
IN_PAIRS = 16
FLOW_PAIRS = 14


def pack_in(
    slab, levels_hbm, popul_hbm, speed_hbm, solid_hbm, heat_hbm, phase_hbm, sent, *scratch
):
    levels_ref, fields, solid_ref, heat_ref, phase_ref, sems = scratch
    copies = [
        pltpu.make_async_copy(source, target, sems.at[number])
        for number, (source, target) in enumerate(
            [
                (heat_hbm, heat_ref),
                (phase_hbm, phase_ref),
                (levels_hbm, levels_ref),
                (speed_hbm, fields.at[pl.ds(SPEED_AT, 3)]),
                (solid_hbm, solid_ref),
                (popul_hbm, fields.at[pl.ds(0, SPEED_AT)]),
            ]
        )
    ]
    for copy in copies:
        copy.start()
    for copy in copies[:3]:
        copy.wait()
    lane = lane_index()
    first = in_first_half(slab)
    columns = []
    for part in range(slab.grp):
        span = pl.ds(part * LANES, LANES)
        phase = phase_ref[0, :, span]
        chosen = jnp.zeros((SUBLANES, LANES), F32)
        for level in range(levels_ref.shape[0]):
            chosen = jnp.where(phase == level, levels_ref[level], chosen)
        columns.append([heat_ref[k, 0, :, span] for k in range(7)] + [1.0 / (0.5 + 4.0 * chosen)])
    for part in range(slab.grp):
        own, after = columns[part], columns[(part + 1) % slab.grp]
        before = columns[part - 1]
        beside = []
        for k in range(8):
            above = jnp.where(lane < slab.planes, after[k], own[k])
            below = jnp.where(lane >= LANES - slab.planes, before[k], own[k])
            beside.append(
                jnp.where(first, lane_roll(above, -slab.planes), lane_roll(below, slab.planes))
            )
        holders = slab.holders(part)
        for which, sources in enumerate((own, beside)):
            for place, value in enumerate(swap_groups(sources, slab.planes)):
                sent[holders[place], IN_PAIRS + 2 * part + which] = value
    for copy in copies[3:]:
        copy.wait()
    fields[SOLID_AT] = solid_ref[...].astype(F32)
    fields[SOLID_AT + 1] = jnp.zeros(solid_ref.shape, F32)
    holders = slab.holders(lax.axis_index("grp"))
    for pair in range(IN_PAIRS):
        sources = [fields[2 * pair + h, x] for x in range(slab.block_x) for h in range(2)]
        for place, value in enumerate(swap_groups(sources, slab.planes)):
            sent[holders[place], pair] = value


def in_first_half(slab):
    return lane_index() % slab.planes < slab.halo


def collect(slab, parts, came):
    mine = slab.place_in_plane()
    for part, step in zip(parts, slab.steps):
        came[jnp.bitwise_xor(mine, step)] = part[...]


def offer_halo(slab, *refs):
    parts, (came, low_out, high_out, *heat_outs) = refs[: slab.sub], refs[slab.sub :]
    collect(slab, parts, came)
    mine = lax.axis_index("grp")
    for step, heat_out in enumerate(heat_outs):
        slots = pl.ds(IN_PAIRS + 2 * jnp.bitwise_xor(mine, step), 2)
        for tile in range(slab.sub):
            heat_out[tile] = came[tile, slots]

    def one(number, _):
        tile = 2 * number
        first = in_first_half(slab)
        for pair in range(IN_PAIRS):
            a, b = came[tile, pair], came[tile + 1, pair]
            low_out[number, pair] = jnp.where(first, a, lane_roll(b, slab.halo))
            high_out[number, pair] = jnp.where(first, lane_roll(b, -slab.halo), a)
        return 0

    lax.fori_loop(0, slab.sub // 2, one, 0)


def make_heat_tiles(slab, parts, held, heat_tiles):
    mine = lax.axis_index("grp")
    for step, part in enumerate(parts):
        held[jnp.bitwise_xor(mine, step)] = part[...]
    first = in_first_half(slab)
    for tile in range(slab.sub):
        sources = []
        for x in range(slab.block_x):
            after = held[(x + 1) % slab.block_x, tile, 1]
            sources += [held[x, tile, 0], jnp.where(first, held[x, tile, 1], after)]
        for k, value in enumerate(swap_groups(sources, slab.planes)):
            heat_tiles[k, tile] = value


def make_tiles(slab, came, below_ref, above_ref, state):
    def one(number, _):
        first = in_first_half(slab)
        even = (lane_index() // slab.planes) % 2 == 0
        back = 2 * slab.planes
        for pair in range(IN_PAIRS):
            below, above = below_ref[number, pair], above_ref[number, pair]
            beside = (
                jnp.where(first, above, lane_roll(below, -back)),
                jnp.where(first, lane_roll(above, -slab.halo), lane_roll(below, slab.halo - back)),
            )
            for which in range(2):
                tile = 2 * number + which
                own, halo = came[tile, pair], beside[which]
                state[2 * pair, tile] = jnp.where(even, own, lane_roll(halo, slab.planes))
                state[2 * pair + 1, tile] = jnp.where(even, lane_roll(own, -slab.planes), halo)
        return 0

    lax.fori_loop(0, slab.sub // 2, one, 0)


def pack_out(slab, flow, came, tile, sent):
    even = (lane_index() // slab.planes) % 2 == 0
    flags = came[tile, SOLID_AT // 2]
    solid = jnp.where(even, flags, lane_roll(flags, slab.planes)) != 0.0
    partner = jnp.bitwise_xor(tile, slab.place_in_plane())
    for pair in range(FLOW_PAIRS):
        value = flow[2 * pair]
        if 2 * pair + 1 < len(flow):
            value = jnp.where(even, value, lane_roll(flow[2 * pair + 1], slab.planes))
        sent[partner, pair] = jnp.where(solid, came[tile, pair], value)


def add_heat(slab, sent_in, *refs):
    parts, (sent, packed, sem) = refs[: slab.grp], refs[slab.grp :]
    mine = slab.place_in_plane()
    for tile in range(slab.sub):
        for step in range(slab.grp):
            packed[jnp.bitwise_xor(mine, tile), step] = parts[step][tile]
    copy = pltpu.make_async_copy(packed, sent.at[:, pl.ds(FLOW_PAIRS, slab.grp)], sem)
    copy.start()
    copy.wait()


def unpack_out(slab, *refs):
    parts, (popul_hbm, thermal_hbm, came, popul, thermal, sems) = refs[: slab.sub], refs[slab.sub :]
    for part, step in zip(parts, slab.steps):
        came[step] = part[...]
    mine = lax.axis_index("grp")
    for step in range(slab.grp):
        part = jnp.bitwise_xor(mine, step)
        holders = slab.holders(part)
        span = pl.ds(pl.multiple_of(part * LANES, LANES), LANES)
        sources = [came[holders[place], FLOW_PAIRS + step] for place in range(slab.sub)]
        for k, value in enumerate(swap_groups(sources, slab.planes)[:7]):
            thermal[k, 0, :, span] = value
    copies = [pltpu.make_async_copy(thermal, thermal_hbm, sems.at[0])]
    copies[0].start()
    holders = slab.holders(mine)
    begin = 0
    for pair in range(FLOW_PAIRS):
        sources = [came[holders[place], pair] for place in range(slab.sub)]
        for number, value in enumerate(swap_groups(sources, slab.planes)):
            if 2 * pair + number % 2 < 27:
                popul[2 * pair + number % 2, number // 2] = value
        end = min(2 * pair + 2, 27)
        if pair % 4 == 3 or end == 27:
            rows = pl.ds(begin, end - begin)
            sem = sems.at[len(copies)]
            copies.append(pltpu.make_async_copy(popul.at[rows], popul_hbm.at[rows], sem))
            copies[-1].start()
            begin = end
    for copy in copies:
        copy.wait()


def forward3(values):
    for stride in (9, 3, 1):
        out = [None] * 27
        for n in range(27):
            if n // stride % 3 == 0:
                a, b, c = values[n], values[n + stride], values[n + 2 * stride]
                both = a + c
                out[n], out[n + stride], out[n + 2 * stride] = both + b, c - a, both
        values = out
    return values


def backward3(values):
    for stride in (9, 3, 1):
        out = [None] * 27
        for n in range(27):
            if n // stride % 3 == 0:
                a, b, c = values[n], values[n + stride], values[n + 2 * stride]
                even, odd = 0.5 * c, 0.5 * b
                out[n], out[n + stride], out[n + 2 * stride] = even - odd, a - c, even + odd
        values = out
    return values


def collide_tile(values, force, rate, solid):
    moments = forward3(values)
    density = moments[0]
    jx, jy, jz = moments[9], moments[3], moments[1] + 0.5 * force
    inverse = 1.0 / density
    flux = (jx, jy, jz)
    u = tuple(j * inverse for j in flux)
    third = 1.0 / 3.0
    base = {0: density}
    for k in (1, 2, 3):
        base[k] = density * third**k
    squares = [flux[d] * u[d] for d in range(3)]
    square_at = {}
    scaled = {}

    def scale(key, value, count):
        if count == 0:
            return value
        if (key, count) not in scaled:
            scaled[key, count] = value * third**count
        return scaled[key, count]

    cross = {(0, 1): jx * u[1], (0, 2): jx * u[2], (1, 2): jy * u[2]}
    out = [None] * 27
    for n in range(27):
        powers = (n // 9, n // 3 % 3, n % 3)
        if n in (0, 3, 9):
            out[n] = moments[n]
            continue
        if n == 1:
            out[n] = moments[n] + force
            continue
        odd = tuple(d for d in range(3) if powers[d] == 1)
        even = tuple(d for d in range(3) if powers[d] == 2)
        count = len(even)
        if len(odd) == 3:
            out[n] = moments[n] - rate(n) * moments[n]
            continue
        if len(odd) == 0:
            if even not in square_at:
                total = squares[even[0]]
                for d in even[1:]:
                    total = total + squares[d]
                square_at[even] = base[count] + (total * (3.0 * third**count) if count > 1 else total)
            level = square_at[even]
        elif len(odd) == 1:
            level = scale(odd, flux[odd[0]], count)
        else:
            level = scale(odd, cross[odd], count)
        out[n] = moments[n] - rate(n) * (moments[n] - level)
    out[26] = jnp.where(solid, jnp.nan, out[26])
    return backward3(out)


HEAT_OFFSETS = [(0, 0, 0), (1, 0, 0), (-1, 0, 0), (0, 1, 0), (0, -1, 0), (0, 0, 1), (0, 0, -1)]


def collide_flow(rates_ref, flow, force, solid, target, tile):
    for n, value in enumerate(collide_tile(flow, force, lambda n: rates_ref[n], solid)):
        target[n, tile] = value


def collide_heat(heat, omega, speeds, target, tile):
    total = heat[0]
    for k in range(1, 7):
        total = total + heat[k]
    side = 0.125 * total
    half = 0.5 * total
    for k in range(7):
        if k == 0:
            level = 0.25 * total
        else:
            drift = half * speeds[(k - 1) // 2]
            level = side + drift if k % 2 == 1 else side - drift
        target[k, tile] = heat[k] - (heat[k] - level) * omega


def stream(slab, post, tile, offsets):
    block_x, block_y = lax.div(tile, slab.gy), lax.rem(tile, slab.gy)
    x_of = {a: lax.rem(block_x + slab.gx - a, slab.gx) for a in (-1, 0, 1)}
    y_of = {b: lax.rem(block_y + slab.gy - b, slab.gy) for b in (-1, 0, 1)}
    row = row_index()
    per_x = 2 * slab.planes
    in_x = (lane_index() + slab.halo) % LANES // per_x
    last_x = {1: in_x == slab.block_x - 1, -1: in_x == 0}
    last_y = {1: row == SUBLANES - 1, -1: row == 0}

    def arrive(number, offset):
        a, b, c = offset

        def take(x):
            value = post[number, x_of[x] * slab.gy + block_y]
            if b != 0:
                other = post[number, x_of[x] * slab.gy + y_of[b]]
                value = jnp.where(last_y[b], other, value)
            return value

        value = take(0)
        if a != 0:
            value = jnp.where(last_x[a], take(a), value)
        if b != 0:
            value = pltpu.roll(value, b % SUBLANES, 0)
        return lane_roll(value, a * per_x + c)

    return [arrive(number, offset) for number, offset in enumerate(offsets)]


def stream_flow(slab, post, tile):
    return [
        jnp.where(value != value, post[26 - n, tile], value)
        for n, value in enumerate(stream(slab, post, tile, OFFSET_TABLE))
    ]


def over_tiles(slab, body, unroll=1):
    def one(tile, _):
        body(tile)
        return 0

    lax.fori_loop(0, slab.sub, one, 0, unroll=unroll)


def one_ahead(slab, arrive, collide, held):
    def bring(tile):
        for number, value in enumerate(arrive(tile)):
            held[number] = value

    def body(tile):
        values = [held[number] for number in range(held.shape[0])]
        bring(lax.rem(tile + 1, slab.sub))
        collide(tile, values)

    bring(jnp.int32(0))
    over_tiles(slab, body)


def over_steps(count, body):
    def one(number, _):
        body(number)
        return 0

    lax.fori_loop(0, count, one, 0)


def first_window(slab, rates_hbm, state, *refs):
    heat_parts, refs = refs[: slab.grp], refs[slab.grp :]
    flow_out, keep_out, heat_outs = refs[0], refs[1], refs[2 : 2 + slab.grp]
    (rates_ref, sem, speed, heat_tiles, flow_post, heat_post, heat_a, heat_b, held, came_heat, ahead) = (
        refs[2 + slab.grp :]
    )
    rates_copy = pltpu.make_async_copy(rates_hbm, rates_ref, sem)
    rates_copy.start()
    make_heat_tiles(slab, heat_parts, came_heat, heat_tiles)
    rates_copy.wait()

    def speeds_of(tile):
        return [speed[d, tile] for d in range(3)]

    def begin(tile):
        solid = state[SOLID_AT, tile]
        heat = [heat_tiles[k, tile] for k in range(7)]
        for d in range(3):
            speed[d, tile] = state[SPEED_AT + d, tile]
        force = heat_force(heat)
        keep_out[0, tile] = force
        keep_out[1, tile] = solid
        flow = [state[n, tile] for n in range(27)]
        collide_flow(rates_ref, flow, force, solid != 0.0, flow_post.at[0], tile)
        collide_heat(heat, heat_tiles[7, tile], speeds_of(tile), heat_post.at[0], tile)

    over_tiles(slab, begin)

    def arrive(tile, source):
        flow = stream_flow(slab, flow_post.at[source], tile)
        return flow + stream(slab, heat_post.at[source], tile, HEAT_OFFSETS)

    def step(number):
        source = lax.rem(number, 2)

        def go_on(tile, values):
            flow, heat = values[:27], values[27:]
            solid = state[SOLID_AT, tile] != 0.0
            collide_flow(rates_ref, flow, keep_out[0, tile], solid, flow_post.at[1 - source], tile)
            omega = heat_tiles[7, tile]
            collide_heat(heat, omega, speeds_of(tile), heat_post.at[1 - source], tile)

        one_ahead(slab, lambda tile: arrive(tile, source), go_on, ahead)

    over_steps(STEPS - 1, step)
    source = (STEPS - 1) % 2

    def next_window(tile, values):
        flow, heat = values[:27], values[27:]
        solid = state[SOLID_AT, tile] != 0.0
        speeds = [
            jnp.where(solid, 0.0, each) for each in flow_speed_tile(flow, keep_out[0, tile])
        ]
        for d in range(3):
            speed[d, tile] = speeds[d]
        force = heat_force(heat)
        keep_out[0, tile] = force
        collide_flow(rates_ref, flow, force, solid, flow_out, tile)
        collide_heat(heat, heat_tiles[7, tile], speeds, heat_a, tile)

    one_ahead(slab, lambda tile: arrive(tile, source), next_window, ahead)
    here, there = heat_a, heat_b
    for _ in range(STEPS - 1):

        def heat_alone(tile, here=here, there=there):
            heat = stream(slab, here, tile, HEAT_OFFSETS)
            collide_heat(heat, heat_tiles[7, tile], speeds_of(tile), there, tile)

        over_tiles(slab, heat_alone, unroll=4)
        here, there = there, here
    zero = jnp.zeros((SUBLANES, LANES), F32)

    def end_heat(tile):
        heat = stream(slab, here, tile, HEAT_OFFSETS)
        heat += [zero] * (slab.sub - 7)
        for x, value in enumerate(swap_groups(heat, slab.planes)[0::2]):
            held[x, tile] = value

    over_tiles(slab, end_heat, unroll=2)
    mine = lax.axis_index("grp")
    for step_number in range(slab.grp):
        heat_outs[step_number][...] = held[jnp.bitwise_xor(mine, step_number)]


def last_window(slab, rates_hbm, came, flow_in, keep_ref, sent, rates_ref, sem, flow_post, ahead):
    rates_copy = pltpu.make_async_copy(rates_hbm, rates_ref, sem)
    rates_copy.start()

    def copy(n, _):
        flow_post[0, n] = flow_in[n]
        return 0

    lax.fori_loop(0, 27, copy, 0, unroll=3)
    rates_copy.wait()

    def step(number):
        source = lax.rem(number, 2)

        def go_on(tile, flow):
            solid = keep_ref[1, tile] != 0.0
            collide_flow(rates_ref, flow, keep_ref[0, tile], solid, flow_post.at[1 - source], tile)

        one_ahead(slab, lambda tile: stream_flow(slab, flow_post.at[source], tile), go_on, ahead)

    over_steps(STEPS - 1, step)

    def end(tile):
        flow = stream_flow(slab, flow_post.at[(STEPS - 1) % 2], tile)
        pack_out(slab, flow, came, tile, sent)

    over_tiles(slab, end)


def heat_force(heat):
    total = heat[0]
    for k in range(1, 7):
        total = total + heat[k]
    return BUOYANCY * (total - REFERENCE_HEAT)


def flow_speed_tile(values, force):
    total = values[0]
    for n in range(1, 27):
        total = total + values[n]
    sums = []
    for d in range(3):
        plus, minus = None, None
        for n in range(27):
            part = OFFSET_TABLE[n][d]
            if part == 1:
                plus = values[n] if plus is None else plus + values[n]
            if part == -1:
                minus = values[n] if minus is None else minus + values[n]
        sums.append(plus - minus)
    sums[2] = sums[2] + 0.5 * force
    return [each / total for each in sums]


def local_call(body, slab, arrays, outs, scratch=(), in_hbm=0, carried=False, outs_in_hbm=False):
    def kernel(*refs):
        body(slab, *refs)

    return pl.pallas_call(
        kernel,
        out_shape=[jax.ShapeDtypeStruct(shape, F32) for shape in outs],
        in_specs=[
            pl.BlockSpec(
                memory_space=pltpu.HBM if i < in_hbm else pl.ANY if carried and i == 0 else pltpu.VMEM
            )
            for i in range(len(arrays))
        ],
        out_specs=[
            pl.BlockSpec(memory_space=pl.ANY if carried or outs_in_hbm else pltpu.VMEM)
        ]
        * len(outs),
        input_output_aliases={0: 0} if carried else {},
        scratch_shapes=[pltpu.VMEM(s, F32) if isinstance(s, tuple) else s for s in scratch],
        compiler_params=pltpu.CompilerParams(vmem_limit_bytes=24 * 1024 * 1024),
    )(
        *(
            pltpu.with_memory_space_constraint(array, pltpu.HBM) if i < in_hbm else array
            for i, array in enumerate(arrays)
        )
    )


RING = ("grp", "gx", "gy")


def exchange(slab, low, high):
    ring = slab.ring
    upward = [(ring[i - 1], ring[i]) for i in range(len(ring))]
    from_below = lax.ppermute(high, RING, upward)
    from_above = lax.ppermute(low, RING, [(b, a) for a, b in upward])
    return from_below, from_above


def across_plane(slab, sent):
    came = {0: sent[0]}
    for step in slab.steps[1:]:
        pairs = [(i, i ^ step) for i in range(slab.sub)]
        came[step] = lax.ppermute(sent[step], ("gx", "gy"), pairs)
    return [came[step] for step in slab.steps]


def across_planes(slab, parts):
    return [parts[0]] + [
        lax.ppermute(parts[step], "grp", [(i, i ^ step) for i in range(slab.grp)])
        for step in range(1, slab.grp)
    ]


def on_slabs(slab, populations, thermal, velocity_prev, solid, phase_ids, conductivity, rates):
    tile = (SUBLANES, LANES)

    def vmem_like(array):
        return pltpu.VMEM(array.shape, array.dtype)

    sent_shape = (slab.sub, IN_PAIRS + 2 * slab.grp) + tile
    (sent,) = local_call(
        pack_in,
        slab,
        [conductivity, populations, velocity_prev, solid, thermal, phase_ids],
        [sent_shape],
        [
            pltpu.SMEM(conductivity.shape, F32),
            (2 * IN_PAIRS,) + solid.shape,
            vmem_like(solid),
            vmem_like(thermal),
            vmem_like(phase_ids),
            pltpu.SemaphoreType.DMA((6,)),
        ],
        in_hbm=6,
    )
    plane = (slab.sub,) + tile
    halo_shape = (slab.sub // 2, IN_PAIRS) + tile
    heat_shape = (slab.sub, 2) + tile
    came, low, high, *parts = local_call(
        offer_halo,
        slab,
        across_plane(slab, sent),
        [sent_shape, halo_shape, halo_shape] + [heat_shape] * slab.grp,
    )
    below, above = exchange(slab, low, high)
    parts = across_planes(slab, parts)
    (state,) = local_call(make_tiles, slab, [came, below, above], [(2 * IN_PAIRS,) + plane])
    scalars = [pltpu.SMEM(rates.shape, F32), pltpu.SemaphoreType.DMA]
    flow, keep, *parts = local_call(
        first_window,
        slab,
        [rates, state] + parts,
        [(27,) + plane, (2,) + plane] + [plane] * slab.grp,
        scalars
        + [(3,) + plane, (8,) + plane, (2, 27) + plane, (2, 7) + plane]
        + [(7,) + plane] * 2
        + [(slab.grp,) + plane, (slab.grp,) + heat_shape, (34,) + tile],
        in_hbm=1,
    )
    parts = across_planes(slab, parts)
    last_shape = (slab.sub, FLOW_PAIRS + slab.grp) + tile
    (sent,) = local_call(
        last_window,
        slab,
        [rates, came, flow, keep],
        [last_shape],
        scalars + [(2, 27) + plane, (27,) + tile],
        in_hbm=1,
    )
    (sent,) = local_call(
        add_heat,
        slab,
        [sent] + parts,
        [last_shape],
        [(slab.sub, slab.grp) + tile, pltpu.SemaphoreType.DMA],
        carried=True,
    )
    return tuple(
        local_call(
            unpack_out,
            slab,
            across_plane(slab, sent),
            [populations.shape, thermal.shape],
            [
                last_shape,
                populations.shape,
                thermal.shape,
                pltpu.SemaphoreType.DMA((1 + -(-FLOW_PAIRS // 4),)),
            ],
            outs_in_hbm=True,
        )
    )


def solution(mesh):
    in_specs = (
        P(None, "gx", "gy", "grp"),
        P(None, ("gx", "grp"), "gy", None),
        P(None, "gx", "gy", "grp"),
        P("gx", "gy", "grp"),
        P(("gx", "grp"), "gy", None),
        P(),
        P(),
    )
    out_specs = (P(None, "gx", "gy", "grp"), P(None, ("gx", "grp"), "gy", None))

    def per_device(populations, thermal, *others):
        slab = Slab(mesh.shape, populations.shape[1:], thermal.shape[1:])
        plan = (lambda *arrays: on_slabs(slab, *arrays)) if slab.fits else on_device
        return plan(populations, thermal, *others)

    return jax.shard_map(
        per_device, mesh=mesh, in_specs=in_specs, out_specs=out_specs, check_vma=False
    )
```

```python
import jax
import jax.numpy as jnp
import numpy as np
from jax import lax
from jax.experimental import pallas as pl
from jax.experimental.pallas import tpu as pltpu
from jax.sharding import PartitionSpec as P

STEPS = 4
WINDOWS = 2


HIGHEST = lax.Precision.HIGHEST
BUOYANCY = 0.03
REFERENCE_HEAT = 1.0
OFFSET_TABLE = [(number // 9 - 1, number // 3 % 3 - 1, number % 3 - 1) for number in range(27)]
LATTICE_WEIGHTS = np.array(
    [
        np.prod([2.0 / 3.0 if component == 0 else 1.0 / 6.0 for component in triple])
        for triple in OFFSET_TABLE
    ]
)
VANDERMONDE = np.array([[1.0, 1.0, 1.0], [-1.0, 0.0, 1.0], [1.0, 0.0, 1.0]])
VANDER_INVERSE = np.array([[0.0, -0.5, 0.5], [1.0, 0.0, -1.0], [0.0, 0.5, 0.5]])
MOMENT_MATRIX = np.kron(np.kron(VANDERMONDE, VANDERMONDE), VANDERMONDE)
MOMENT_INVERSE = np.kron(np.kron(VANDER_INVERSE, VANDER_INVERSE), VANDER_INVERSE)
RELAXED = np.array([0.0 if number in (0, 1, 3, 9) else 1.0 for number in range(27)])
SUMMING = np.concatenate([np.ones((1, 27)), 1.0 * np.array(OFFSET_TABLE).T], axis=0)
HEAT_WEIGHTS = np.array([0.25] + [0.125] * 6)


def from_behind(value, axis, steps):
    count = lax.axis_size(axis)
    pairs = [(source, (source + steps) % count) for source in range(count)]
    return lax.ppermute(value, axis, pairs)


def extended(cells, sides, width):
    for axis, dim in sides:
        count = lax.axis_size(axis)
        head = lax.slice_in_dim(cells, 0, width, axis=dim)
        tail = lax.slice_in_dim(cells, cells.shape[dim] - width, cells.shape[dim], axis=dim)
        cells = jnp.concatenate(
            [
                lax.ppermute(tail, axis, [(i, (i + 1) % count) for i in range(count)]),
                cells,
                lax.ppermute(head, axis, [((i + 1) % count, i) for i in range(count)]),
            ],
            axis=dim,
        )
    return cells


def flow_state(flat, heat_flat):
    sums = jnp.dot(jnp.asarray(SUMMING, jnp.float32), flat, precision=HIGHEST)
    density = sums[0]
    force = BUOYANCY * (heat_flat - REFERENCE_HEAT)
    speed = jnp.stack([sums[1], sums[2], sums[3] + 0.5 * force]) / density
    return (density, force, speed)


def collide(popul, heat, rates):
    flat = popul.reshape(27, -1)
    density, force, speed = flow_state(flat, heat.reshape(-1))
    along = jnp.dot(jnp.asarray(SUMMING[1:].T, jnp.float32), speed, precision=HIGHEST)
    square = jnp.sum(speed * speed, axis=0)
    balance = (
        density
        * jnp.asarray(LATTICE_WEIGHTS, jnp.float32)[:, None]
        * (1.0 + 3.0 * along + 4.5 * along * along - 1.5 * square)
    )
    scaled = (
        jnp.asarray(MOMENT_INVERSE, jnp.float32)
        * (rates * jnp.asarray(RELAXED, jnp.float32))[None, :]
    )
    relax = jnp.dot(scaled, jnp.asarray(MOMENT_MATRIX, jnp.float32), precision=HIGHEST)
    post = (
        flat
        - jnp.dot(relax, flat - balance, precision=HIGHEST)
        + jnp.asarray(MOMENT_INVERSE[:, 1], jnp.float32)[:, None] * force[None, :]
    )
    return post.reshape(popul.shape)


def flow_speed(popul, heat, solid):
    density, force, speed = flow_state(popul.reshape(27, -1), heat.reshape(-1))
    return jnp.where(solid[None] == 0, speed.reshape((3,) + solid.shape), 0.0)


def heat_collide(heat_pops, speed, relax_time):
    total = jnp.sum(heat_pops, axis=0)
    still = jnp.zeros_like(speed[0])
    along = jnp.stack([still, speed[0], -speed[0], speed[1], -speed[1], speed[2], -speed[2]])
    balance = (
        jnp.asarray(HEAT_WEIGHTS, jnp.float32)[:, None, None, None]
        * total[None]
        * (1.0 + 4.0 * along)
    )
    return heat_pops - (heat_pops - balance) / relax_time[None]


def relaxation(phase_ids, conductivity):
    levels = jnp.arange(conductivity.shape[0], dtype=jnp.int32)
    chosen = jnp.sum(
        jnp.where(
            phase_ids[None] == levels[:, None, None, None], conductivity[:, None, None, None], 0.0
        ),
        axis=0,
    )
    return 0.5 + 4.0 * chosen


def inner_window(padded, triple, sizes):
    return padded[
        1 - triple[0] : 1 - triple[0] + sizes[0],
        1 - triple[1] : 1 - triple[1] + sizes[1],
        1 - triple[2] : 1 - triple[2] + sizes[2],
    ]


def advance(grid, axis_number, send_up, send_down):
    space = 3 + axis_number
    length = grid.shape[space]
    rising = lax.index_in_dim(grid, 2, axis_number, keepdims=True)
    resting = lax.index_in_dim(grid, 1, axis_number, keepdims=True)
    falling = lax.index_in_dim(grid, 0, axis_number, keepdims=True)
    from_below = send_up(lax.slice_in_dim(rising, length - 1, length, axis=space))
    from_above = send_down(lax.slice_in_dim(falling, 0, 1, axis=space))
    rising = jnp.concatenate(
        [from_below, lax.slice_in_dim(rising, 0, length - 1, axis=space)], axis=space
    )
    falling = jnp.concatenate(
        [lax.slice_in_dim(falling, 1, length, axis=space), from_above], axis=space
    )
    return jnp.concatenate([falling, resting, rising], axis=axis_number)


def flow_arrivals(post):
    sizes = post.shape[1:]
    grid = post.reshape((3, 3, 3) + sizes)
    grid = advance(
        grid,
        0,
        lambda plane: from_behind(plane, "gx", 1),
        lambda plane: from_behind(plane, "gx", -1),
    )
    grid = advance(
        grid,
        1,
        lambda plane: from_behind(plane, "gy", 1),
        lambda plane: from_behind(plane, "gy", -1),
    )
    grid = advance(
        grid,
        2,
        lambda plane: from_behind(plane, "grp", 1),
        lambda plane: from_behind(plane, "grp", -1),
    )
    return grid.reshape(post.shape)


def stream_heat(post, grp_index, last_grp):
    length = post.shape[1]
    size_y = post.shape[2]
    eastward = post[1]
    westward = post[2]
    lower_first = from_behind(eastward, "grp", 1)
    lower_second = from_behind(lower_first, "gx", 1)
    entering = jnp.where(grp_index == 0, lower_second, lower_first)
    eastward = jnp.concatenate([entering, eastward[: length - 1]], axis=0)
    upper_first = from_behind(westward, "grp", -1)
    upper_second = from_behind(upper_first, "gx", -1)
    entering = jnp.where(grp_index == last_grp, upper_second, upper_first)
    westward = jnp.concatenate([westward[1:], entering], axis=0)
    sides = extended(post[3:5], (("gy", 2),), 1)
    northward = sides[0, :, 0:size_y]
    southward = sides[1, :, 2 : size_y + 2]
    upward = jnp.roll(post[5], 1, axis=2)
    downward = jnp.roll(post[6], -1, axis=2)
    return jnp.stack([post[0], eastward, westward, northward, southward, upward, downward])


def on_device(populations, thermal, velocity_prev, solid, phase_ids, conductivity, rates):
    padded_solid = extended(solid, (("grp", 2), ("gx", 0), ("gy", 1)), 1)
    sizes = solid.shape
    blocked = jnp.stack(
        [inner_window(padded_solid, OFFSET_TABLE[number], sizes) != 0 for number in range(27)]
    )
    fluid_cells = (solid == 0)[None]
    grp_index = lax.axis_index("grp")
    last_grp = lax.axis_size("grp") - 1
    relax_time = relaxation(phase_ids, conductivity)
    speed_brick = velocity_prev
    popul = populations
    heat_pops = thermal
    for window_number in range(WINDOWS):
        heat_brick = lax.all_to_all(
            jnp.sum(heat_pops, axis=0), "grp", split_axis=2, concat_axis=0, tiled=True
        )
        speed_column = lax.all_to_all(speed_brick, "grp", split_axis=1, concat_axis=3, tiled=True)
        for step_number in range(STEPS):
            post = collide(popul, heat_brick, rates)
            arrived = flow_arrivals(post)
            popul = jnp.where(fluid_cells, jnp.where(blocked, post[::-1], arrived), popul)
        for step_number in range(STEPS):
            heat_pops = stream_heat(
                heat_collide(heat_pops, speed_column, relax_time), grp_index, last_grp
            )
        if window_number + 1 < WINDOWS:
            speed_brick = flow_speed(popul, heat_brick, solid)
    return (popul, heat_pops)


SUBLANES = 8
LANES = 128
F32 = jnp.float32


class Slab:
    def __init__(self, mesh_shape, flow_block, heat_block):
        self.grp, self.gx, self.gy = (mesh_shape[name] for name in ("grp", "gx", "gy"))
        self.block_x, self.block_y, self.block_z = flow_block
        self.sub = self.gx * self.gy
        self.planes = self.block_z // self.sub
        self.halo = self.planes // 2
        self.fits = (
            self.block_y == SUBLANES
            and self.block_z == LANES
            and self.planes * self.sub == LANES
            and self.halo * 2 == self.planes
            and WINDOWS == 2
            and self.halo == STEPS * WINDOWS
            and self.sub >= 8
            and 2 * self.block_x == self.sub
            and self.block_x == self.grp
            and heat_block == (1, SUBLANES, self.grp * LANES)
            and self.sub & (self.sub - 1) == 0
            and self.grp & (self.grp - 1) == 0
            and self.gy % 2 == 0
            and self.sub % self.grp == 0
        )
        if self.fits:
            self.turn = self.sub // self.grp
            partners = [step for k in (1, 0) for step in range(self.sub - 2 + k, 1, -2)]
            partners.sort(key=lambda step: bin(step >> 1).count("1"))
            self.steps = [0, 1] + partners
            self.ring = [
                part * self.sub + self.round_plane((place - self.turn * part) % self.sub)
                for part in range(self.grp)
                for place in range(self.sub)
            ]

    def round_plane(self, number):
        x, y = number // self.gy, number % self.gy
        back = x % 2
        return x * self.gy + y + back * (self.gy - 1 - 2 * y)

    def holders(self, part):
        begin = self.sub * self.grp - self.turn * part
        mine = self.place_in_plane()
        return [
            jnp.bitwise_xor(self.round_plane(lax.rem(begin + place, self.sub)), mine)
            for place in range(self.sub)
        ]

    def place_in_plane(self):
        return lax.axis_index("gx") * self.gy + lax.axis_index("gy")


def lane_index():
    return lax.broadcasted_iota(jnp.int32, (SUBLANES, LANES), 1)


def row_index():
    return lax.broadcasted_iota(jnp.int32, (SUBLANES, LANES), 0)


def lane_roll(value, amount):
    amount = amount % LANES
    return value if amount == 0 else pltpu.roll(value, amount, 1)


def swap_groups(values, group):
    count = len(values)
    lane = lane_index()
    values = list(values)
    bit = 1
    while bit < count:
        low = (lane // (group * bit)) % 2 == 0
        for first in range(count):
            if first & bit == 0:
                a, b = values[first], values[first | bit]
                if 2 * group * bit == LANES:
                    crossed = lane_roll(jnp.where(low, b, a), group * bit)
                    values[first] = jnp.where(low, a, crossed)
                    values[first | bit] = jnp.where(low, crossed, b)
                    continue
                values[first] = jnp.where(low, a, lane_roll(b, group * bit))
                values[first | bit] = jnp.where(low, lane_roll(a, -group * bit), b)
        bit *= 2
    return values


SPEED_AT, SOLID_AT = 27, 30
IN_PAIRS = 16
FLOW_PAIRS = 14


def pack_in(
    slab, levels_hbm, popul_hbm, speed_hbm, solid_hbm, heat_hbm, phase_hbm, sent, *scratch
):
    levels_ref, fields, solid_ref, heat_ref, phase_ref, sems = scratch
    copies = [
        pltpu.make_async_copy(source, target, sems.at[number])
        for number, (source, target) in enumerate(
            [
                (heat_hbm, heat_ref),
                (phase_hbm, phase_ref),
                (levels_hbm, levels_ref),
                (speed_hbm, fields.at[pl.ds(SPEED_AT, 3)]),
                (solid_hbm, solid_ref),
                (popul_hbm, fields.at[pl.ds(0, SPEED_AT)]),
            ]
        )
    ]
    for copy in copies:
        copy.start()
    for copy in copies[:3]:
        copy.wait()
    lane = lane_index()
    first = in_first_half(slab)
    columns = []
    for part in range(slab.grp):
        span = pl.ds(part * LANES, LANES)
        phase = phase_ref[0, :, span]
        chosen = jnp.zeros((SUBLANES, LANES), F32)
        for level in range(levels_ref.shape[0]):
            chosen = jnp.where(phase == level, levels_ref[level], chosen)
        columns.append([heat_ref[k, 0, :, span] for k in range(7)] + [1.0 / (0.5 + 4.0 * chosen)])
    for part in range(slab.grp):
        own, after = columns[part], columns[(part + 1) % slab.grp]
        before = columns[part - 1]
        beside = []
        for k in range(8):
            above = jnp.where(lane < slab.planes, after[k], own[k])
            below = jnp.where(lane >= LANES - slab.planes, before[k], own[k])
            beside.append(
                jnp.where(first, lane_roll(above, -slab.planes), lane_roll(below, slab.planes))
            )
        holders = slab.holders(part)
        for which, sources in enumerate((own, beside)):
            for place, value in enumerate(swap_groups(sources, slab.planes)):
                sent[holders[place], IN_PAIRS + 2 * part + which] = value
    for copy in copies[3:]:
        copy.wait()
    fields[SOLID_AT] = solid_ref[...].astype(F32)
    fields[SOLID_AT + 1] = jnp.zeros(solid_ref.shape, F32)
    holders = slab.holders(lax.axis_index("grp"))
    for pair in range(IN_PAIRS):
        sources = [fields[2 * pair + h, x] for x in range(slab.block_x) for h in range(2)]
        for place, value in enumerate(swap_groups(sources, slab.planes)):
            sent[holders[place], pair] = value


def in_first_half(slab):
    return lane_index() % slab.planes < slab.halo


def collect(slab, parts, came):
    mine = slab.place_in_plane()
    for part, step in zip(parts, slab.steps):
        came[jnp.bitwise_xor(mine, step)] = part[...]


def offer_halo(slab, *refs):
    parts, (came, low_out, high_out, *heat_outs) = refs[: slab.sub], refs[slab.sub :]
    collect(slab, parts, came)
    mine = lax.axis_index("grp")
    for step, heat_out in enumerate(heat_outs):
        slots = pl.ds(IN_PAIRS + 2 * jnp.bitwise_xor(mine, step), 2)
        for tile in range(slab.sub):
            heat_out[tile] = came[tile, slots]

    def one(number, _):
        tile = 2 * number
        first = in_first_half(slab)
        for pair in range(IN_PAIRS):
            a, b = came[tile, pair], came[tile + 1, pair]
            low_out[number, pair] = jnp.where(first, a, lane_roll(b, slab.halo))
            high_out[number, pair] = jnp.where(first, lane_roll(b, -slab.halo), a)
        return 0

    lax.fori_loop(0, slab.sub // 2, one, 0)


def make_heat_tiles(slab, parts, held, heat_tiles):
    mine = lax.axis_index("grp")
    for step, part in enumerate(parts):
        held[jnp.bitwise_xor(mine, step)] = part[...]
    first = in_first_half(slab)
    for tile in range(slab.sub):
        sources = []
        for x in range(slab.block_x):
            after = held[(x + 1) % slab.block_x, tile, 1]
            sources += [held[x, tile, 0], jnp.where(first, held[x, tile, 1], after)]
        for k, value in enumerate(swap_groups(sources, slab.planes)):
            heat_tiles[k, tile] = value


def make_tiles(slab, came, below_ref, above_ref, state):
    def one(number, _):
        first = in_first_half(slab)
        even = (lane_index() // slab.planes) % 2 == 0
        back = 2 * slab.planes
        for pair in range(IN_PAIRS):
            below, above = below_ref[number, pair], above_ref[number, pair]
            beside = (
                jnp.where(first, above, lane_roll(below, -back)),
                jnp.where(first, lane_roll(above, -slab.halo), lane_roll(below, slab.halo - back)),
            )
            for which in range(2):
                tile = 2 * number + which
                own, halo = came[tile, pair], beside[which]
                state[2 * pair, tile] = jnp.where(even, own, lane_roll(halo, slab.planes))
                state[2 * pair + 1, tile] = jnp.where(even, lane_roll(own, -slab.planes), halo)
        return 0

    lax.fori_loop(0, slab.sub // 2, one, 0)


def pack_out(slab, flow, came, tile, sent):
    even = (lane_index() // slab.planes) % 2 == 0
    flags = came[tile, SOLID_AT // 2]
    solid = jnp.where(even, flags, lane_roll(flags, slab.planes)) != 0.0
    partner = jnp.bitwise_xor(tile, slab.place_in_plane())
    for pair in range(FLOW_PAIRS):
        value = flow[2 * pair]
        if 2 * pair + 1 < len(flow):
            value = jnp.where(even, value, lane_roll(flow[2 * pair + 1], slab.planes))
        sent[partner, pair] = jnp.where(solid, came[tile, pair], value)


def add_heat(slab, sent_in, *refs):
    parts, (sent, packed, sem) = refs[: slab.grp], refs[slab.grp :]
    mine = slab.place_in_plane()
    for tile in range(slab.sub):
        for step in range(slab.grp):
            packed[jnp.bitwise_xor(mine, tile), step] = parts[step][tile]
    copy = pltpu.make_async_copy(packed, sent.at[:, pl.ds(FLOW_PAIRS, slab.grp)], sem)
    copy.start()
    copy.wait()


def unpack_out(slab, *refs):
    parts, (popul_hbm, thermal_hbm, came, popul, thermal, sems) = refs[: slab.sub], refs[slab.sub :]
    for part, step in zip(parts, slab.steps):
        came[step] = part[...]
    mine = lax.axis_index("grp")
    for step in range(slab.grp):
        part = jnp.bitwise_xor(mine, step)
        holders = slab.holders(part)
        span = pl.ds(pl.multiple_of(part * LANES, LANES), LANES)
        sources = [came[holders[place], FLOW_PAIRS + step] for place in range(slab.sub)]
        for k, value in enumerate(swap_groups(sources, slab.planes)[:7]):
            thermal[k, 0, :, span] = value
    copies = [pltpu.make_async_copy(thermal, thermal_hbm, sems.at[0])]
    copies[0].start()
    holders = slab.holders(mine)
    begin = 0
    for pair in range(FLOW_PAIRS):
        sources = [came[holders[place], pair] for place in range(slab.sub)]
        for number, value in enumerate(swap_groups(sources, slab.planes)):
            if 2 * pair + number % 2 < 27:
                popul[2 * pair + number % 2, number // 2] = value
        end = min(2 * pair + 2, 27)
        if pair % 4 == 3 or end == 27:
            rows = pl.ds(begin, end - begin)
            sem = sems.at[len(copies)]
            copies.append(pltpu.make_async_copy(popul.at[rows], popul_hbm.at[rows], sem))
            copies[-1].start()
            begin = end
    for copy in copies:
        copy.wait()


def forward3(values):
    for stride in (9, 3, 1):
        out = [None] * 27
        for n in range(27):
            if n // stride % 3 == 0:
                a, b, c = values[n], values[n + stride], values[n + 2 * stride]
                both = a + c
                out[n], out[n + stride], out[n + 2 * stride] = both + b, c - a, both
        values = out
    return values


def backward3(values):
    for stride in (9, 3, 1):
        out = [None] * 27
        for n in range(27):
            if n // stride % 3 == 0:
                a, b, c = values[n], values[n + stride], values[n + 2 * stride]
                out[n], out[n + stride], out[n + 2 * stride] = c - b, (a - c) - c, c + b
        values = out
    return values


CONSERVED = (0, 1, 3, 9)


def powers_of(n):
    return (n // 9, n // 3 % 3, n % 3)


def weigh_rates(rates_ref, keep_ref, blend_ref):
    for n in range(27):
        if n not in CONSERVED:
            powers = powers_of(n)
            half = 0.5 ** sum(power > 0 for power in powers)
            keep_ref[n] = (1.0 - rates_ref[n]) * half
            blend_ref[n] = rates_ref[n] * (half * (1.0 / 3.0) ** powers.count(2))


def collide_tile(values, force, shares, solid):
    keep_ref, blend_ref = shares
    moments = forward3(values)
    density = moments[0]
    flux = (moments[9], moments[3], moments[1] + 0.5 * force)
    inverse = 1.0 / density
    u = tuple(j * inverse for j in flux)
    triple = 3.0 * inverse
    squares = [j * (j * triple) for j in flux]
    cross = {(0, 1): flux[0] * u[1], (0, 2): flux[0] * u[2], (1, 2): flux[1] * u[2]}
    level_of = {}
    out = [None] * 27
    for n in range(27):
        powers = powers_of(n)
        if n in CONSERVED:
            value = moments[n] + force if n == 1 else moments[n]
            out[n] = value if n == 0 else 0.5 * value
            continue
        odd = tuple(d for d in range(3) if powers[d] == 1)
        even = tuple(d for d in range(3) if powers[d] == 2)
        out[n] = keep_ref[n] * moments[n]
        if len(odd) == 3:
            continue
        if len(odd) == 0:
            if even not in level_of:
                level_of[even] = level_of.get(even[:-1], density) + squares[even[-1]]
            level = level_of[even]
        elif len(odd) == 1:
            level = flux[odd[0]]
        else:
            level = cross[odd]
        out[n] = out[n] + blend_ref[n] * level
    out[26] = jnp.where(solid, jnp.nan, out[26])
    return backward3(out)


HEAT_OFFSETS = [(0, 0, 0), (1, 0, 0), (-1, 0, 0), (0, 1, 0), (0, -1, 0), (0, 0, 1), (0, 0, -1)]


def collide_flow(shares, flow, force, solid, target, tile):
    for n, value in enumerate(collide_tile(flow, force, shares, solid)):
        target[n, tile] = value


def collide_heat(heat, omega, speeds, target, tile):
    total = heat[0]
    for k in range(1, 7):
        total = total + heat[k]
    side = 0.125 * total
    half = 0.5 * total
    for k in range(7):
        if k == 0:
            level = 0.25 * total
        else:
            drift = half * speeds[(k - 1) // 2]
            level = side + drift if k % 2 == 1 else side - drift
        target[k, tile] = heat[k] - (heat[k] - level) * omega


def stream(slab, post, tile, offsets):
    block_x, block_y = lax.div(tile, slab.gy), lax.rem(tile, slab.gy)
    x_of = {a: lax.rem(block_x + slab.gx - a, slab.gx) for a in (-1, 0, 1)}
    y_of = {b: lax.rem(block_y + slab.gy - b, slab.gy) for b in (-1, 0, 1)}
    row = row_index()
    per_x = 2 * slab.planes
    in_x = (lane_index() + slab.halo) % LANES // per_x
    last_x = {1: in_x == slab.block_x - 1, -1: in_x == 0}
    last_y = {1: row == SUBLANES - 1, -1: row == 0}

    def arrive(number, offset):
        a, b, c = offset

        def take(x):
            value = post[number, x_of[x] * slab.gy + block_y]
            if b != 0:
                other = post[number, x_of[x] * slab.gy + y_of[b]]
                value = jnp.where(last_y[b], other, value)
            return value

        value = take(0)
        if a != 0:
            value = jnp.where(last_x[a], take(a), value)
        if b != 0:
            value = pltpu.roll(value, b % SUBLANES, 0)
        return lane_roll(value, a * per_x + c)

    return [arrive(number, offset) for number, offset in enumerate(offsets)]


def stream_flow(slab, post, tile):
    return [
        jnp.where(value != value, post[26 - n, tile], value)
        for n, value in enumerate(stream(slab, post, tile, OFFSET_TABLE))
    ]


def over_tiles(slab, body, unroll=1):
    def one(tile, _):
        body(tile)
        return 0

    lax.fori_loop(0, slab.sub, one, 0, unroll=unroll)


def one_ahead(slab, arrive, collide, held):
    def bring(tile):
        for number, value in enumerate(arrive(tile)):
            held[number] = value

    def body(tile):
        values = [held[number] for number in range(held.shape[0])]
        bring(lax.rem(tile + 1, slab.sub))
        collide(tile, values)

    bring(jnp.int32(0))
    over_tiles(slab, body)


def over_steps(count, body):
    def one(number, _):
        body(number)
        return 0

    lax.fori_loop(0, count, one, 0)


def first_window(slab, rates_hbm, state, *refs):
    heat_parts, refs = refs[: slab.grp], refs[slab.grp :]
    flow_out, keep_out, heat_outs = refs[0], refs[1], refs[2 : 2 + slab.grp]
    (rates_ref, sem, speed, heat_tiles, flow_post, heat_post, heat_a, heat_b, held, came_heat, ahead, *shares) = (
        refs[2 + slab.grp :]
    )
    rates_copy = pltpu.make_async_copy(rates_hbm, rates_ref, sem)
    rates_copy.start()
    make_heat_tiles(slab, heat_parts, came_heat, heat_tiles)
    rates_copy.wait()
    weigh_rates(rates_ref, *shares)

    def speeds_of(tile):
        return [speed[d, tile] for d in range(3)]

    def begin(tile):
        solid = state[SOLID_AT, tile]
        heat = [heat_tiles[k, tile] for k in range(7)]
        for d in range(3):
            speed[d, tile] = state[SPEED_AT + d, tile]
        force = heat_force(heat)
        keep_out[0, tile] = force
        keep_out[1, tile] = solid
        flow = [state[n, tile] for n in range(27)]
        collide_flow(shares, flow, force, solid != 0.0, flow_post.at[0], tile)
        collide_heat(heat, heat_tiles[7, tile], speeds_of(tile), heat_post.at[0], tile)

    over_tiles(slab, begin)

    def arrive(tile, source):
        flow = stream_flow(slab, flow_post.at[source], tile)
        return flow + stream(slab, heat_post.at[source], tile, HEAT_OFFSETS)

    def step(number):
        source = lax.rem(number, 2)

        def go_on(tile, values):
            flow, heat = values[:27], values[27:]
            solid = state[SOLID_AT, tile] != 0.0
            collide_flow(shares, flow, keep_out[0, tile], solid, flow_post.at[1 - source], tile)
            omega = heat_tiles[7, tile]
            collide_heat(heat, omega, speeds_of(tile), heat_post.at[1 - source], tile)

        one_ahead(slab, lambda tile: arrive(tile, source), go_on, ahead)

    over_steps(STEPS - 1, step)
    source = (STEPS - 1) % 2

    def next_window(tile, values):
        flow, heat = values[:27], values[27:]
        solid = state[SOLID_AT, tile] != 0.0
        speeds = [
            jnp.where(solid, 0.0, each) for each in flow_speed_tile(flow, keep_out[0, tile])
        ]
        for d in range(3):
            speed[d, tile] = speeds[d]
        force = heat_force(heat)
        keep_out[0, tile] = force
        collide_flow(shares, flow, force, solid, flow_out, tile)
        collide_heat(heat, heat_tiles[7, tile], speeds, heat_a, tile)

    one_ahead(slab, lambda tile: arrive(tile, source), next_window, ahead)
    here, there = heat_a, heat_b
    for _ in range(STEPS - 1):

        def heat_alone(tile, here=here, there=there):
            heat = stream(slab, here, tile, HEAT_OFFSETS)
            collide_heat(heat, heat_tiles[7, tile], speeds_of(tile), there, tile)

        over_tiles(slab, heat_alone, unroll=4)
        here, there = there, here
    zero = jnp.zeros((SUBLANES, LANES), F32)

    def end_heat(tile):
        heat = stream(slab, here, tile, HEAT_OFFSETS)
        heat += [zero] * (slab.sub - 7)
        for x, value in enumerate(swap_groups(heat, slab.planes)[0::2]):
            held[x, tile] = value

    over_tiles(slab, end_heat, unroll=2)
    mine = lax.axis_index("grp")
    for step_number in range(slab.grp):
        heat_outs[step_number][...] = held[jnp.bitwise_xor(mine, step_number)]


def last_window(slab, rates_hbm, came, flow_in, keep_ref, sent, *refs):
    rates_ref, sem, flow_post, ahead, *shares = refs
    rates_copy = pltpu.make_async_copy(rates_hbm, rates_ref, sem)
    rates_copy.start()

    def copy(n, _):
        flow_post[0, n] = flow_in[n]
        return 0

    lax.fori_loop(0, 27, copy, 0, unroll=3)
    rates_copy.wait()
    weigh_rates(rates_ref, *shares)

    def step(number):
        source = lax.rem(number, 2)

        def go_on(tile, flow):
            solid = keep_ref[1, tile] != 0.0
            collide_flow(shares, flow, keep_ref[0, tile], solid, flow_post.at[1 - source], tile)

        one_ahead(slab, lambda tile: stream_flow(slab, flow_post.at[source], tile), go_on, ahead)

    over_steps(STEPS - 1, step)

    def arrive(tile):
        return stream_flow(slab, flow_post.at[(STEPS - 1) % 2], tile)

    one_ahead(slab, arrive, lambda tile, flow: pack_out(slab, flow, came, tile, sent), ahead)


def heat_force(heat):
    total = heat[0]
    for k in range(1, 7):
        total = total + heat[k]
    return BUOYANCY * (total - REFERENCE_HEAT)


def flow_speed_tile(values, force):
    total = values[0]
    for n in range(1, 27):
        total = total + values[n]
    sums = []
    for d in range(3):
        plus, minus = None, None
        for n in range(27):
            part = OFFSET_TABLE[n][d]
            if part == 1:
                plus = values[n] if plus is None else plus + values[n]
            if part == -1:
                minus = values[n] if minus is None else minus + values[n]
        sums.append(plus - minus)
    sums[2] = sums[2] + 0.5 * force
    return [each / total for each in sums]


def local_call(body, slab, arrays, outs, scratch=(), in_hbm=0, carried=False, outs_in_hbm=False):
    def kernel(*refs):
        body(slab, *refs)

    return pl.pallas_call(
        kernel,
        out_shape=[jax.ShapeDtypeStruct(shape, F32) for shape in outs],
        in_specs=[
            pl.BlockSpec(
                memory_space=pltpu.HBM if i < in_hbm else pl.ANY if carried and i == 0 else pltpu.VMEM
            )
            for i in range(len(arrays))
        ],
        out_specs=[
            pl.BlockSpec(memory_space=pl.ANY if carried or outs_in_hbm else pltpu.VMEM)
        ]
        * len(outs),
        input_output_aliases={0: 0} if carried else {},
        scratch_shapes=[pltpu.VMEM(s, F32) if isinstance(s, tuple) else s for s in scratch],
        compiler_params=pltpu.CompilerParams(vmem_limit_bytes=24 * 1024 * 1024),
    )(
        *(
            pltpu.with_memory_space_constraint(array, pltpu.HBM) if i < in_hbm else array
            for i, array in enumerate(arrays)
        )
    )


RING = ("grp", "gx", "gy")


def exchange(slab, low, high):
    ring = slab.ring
    upward = [(ring[i - 1], ring[i]) for i in range(len(ring))]
    from_below = lax.ppermute(high, RING, upward)
    from_above = lax.ppermute(low, RING, [(b, a) for a, b in upward])
    return from_below, from_above


def across_plane(slab, sent):
    came = {0: sent[0]}
    for step in slab.steps[1:]:
        pairs = [(i, i ^ step) for i in range(slab.sub)]
        came[step] = lax.ppermute(sent[step], ("gx", "gy"), pairs)
    return [came[step] for step in slab.steps]


def across_planes(slab, parts):
    return [parts[0]] + [
        lax.ppermute(parts[step], "grp", [(i, i ^ step) for i in range(slab.grp)])
        for step in range(1, slab.grp)
    ]


def on_slabs(slab, populations, thermal, velocity_prev, solid, phase_ids, conductivity, rates):
    tile = (SUBLANES, LANES)

    def vmem_like(array):
        return pltpu.VMEM(array.shape, array.dtype)

    sent_shape = (slab.sub, IN_PAIRS + 2 * slab.grp) + tile
    (sent,) = local_call(
        pack_in,
        slab,
        [conductivity, populations, velocity_prev, solid, thermal, phase_ids],
        [sent_shape],
        [
            pltpu.SMEM(conductivity.shape, F32),
            (2 * IN_PAIRS,) + solid.shape,
            vmem_like(solid),
            vmem_like(thermal),
            vmem_like(phase_ids),
            pltpu.SemaphoreType.DMA((6,)),
        ],
        in_hbm=6,
    )
    plane = (slab.sub,) + tile
    halo_shape = (slab.sub // 2, IN_PAIRS) + tile
    heat_shape = (slab.sub, 2) + tile
    came, low, high, *parts = local_call(
        offer_halo,
        slab,
        across_plane(slab, sent),
        [sent_shape, halo_shape, halo_shape] + [heat_shape] * slab.grp,
    )
    below, above = exchange(slab, low, high)
    parts = across_planes(slab, parts)
    (state,) = local_call(make_tiles, slab, [came, below, above], [(2 * IN_PAIRS,) + plane])
    scalars = [pltpu.SMEM(rates.shape, F32), pltpu.SemaphoreType.DMA]
    shares = [pltpu.SMEM(rates.shape, F32)] * 2
    flow, keep, *parts = local_call(
        first_window,
        slab,
        [rates, state] + parts,
        [(27,) + plane, (2,) + plane] + [plane] * slab.grp,
        scalars
        + [(3,) + plane, (8,) + plane, (2, 27) + plane, (2, 7) + plane]
        + [(7,) + plane] * 2
        + [(slab.grp,) + plane, (slab.grp,) + heat_shape, (34,) + tile]
        + shares,
        in_hbm=1,
    )
    parts = across_planes(slab, parts)
    last_shape = (slab.sub, FLOW_PAIRS + slab.grp) + tile
    (sent,) = local_call(
        last_window,
        slab,
        [rates, came, flow, keep],
        [last_shape],
        scalars + [(2, 27) + plane, (27,) + tile] + shares,
        in_hbm=1,
    )
    (sent,) = local_call(
        add_heat,
        slab,
        [sent] + parts,
        [last_shape],
        [(slab.sub, slab.grp) + tile, pltpu.SemaphoreType.DMA],
        carried=True,
    )
    return tuple(
        local_call(
            unpack_out,
            slab,
            across_plane(slab, sent),
            [populations.shape, thermal.shape],
            [
                last_shape,
                populations.shape,
                thermal.shape,
                pltpu.SemaphoreType.DMA((1 + -(-FLOW_PAIRS // 4),)),
            ],
            outs_in_hbm=True,
        )
    )


def solution(mesh):
    in_specs = (
        P(None, "gx", "gy", "grp"),
        P(None, ("gx", "grp"), "gy", None),
        P(None, "gx", "gy", "grp"),
        P("gx", "gy", "grp"),
        P(("gx", "grp"), "gy", None),
        P(),
        P(),
    )
    out_specs = (P(None, "gx", "gy", "grp"), P(None, ("gx", "grp"), "gy", None))

    def per_device(populations, thermal, *others):
        slab = Slab(mesh.shape, populations.shape[1:], thermal.shape[1:])
        plan = (lambda *arrays: on_slabs(slab, *arrays)) if slab.fits else on_device
        return plan(populations, thermal, *others)

    return jax.shard_map(
        per_device, mesh=mesh, in_specs=in_specs, out_specs=out_specs, check_vma=False
    )
```

```python
import jax
import jax.numpy as jnp
import numpy as np
from jax import lax
from jax.experimental import pallas as pl
from jax.experimental.pallas import tpu as pltpu
from jax.sharding import PartitionSpec as P

STEPS = 4
WINDOWS = 2


HIGHEST = lax.Precision.HIGHEST
BUOYANCY = 0.03
REFERENCE_HEAT = 1.0
OFFSET_TABLE = [(number // 9 - 1, number // 3 % 3 - 1, number % 3 - 1) for number in range(27)]
LATTICE_WEIGHTS = np.array(
    [
        np.prod([2.0 / 3.0 if component == 0 else 1.0 / 6.0 for component in triple])
        for triple in OFFSET_TABLE
    ]
)
VANDERMONDE = np.array([[1.0, 1.0, 1.0], [-1.0, 0.0, 1.0], [1.0, 0.0, 1.0]])
VANDER_INVERSE = np.array([[0.0, -0.5, 0.5], [1.0, 0.0, -1.0], [0.0, 0.5, 0.5]])
MOMENT_MATRIX = np.kron(np.kron(VANDERMONDE, VANDERMONDE), VANDERMONDE)
MOMENT_INVERSE = np.kron(np.kron(VANDER_INVERSE, VANDER_INVERSE), VANDER_INVERSE)
RELAXED = np.array([0.0 if number in (0, 1, 3, 9) else 1.0 for number in range(27)])
SUMMING = np.concatenate([np.ones((1, 27)), 1.0 * np.array(OFFSET_TABLE).T], axis=0)
HEAT_WEIGHTS = np.array([0.25] + [0.125] * 6)


def from_behind(value, axis, steps):
    count = lax.axis_size(axis)
    pairs = [(source, (source + steps) % count) for source in range(count)]
    return lax.ppermute(value, axis, pairs)


def extended(cells, sides, width):
    for axis, dim in sides:
        count = lax.axis_size(axis)
        head = lax.slice_in_dim(cells, 0, width, axis=dim)
        tail = lax.slice_in_dim(cells, cells.shape[dim] - width, cells.shape[dim], axis=dim)
        cells = jnp.concatenate(
            [
                lax.ppermute(tail, axis, [(i, (i + 1) % count) for i in range(count)]),
                cells,
                lax.ppermute(head, axis, [((i + 1) % count, i) for i in range(count)]),
            ],
            axis=dim,
        )
    return cells


def flow_state(flat, heat_flat):
    sums = jnp.dot(jnp.asarray(SUMMING, jnp.float32), flat, precision=HIGHEST)
    density = sums[0]
    force = BUOYANCY * (heat_flat - REFERENCE_HEAT)
    speed = jnp.stack([sums[1], sums[2], sums[3] + 0.5 * force]) / density
    return (density, force, speed)


def collide(popul, heat, rates):
    flat = popul.reshape(27, -1)
    density, force, speed = flow_state(flat, heat.reshape(-1))
    along = jnp.dot(jnp.asarray(SUMMING[1:].T, jnp.float32), speed, precision=HIGHEST)
    square = jnp.sum(speed * speed, axis=0)
    balance = (
        density
        * jnp.asarray(LATTICE_WEIGHTS, jnp.float32)[:, None]
        * (1.0 + 3.0 * along + 4.5 * along * along - 1.5 * square)
    )
    scaled = (
        jnp.asarray(MOMENT_INVERSE, jnp.float32)
        * (rates * jnp.asarray(RELAXED, jnp.float32))[None, :]
    )
    relax = jnp.dot(scaled, jnp.asarray(MOMENT_MATRIX, jnp.float32), precision=HIGHEST)
    post = (
        flat
        - jnp.dot(relax, flat - balance, precision=HIGHEST)
        + jnp.asarray(MOMENT_INVERSE[:, 1], jnp.float32)[:, None] * force[None, :]
    )
    return post.reshape(popul.shape)


def flow_speed(popul, heat, solid):
    density, force, speed = flow_state(popul.reshape(27, -1), heat.reshape(-1))
    return jnp.where(solid[None] == 0, speed.reshape((3,) + solid.shape), 0.0)


def heat_collide(heat_pops, speed, relax_time):
    total = jnp.sum(heat_pops, axis=0)
    still = jnp.zeros_like(speed[0])
    along = jnp.stack([still, speed[0], -speed[0], speed[1], -speed[1], speed[2], -speed[2]])
    balance = (
        jnp.asarray(HEAT_WEIGHTS, jnp.float32)[:, None, None, None]
        * total[None]
        * (1.0 + 4.0 * along)
    )
    return heat_pops - (heat_pops - balance) / relax_time[None]


def relaxation(phase_ids, conductivity):
    levels = jnp.arange(conductivity.shape[0], dtype=jnp.int32)
    chosen = jnp.sum(
        jnp.where(
            phase_ids[None] == levels[:, None, None, None], conductivity[:, None, None, None], 0.0
        ),
        axis=0,
    )
    return 0.5 + 4.0 * chosen


def inner_window(padded, triple, sizes):
    return padded[
        1 - triple[0] : 1 - triple[0] + sizes[0],
        1 - triple[1] : 1 - triple[1] + sizes[1],
        1 - triple[2] : 1 - triple[2] + sizes[2],
    ]


def advance(grid, axis_number, send_up, send_down):
    space = 3 + axis_number
    length = grid.shape[space]
    rising = lax.index_in_dim(grid, 2, axis_number, keepdims=True)
    resting = lax.index_in_dim(grid, 1, axis_number, keepdims=True)
    falling = lax.index_in_dim(grid, 0, axis_number, keepdims=True)
    from_below = send_up(lax.slice_in_dim(rising, length - 1, length, axis=space))
    from_above = send_down(lax.slice_in_dim(falling, 0, 1, axis=space))
    rising = jnp.concatenate(
        [from_below, lax.slice_in_dim(rising, 0, length - 1, axis=space)], axis=space
    )
    falling = jnp.concatenate(
        [lax.slice_in_dim(falling, 1, length, axis=space), from_above], axis=space
    )
    return jnp.concatenate([falling, resting, rising], axis=axis_number)


def flow_arrivals(post):
    sizes = post.shape[1:]
    grid = post.reshape((3, 3, 3) + sizes)
    grid = advance(
        grid,
        0,
        lambda plane: from_behind(plane, "gx", 1),
        lambda plane: from_behind(plane, "gx", -1),
    )
    grid = advance(
        grid,
        1,
        lambda plane: from_behind(plane, "gy", 1),
        lambda plane: from_behind(plane, "gy", -1),
    )
    grid = advance(
        grid,
        2,
        lambda plane: from_behind(plane, "grp", 1),
        lambda plane: from_behind(plane, "grp", -1),
    )
    return grid.reshape(post.shape)


def stream_heat(post, grp_index, last_grp):
    length = post.shape[1]
    size_y = post.shape[2]
    eastward = post[1]
    westward = post[2]
    lower_first = from_behind(eastward, "grp", 1)
    lower_second = from_behind(lower_first, "gx", 1)
    entering = jnp.where(grp_index == 0, lower_second, lower_first)
    eastward = jnp.concatenate([entering, eastward[: length - 1]], axis=0)
    upper_first = from_behind(westward, "grp", -1)
    upper_second = from_behind(upper_first, "gx", -1)
    entering = jnp.where(grp_index == last_grp, upper_second, upper_first)
    westward = jnp.concatenate([westward[1:], entering], axis=0)
    sides = extended(post[3:5], (("gy", 2),), 1)
    northward = sides[0, :, 0:size_y]
    southward = sides[1, :, 2 : size_y + 2]
    upward = jnp.roll(post[5], 1, axis=2)
    downward = jnp.roll(post[6], -1, axis=2)
    return jnp.stack([post[0], eastward, westward, northward, southward, upward, downward])


def on_device(populations, thermal, velocity_prev, solid, phase_ids, conductivity, rates):
    padded_solid = extended(solid, (("grp", 2), ("gx", 0), ("gy", 1)), 1)
    sizes = solid.shape
    blocked = jnp.stack(
        [inner_window(padded_solid, OFFSET_TABLE[number], sizes) != 0 for number in range(27)]
    )
    fluid_cells = (solid == 0)[None]
    grp_index = lax.axis_index("grp")
    last_grp = lax.axis_size("grp") - 1
    relax_time = relaxation(phase_ids, conductivity)
    speed_brick = velocity_prev
    popul = populations
    heat_pops = thermal
    for window_number in range(WINDOWS):
        heat_brick = lax.all_to_all(
            jnp.sum(heat_pops, axis=0), "grp", split_axis=2, concat_axis=0, tiled=True
        )
        speed_column = lax.all_to_all(speed_brick, "grp", split_axis=1, concat_axis=3, tiled=True)
        for step_number in range(STEPS):
            post = collide(popul, heat_brick, rates)
            arrived = flow_arrivals(post)
            popul = jnp.where(fluid_cells, jnp.where(blocked, post[::-1], arrived), popul)
        for step_number in range(STEPS):
            heat_pops = stream_heat(
                heat_collide(heat_pops, speed_column, relax_time), grp_index, last_grp
            )
        if window_number + 1 < WINDOWS:
            speed_brick = flow_speed(popul, heat_brick, solid)
    return (popul, heat_pops)


SUBLANES = 8
LANES = 128
F32 = jnp.float32


class Slab:
    def __init__(self, mesh_shape, flow_block, heat_block):
        self.grp, self.gx, self.gy = (mesh_shape[name] for name in ("grp", "gx", "gy"))
        self.block_x, self.block_y, self.block_z = flow_block
        self.sub = self.gx * self.gy
        self.planes = self.block_z // self.sub
        self.halo = self.planes // 2
        self.fits = (
            self.block_y == SUBLANES
            and self.block_z == LANES
            and self.planes * self.sub == LANES
            and self.halo * 2 == self.planes
            and WINDOWS == 2
            and self.halo == STEPS * WINDOWS
            and self.sub >= 8
            and 2 * self.block_x == self.sub
            and self.block_x == self.grp
            and heat_block == (1, SUBLANES, self.grp * LANES)
            and self.sub & (self.sub - 1) == 0
            and self.grp & (self.grp - 1) == 0
            and self.gy % 2 == 0
            and self.sub % self.grp == 0
        )
        if self.fits:
            self.turn = self.sub // self.grp
            partners = [step for k in (1, 0) for step in range(self.sub - 2 + k, 1, -2)]
            partners.sort(key=lambda step: bin(step >> 1).count("1"))
            self.steps = [0, 1] + partners
            self.ring = [
                part * self.sub + self.round_plane((place - self.turn * part) % self.sub)
                for part in range(self.grp)
                for place in range(self.sub)
            ]

    def round_plane(self, number):
        x, y = number // self.gy, number % self.gy
        back = x % 2
        return x * self.gy + y + back * (self.gy - 1 - 2 * y)

    def holders(self, part):
        begin = self.sub * self.grp - self.turn * part
        mine = self.place_in_plane()
        return [
            jnp.bitwise_xor(self.round_plane(lax.rem(begin + place, self.sub)), mine)
            for place in range(self.sub)
        ]

    def planes_far_first(self):
        return [0] + list(range(self.grp - 1, 0, -1))

    def place_in_plane(self):
        return lax.axis_index("gx") * self.gy + lax.axis_index("gy")


def lane_index():
    return lax.broadcasted_iota(jnp.int32, (SUBLANES, LANES), 1)


def row_index():
    return lax.broadcasted_iota(jnp.int32, (SUBLANES, LANES), 0)


def lane_roll(value, amount):
    amount = amount % LANES
    return value if amount == 0 else pltpu.roll(value, amount, 1)


def swap_groups(values, group):
    count = len(values)
    lane = lane_index()
    values = list(values)
    bit = 1
    while bit < count:
        low = (lane // (group * bit)) % 2 == 0
        for first in range(count):
            if first & bit == 0:
                a, b = values[first], values[first | bit]
                if 2 * group * bit == LANES:
                    crossed = lane_roll(jnp.where(low, b, a), group * bit)
                    values[first] = jnp.where(low, a, crossed)
                    values[first | bit] = jnp.where(low, crossed, b)
                    continue
                values[first] = jnp.where(low, a, lane_roll(b, group * bit))
                values[first | bit] = jnp.where(low, lane_roll(a, -group * bit), b)
        bit *= 2
    return values


SPEED_AT, SOLID_AT = 27, 30
IN_PAIRS = 16
FLOW_PAIRS = 14


def pack_in(
    slab, levels_hbm, popul_hbm, speed_hbm, solid_hbm, heat_hbm, phase_hbm, sent, *scratch
):
    levels_ref, fields, solid_ref, heat_ref, phase_ref, sems = scratch
    copies = [
        pltpu.make_async_copy(source, target, sems.at[number])
        for number, (source, target) in enumerate(
            [
                (heat_hbm, heat_ref),
                (phase_hbm, phase_ref),
                (levels_hbm, levels_ref),
                (speed_hbm, fields.at[pl.ds(SPEED_AT, 3)]),
                (solid_hbm, solid_ref),
                (popul_hbm, fields.at[pl.ds(0, SPEED_AT)]),
            ]
        )
    ]
    for copy in copies:
        copy.start()
    for copy in copies[:3]:
        copy.wait()
    lane = lane_index()
    first = in_first_half(slab)
    columns = []
    for part in range(slab.grp):
        span = pl.ds(part * LANES, LANES)
        phase = phase_ref[0, :, span]
        chosen = jnp.zeros((SUBLANES, LANES), F32)
        for level in range(levels_ref.shape[0]):
            chosen = jnp.where(phase == level, levels_ref[level], chosen)
        columns.append([heat_ref[k, 0, :, span] for k in range(7)] + [1.0 / (0.5 + 4.0 * chosen)])
    for part in range(slab.grp):
        own, after = columns[part], columns[(part + 1) % slab.grp]
        before = columns[part - 1]
        beside = []
        for k in range(8):
            above = jnp.where(lane < slab.planes, after[k], own[k])
            below = jnp.where(lane >= LANES - slab.planes, before[k], own[k])
            beside.append(
                jnp.where(first, lane_roll(above, -slab.planes), lane_roll(below, slab.planes))
            )
        holders = slab.holders(part)
        for which, sources in enumerate((own, beside)):
            for place, value in enumerate(swap_groups(sources, slab.planes)):
                sent[holders[place], IN_PAIRS + 2 * part + which] = value
    for copy in copies[3:]:
        copy.wait()
    fields[SOLID_AT] = solid_ref[...].astype(F32)
    fields[SOLID_AT + 1] = jnp.zeros(solid_ref.shape, F32)
    holders = slab.holders(lax.axis_index("grp"))
    for pair in range(IN_PAIRS):
        sources = [fields[2 * pair + h, x] for x in range(slab.block_x) for h in range(2)]
        for place, value in enumerate(swap_groups(sources, slab.planes)):
            sent[holders[place], pair] = value


def in_first_half(slab):
    return lane_index() % slab.planes < slab.halo


def collect(slab, parts, came):
    mine = slab.place_in_plane()
    for part, step in zip(parts, slab.steps):
        came[jnp.bitwise_xor(mine, step)] = part[...]


def offer_halo(slab, *refs):
    parts, (came, low_out, high_out, *heat_outs) = refs[: slab.sub], refs[slab.sub :]
    collect(slab, parts, came)
    mine = lax.axis_index("grp")
    for step, heat_out in enumerate(heat_outs):
        slots = pl.ds(IN_PAIRS + 2 * jnp.bitwise_xor(mine, step), 2)
        for tile in range(slab.sub):
            heat_out[tile] = came[tile, slots]

    def one(number, _):
        tile = 2 * number
        first = in_first_half(slab)
        for pair in range(IN_PAIRS):
            a, b = came[tile, pair], came[tile + 1, pair]
            low_out[number, pair] = jnp.where(first, a, lane_roll(b, slab.halo))
            high_out[number, pair] = jnp.where(first, lane_roll(b, -slab.halo), a)
        return 0

    lax.fori_loop(0, slab.sub // 2, one, 0)


def make_heat_tiles(slab, parts, held, heat_tiles):
    mine = lax.axis_index("grp")
    for step, part in zip(slab.planes_far_first(), parts):
        held[jnp.bitwise_xor(mine, step)] = part[...]
    first = in_first_half(slab)
    for tile in range(slab.sub):
        sources = []
        for x in range(slab.block_x):
            after = held[(x + 1) % slab.block_x, tile, 1]
            sources += [held[x, tile, 0], jnp.where(first, held[x, tile, 1], after)]
        for k, value in enumerate(swap_groups(sources, slab.planes)):
            heat_tiles[k, tile] = value


def make_tiles(slab, came, below_ref, above_ref, state):
    def one(number, _):
        first = in_first_half(slab)
        even = (lane_index() // slab.planes) % 2 == 0
        back = 2 * slab.planes
        for pair in range(IN_PAIRS):
            below, above = below_ref[number, pair], above_ref[number, pair]
            beside = (
                jnp.where(first, above, lane_roll(below, -back)),
                jnp.where(first, lane_roll(above, -slab.halo), lane_roll(below, slab.halo - back)),
            )
            for which in range(2):
                tile = 2 * number + which
                own, halo = came[tile, pair], beside[which]
                state[2 * pair, tile] = jnp.where(even, own, lane_roll(halo, slab.planes))
                state[2 * pair + 1, tile] = jnp.where(even, lane_roll(own, -slab.planes), halo)
        return 0

    lax.fori_loop(0, slab.sub // 2, one, 0)


def pack_out(slab, flow, came, tile, sent):
    even = (lane_index() // slab.planes) % 2 == 0
    flags = came[tile, SOLID_AT // 2]
    solid = jnp.where(even, flags, lane_roll(flags, slab.planes)) != 0.0
    partner = jnp.bitwise_xor(tile, slab.place_in_plane())
    for pair in range(FLOW_PAIRS):
        value = flow[2 * pair]
        if 2 * pair + 1 < len(flow):
            value = jnp.where(even, value, lane_roll(flow[2 * pair + 1], slab.planes))
        sent[partner, pair] = jnp.where(solid, came[tile, pair], value)


def add_heat(slab, sent_in, *refs):
    parts, (sent, packed, sem) = refs[: slab.grp], refs[slab.grp :]
    mine = slab.place_in_plane()
    for tile in range(slab.sub):
        for step in range(slab.grp):
            packed[jnp.bitwise_xor(mine, tile), step] = parts[step][tile]
    copy = pltpu.make_async_copy(packed, sent.at[:, pl.ds(FLOW_PAIRS, slab.grp)], sem)
    copy.start()
    copy.wait()


def unpack_out(slab, *refs):
    parts, (popul_hbm, thermal_hbm, came, popul, thermal, sems) = refs[: slab.sub], refs[slab.sub :]
    for part, step in zip(parts, slab.steps):
        came[step] = part[...]
    mine = lax.axis_index("grp")
    for step in range(slab.grp):
        part = jnp.bitwise_xor(mine, step)
        holders = slab.holders(part)
        span = pl.ds(pl.multiple_of(part * LANES, LANES), LANES)
        sources = [came[holders[place], FLOW_PAIRS + step] for place in range(slab.sub)]
        for k, value in enumerate(swap_groups(sources, slab.planes)[:7]):
            thermal[k, 0, :, span] = value
    copies = [pltpu.make_async_copy(thermal, thermal_hbm, sems.at[0])]
    copies[0].start()
    holders = slab.holders(mine)
    begin = 0
    for pair in range(FLOW_PAIRS):
        sources = [came[holders[place], pair] for place in range(slab.sub)]
        for number, value in enumerate(swap_groups(sources, slab.planes)):
            if 2 * pair + number % 2 < 27:
                popul[2 * pair + number % 2, number // 2] = value
        end = min(2 * pair + 2, 27)
        if pair % 4 == 3 or end == 27:
            rows = pl.ds(begin, end - begin)
            sem = sems.at[len(copies)]
            copies.append(pltpu.make_async_copy(popul.at[rows], popul_hbm.at[rows], sem))
            copies[-1].start()
            begin = end
    for copy in copies:
        copy.wait()


def forward3(values):
    for stride in (9, 3, 1):
        out = [None] * 27
        for n in range(27):
            if n // stride % 3 == 0:
                a, b, c = values[n], values[n + stride], values[n + 2 * stride]
                both = a + c
                out[n], out[n + stride], out[n + 2 * stride] = both + b, c - a, both
        values = out
    return values


def backward3(values):
    for stride in (9, 3, 1):
        out = [None] * 27
        for n in range(27):
            if n // stride % 3 == 0:
                a, b, c = values[n], values[n + stride], values[n + 2 * stride]
                even, odd = 0.5 * c, 0.5 * b
                out[n], out[n + stride], out[n + 2 * stride] = even - odd, a - c, even + odd
        values = out
    return values


def collide_tile(values, force, rate, solid):
    moments = forward3(values)
    density = moments[0]
    jx, jy, jz = moments[9], moments[3], moments[1] + 0.5 * force
    inverse = 1.0 / density
    flux = (jx, jy, jz)
    u = tuple(j * inverse for j in flux)
    third = 1.0 / 3.0
    base = {0: density}
    for k in (1, 2, 3):
        base[k] = density * third**k
    squares = [flux[d] * u[d] for d in range(3)]
    square_at = {}
    scaled = {}

    def scale(key, value, count):
        if count == 0:
            return value
        if (key, count) not in scaled:
            scaled[key, count] = value * third**count
        return scaled[key, count]

    cross = {(0, 1): jx * u[1], (0, 2): jx * u[2], (1, 2): jy * u[2]}
    out = [None] * 27
    for n in range(27):
        powers = (n // 9, n // 3 % 3, n % 3)
        if n in (0, 3, 9):
            out[n] = moments[n]
            continue
        if n == 1:
            out[n] = moments[n] + force
            continue
        odd = tuple(d for d in range(3) if powers[d] == 1)
        even = tuple(d for d in range(3) if powers[d] == 2)
        count = len(even)
        if len(odd) == 3:
            out[n] = moments[n] - rate(n) * moments[n]
            continue
        if len(odd) == 0:
            if even not in square_at:
                total = squares[even[0]]
                for d in even[1:]:
                    total = total + squares[d]
                square_at[even] = base[count] + (total * (3.0 * third**count) if count > 1 else total)
            level = square_at[even]
        elif len(odd) == 1:
            level = scale(odd, flux[odd[0]], count)
        else:
            level = scale(odd, cross[odd], count)
        out[n] = moments[n] - rate(n) * (moments[n] - level)
    out[26] = jnp.where(solid, jnp.nan, out[26])
    return backward3(out)


HEAT_OFFSETS = [(0, 0, 0), (1, 0, 0), (-1, 0, 0), (0, 1, 0), (0, -1, 0), (0, 0, 1), (0, 0, -1)]


def collide_flow(rates_ref, flow, force, solid, target, tile):
    for n, value in enumerate(collide_tile(flow, force, lambda n: rates_ref[n], solid)):
        target[n, tile] = value


def collide_heat(heat, omega, speeds, target, tile):
    total = heat[0]
    for k in range(1, 7):
        total = total + heat[k]
    side = 0.125 * total
    half = 0.5 * total
    for k in range(7):
        if k == 0:
            level = 0.25 * total
        else:
            drift = half * speeds[(k - 1) // 2]
            level = side + drift if k % 2 == 1 else side - drift
        target[k, tile] = heat[k] - (heat[k] - level) * omega


def stream(slab, post, tile, offsets):
    block_x, block_y = lax.div(tile, slab.gy), lax.rem(tile, slab.gy)
    x_of = {a: lax.rem(block_x + slab.gx - a, slab.gx) for a in (-1, 0, 1)}
    y_of = {b: lax.rem(block_y + slab.gy - b, slab.gy) for b in (-1, 0, 1)}
    row = row_index()
    per_x = 2 * slab.planes
    in_x = (lane_index() + slab.halo) % LANES // per_x
    last_x = {1: in_x == slab.block_x - 1, -1: in_x == 0}
    last_y = {1: row == SUBLANES - 1, -1: row == 0}

    def arrive(number, offset):
        a, b, c = offset

        def take(x):
            value = post[number, x_of[x] * slab.gy + block_y]
            if b != 0:
                other = post[number, x_of[x] * slab.gy + y_of[b]]
                value = jnp.where(last_y[b], other, value)
            return value

        value = take(0)
        if a != 0:
            value = jnp.where(last_x[a], take(a), value)
        if b != 0:
            value = pltpu.roll(value, b % SUBLANES, 0)
        return lane_roll(value, a * per_x + c)

    return [arrive(number, offset) for number, offset in enumerate(offsets)]


def stream_flow(slab, post, tile):
    return [
        jnp.where(value != value, post[26 - n, tile], value)
        for n, value in enumerate(stream(slab, post, tile, OFFSET_TABLE))
    ]


def over_tiles(slab, body, unroll=1):
    def one(tile, _):
        body(tile)
        return 0

    lax.fori_loop(0, slab.sub, one, 0, unroll=unroll)


def one_ahead(slab, arrive, collide, held):
    def bring(tile):
        for number, value in enumerate(arrive(tile)):
            held[number] = value

    def body(tile):
        values = [held[number] for number in range(held.shape[0])]
        bring(lax.rem(tile + 1, slab.sub))
        collide(tile, values)

    bring(jnp.int32(0))
    over_tiles(slab, body)


def over_steps(count, body):
    def one(number, _):
        body(number)
        return 0

    lax.fori_loop(0, count, one, 0)


def first_window(slab, rates_hbm, state, *refs):
    heat_parts, refs = refs[: slab.grp], refs[slab.grp :]
    flow_out, keep_out, heat_outs = refs[0], refs[1], refs[2 : 2 + slab.grp]
    (rates_ref, sem, speed, heat_tiles, flow_post, heat_post, heat_a, heat_b, held, came_heat, ahead) = (
        refs[2 + slab.grp :]
    )
    rates_copy = pltpu.make_async_copy(rates_hbm, rates_ref, sem)
    rates_copy.start()
    make_heat_tiles(slab, heat_parts, came_heat, heat_tiles)
    rates_copy.wait()

    def speeds_of(tile):
        return [speed[d, tile] for d in range(3)]

    def begin(tile):
        solid = state[SOLID_AT, tile]
        heat = [heat_tiles[k, tile] for k in range(7)]
        for d in range(3):
            speed[d, tile] = state[SPEED_AT + d, tile]
        force = heat_force(heat)
        keep_out[0, tile] = force
        keep_out[1, tile] = solid
        flow = [state[n, tile] for n in range(27)]
        collide_flow(rates_ref, flow, force, solid != 0.0, flow_post.at[0], tile)
        collide_heat(heat, heat_tiles[7, tile], speeds_of(tile), heat_post.at[0], tile)

    over_tiles(slab, begin)

    def arrive(tile, source):
        flow = stream_flow(slab, flow_post.at[source], tile)
        return flow + stream(slab, heat_post.at[source], tile, HEAT_OFFSETS)

    def step(number):
        source = lax.rem(number, 2)

        def go_on(tile, values):
            flow, heat = values[:27], values[27:]
            solid = state[SOLID_AT, tile] != 0.0
            collide_flow(rates_ref, flow, keep_out[0, tile], solid, flow_post.at[1 - source], tile)
            omega = heat_tiles[7, tile]
            collide_heat(heat, omega, speeds_of(tile), heat_post.at[1 - source], tile)

        one_ahead(slab, lambda tile: arrive(tile, source), go_on, ahead)

    over_steps(STEPS - 1, step)
    source = (STEPS - 1) % 2

    def next_window(tile, values):
        flow, heat = values[:27], values[27:]
        solid = state[SOLID_AT, tile] != 0.0
        speeds = [
            jnp.where(solid, 0.0, each) for each in flow_speed_tile(flow, keep_out[0, tile])
        ]
        for d in range(3):
            speed[d, tile] = speeds[d]
        force = heat_force(heat)
        keep_out[0, tile] = force
        collide_flow(rates_ref, flow, force, solid, flow_out, tile)
        collide_heat(heat, heat_tiles[7, tile], speeds, heat_a, tile)

    one_ahead(slab, lambda tile: arrive(tile, source), next_window, ahead)
    here, there = heat_a, heat_b
    for _ in range(STEPS - 1):

        def heat_alone(tile, here=here, there=there):
            heat = stream(slab, here, tile, HEAT_OFFSETS)
            collide_heat(heat, heat_tiles[7, tile], speeds_of(tile), there, tile)

        over_tiles(slab, heat_alone, unroll=4)
        here, there = there, here
    zero = jnp.zeros((SUBLANES, LANES), F32)

    def end_heat(tile):
        heat = stream(slab, here, tile, HEAT_OFFSETS)
        heat += [zero] * (slab.sub - 7)
        for x, value in enumerate(swap_groups(heat, slab.planes)[0::2]):
            held[x, tile] = value

    over_tiles(slab, end_heat, unroll=2)
    mine = lax.axis_index("grp")
    for step_number in range(slab.grp):
        heat_outs[step_number][...] = held[jnp.bitwise_xor(mine, step_number)]


def last_window(slab, rates_hbm, came, flow_in, keep_ref, sent, rates_ref, sem, flow_post, ahead):
    rates_copy = pltpu.make_async_copy(rates_hbm, rates_ref, sem)
    rates_copy.start()

    def copy(n, _):
        flow_post[0, n] = flow_in[n]
        return 0

    lax.fori_loop(0, 27, copy, 0, unroll=3)
    rates_copy.wait()

    def step(number):
        source = lax.rem(number, 2)

        def go_on(tile, flow):
            solid = keep_ref[1, tile] != 0.0
            collide_flow(rates_ref, flow, keep_ref[0, tile], solid, flow_post.at[1 - source], tile)

        one_ahead(slab, lambda tile: stream_flow(slab, flow_post.at[source], tile), go_on, ahead)

    over_steps(STEPS - 1, step)

    def arrive(tile):
        return stream_flow(slab, flow_post.at[(STEPS - 1) % 2], tile)

    one_ahead(slab, arrive, lambda tile, flow: pack_out(slab, flow, came, tile, sent), ahead)


def heat_force(heat):
    total = heat[0]
    for k in range(1, 7):
        total = total + heat[k]
    return BUOYANCY * (total - REFERENCE_HEAT)


def flow_speed_tile(values, force):
    total = values[0]
    for n in range(1, 27):
        total = total + values[n]
    sums = []
    for d in range(3):
        plus, minus = None, None
        for n in range(27):
            part = OFFSET_TABLE[n][d]
            if part == 1:
                plus = values[n] if plus is None else plus + values[n]
            if part == -1:
                minus = values[n] if minus is None else minus + values[n]
        sums.append(plus - minus)
    sums[2] = sums[2] + 0.5 * force
    return [each / total for each in sums]


def local_call(body, slab, arrays, outs, scratch=(), in_hbm=0, carried=False, outs_in_hbm=False):
    def kernel(*refs):
        body(slab, *refs)

    return pl.pallas_call(
        kernel,
        out_shape=[jax.ShapeDtypeStruct(shape, F32) for shape in outs],
        in_specs=[
            pl.BlockSpec(
                memory_space=pltpu.HBM if i < in_hbm else pl.ANY if carried and i == 0 else pltpu.VMEM
            )
            for i in range(len(arrays))
        ],
        out_specs=[
            pl.BlockSpec(memory_space=pl.ANY if carried or outs_in_hbm else pltpu.VMEM)
        ]
        * len(outs),
        input_output_aliases={0: 0} if carried else {},
        scratch_shapes=[pltpu.VMEM(s, F32) if isinstance(s, tuple) else s for s in scratch],
        compiler_params=pltpu.CompilerParams(vmem_limit_bytes=24 * 1024 * 1024),
    )(
        *(
            pltpu.with_memory_space_constraint(array, pltpu.HBM) if i < in_hbm else array
            for i, array in enumerate(arrays)
        )
    )


RING = ("grp", "gx", "gy")


def exchange(slab, low, high):
    ring = slab.ring
    upward = [(ring[i - 1], ring[i]) for i in range(len(ring))]
    from_below = lax.ppermute(high, RING, upward)
    from_above = lax.ppermute(low, RING, [(b, a) for a, b in upward])
    return from_below, from_above


def across_plane(slab, sent):
    came = {0: sent[0]}
    for step in slab.steps[1:]:
        pairs = [(i, i ^ step) for i in range(slab.sub)]
        came[step] = lax.ppermute(sent[step], ("gx", "gy"), pairs)
    return [came[step] for step in slab.steps]


def across_planes(slab, parts):
    return [parts[0]] + [
        lax.ppermute(parts[step], "grp", [(i, i ^ step) for i in range(slab.grp)])
        for step in range(1, slab.grp)
    ]


def on_slabs(slab, populations, thermal, velocity_prev, solid, phase_ids, conductivity, rates):
    tile = (SUBLANES, LANES)

    def vmem_like(array):
        return pltpu.VMEM(array.shape, array.dtype)

    sent_shape = (slab.sub, IN_PAIRS + 2 * slab.grp) + tile
    (sent,) = local_call(
        pack_in,
        slab,
        [conductivity, populations, velocity_prev, solid, thermal, phase_ids],
        [sent_shape],
        [
            pltpu.SMEM(conductivity.shape, F32),
            (2 * IN_PAIRS,) + solid.shape,
            vmem_like(solid),
            vmem_like(thermal),
            vmem_like(phase_ids),
            pltpu.SemaphoreType.DMA((6,)),
        ],
        in_hbm=6,
    )
    plane = (slab.sub,) + tile
    halo_shape = (slab.sub // 2, IN_PAIRS) + tile
    heat_shape = (slab.sub, 2) + tile
    came, low, high, *parts = local_call(
        offer_halo,
        slab,
        across_plane(slab, sent),
        [sent_shape, halo_shape, halo_shape] + [heat_shape] * slab.grp,
    )
    below, above = exchange(slab, low, high)
    parts = across_planes(slab, parts)
    (state,) = local_call(make_tiles, slab, [came, below, above], [(2 * IN_PAIRS,) + plane])
    scalars = [pltpu.SMEM(rates.shape, F32), pltpu.SemaphoreType.DMA]
    flow, keep, *parts = local_call(
        first_window,
        slab,
        [rates, state] + [parts[step] for step in slab.planes_far_first()],
        [(27,) + plane, (2,) + plane] + [plane] * slab.grp,
        scalars
        + [(3,) + plane, (8,) + plane, (2, 27) + plane, (2, 7) + plane]
        + [(7,) + plane] * 2
        + [(slab.grp,) + plane, (slab.grp,) + heat_shape, (34,) + tile],
        in_hbm=1,
    )
    parts = across_planes(slab, parts)
    last_shape = (slab.sub, FLOW_PAIRS + slab.grp) + tile
    (sent,) = local_call(
        last_window,
        slab,
        [rates, came, flow, keep],
        [last_shape],
        scalars + [(2, 27) + plane, (27,) + tile],
        in_hbm=1,
    )
    (sent,) = local_call(
        add_heat,
        slab,
        [sent] + parts,
        [last_shape],
        [(slab.sub, slab.grp) + tile, pltpu.SemaphoreType.DMA],
        carried=True,
    )
    return tuple(
        local_call(
            unpack_out,
            slab,
            across_plane(slab, sent),
            [populations.shape, thermal.shape],
            [
                last_shape,
                populations.shape,
                thermal.shape,
                pltpu.SemaphoreType.DMA((1 + -(-FLOW_PAIRS // 4),)),
            ],
            outs_in_hbm=True,
        )
    )


def solution(mesh):
    in_specs = (
        P(None, "gx", "gy", "grp"),
        P(None, ("gx", "grp"), "gy", None),
        P(None, "gx", "gy", "grp"),
        P("gx", "gy", "grp"),
        P(("gx", "grp"), "gy", None),
        P(),
        P(),
    )
    out_specs = (P(None, "gx", "gy", "grp"), P(None, ("gx", "grp"), "gy", None))

    def per_device(populations, thermal, *others):
        slab = Slab(mesh.shape, populations.shape[1:], thermal.shape[1:])
        plan = (lambda *arrays: on_slabs(slab, *arrays)) if slab.fits else on_device
        return plan(populations, thermal, *others)

    return jax.shard_map(
        per_device, mesh=mesh, in_specs=in_specs, out_specs=out_specs, check_vma=False
    )
```

```python
import jax
import jax.numpy as jnp
import numpy as np
from jax import lax
from jax.experimental import pallas as pl
from jax.experimental.pallas import tpu as pltpu
from jax.sharding import PartitionSpec as P

STEPS = 4
WINDOWS = 2


HIGHEST = lax.Precision.HIGHEST
BUOYANCY = 0.03
REFERENCE_HEAT = 1.0
OFFSET_TABLE = [(number // 9 - 1, number // 3 % 3 - 1, number % 3 - 1) for number in range(27)]
LATTICE_WEIGHTS = np.array(
    [
        np.prod([2.0 / 3.0 if component == 0 else 1.0 / 6.0 for component in triple])
        for triple in OFFSET_TABLE
    ]
)
VANDERMONDE = np.array([[1.0, 1.0, 1.0], [-1.0, 0.0, 1.0], [1.0, 0.0, 1.0]])
VANDER_INVERSE = np.array([[0.0, -0.5, 0.5], [1.0, 0.0, -1.0], [0.0, 0.5, 0.5]])
MOMENT_MATRIX = np.kron(np.kron(VANDERMONDE, VANDERMONDE), VANDERMONDE)
MOMENT_INVERSE = np.kron(np.kron(VANDER_INVERSE, VANDER_INVERSE), VANDER_INVERSE)
RELAXED = np.array([0.0 if number in (0, 1, 3, 9) else 1.0 for number in range(27)])
SUMMING = np.concatenate([np.ones((1, 27)), 1.0 * np.array(OFFSET_TABLE).T], axis=0)
HEAT_WEIGHTS = np.array([0.25] + [0.125] * 6)


def from_behind(value, axis, steps):
    count = lax.axis_size(axis)
    pairs = [(source, (source + steps) % count) for source in range(count)]
    return lax.ppermute(value, axis, pairs)


def extended(cells, sides, width):
    for axis, dim in sides:
        count = lax.axis_size(axis)
        head = lax.slice_in_dim(cells, 0, width, axis=dim)
        tail = lax.slice_in_dim(cells, cells.shape[dim] - width, cells.shape[dim], axis=dim)
        cells = jnp.concatenate(
            [
                lax.ppermute(tail, axis, [(i, (i + 1) % count) for i in range(count)]),
                cells,
                lax.ppermute(head, axis, [((i + 1) % count, i) for i in range(count)]),
            ],
            axis=dim,
        )
    return cells


def flow_state(flat, heat_flat):
    sums = jnp.dot(jnp.asarray(SUMMING, jnp.float32), flat, precision=HIGHEST)
    density = sums[0]
    force = BUOYANCY * (heat_flat - REFERENCE_HEAT)
    speed = jnp.stack([sums[1], sums[2], sums[3] + 0.5 * force]) / density
    return (density, force, speed)


def collide(popul, heat, rates):
    flat = popul.reshape(27, -1)
    density, force, speed = flow_state(flat, heat.reshape(-1))
    along = jnp.dot(jnp.asarray(SUMMING[1:].T, jnp.float32), speed, precision=HIGHEST)
    square = jnp.sum(speed * speed, axis=0)
    balance = (
        density
        * jnp.asarray(LATTICE_WEIGHTS, jnp.float32)[:, None]
        * (1.0 + 3.0 * along + 4.5 * along * along - 1.5 * square)
    )
    scaled = (
        jnp.asarray(MOMENT_INVERSE, jnp.float32)
        * (rates * jnp.asarray(RELAXED, jnp.float32))[None, :]
    )
    relax = jnp.dot(scaled, jnp.asarray(MOMENT_MATRIX, jnp.float32), precision=HIGHEST)
    post = (
        flat
        - jnp.dot(relax, flat - balance, precision=HIGHEST)
        + jnp.asarray(MOMENT_INVERSE[:, 1], jnp.float32)[:, None] * force[None, :]
    )
    return post.reshape(popul.shape)


def flow_speed(popul, heat, solid):
    density, force, speed = flow_state(popul.reshape(27, -1), heat.reshape(-1))
    return jnp.where(solid[None] == 0, speed.reshape((3,) + solid.shape), 0.0)


def heat_collide(heat_pops, speed, relax_time):
    total = jnp.sum(heat_pops, axis=0)
    still = jnp.zeros_like(speed[0])
    along = jnp.stack([still, speed[0], -speed[0], speed[1], -speed[1], speed[2], -speed[2]])
    balance = (
        jnp.asarray(HEAT_WEIGHTS, jnp.float32)[:, None, None, None]
        * total[None]
        * (1.0 + 4.0 * along)
    )
    return heat_pops - (heat_pops - balance) / relax_time[None]


def relaxation(phase_ids, conductivity):
    levels = jnp.arange(conductivity.shape[0], dtype=jnp.int32)
    chosen = jnp.sum(
        jnp.where(
            phase_ids[None] == levels[:, None, None, None], conductivity[:, None, None, None], 0.0
        ),
        axis=0,
    )
    return 0.5 + 4.0 * chosen


def inner_window(padded, triple, sizes):
    return padded[
        1 - triple[0] : 1 - triple[0] + sizes[0],
        1 - triple[1] : 1 - triple[1] + sizes[1],
        1 - triple[2] : 1 - triple[2] + sizes[2],
    ]


def advance(grid, axis_number, send_up, send_down):
    space = 3 + axis_number
    length = grid.shape[space]
    rising = lax.index_in_dim(grid, 2, axis_number, keepdims=True)
    resting = lax.index_in_dim(grid, 1, axis_number, keepdims=True)
    falling = lax.index_in_dim(grid, 0, axis_number, keepdims=True)
    from_below = send_up(lax.slice_in_dim(rising, length - 1, length, axis=space))
    from_above = send_down(lax.slice_in_dim(falling, 0, 1, axis=space))
    rising = jnp.concatenate(
        [from_below, lax.slice_in_dim(rising, 0, length - 1, axis=space)], axis=space
    )
    falling = jnp.concatenate(
        [lax.slice_in_dim(falling, 1, length, axis=space), from_above], axis=space
    )
    return jnp.concatenate([falling, resting, rising], axis=axis_number)


def flow_arrivals(post):
    sizes = post.shape[1:]
    grid = post.reshape((3, 3, 3) + sizes)
    grid = advance(
        grid,
        0,
        lambda plane: from_behind(plane, "gx", 1),
        lambda plane: from_behind(plane, "gx", -1),
    )
    grid = advance(
        grid,
        1,
        lambda plane: from_behind(plane, "gy", 1),
        lambda plane: from_behind(plane, "gy", -1),
    )
    grid = advance(
        grid,
        2,
        lambda plane: from_behind(plane, "grp", 1),
        lambda plane: from_behind(plane, "grp", -1),
    )
    return grid.reshape(post.shape)


def stream_heat(post, grp_index, last_grp):
    length = post.shape[1]
    size_y = post.shape[2]
    eastward = post[1]
    westward = post[2]
    lower_first = from_behind(eastward, "grp", 1)
    lower_second = from_behind(lower_first, "gx", 1)
    entering = jnp.where(grp_index == 0, lower_second, lower_first)
    eastward = jnp.concatenate([entering, eastward[: length - 1]], axis=0)
    upper_first = from_behind(westward, "grp", -1)
    upper_second = from_behind(upper_first, "gx", -1)
    entering = jnp.where(grp_index == last_grp, upper_second, upper_first)
    westward = jnp.concatenate([westward[1:], entering], axis=0)
    sides = extended(post[3:5], (("gy", 2),), 1)
    northward = sides[0, :, 0:size_y]
    southward = sides[1, :, 2 : size_y + 2]
    upward = jnp.roll(post[5], 1, axis=2)
    downward = jnp.roll(post[6], -1, axis=2)
    return jnp.stack([post[0], eastward, westward, northward, southward, upward, downward])


def on_device(populations, thermal, velocity_prev, solid, phase_ids, conductivity, rates):
    padded_solid = extended(solid, (("grp", 2), ("gx", 0), ("gy", 1)), 1)
    sizes = solid.shape
    blocked = jnp.stack(
        [inner_window(padded_solid, OFFSET_TABLE[number], sizes) != 0 for number in range(27)]
    )
    fluid_cells = (solid == 0)[None]
    grp_index = lax.axis_index("grp")
    last_grp = lax.axis_size("grp") - 1
    relax_time = relaxation(phase_ids, conductivity)
    speed_brick = velocity_prev
    popul = populations
    heat_pops = thermal
    for window_number in range(WINDOWS):
        heat_brick = lax.all_to_all(
            jnp.sum(heat_pops, axis=0), "grp", split_axis=2, concat_axis=0, tiled=True
        )
        speed_column = lax.all_to_all(speed_brick, "grp", split_axis=1, concat_axis=3, tiled=True)
        for step_number in range(STEPS):
            post = collide(popul, heat_brick, rates)
            arrived = flow_arrivals(post)
            popul = jnp.where(fluid_cells, jnp.where(blocked, post[::-1], arrived), popul)
        for step_number in range(STEPS):
            heat_pops = stream_heat(
                heat_collide(heat_pops, speed_column, relax_time), grp_index, last_grp
            )
        if window_number + 1 < WINDOWS:
            speed_brick = flow_speed(popul, heat_brick, solid)
    return (popul, heat_pops)


SUBLANES = 8
LANES = 128
F32 = jnp.float32


class Slab:
    def __init__(self, mesh_shape, flow_block, heat_block):
        self.grp, self.gx, self.gy = (mesh_shape[name] for name in ("grp", "gx", "gy"))
        self.block_x, self.block_y, self.block_z = flow_block
        self.sub = self.gx * self.gy
        self.planes = self.block_z // self.sub
        self.halo = self.planes // 2
        self.fits = (
            self.block_y == SUBLANES
            and self.block_z == LANES
            and self.planes * self.sub == LANES
            and self.halo * 2 == self.planes
            and WINDOWS == 2
            and self.halo == STEPS * WINDOWS
            and self.sub >= 8
            and 2 * self.block_x == self.sub
            and self.block_x == self.grp
            and heat_block == (1, SUBLANES, self.grp * LANES)
            and self.sub & (self.sub - 1) == 0
            and self.grp & (self.grp - 1) == 0
            and self.gy % 2 == 0
            and self.sub % self.grp == 0
        )
        if self.fits:
            self.turn = self.sub // self.grp
            partners = [step for k in (1, 0) for step in range(self.sub - 2 + k, 1, -2)]
            partners.sort(key=lambda step: bin(step >> 1).count("1"))
            self.steps = [0, 1] + partners
            self.ring = [
                part * self.sub + self.round_plane((place - self.turn * part) % self.sub)
                for part in range(self.grp)
                for place in range(self.sub)
            ]

    def round_plane(self, number):
        x, y = number // self.gy, number % self.gy
        back = x % 2
        return x * self.gy + y + back * (self.gy - 1 - 2 * y)

    def holders(self, part):
        begin = self.sub * self.grp - self.turn * part
        mine = self.place_in_plane()
        return [
            jnp.bitwise_xor(self.round_plane(lax.rem(begin + place, self.sub)), mine)
            for place in range(self.sub)
        ]

    def planes_far_first(self):
        return [0] + list(range(self.grp - 1, 0, -1))

    def place_in_plane(self):
        return lax.axis_index("gx") * self.gy + lax.axis_index("gy")


def lane_index():
    return lax.broadcasted_iota(jnp.int32, (SUBLANES, LANES), 1)


def row_index():
    return lax.broadcasted_iota(jnp.int32, (SUBLANES, LANES), 0)


def lane_roll(value, amount):
    amount = amount % LANES
    return value if amount == 0 else pltpu.roll(value, amount, 1)


def swap_groups(values, group):
    count = len(values)
    lane = lane_index()
    values = list(values)
    bit = 1
    while bit < count:
        low = (lane // (group * bit)) % 2 == 0
        for first in range(count):
            if first & bit == 0:
                a, b = values[first], values[first | bit]
                if 2 * group * bit == LANES:
                    crossed = lane_roll(jnp.where(low, b, a), group * bit)
                    values[first] = jnp.where(low, a, crossed)
                    values[first | bit] = jnp.where(low, crossed, b)
                    continue
                values[first] = jnp.where(low, a, lane_roll(b, group * bit))
                values[first | bit] = jnp.where(low, lane_roll(a, -group * bit), b)
        bit *= 2
    return values


SPEED_AT, SOLID_AT = 27, 30
IN_PAIRS = 16
FLOW_PAIRS = 14


def pack_in(
    slab, levels_hbm, popul_hbm, speed_hbm, solid_hbm, heat_hbm, phase_hbm, sent, *scratch
):
    levels_ref, fields, solid_ref, heat_ref, phase_ref, sems = scratch
    copies = [
        pltpu.make_async_copy(source, target, sems.at[number])
        for number, (source, target) in enumerate(
            [
                (heat_hbm, heat_ref),
                (phase_hbm, phase_ref),
                (levels_hbm, levels_ref),
                (speed_hbm, fields.at[pl.ds(SPEED_AT, 3)]),
                (solid_hbm, solid_ref),
                (popul_hbm, fields.at[pl.ds(0, SPEED_AT)]),
            ]
        )
    ]
    for copy in copies:
        copy.start()
    for copy in copies[:3]:
        copy.wait()
    lane = lane_index()
    first = in_first_half(slab)
    columns = []
    for part in range(slab.grp):
        span = pl.ds(part * LANES, LANES)
        phase = phase_ref[0, :, span]
        chosen = jnp.zeros((SUBLANES, LANES), F32)
        for level in range(levels_ref.shape[0]):
            chosen = jnp.where(phase == level, levels_ref[level], chosen)
        columns.append([heat_ref[k, 0, :, span] for k in range(7)] + [1.0 / (0.5 + 4.0 * chosen)])
    for part in range(slab.grp):
        own, after = columns[part], columns[(part + 1) % slab.grp]
        before = columns[part - 1]
        beside = []
        for k in range(8):
            above = jnp.where(lane < slab.planes, after[k], own[k])
            below = jnp.where(lane >= LANES - slab.planes, before[k], own[k])
            beside.append(
                jnp.where(first, lane_roll(above, -slab.planes), lane_roll(below, slab.planes))
            )
        holders = slab.holders(part)
        for which, sources in enumerate((own, beside)):
            for place, value in enumerate(swap_groups(sources, slab.planes)):
                sent[holders[place], IN_PAIRS + 2 * part + which] = value
    for copy in copies[3:]:
        copy.wait()
    fields[SOLID_AT] = solid_ref[...].astype(F32)
    fields[SOLID_AT + 1] = jnp.zeros(solid_ref.shape, F32)
    holders = slab.holders(lax.axis_index("grp"))
    for pair in range(IN_PAIRS):
        sources = [fields[2 * pair + h, x] for x in range(slab.block_x) for h in range(2)]
        for place, value in enumerate(swap_groups(sources, slab.planes)):
            sent[holders[place], pair] = value


def in_first_half(slab):
    return lane_index() % slab.planes < slab.halo


def collect(slab, parts, came):
    mine = slab.place_in_plane()
    for part, step in zip(parts, slab.steps):
        came[jnp.bitwise_xor(mine, step)] = part[...]


def offer_halo(slab, *refs):
    parts, (came, low_out, high_out, *heat_outs) = refs[: slab.sub], refs[slab.sub :]
    collect(slab, parts, came)
    mine = lax.axis_index("grp")
    for step, heat_out in enumerate(heat_outs):
        slots = pl.ds(IN_PAIRS + 2 * jnp.bitwise_xor(mine, step), 2)
        for tile in range(slab.sub):
            heat_out[tile] = came[tile, slots]

    def one(number, _):
        tile = 2 * number
        first = in_first_half(slab)
        for pair in range(IN_PAIRS):
            a, b = came[tile, pair], came[tile + 1, pair]
            low_out[number, pair] = jnp.where(first, a, lane_roll(b, slab.halo))
            high_out[number, pair] = jnp.where(first, lane_roll(b, -slab.halo), a)
        return 0

    lax.fori_loop(0, slab.sub // 2, one, 0)


def make_heat_tiles(slab, parts, held, heat_tiles):
    mine = lax.axis_index("grp")
    for step, part in zip(slab.planes_far_first(), parts):
        held[jnp.bitwise_xor(mine, step)] = part[...]
    first = in_first_half(slab)
    for tile in range(slab.sub):
        sources = []
        for x in range(slab.block_x):
            after = held[(x + 1) % slab.block_x, tile, 1]
            sources += [held[x, tile, 0], jnp.where(first, held[x, tile, 1], after)]
        for k, value in enumerate(swap_groups(sources, slab.planes)):
            heat_tiles[k, tile] = value


def make_tiles(slab, came, below_ref, above_ref, state):
    def one(number, _):
        first = in_first_half(slab)
        even = (lane_index() // slab.planes) % 2 == 0
        back = 2 * slab.planes
        for pair in range(IN_PAIRS):
            below, above = below_ref[number, pair], above_ref[number, pair]
            beside = (
                jnp.where(first, above, lane_roll(below, -back)),
                jnp.where(first, lane_roll(above, -slab.halo), lane_roll(below, slab.halo - back)),
            )
            for which in range(2):
                tile = 2 * number + which
                own, halo = came[tile, pair], beside[which]
                state[2 * pair, tile] = jnp.where(even, own, lane_roll(halo, slab.planes))
                state[2 * pair + 1, tile] = jnp.where(even, lane_roll(own, -slab.planes), halo)
        return 0

    lax.fori_loop(0, slab.sub // 2, one, 0)


def pack_out(slab, flow, came, tile, sent):
    even = (lane_index() // slab.planes) % 2 == 0
    flags = came[tile, SOLID_AT // 2]
    solid = jnp.where(even, flags, lane_roll(flags, slab.planes)) != 0.0
    partner = jnp.bitwise_xor(tile, slab.place_in_plane())
    for pair in range(FLOW_PAIRS):
        value = flow[2 * pair]
        if 2 * pair + 1 < len(flow):
            value = jnp.where(even, value, lane_roll(flow[2 * pair + 1], slab.planes))
        sent[partner, pair] = jnp.where(solid, came[tile, pair], value)


def add_heat(slab, sent_in, *refs):
    parts, (sent, packed, sem) = refs[: slab.grp], refs[slab.grp :]
    mine = slab.place_in_plane()
    for tile in range(slab.sub):
        for step in range(slab.grp):
            packed[jnp.bitwise_xor(mine, tile), step] = parts[step][tile]
    copy = pltpu.make_async_copy(packed, sent.at[:, pl.ds(FLOW_PAIRS, slab.grp)], sem)
    copy.start()
    copy.wait()


def unpack_out(slab, *refs):
    parts, (popul_hbm, thermal_hbm, came, popul, thermal, sems) = refs[: slab.sub], refs[slab.sub :]
    for part, step in zip(parts, slab.steps):
        came[step] = part[...]
    mine = lax.axis_index("grp")
    for step in range(slab.grp):
        part = jnp.bitwise_xor(mine, step)
        holders = slab.holders(part)
        span = pl.ds(pl.multiple_of(part * LANES, LANES), LANES)
        sources = [came[holders[place], FLOW_PAIRS + step] for place in range(slab.sub)]
        for k, value in enumerate(swap_groups(sources, slab.planes)[:7]):
            thermal[k, 0, :, span] = value
    copies = [pltpu.make_async_copy(thermal, thermal_hbm, sems.at[0])]
    copies[0].start()
    holders = slab.holders(mine)
    begin = 0
    for pair in range(FLOW_PAIRS):
        sources = [came[holders[place], pair] for place in range(slab.sub)]
        for number, value in enumerate(swap_groups(sources, slab.planes)):
            if 2 * pair + number % 2 < 27:
                popul[2 * pair + number % 2, number // 2] = value
        end = min(2 * pair + 2, 27)
        if pair % 4 == 3 or end == 27:
            rows = pl.ds(begin, end - begin)
            sem = sems.at[len(copies)]
            copies.append(pltpu.make_async_copy(popul.at[rows], popul_hbm.at[rows], sem))
            copies[-1].start()
            begin = end
    for copy in copies:
        copy.wait()


def forward3(values):
    for stride in (9, 3, 1):
        out = [None] * 27
        for n in range(27):
            if n // stride % 3 == 0:
                a, b, c = values[n], values[n + stride], values[n + 2 * stride]
                both = a + c
                out[n], out[n + stride], out[n + 2 * stride] = both + b, c - a, both
        values = out
    return values


def backward3(values):
    for stride in (9, 3, 1):
        out = [None] * 27
        for n in range(27):
            if n // stride % 3 == 0:
                a, b, c = values[n], values[n + stride], values[n + 2 * stride]
                even, odd = 0.5 * c, 0.5 * b
                out[n], out[n + stride], out[n + 2 * stride] = even - odd, a - c, even + odd
        values = out
    return values


def collide_tile(values, force, rate, solid):
    moments = forward3(values)
    density = moments[0]
    jx, jy, jz = moments[9], moments[3], moments[1] + 0.5 * force
    inverse = 1.0 / density
    flux = (jx, jy, jz)
    u = tuple(j * inverse for j in flux)
    third = 1.0 / 3.0
    base = {0: density}
    for k in (1, 2, 3):
        base[k] = density * third**k
    squares = [flux[d] * u[d] for d in range(3)]
    square_at = {}
    scaled = {}

    def scale(key, value, count):
        if count == 0:
            return value
        if (key, count) not in scaled:
            scaled[key, count] = value * third**count
        return scaled[key, count]

    cross = {(0, 1): jx * u[1], (0, 2): jx * u[2], (1, 2): jy * u[2]}
    out = [None] * 27
    for n in range(27):
        powers = (n // 9, n // 3 % 3, n % 3)
        if n in (0, 3, 9):
            out[n] = moments[n]
            continue
        if n == 1:
            out[n] = moments[n] + force
            continue
        odd = tuple(d for d in range(3) if powers[d] == 1)
        even = tuple(d for d in range(3) if powers[d] == 2)
        count = len(even)
        if len(odd) == 3:
            out[n] = moments[n] - rate(n) * moments[n]
            continue
        if len(odd) == 0:
            if even not in square_at:
                total = squares[even[0]]
                for d in even[1:]:
                    total = total + squares[d]
                square_at[even] = base[count] + (total * (3.0 * third**count) if count > 1 else total)
            level = square_at[even]
        elif len(odd) == 1:
            level = scale(odd, flux[odd[0]], count)
        else:
            level = scale(odd, cross[odd], count)
        out[n] = moments[n] - rate(n) * (moments[n] - level)
    out[26] = jnp.where(solid, jnp.nan, out[26])
    return backward3(out)


HEAT_OFFSETS = [(0, 0, 0), (1, 0, 0), (-1, 0, 0), (0, 1, 0), (0, -1, 0), (0, 0, 1), (0, 0, -1)]


def collide_flow(rates_ref, flow, force, solid, target, tile):
    for n, value in enumerate(collide_tile(flow, force, lambda n: rates_ref[n], solid)):
        target[n, tile] = value


def collide_heat(heat, omega, speeds, target, tile):
    total = heat[0]
    for k in range(1, 7):
        total = total + heat[k]
    side = 0.125 * total
    half = 0.5 * total
    for k in range(7):
        if k == 0:
            level = 0.25 * total
        else:
            drift = half * speeds[(k - 1) // 2]
            level = side + drift if k % 2 == 1 else side - drift
        target[k, tile] = heat[k] - (heat[k] - level) * omega


def stream(slab, post, tile, offsets):
    block_x, block_y = lax.div(tile, slab.gy), lax.rem(tile, slab.gy)
    x_of = {a: lax.rem(block_x + slab.gx - a, slab.gx) for a in (-1, 0, 1)}
    y_of = {b: lax.rem(block_y + slab.gy - b, slab.gy) for b in (-1, 0, 1)}
    row = row_index()
    per_x = 2 * slab.planes
    in_x = (lane_index() + slab.halo) % LANES // per_x
    last_x = {1: in_x == slab.block_x - 1, -1: in_x == 0}
    last_y = {1: row == SUBLANES - 1, -1: row == 0}

    def arrive(number, offset):
        a, b, c = offset

        def take(x):
            value = post[number, x_of[x] * slab.gy + block_y]
            if b != 0:
                other = post[number, x_of[x] * slab.gy + y_of[b]]
                value = jnp.where(last_y[b], other, value)
            return value

        value = take(0)
        if a != 0:
            value = jnp.where(last_x[a], take(a), value)
        if b != 0:
            value = pltpu.roll(value, b % SUBLANES, 0)
        return lane_roll(value, a * per_x + c)

    return [arrive(number, offset) for number, offset in enumerate(offsets)]


def stream_flow(slab, post, tile):
    return [
        jnp.where(value != value, post[26 - n, tile], value)
        for n, value in enumerate(stream(slab, post, tile, OFFSET_TABLE))
    ]


def over_tiles(slab, body, unroll=1):
    def one(tile, _):
        body(tile)
        return 0

    lax.fori_loop(0, slab.sub, one, 0, unroll=unroll)


def one_ahead(slab, arrive, collide, held):
    def bring(tile):
        for number, value in enumerate(arrive(tile)):
            held[number] = value

    def body(tile):
        values = [held[number] for number in range(held.shape[0])]
        bring(lax.rem(tile + 1, slab.sub))
        collide(tile, values)

    bring(jnp.int32(0))
    over_tiles(slab, body)


def over_steps(count, body):
    def one(number, _):
        body(number)
        return 0

    lax.fori_loop(0, count, one, 0)


def first_window(slab, rates_hbm, state, *refs):
    heat_parts, refs = refs[: slab.grp], refs[slab.grp :]
    flow_out, keep_out, heat_outs = refs[0], refs[1], refs[2 : 2 + slab.grp]
    (rates_ref, sem, speed, heat_tiles, flow_post, heat_post, heat_a, heat_b, held, came_heat, ahead) = (
        refs[2 + slab.grp :]
    )
    rates_copy = pltpu.make_async_copy(rates_hbm, rates_ref, sem)
    rates_copy.start()
    make_heat_tiles(slab, heat_parts, came_heat, heat_tiles)
    rates_copy.wait()

    def speeds_of(tile):
        return [speed[d, tile] for d in range(3)]

    def begin(tile):
        solid = state[SOLID_AT, tile]
        heat = [heat_tiles[k, tile] for k in range(7)]
        for d in range(3):
            speed[d, tile] = state[SPEED_AT + d, tile]
        force = heat_force(heat)
        keep_out[0, tile] = force
        keep_out[1, tile] = solid
        flow = [state[n, tile] for n in range(27)]
        collide_flow(rates_ref, flow, force, solid != 0.0, flow_post.at[0], tile)
        collide_heat(heat, heat_tiles[7, tile], speeds_of(tile), heat_post.at[0], tile)

    over_tiles(slab, begin)

    def arrive(tile, source):
        flow = stream_flow(slab, flow_post.at[source], tile)
        return flow + stream(slab, heat_post.at[source], tile, HEAT_OFFSETS)

    def step(number):
        source = lax.rem(number, 2)

        def go_on(tile, values):
            flow, heat = values[:27], values[27:]
            solid = state[SOLID_AT, tile] != 0.0
            collide_flow(rates_ref, flow, keep_out[0, tile], solid, flow_post.at[1 - source], tile)
            omega = heat_tiles[7, tile]
            collide_heat(heat, omega, speeds_of(tile), heat_post.at[1 - source], tile)

        one_ahead(slab, lambda tile: arrive(tile, source), go_on, ahead)

    over_steps(STEPS - 1, step)
    source = (STEPS - 1) % 2

    def next_window(tile, values):
        flow, heat = values[:27], values[27:]
        solid = state[SOLID_AT, tile] != 0.0
        speeds = [
            jnp.where(solid, 0.0, each) for each in flow_speed_tile(flow, keep_out[0, tile])
        ]
        for d in range(3):
            speed[d, tile] = speeds[d]
        force = heat_force(heat)
        keep_out[0, tile] = force
        collide_flow(rates_ref, flow, force, solid, flow_out, tile)
        collide_heat(heat, heat_tiles[7, tile], speeds, heat_a, tile)

    one_ahead(slab, lambda tile: arrive(tile, source), next_window, ahead)
    here, there = heat_a, heat_b
    for _ in range(STEPS - 1):

        def heat_alone(tile, here=here, there=there):
            heat = stream(slab, here, tile, HEAT_OFFSETS)
            collide_heat(heat, heat_tiles[7, tile], speeds_of(tile), there, tile)

        over_tiles(slab, heat_alone, unroll=4)
        here, there = there, here
    zero = jnp.zeros((SUBLANES, LANES), F32)

    def end_heat(tile):
        heat = stream(slab, here, tile, HEAT_OFFSETS)
        heat += [zero] * (slab.sub - 7)
        for x, value in enumerate(swap_groups(heat, slab.planes)[0::2]):
            held[x, tile] = value

    over_tiles(slab, end_heat, unroll=2)
    mine = lax.axis_index("grp")
    for step_number in range(slab.grp):
        heat_outs[step_number][...] = held[jnp.bitwise_xor(mine, step_number)]


def last_window(slab, rates_hbm, came, flow_in, keep_ref, sent, *refs):
    rates_ref, sem, flow_a, flow_b, ahead = refs
    fetch = pltpu.make_async_copy(rates_hbm, rates_ref, sem)
    fetch.start()
    fetch.wait()
    source, target, spare = flow_in, flow_a, flow_b
    for _ in range(STEPS - 1):

        def go_on(tile, flow, target=target):
            solid = keep_ref[1, tile] != 0.0
            collide_flow(rates_ref, flow, keep_ref[0, tile], solid, target, tile)

        one_ahead(slab, lambda tile, source=source: stream_flow(slab, source, tile), go_on, ahead)
        source, target, spare = target, spare, target

    def end(tile, flow):
        pack_out(slab, flow, came, tile, sent)

    one_ahead(slab, lambda tile: stream_flow(slab, source, tile), end, ahead)


def heat_force(heat):
    total = heat[0]
    for k in range(1, 7):
        total = total + heat[k]
    return BUOYANCY * (total - REFERENCE_HEAT)


def flow_speed_tile(values, force):
    total = values[0]
    for n in range(1, 27):
        total = total + values[n]
    sums = []
    for d in range(3):
        plus, minus = None, None
        for n in range(27):
            part = OFFSET_TABLE[n][d]
            if part == 1:
                plus = values[n] if plus is None else plus + values[n]
            if part == -1:
                minus = values[n] if minus is None else minus + values[n]
        sums.append(plus - minus)
    sums[2] = sums[2] + 0.5 * force
    return [each / total for each in sums]


def local_call(body, slab, arrays, outs, scratch=(), in_hbm=0, carried=False, outs_in_hbm=False):
    def kernel(*refs):
        body(slab, *refs)

    return pl.pallas_call(
        kernel,
        out_shape=[jax.ShapeDtypeStruct(shape, F32) for shape in outs],
        in_specs=[
            pl.BlockSpec(
                memory_space=pltpu.HBM if i < in_hbm else pl.ANY if carried and i == 0 else pltpu.VMEM
            )
            for i in range(len(arrays))
        ],
        out_specs=[
            pl.BlockSpec(memory_space=pl.ANY if carried or outs_in_hbm else pltpu.VMEM)
        ]
        * len(outs),
        input_output_aliases={0: 0} if carried else {},
        scratch_shapes=[pltpu.VMEM(s, F32) if isinstance(s, tuple) else s for s in scratch],
        compiler_params=pltpu.CompilerParams(vmem_limit_bytes=24 * 1024 * 1024),
    )(
        *(
            pltpu.with_memory_space_constraint(array, pltpu.HBM) if i < in_hbm else array
            for i, array in enumerate(arrays)
        )
    )


RING = ("grp", "gx", "gy")


def exchange(slab, low, high):
    ring = slab.ring
    upward = [(ring[i - 1], ring[i]) for i in range(len(ring))]
    from_below = lax.ppermute(high, RING, upward)
    from_above = lax.ppermute(low, RING, [(b, a) for a, b in upward])
    return from_below, from_above


def across_plane(slab, sent):
    came = {0: sent[0]}
    for step in slab.steps[1:]:
        pairs = [(i, i ^ step) for i in range(slab.sub)]
        came[step] = lax.ppermute(sent[step], ("gx", "gy"), pairs)
    return [came[step] for step in slab.steps]


def across_planes(slab, parts):
    return [parts[0]] + [
        lax.ppermute(parts[step], "grp", [(i, i ^ step) for i in range(slab.grp)])
        for step in range(1, slab.grp)
    ]


def on_slabs(slab, populations, thermal, velocity_prev, solid, phase_ids, conductivity, rates):
    tile = (SUBLANES, LANES)

    def vmem_like(array):
        return pltpu.VMEM(array.shape, array.dtype)

    sent_shape = (slab.sub, IN_PAIRS + 2 * slab.grp) + tile
    (sent,) = local_call(
        pack_in,
        slab,
        [conductivity, populations, velocity_prev, solid, thermal, phase_ids],
        [sent_shape],
        [
            pltpu.SMEM(conductivity.shape, F32),
            (2 * IN_PAIRS,) + solid.shape,
            vmem_like(solid),
            vmem_like(thermal),
            vmem_like(phase_ids),
            pltpu.SemaphoreType.DMA((6,)),
        ],
        in_hbm=6,
    )
    plane = (slab.sub,) + tile
    halo_shape = (slab.sub // 2, IN_PAIRS) + tile
    heat_shape = (slab.sub, 2) + tile
    came, low, high, *parts = local_call(
        offer_halo,
        slab,
        across_plane(slab, sent),
        [sent_shape, halo_shape, halo_shape] + [heat_shape] * slab.grp,
    )
    below, above = exchange(slab, low, high)
    parts = across_planes(slab, parts)
    (state,) = local_call(make_tiles, slab, [came, below, above], [(2 * IN_PAIRS,) + plane])
    scalars = [pltpu.SMEM(rates.shape, F32), pltpu.SemaphoreType.DMA]
    flow, keep, *parts = local_call(
        first_window,
        slab,
        [rates, state] + [parts[step] for step in slab.planes_far_first()],
        [(27,) + plane, (2,) + plane] + [plane] * slab.grp,
        scalars
        + [(3,) + plane, (8,) + plane, (2, 27) + plane, (2, 7) + plane]
        + [(7,) + plane] * 2
        + [(slab.grp,) + plane, (slab.grp,) + heat_shape, (34,) + tile],
        in_hbm=1,
    )
    parts = across_planes(slab, parts)
    last_shape = (slab.sub, FLOW_PAIRS + slab.grp) + tile
    (sent,) = local_call(
        last_window,
        slab,
        [rates, came, flow, keep],
        [last_shape],
        scalars + [(27,) + plane, (27,) + plane, (27,) + tile],
        in_hbm=1,
    )
    (sent,) = local_call(
        add_heat,
        slab,
        [sent] + parts,
        [last_shape],
        [(slab.sub, slab.grp) + tile, pltpu.SemaphoreType.DMA],
        carried=True,
    )
    return tuple(
        local_call(
            unpack_out,
            slab,
            across_plane(slab, sent),
            [populations.shape, thermal.shape],
            [
                last_shape,
                populations.shape,
                thermal.shape,
                pltpu.SemaphoreType.DMA((1 + -(-FLOW_PAIRS // 4),)),
            ],
            outs_in_hbm=True,
        )
    )


def solution(mesh):
    in_specs = (
        P(None, "gx", "gy", "grp"),
        P(None, ("gx", "grp"), "gy", None),
        P(None, "gx", "gy", "grp"),
        P("gx", "gy", "grp"),
        P(("gx", "grp"), "gy", None),
        P(),
        P(),
    )
    out_specs = (P(None, "gx", "gy", "grp"), P(None, ("gx", "grp"), "gy", None))

    def per_device(populations, thermal, *others):
        slab = Slab(mesh.shape, populations.shape[1:], thermal.shape[1:])
        plan = (lambda *arrays: on_slabs(slab, *arrays)) if slab.fits else on_device
        return plan(populations, thermal, *others)

    return jax.shard_map(
        per_device, mesh=mesh, in_specs=in_specs, out_specs=out_specs, check_vma=False
    )
```
